128 devices in a mesh: seq: 32 (over x, z, core), tp: 4 (over y).
Axes of the slice: x: 4, y: 4, z: 4, core: 2. Of those that a mesh axis runs over, the one named last changes fastest.
Arguments:
- tokens: bfloat16 [16384, 1024], P('seq'), may hold values from -6 to 6
- segment_start: int32 [8, 4], replicated, may hold values from 0 to 1, as said below
- norm_win: float32 [1024], replicated, may hold values from 0.5 to 1.5
- qkv_win: bfloat16 [1024, 3, 1024], P(None, None, 'tp'), may hold values from -0.1875 to 0.1875
- out_win: bfloat16 [1024, 1024], P('tp'), may hold values from -2 to 2
- norm_wffn: float32 [1024], replicated, may hold values from 0.5 to 1.5
- up_win: bfloat16 [1024, 4096], P(None, 'tp'), may hold values from -0.1875 to 0.1875
- down_win: bfloat16 [4096, 1024], P('tp'), may hold values from -0.09375 to 0.09375
- norm_tok: float32 [1024], replicated, may hold values from 0.5 to 1.5
- qkv_tok: bfloat16 [1024, 3, 1024], P(None, None, 'tp'), may hold values from -0.1875 to 0.1875
- out_tok: bfloat16 [2, 1024, 1024], P(None, 'tp'), may hold values from -2 to 2
- norm_ffn: float32 [1024], replicated, may hold values from 0.5 to 1.5
- up_tok: bfloat16 [1024, 4096], P(None, 'tp'), may hold values from -0.1875 to 0.1875
- down_tok: bfloat16 [4096, 1024], P('tp'), may hold values from -0.09375 to 0.09375
- norm_state: float32 [1024], replicated, may hold values from 0.5 to 1.5
- qkv_state: bfloat16 [1024, 3, 1024], P(None, None, 'tp'), may hold values from -0.1875 to 0.1875
- out_state: bfloat16 [2, 1024, 1024], P(None, 'tp'), may hold values from -2 to 2
- gate_bias: float32 [2, 1024], replicated, may hold values from 0 to 5
- norm_sffn: float32 [1024], replicated, may hold values from 0.5 to 1.5
- up_state: bfloat16 [1024, 4096], P(None, 'tp'), may hold values from -0.1875 to 0.1875
- down_state: bfloat16 [4096, 1024], P('tp'), may hold values from -0.09375 to 0.09375
- init_state: bfloat16 [512, 1024], replicated, may hold values from -6 to 6
- cotangent: bfloat16 [16384, 1024], P('seq'), may hold values from -6 to 6
Outputs:
- layer_output: bfloat16 [16384, 1024], P('seq')
- block_states: bfloat16 [16384, 1024], P('seq')
- grad_tokens: bfloat16 [16384, 1024], P('seq')
- grad_norm_win: float32 [1024], P('seq')
- grad_qkv_win: float32 [1024, 3, 1024], P('seq', None, 'tp')
- grad_out_win: float32 [1024, 1024], P('tp', 'seq')
- grad_norm_wffn: float32 [1024], P('seq')
- grad_up_win: float32 [1024, 4096], P('seq', 'tp')
- grad_down_win: float32 [4096, 1024], P('tp', 'seq')
- grad_norm_tok: float32 [1024], P('seq')
- grad_qkv_tok: float32 [1024, 3, 1024], P('seq', None, 'tp')
- grad_out_tok: float32 [2, 1024, 1024], P(None, 'tp', 'seq')
- grad_norm_ffn: float32 [1024], P('seq')
- grad_up_tok: float32 [1024, 4096], P('seq', 'tp')
- grad_down_tok: float32 [4096, 1024], P('tp', 'seq')
- grad_norm_state: float32 [1024], P('seq')
- grad_qkv_state: float32 [1024, 3, 1024], P('seq', None, 'tp')
- grad_out_state: float32 [2, 1024, 1024], P(None, 'tp', 'seq')
- grad_gate_bias: float32 [2, 1024], P(None, 'seq')
- grad_norm_sffn: float32 [1024], P('seq')
- grad_up_state: float32 [1024, 4096], P('seq', 'tp')
- grad_down_state: float32 [4096, 1024], P('tp', 'seq')
- grad_init_state: float32 [512, 1024], P(None, 'seq')
The draws below stay inside these ranges and needn't reach their ends.
Inputs may be any that keep to these rules, and one draw needn't show every extreme that they name: segment_start[m, 0] = 1 for every m; segment_start[m, j] may be 1 only at j = 2 besides, so that segments span 4 or 2 blocks; at least one sequence is a single segment.
All inputs are finite; a program needn't handle non-finite values.
Results may differ from the reference program's by a relative error of at most 0.03.
Values may be sent and summed in bfloat16 or wider, within the bound.
No kernel may reach another device: no remote copies, remote signals or barrier semaphores. Data moves between devices by JAX's collectives and lax.ppermute only.
A program may use at most 256 MiB of HBM per device.

```python
from functools import partial
import jax
import jax.numpy as jnp
from jax import lax

D = 1024
H = 8
E = 128
FF = 4096
S = 512
BLK = 512
CHAIN = 4
MICRO = 8
TOKENS = 16384
STATES = 16384


def draw_segment_start(key, part):
    key = jax.random.fold_in(key, 7)
    split_key, whole_key = jax.random.split(key)
    halves = jax.random.randint(split_key, (MICRO,), 0, 2)
    whole_one = jax.random.randint(whole_key, (), 0, MICRO)
    middle = jnp.where(jnp.arange(MICRO) == whole_one, 0, halves)
    column_ids = lax.broadcasted_iota(jnp.int32, (MICRO, CHAIN), 1)
    marked = jnp.where(column_ids == CHAIN // 2, middle[:, None], 0)
    return jnp.where(column_ids == 0, 1, marked).astype(jnp.int32)


def shard_levels(key, shape, cuts, low, top_value):
    loudness = 1.0
    for axis_at, parts in cuts:
        heights = jax.random.uniform(jax.random.fold_in(jax.random.fold_in(key, 6), axis_at), (parts,), jnp.float32, low / len(cuts), top_value / len(cuts))
        loudness = loudness * jnp.repeat(jnp.exp(heights), shape[axis_at] // parts).reshape((-1,) + (1,) * (len(shape) - 1 - axis_at))
    return loudness


def bell_draw(stream_key, shape, scale, limit, cuts=(), held_as=jnp.bfloat16):
    drawn = scale * jax.random.normal(stream_key, shape, jnp.float32)
    if cuts:
        drawn = drawn * shard_levels(stream_key, shape, cuts, -0.22, 0.18)
    return jnp.clip(drawn, -limit, limit).astype(held_as)


def setup_inputs(seed: int = 0) -> dict:
    arg_keys = jax.random.split(jax.random.key(seed), 24)
    return {
        "tokens": bell_draw(arg_keys[0], (TOKENS, D), 1.0, 6.0, ((0, 32),)),
        "segment_start": draw_segment_start(jax.random.fold_in(arg_keys[23], 71), 0),
        "norm_win": jnp.clip(1.0 + 0.1 * jax.random.normal(arg_keys[2], (D,), jnp.float32), 0.5, 1.5),
        "qkv_win": bell_draw(arg_keys[3], (D, 3, H * E), D ** -0.5, 0.1875, ((2, 4),)),
        "out_win": bell_draw(arg_keys[4], (H * E, D), (max(H * E // 128, 1)) ** -0.5, 2.0, ((0, 4),)),
        "norm_wffn": jnp.clip(1.0 + 0.1 * jax.random.normal(arg_keys[5], (D,), jnp.float32), 0.5, 1.5),
        "up_win": bell_draw(arg_keys[6], (D, FF), D ** -0.5, 0.1875, ((1, 4),)),
        "down_win": bell_draw(arg_keys[7], (FF, D), FF ** -0.5, 0.09375, ((0, 4),)),
        "norm_tok": jnp.clip(1.0 + 0.1 * jax.random.normal(arg_keys[8], (D,), jnp.float32), 0.5, 1.5),
        "qkv_tok": bell_draw(arg_keys[9], (D, 3, H * E), D ** -0.5, 0.1875, ((2, 4),)),
        "out_tok": bell_draw(arg_keys[10], (2, H * E, D), (max(H * E // 128, 1)) ** -0.5, 2.0, ((1, 4),)),
        "norm_ffn": jnp.clip(1.0 + 0.1 * jax.random.normal(arg_keys[11], (D,), jnp.float32), 0.5, 1.5),
        "up_tok": bell_draw(arg_keys[12], (D, FF), D ** -0.5, 0.1875, ((1, 4),)),
        "down_tok": bell_draw(arg_keys[13], (FF, D), FF ** -0.5, 0.09375, ((0, 4),)),
        "norm_state": jnp.clip(1.0 + 0.1 * jax.random.normal(arg_keys[14], (D,), jnp.float32), 0.5, 1.5),
        "qkv_state": bell_draw(arg_keys[15], (D, 3, H * E), D ** -0.5, 0.1875, ((2, 4),)),
        "out_state": bell_draw(arg_keys[16], (2, H * E, D), (max(H * E // 128, 1)) ** -0.5, 2.0, ((1, 4),)),
        "gate_bias": jnp.clip(jax.random.uniform(arg_keys[17], (2, D), jnp.float32, 0.0, 5.0), 0.0, 5.0),
        "norm_sffn": jnp.clip(1.0 + 0.1 * jax.random.normal(arg_keys[18], (D,), jnp.float32), 0.5, 1.5),
        "up_state": bell_draw(arg_keys[19], (D, FF), D ** -0.5, 0.1875, ((1, 4),)),
        "down_state": bell_draw(arg_keys[20], (FF, D), FF ** -0.5, 0.09375, ((0, 4),)),
        "init_state": bell_draw(arg_keys[21], (S, D), 1.0, 6.0),
        "cotangent": bell_draw(arg_keys[22], (TOKENS, D), 1.0, 6.0, ((0, 32),)),
    }


PRECISE = lax.Precision.HIGHEST
EPSILON = 1e-05
MASKED = -1e+30

@jax.custom_vjp
def low(v):
    return lax.optimization_barrier(v.astype(jnp.bfloat16)).astype(jnp.float32)

@jax.custom_vjp
def low_back(v):
    return v

def low_keep(v):
    return (low(v), None)

def low_pass(kept, grad):
    return (grad,)

def back_keep(v):
    return (v, None)

def back_low(kept, grad):
    return (low(grad),)
low.defvjp(low_keep, low_pass)
low_back.defvjp(back_keep, back_low)

def layer_norm(matrix, weights):
    average = lax.optimization_barrier(jnp.mean(matrix, axis=-1, keepdims=True))
    centred = matrix - average
    spread = lax.optimization_barrier(jnp.mean(centred * centred, axis=-1, keepdims=True))
    return centred * lax.rsqrt(spread + EPSILON) * weights

def rounded_both(matrix):
    return low(low_back(matrix))

def project(matrix, weights):
    return jnp.dot(matrix, weights, precision=PRECISE, preferred_element_type=jnp.float32)

def attend(queries, key_rows, value_rows, allowed):
    row_count = queries.shape[0]
    query_heads = queries.reshape(row_count, H, E)
    key_heads = key_rows.reshape(key_rows.shape[0], H, E)
    value_heads = value_rows.reshape(value_rows.shape[0], H, E)
    raw_scores = low_back(jnp.einsum('rhe,khe->hrk', query_heads, key_heads, precision=PRECISE))
    scores = jnp.where(allowed, raw_scores * E ** (-0.5), MASKED)
    row_max = lax.optimization_barrier(jnp.max(scores, axis=-1, keepdims=True))
    powers = jnp.exp(scores - row_max)
    chances = low(powers / lax.optimization_barrier(jnp.sum(powers, axis=-1, keepdims=True)))
    result = jnp.einsum('hrk,khe->rhe', chances, value_heads, precision=PRECISE)
    return rounded_both(result.reshape(row_count, H * E))

def run_block(weights, loop_carry, block_inputs):
    norm_win, qkv_win, out_win, norm_wffn, up_win, down_win, norm_tok, qkv_tok, out_tok, norm_ffn, up_tok, down_tok, norm_state, qkv_state, out_state, gate_bias, norm_sffn, up_state, down_state, init_state = weights
    state_prev, win_keys_prev, win_values_prev, keys_prev, values_prev = loop_carry
    block_tokens, start_flag = block_inputs
    starts_here = start_flag == 1
    row_ids = lax.broadcasted_iota(jnp.int32, (BLK, 2 * BLK), 0)
    col_ids = lax.broadcasted_iota(jnp.int32, (BLK, 2 * BLK), 1)
    allowed = (col_ids >= BLK) & (col_ids - BLK <= row_ids) | (col_ids < BLK) & (col_ids > row_ids) & jnp.logical_not(starts_here)
    win_normed = low(layer_norm(block_tokens, norm_win))
    win_parts = jnp.split(project(win_normed, qkv_win.reshape(D, 3 * H * E)), 3, axis=1)
    win_queries = rounded_both(win_parts[0])
    win_keys = rounded_both(win_parts[1])
    win_values = rounded_both(win_parts[2])
    win_heads = attend(win_queries, jnp.concatenate([win_keys_prev, win_keys]), jnp.concatenate([win_values_prev, win_values]), allowed)
    win_mixed = block_tokens + low_back(project(win_heads, out_win))
    win_ffn_in = low(layer_norm(win_mixed, norm_wffn))
    win_hidden = low_back(project(win_ffn_in, up_win))
    win_active = low(jax.nn.gelu(win_hidden, approximate=False))
    token_rows = win_mixed + low_back(project(win_active, down_win))
    incoming = jnp.where(starts_here, init_state, state_prev)
    normed = low(layer_norm(token_rows, norm_tok))
    token_parts = jnp.split(project(normed, qkv_tok.reshape(D, 3 * H * E)), 3, axis=1)
    queries = rounded_both(token_parts[0])
    key_rows = rounded_both(token_parts[1])
    value_rows = rounded_both(token_parts[2])
    state_normed = low(layer_norm(incoming, norm_state))
    state_parts = jnp.split(project(state_normed, qkv_state.reshape(D, 3 * H * E)), 3, axis=1)
    state_queries = rounded_both(state_parts[0])
    state_keys = rounded_both(state_parts[1])
    state_values = rounded_both(state_parts[2])
    own_heads = attend(queries, jnp.concatenate([keys_prev, key_rows]), jnp.concatenate([values_prev, value_rows]), allowed)
    cross_heads = attend(queries, state_keys, state_values, True)
    mixed_one = token_rows + low_back(project(jnp.concatenate([own_heads, cross_heads], axis=1), out_tok.reshape(2 * H * E, D)))
    ffn_in = low(layer_norm(mixed_one, norm_ffn))
    hidden = low_back(project(ffn_in, up_tok))
    active = low(jax.nn.gelu(hidden, approximate=False))
    layer_output = mixed_one + low_back(project(active, down_tok))
    state_own = attend(state_queries, state_keys, state_values, True)
    state_cross = attend(state_queries, key_rows, value_rows, True)
    update = low_back(project(jnp.concatenate([state_own, state_cross], axis=1), out_state.reshape(2 * H * E, D)))
    keep_gates = jax.nn.sigmoid(gate_bias)
    mid_state = keep_gates[0] * incoming + (1.0 - keep_gates[0]) * update
    state_ffn_in = low(layer_norm(mid_state, norm_sffn))
    state_hidden = low_back(project(state_ffn_in, up_state))
    state_active = low(jax.nn.gelu(state_hidden, approximate=False))
    state_mlp = low_back(project(state_active, down_state))
    state_next = low(keep_gates[1] * mid_state + (1.0 - keep_gates[1]) * state_mlp)
    return ((state_next, win_keys, win_values, key_rows, value_rows), (layer_output, state_next))

def run_sequence(weights, token_blocks, start_flags):
    zero_rows = jnp.zeros((BLK, H * E), jnp.float32)
    block_step = jax.checkpoint(partial(run_block, weights))
    loop_carry = (weights[-1], zero_rows, zero_rows, zero_rows, zero_rows)
    loop_carry, (outputs, states) = lax.scan(block_step, loop_carry, (token_blocks, start_flags))
    return (outputs, states)

def reference(tokens, segment_start, norm_win, qkv_win, out_win, norm_wffn, up_win, down_win, norm_tok, qkv_tok, out_tok, norm_ffn, up_tok, down_tok, norm_state, qkv_state, out_state, gate_bias, norm_sffn, up_state, down_state, init_state, cotangent):
    weights = tuple((argument.astype(jnp.float32) for argument in (norm_win, qkv_win, out_win, norm_wffn, up_win, down_win, norm_tok, qkv_tok, out_tok, norm_ffn, up_tok, down_tok, norm_state, qkv_state, out_state, gate_bias, norm_sffn, up_state, down_state, init_state)))

    def forward(weights_in, token_values):
        token_blocks = token_values.reshape(MICRO, CHAIN, BLK, D)

        def one_sequence(paired):
            return run_sequence(weights_in, paired[0], paired[1])
        outputs, states = lax.map(one_sequence, (token_blocks, segment_start))
        return (outputs.reshape(TOKENS, D), states.reshape(STATES, D))
    layer_output, pullback, block_states = jax.vjp(forward, weights, tokens.astype(jnp.float32), has_aux=True)
    weight_grads, token_grads = pullback(cotangent.astype(jnp.float32))
    results = [layer_output.astype(jnp.bfloat16), block_states.astype(jnp.bfloat16), token_grads.astype(jnp.bfloat16)]
    results = results + [grad.astype(jnp.float32) for grad in weight_grads]
    return (results[0], results[1], results[2], results[3], results[4], results[5], results[6], results[7], results[8], results[9], results[10], results[11], results[12], results[13], results[14], results[15], results[16], results[17], results[18], results[19], results[20], results[21], results[22])
```

```python
import jax
import jax.numpy as jnp
from jax import lax
from jax.sharding import PartitionSpec as P

E = 128
CHAIN = 4
CORES = 2

EPSILON = 1e-05
MASKED = -1e30
LOW = jnp.bfloat16
HIGH = jnp.float32


def layer_norm(matrix, weights):
    average = jnp.mean(matrix, axis=-1, keepdims=True)
    centred = matrix - average
    spread = jnp.mean(centred * centred, axis=-1, keepdims=True)
    return centred * lax.rsqrt(spread + EPSILON) * weights


def gelu_exact(matrix):
    return jax.nn.gelu(matrix, approximate=False)


def gelu_slope(matrix, grad):
    return jax.vjp(gelu_exact, matrix)[1](grad)[0]


def plain_dot(former, latter):
    return jnp.dot(former, latter, preferred_element_type=HIGH)


def dot_first(former, latter):
    return lax.dot_general(
        former, latter, (((0,), (0,)), ((), ())), preferred_element_type=HIGH
    )


def dot_second(former, latter):
    return lax.dot_general(
        former, latter, (((1,), (1,)), ((), ())), preferred_element_type=HIGH
    )


def tp_from(array, k):
    n = lax.axis_size("tp")
    return lax.ppermute(array, "tp", [((i + k) % n, i) for i in range(n)])


def tp_to(array, k):
    n = lax.axis_size("tp")
    return lax.ppermute(array, "tp", [(i, (i + k) % n) for i in range(n)])


def far_first(n):
    return sorted(range(1, n), key=lambda k: -min(k, n - k))


def tp_gather(piece):
    n = lax.axis_size("tp")
    found = {k: tp_from(piece, k) for k in far_first(n)}
    return [piece] + [found[k] for k in range(1, n)]


def tp_scatter(parts):
    n = lax.axis_size("tp")
    total = parts[0]
    for k in far_first(n):
        total = total + tp_to(parts[k].astype(LOW), k).astype(HIGH)
    return total


def split_rows(matrix, n):
    size = matrix.shape[0] // n
    return [matrix[k * size : (k + 1) * size] for k in range(n)]


def group_pairs(k):
    n = lax.axis_size("seq")
    return [(s, s - s % CHAIN + (s + k) % CHAIN) for s in range(n)]


def pos_to(array, k):
    return lax.ppermute(array, "seq", group_pairs(k))


def pos_from(array, k):
    return lax.ppermute(array, "seq", group_pairs(-k))


def pos_gather(piece):
    return [piece] + [pos_from(piece, k) for k in range(1, CHAIN)]


def pos_scatter(parts):
    total = parts[0]
    for k in range(1, CHAIN):
        total = total + pos_to(parts[k].astype(LOW), k).astype(HIGH)
    return total


def choose(stacked, index):
    return lax.dynamic_index_in_dim(stacked, index, 0, keepdims=False)


def turned(array, start):
    twice = jnp.concatenate([array, array])
    return lax.dynamic_slice_in_dim(twice, start, array.shape[0], 0)


def seq_sum(grads):
    n = lax.axis_size("seq")
    z_size = 4 if n % 8 == 0 else n // CORES
    x_size = n // (z_size * CORES)
    here = lax.axis_index("seq")
    core, z_at, x_at = here % CORES, here // CORES % z_size, here // (CORES * z_size)

    def place(x, z, c):
        return (x % x_size * z_size + z % z_size) * CORES + c % CORES

    def pairs(dx, dz, dc):
        return [
            (place(x, z, c), place(x + dx, z + dz, c + dc))
            for x in range(x_size)
            for z in range(z_size)
            for c in range(CORES)
        ]

    def stage(array, dim, at, size, step):
        total = lax.dynamic_index_in_dim(array, at, dim, False).astype(HIGH)
        for k in far_first(size):
            sent = lax.dynamic_index_in_dim(array, (at + k) % size, dim, False)
            total = total + lax.ppermute(sent, "seq", pairs(*step(k))).astype(HIGH)
        return total.astype(LOW)

    width = grads.shape[1]
    array = grads.reshape(x_size * z_size, CORES, -1, width)
    array = stage(array, 1, core, CORES, lambda k: (0, 0, k))
    array = array.reshape(x_size, z_size, -1, width)
    half = width // 256 * 128
    one, two = array[..., :half], array[..., half:]

    def over_z(part, dim):
        return stage(part, dim, z_at, z_size, lambda k: (0, k, 0))

    def over_x(part, dim):
        return stage(part, dim, x_at, x_size, lambda k: (k, 0, 0))

    one, two = over_z(one, 1), over_x(two, 0)
    one, two = over_x(one, 0), over_z(two, 0)
    return jnp.concatenate([one, two], axis=1)


def heads_of(matrix):
    return [matrix[:, h * E : (h + 1) * E] for h in range(matrix.shape[1] // E)]


def full_attend(queries, key_rows, value_rows):
    results, logs = [], []
    for q, k, v in zip(heads_of(queries), heads_of(key_rows), heads_of(value_rows)):
        scores = dot_second(q, k) * E ** (-0.5)
        row_max = jnp.max(scores, axis=-1, keepdims=True)
        powers = jnp.exp(scores - row_max)
        totals = jnp.sum(powers, axis=-1, keepdims=True)
        results.append(plain_dot((powers / totals).astype(LOW), v).astype(LOW))
        logs.append(row_max + jnp.log(totals))
    return jnp.concatenate(results, axis=1), logs


def full_attend_back(queries, key_rows, value_rows, logs, grad_result):
    grads = ([], [], [])
    for q, k, v, log, g in zip(
        heads_of(queries), heads_of(key_rows), heads_of(value_rows), logs, heads_of(grad_result)
    ):
        chances = jnp.exp(dot_second(q, k) * E ** (-0.5) - log)
        grad_chances = dot_second(g, v)
        inner = jnp.sum(chances * grad_chances, axis=-1, keepdims=True)
        grad_scores = (chances * (grad_chances - inner) * E ** (-0.5)).astype(LOW)
        grads[0].append(plain_dot(grad_scores, k))
        grads[1].append(dot_first(grad_scores, q))
        grads[2].append(dot_first(chances.astype(LOW), g))
    return [jnp.concatenate(each, axis=1) for each in grads]


def band_scores(q, k, k_prev, below, starts_here):
    current = dot_second(q, k) * E ** (-0.5)
    before = jnp.where(starts_here, MASKED, dot_second(q, k_prev) * E ** (-0.5))
    return jnp.where(below, current, before)


def band_attend(queries, pair, pair_prev, below, starts_here):
    width = queries.shape[1]
    results, logs = [], []
    for q, k, v, kp, vp in zip(
        heads_of(queries),
        heads_of(pair[:, :width]),
        heads_of(pair[:, width:]),
        heads_of(pair_prev[:, :width]),
        heads_of(pair_prev[:, width:]),
    ):
        scores = band_scores(q, k, kp, below, starts_here)
        row_max = jnp.max(scores, axis=-1, keepdims=True)
        powers = jnp.exp(scores - row_max)
        totals = jnp.sum(powers, axis=-1, keepdims=True)
        chances = (powers / totals).astype(LOW)
        none = jnp.zeros_like(chances)
        result = plain_dot(jnp.where(below, chances, none), v) + plain_dot(
            jnp.where(below, none, chances), vp
        )
        results.append(result.astype(LOW))
        logs.append(row_max + jnp.log(totals))
    return jnp.concatenate(results, axis=1), logs


def band_attend_back(queries, pair, pair_prev, below, starts_here, logs, grad_result):
    width = queries.shape[1]
    grads = ([], [], [], [], [])
    for q, k, v, kp, vp, log, g in zip(
        heads_of(queries),
        heads_of(pair[:, :width]),
        heads_of(pair[:, width:]),
        heads_of(pair_prev[:, :width]),
        heads_of(pair_prev[:, width:]),
        logs,
        heads_of(grad_result),
    ):
        chances = jnp.exp(band_scores(q, k, kp, below, starts_here) - log)
        grad_chances = jnp.where(below, dot_second(g, v), dot_second(g, vp))
        inner = jnp.sum(chances * grad_chances, axis=-1, keepdims=True)
        grad_scores = (chances * (grad_chances - inner) * E ** (-0.5)).astype(LOW)
        low_chances = chances.astype(LOW)
        none = jnp.zeros_like(low_chances)
        scores_now = jnp.where(below, grad_scores, none)
        scores_prev = jnp.where(below, none, grad_scores)
        grads[0].append(plain_dot(scores_now, k) + plain_dot(scores_prev, kp))
        grads[1].append(dot_first(scores_now, q))
        grads[2].append(dot_first(jnp.where(below, low_chances, none), g))
        grads[3].append(dot_first(scores_prev, q))
        grads[4].append(dot_first(jnp.where(below, none, low_chances), g))
    query_grad = jnp.concatenate(grads[0], axis=1)
    pair_grad = jnp.concatenate(grads[1] + grads[2], axis=1)
    prev_grad = jnp.concatenate(grads[3] + grads[4], axis=1)
    return query_grad, pair_grad, prev_grad


def body(
    tokens,
    segment_start,
    norm_win,
    qkv_win,
    out_win,
    norm_wffn,
    up_win,
    down_win,
    norm_tok,
    qkv_tok,
    out_tok,
    norm_ffn,
    up_tok,
    down_tok,
    norm_state,
    qkv_state,
    out_state,
    gate_bias,
    norm_sffn,
    up_state,
    down_state,
    init_state,
    cotangent,
):
    seq_index = lax.axis_index("seq")
    tp_index = lax.axis_index("tp")
    n_tp = lax.axis_size("tp")
    position = seq_index % CHAIN
    flags = choose(segment_start, seq_index // CHAIN) == 1
    starts_here = choose(flags, position)
    block_rows, model_width = tokens.shape
    piece_rows = block_rows // n_tp
    state_rows = init_state.shape[0]
    slab_rows = state_rows // CHAIN
    thin_rows = slab_rows // n_tp
    width = qkv_tok.shape[2]
    qkv_win_flat = qkv_win.reshape(model_width, 3 * width)
    qkv_tok_flat = qkv_tok.reshape(model_width, 3 * width)
    out_tok_flat = out_tok.reshape(2 * width, model_width)
    qkv_state_flat = qkv_state.reshape(model_width, 3 * width)
    out_state_flat = out_state.reshape(2 * width, model_width)
    keep_one, keep_two = jax.nn.sigmoid(gate_bias)

    row_ids = (jnp.arange(block_rows) + tp_index * piece_rows) % block_rows
    below = row_ids[None, :] <= row_ids[:, None]
    token_rows = turned(tokens, tp_index * piece_rows)
    cotangent_rows = turned(cotangent, tp_index * piece_rows)

    def natural(pieces):
        whole = jnp.concatenate(pieces)
        return turned(whole, (n_tp - tp_index) % n_tp * piece_rows)

    input_rows = token_rows.astype(HIGH)
    win_normed = layer_norm(input_rows, norm_win).astype(LOW)
    win_qkv = plain_dot(win_normed, qkv_win_flat).astype(LOW)
    win_queries, win_pair = win_qkv[:, :width], win_qkv[:, width:]
    onward = [(s, s + 1) for s in range(lax.axis_size("seq")) if (s + 1) % CHAIN]
    win_prev = lax.ppermute(win_pair, "seq", onward)
    win_heads, win_logs = band_attend(win_queries, win_pair, win_prev, below, starts_here)
    own_input = input_rows[:piece_rows]
    win_mixed = own_input + tp_scatter(
        [plain_dot(part, out_win) for part in split_rows(win_heads, n_tp)]
    )
    win_ffn_in = tp_gather(layer_norm(win_mixed, norm_wffn).astype(LOW))
    win_hidden = [plain_dot(part, up_win) for part in win_ffn_in]
    win_active = [gelu_exact(part).astype(LOW) for part in win_hidden]
    layer_one = win_mixed + tp_scatter([plain_dot(part, down_win) for part in win_active])

    normed = jnp.concatenate(tp_gather(layer_norm(layer_one, norm_tok).astype(LOW)))
    token_qkv = plain_dot(normed, qkv_tok_flat).astype(LOW)
    queries, pair = token_qkv[:, :width], token_qkv[:, width:]
    pairs_all = pos_gather(pair)
    pair_prev = pairs_all[CHAIN - 1]
    pairs_stack = jnp.stack(pairs_all)

    init_thin = lax.dynamic_slice_in_dim(
        init_state, position * slab_rows + tp_index * thin_rows, thin_rows, 0
    )
    state_thin = init_thin
    turns = []
    states_out = []
    for turn in range(CHAIN):
        incoming = jnp.where(flags[turn], init_thin, state_thin).astype(HIGH)
        state_normed = jnp.concatenate(tp_gather(layer_norm(incoming, norm_state).astype(LOW)))
        state_qkv = plain_dot(state_normed, qkv_state_flat).astype(LOW)
        state_queries = state_qkv[:, :width]
        state_pair = jnp.concatenate(pos_gather(state_qkv[:, width:]))
        token_pair = choose(pairs_stack, (turn - position) % CHAIN)
        cross, cross_logs = full_attend(
            state_queries, token_pair[:, :width], token_pair[:, width:]
        )
        own, own_logs = full_attend(state_queries, state_pair[:, :width], state_pair[:, width:])
        state_heads = jnp.concatenate([own, cross], axis=1)
        update = tp_scatter(split_rows(plain_dot(state_heads, out_state_flat), n_tp))
        mid_state = keep_one * incoming + (1.0 - keep_one) * update
        state_ffn_in = jnp.concatenate(tp_gather(layer_norm(mid_state, norm_sffn).astype(LOW)))
        state_hidden = plain_dot(state_ffn_in, up_state)
        state_active = gelu_exact(state_hidden).astype(LOW)
        state_mlp = tp_scatter(split_rows(plain_dot(state_active, down_state), n_tp))
        state_thin = (keep_two * mid_state + (1.0 - keep_two) * state_mlp).astype(LOW)
        states_out.append(state_thin)
        turns.append(
            (
                incoming,
                state_normed,
                state_queries,
                state_pair,
                token_pair,
                cross_logs,
                own_logs,
                state_heads,
                update,
                mid_state,
                state_ffn_in,
                state_hidden,
                state_active,
                state_mlp,
            )
        )
    my_state_pair = turns[0][3]
    for turn in range(1, CHAIN):
        my_state_pair = jnp.where(position == turn, turns[turn][3], my_state_pair)

    own_heads, own_token_logs = band_attend(queries, pair, pair_prev, below, starts_here)
    cross_heads, cross_token_logs = full_attend(
        queries, my_state_pair[:, :width], my_state_pair[:, width:]
    )
    token_heads = jnp.concatenate([own_heads, cross_heads], axis=1)
    mixed_one = layer_one + tp_scatter(
        [plain_dot(part, out_tok_flat) for part in split_rows(token_heads, n_tp)]
    )
    ffn_in = tp_gather(layer_norm(mixed_one, norm_ffn).astype(LOW))
    hidden = [plain_dot(part, up_tok) for part in ffn_in]
    active = [gelu_exact(part).astype(LOW) for part in hidden]

    cotangents = split_rows(cotangent_rows, n_tp)
    grad_hidden = [
        gelu_slope(part, dot_second(grad, down_tok)).astype(LOW)
        for part, grad in zip(hidden, cotangents)
    ]
    grad_ffn_in = tp_scatter([dot_second(part, up_tok) for part in grad_hidden])
    back_mixed, grad_norm_ffn = jax.vjp(layer_norm, mixed_one, norm_ffn)[1](grad_ffn_in)
    grad_mixed = cotangents[0].astype(HIGH) + back_mixed
    grad_proj = jnp.concatenate(tp_gather(grad_mixed.astype(LOW)))
    grad_heads = dot_second(grad_proj, out_tok_flat).astype(LOW)
    cross_query_grad, cross_key_grad, cross_value_grad = full_attend_back(
        queries,
        my_state_pair[:, :width],
        my_state_pair[:, width:],
        cross_token_logs,
        grad_heads[:, width:],
    )
    cross_pair_grad = split_rows(
        jnp.concatenate([cross_key_grad, cross_value_grad], axis=1), CHAIN
    )
    cross_pieces = jnp.stack(
        [cross_pair_grad[0]]
        + [pos_to(cross_pair_grad[k].astype(LOW), k).astype(HIGH) for k in range(1, CHAIN)]
    )
    own_query_grad, own_pair_grad, prev_pair_grad = band_attend_back(
        queries, pair, pair_prev, below, starts_here, own_token_logs, grad_heads[:, :width]
    )
    homeward = [(s, s - 1) for s in range(lax.axis_size("seq")) if s % CHAIN]
    returned = lax.ppermute(prev_pair_grad.astype(LOW), "seq", homeward)

    layer_output = mixed_one + tp_scatter([plain_dot(part, down_tok) for part in active])
    output_rows = natural(tp_gather(layer_output.astype(LOW)))
    sum_token = seq_sum(
        jnp.concatenate(
            [
                dot_first(jnp.concatenate(ffn_in), jnp.concatenate(grad_hidden)).astype(LOW),
                dot_first(cotangent_rows, jnp.concatenate(active)).astype(LOW),
                dot_first(grad_proj, token_heads).astype(LOW),
            ],
            axis=1,
        )
    )

    states_stack = jnp.stack(states_out)
    state_pieces = [choose(states_stack, position)] + [
        pos_to(choose(states_stack, (position + k) % CHAIN), k) for k in range(1, CHAIN)
    ]
    by_slab = jnp.stack([state_pieces[(-k) % CHAIN] for k in range(CHAIN)])
    by_slab = turned(by_slab, (CHAIN - position) % CHAIN)
    by_tp = turned(jnp.stack(tp_gather(by_slab)), (n_tp - tp_index) % n_tp)
    state_rows_out = jnp.transpose(by_tp, (1, 0, 2, 3)).reshape(state_rows, model_width)

    grad_state = jnp.zeros((thin_rows, model_width), HIGH)
    init_grad = jnp.zeros((thin_rows, model_width), HIGH)
    bias_one = jnp.zeros((model_width,), HIGH)
    bias_two = jnp.zeros((model_width,), HIGH)
    grad_norm_sffn = jnp.zeros((model_width,), HIGH)
    grad_norm_state = jnp.zeros((model_width,), HIGH)
    kept = []
    token_pair_grads = [None] * CHAIN
    for turn in reversed(range(CHAIN)):
        (
            incoming,
            state_normed,
            state_queries,
            state_pair,
            token_pair,
            cross_logs,
            own_logs,
            state_heads,
            update,
            mid_state,
            state_ffn_in,
            state_hidden,
            state_active,
            state_mlp,
        ) = turns[turn]
        grad_mlp = jnp.concatenate(tp_gather(((1.0 - keep_two) * grad_state).astype(LOW)))
        bias_two = bias_two + jnp.sum(grad_state * (mid_state - state_mlp), axis=0)
        grad_state_hidden = gelu_slope(state_hidden, dot_second(grad_mlp, down_state)).astype(LOW)
        grad_sffn_in = tp_scatter(split_rows(dot_second(grad_state_hidden, up_state), n_tp))
        back_mid, norm_part = jax.vjp(layer_norm, mid_state, norm_sffn)[1](grad_sffn_in)
        grad_norm_sffn = grad_norm_sffn + norm_part
        grad_mid = keep_two * grad_state + back_mid
        bias_one = bias_one + jnp.sum(grad_mid * (incoming - update), axis=0)
        grad_update = jnp.concatenate(tp_gather(((1.0 - keep_one) * grad_mid).astype(LOW)))
        grad_state_heads = dot_second(grad_update, out_state_flat).astype(LOW)
        own_q, own_k, own_v = full_attend_back(
            state_queries,
            state_pair[:, :width],
            state_pair[:, width:],
            own_logs,
            grad_state_heads[:, :width],
        )
        pair_parts = split_rows(jnp.concatenate([own_k, own_v], axis=1), CHAIN)
        pair_total = pos_scatter(pair_parts) + choose(cross_pieces, (position - turn) % CHAIN)
        cross_q, cross_k, cross_v = full_attend_back(
            state_queries,
            token_pair[:, :width],
            token_pair[:, width:],
            cross_logs,
            grad_state_heads[:, width:],
        )
        token_pair_grads[turn] = jnp.concatenate([cross_k, cross_v], axis=1).astype(LOW)
        grad_state_qkv = jnp.concatenate([own_q + cross_q, pair_total], axis=1).astype(LOW)
        grad_state_normed = tp_scatter(
            split_rows(dot_second(grad_state_qkv, qkv_state_flat), n_tp)
        )
        back_state, norm_part = jax.vjp(layer_norm, incoming, norm_state)[1](grad_state_normed)
        grad_norm_state = grad_norm_state + norm_part
        grad_incoming = keep_one * grad_mid + back_state
        init_grad = init_grad + jnp.where(flags[turn], grad_incoming, 0.0)
        grad_state = jnp.where(flags[turn], 0.0, grad_incoming)
        kept.append(
            (
                state_normed,
                grad_state_qkv,
                state_heads,
                grad_update,
                state_ffn_in,
                grad_state_hidden,
                state_active,
                grad_mlp,
            )
        )
    bias_one = bias_one * keep_one * (1.0 - keep_one)
    bias_two = bias_two * keep_two * (1.0 - keep_two)
    (
        state_normed,
        grad_state_qkv,
        state_heads,
        grad_update,
        state_ffn_in,
        grad_state_hidden,
        state_active,
        grad_mlp,
    ) = [jnp.concatenate(each) for each in zip(*kept)]
    sum_state = seq_sum(
        jnp.concatenate(
            [
                dot_first(state_normed, grad_state_qkv).astype(LOW),
                dot_first(grad_update, state_heads).astype(LOW),
                dot_first(state_ffn_in, grad_state_hidden).astype(LOW),
                dot_first(grad_mlp, state_active).astype(LOW),
            ],
            axis=1,
        )
    )

    token_pair_stack = jnp.stack(token_pair_grads)
    pair_grad = own_pair_grad + returned.astype(HIGH)
    pair_grad = pair_grad + choose(token_pair_stack, position).astype(HIGH)
    for k in range(1, CHAIN):
        sent = choose(token_pair_stack, (position + k) % CHAIN)
        pair_grad = pair_grad + pos_to(sent, k).astype(HIGH)
    grad_qkv = jnp.concatenate([own_query_grad + cross_query_grad, pair_grad], axis=1).astype(LOW)
    grad_normed = tp_scatter(
        [dot_second(part, qkv_tok_flat) for part in split_rows(grad_qkv, n_tp)]
    )
    back_tokens, grad_norm_tok = jax.vjp(layer_norm, layer_one, norm_tok)[1](grad_normed)
    grad_layer_one = grad_mixed + back_tokens

    grad_win_out = tp_gather(grad_layer_one.astype(LOW))
    grad_win_hidden = [
        gelu_slope(part, dot_second(grad, down_win)).astype(LOW)
        for part, grad in zip(win_hidden, grad_win_out)
    ]
    grad_win_ffn_in = tp_scatter([dot_second(part, up_win) for part in grad_win_hidden])
    back_win, grad_norm_wffn = jax.vjp(layer_norm, win_mixed, norm_wffn)[1](grad_win_ffn_in)
    grad_win_mixed = grad_layer_one + back_win
    sum_middle = seq_sum(
        jnp.concatenate(
            [
                dot_first(normed, grad_qkv).astype(LOW),
                dot_first(jnp.concatenate(win_ffn_in), jnp.concatenate(grad_win_hidden)).astype(LOW),
                dot_first(jnp.concatenate(grad_win_out), jnp.concatenate(win_active)).astype(LOW),
            ],
            axis=1,
        )
    )
    grad_win_proj = jnp.concatenate(tp_gather(grad_win_mixed.astype(LOW)))
    grad_win_heads = dot_second(grad_win_proj, out_win).astype(LOW)
    win_query_grad, win_pair_grad, win_prev_grad = band_attend_back(
        win_queries, win_pair, win_prev, below, starts_here, win_logs, grad_win_heads
    )
    win_returned = lax.ppermute(win_prev_grad.astype(LOW), "seq", homeward)
    win_pair_grad = win_pair_grad + win_returned.astype(HIGH)
    grad_win_qkv = jnp.concatenate([win_query_grad, win_pair_grad], axis=1).astype(LOW)
    grad_win_normed = tp_scatter(
        [dot_second(part, qkv_win_flat) for part in split_rows(grad_win_qkv, n_tp)]
    )
    back_input, grad_norm_win = jax.vjp(layer_norm, own_input, norm_win)[1](grad_win_normed)
    grad_token_rows = natural(tp_gather((grad_win_mixed + back_input).astype(LOW)))

    init_columns = jnp.concatenate(
        [jnp.where(position == p, init_grad.T, 0.0) for p in range(CHAIN)], axis=1
    )
    vectors = [
        grad_norm_win,
        grad_norm_wffn,
        grad_norm_tok,
        grad_norm_ffn,
        grad_norm_state,
        grad_norm_sffn,
        bias_one,
        bias_two,
    ]
    small = jnp.concatenate([init_columns, jnp.stack(vectors, axis=1)], axis=1)
    small_width = small.shape[1]
    small = jnp.pad(small, ((0, 0), (0, -small_width % 256))).astype(LOW)
    sum_last = seq_sum(
        jnp.concatenate(
            [
                dot_first(win_normed, grad_win_qkv).astype(LOW),
                dot_first(grad_win_proj, win_heads).astype(LOW),
                small,
            ],
            axis=1,
        )
    )
    own_columns = model_width // lax.axis_size("seq")
    small_sums = tp_gather(sum_last[:, 4 * width : 4 * width + small_width])
    init_part = turned(
        jnp.stack([part[:, : CHAIN * thin_rows] for part in small_sums]),
        (n_tp - tp_index) % n_tp,
    ).reshape(n_tp, own_columns, CHAIN, thin_rows)
    sum_init = jnp.transpose(init_part, (2, 0, 3, 1)).reshape(state_rows, own_columns)
    vector_sums = sum(part[:, CHAIN * thin_rows :].astype(HIGH) for part in small_sums)

    def columns(sums, at, count):
        return sums[:, at : at + count].astype(HIGH)

    def qkv_of(sums, at):
        return columns(sums, at, 3 * width).reshape(own_columns, 3, width)

    def out_of(sums, at):
        return columns(sums, at, 2 * width).T.reshape(2, width, own_columns)

    inner_width = up_tok.shape[1]
    return (
        output_rows,
        state_rows_out,
        grad_token_rows,
        vector_sums[:, 0],
        qkv_of(sum_last, 0),
        columns(sum_last, 3 * width, width).T,
        vector_sums[:, 1],
        columns(sum_middle, 3 * width, inner_width),
        columns(sum_middle, 3 * width + inner_width, inner_width).T,
        vector_sums[:, 2],
        qkv_of(sum_middle, 0),
        out_of(sum_token, 2 * inner_width),
        vector_sums[:, 3],
        columns(sum_token, 0, inner_width),
        columns(sum_token, inner_width, inner_width).T,
        vector_sums[:, 4],
        qkv_of(sum_state, 0),
        out_of(sum_state, 3 * width),
        vector_sums[:, 6:8].T,
        vector_sums[:, 5],
        columns(sum_state, 5 * width, inner_width),
        columns(sum_state, 5 * width + inner_width, inner_width).T,
        sum_init.astype(HIGH),
    )

def solution(mesh):
    placed = (
        P("seq", None),
        P(),
        P(),
        P(None, None, "tp"),
        P("tp", None),
        P(),
        P(None, "tp"),
        P("tp", None),
        P(),
        P(None, None, "tp"),
        P(None, "tp", None),
        P(),
        P(None, "tp"),
        P("tp", None),
        P(),
        P(None, None, "tp"),
        P(None, "tp", None),
        P(),
        P(),
        P(None, "tp"),
        P("tp", None),
        P(),
        P("seq", None),
    )
    return jax.shard_map(
        body,
        mesh=mesh,
        in_specs=placed,
        out_specs=(
            P("seq", None),
            P("seq", None),
            P("seq", None),
            P("seq"),
            P("seq", None, "tp"),
            P("tp", "seq"),
            P("seq"),
            P("seq", "tp"),
            P("tp", "seq"),
            P("seq"),
            P("seq", None, "tp"),
            P(None, "tp", "seq"),
            P("seq"),
            P("seq", "tp"),
            P("tp", "seq"),
            P("seq"),
            P("seq", None, "tp"),
            P(None, "tp", "seq"),
            P(None, "seq"),
            P("seq"),
            P("seq", "tp"),
            P("tp", "seq"),
            P(None, "seq"),
        ),
        check_vma=False,
    )
```

```python
import jax
import jax.numpy as jnp
from jax import lax
from jax.experimental import pallas as pl
from jax.experimental.pallas import tpu as pltpu
from jax.sharding import PartitionSpec as P

E = 128
CHAIN = 4
CORES = 2

EPSILON = 1e-05
MASKED = -1e30
LOW = jnp.bfloat16
HIGH = jnp.float32


def layer_norm(matrix, weights):
    average = jnp.mean(matrix, axis=-1, keepdims=True)
    centred = matrix - average
    spread = jnp.mean(centred * centred, axis=-1, keepdims=True)
    return centred * lax.rsqrt(spread + EPSILON) * weights


def gelu_exact(matrix):
    return jax.nn.gelu(matrix, approximate=False)


def gelu_slope(matrix, grad):
    return jax.vjp(gelu_exact, matrix)[1](grad)[0]


def plain_dot(former, latter):
    return jnp.dot(former, latter, preferred_element_type=HIGH)


def dot_first(former, latter):
    return lax.dot_general(
        former, latter, (((0,), (0,)), ((), ())), preferred_element_type=HIGH
    )


def dot_second(former, latter):
    return lax.dot_general(
        former, latter, (((1,), (1,)), ((), ())), preferred_element_type=HIGH
    )


def tied(value, *others):
    return lax.optimization_barrier((value,) + others)[0]


def norm_back(matrix, weights, grad):
    average = jnp.mean(matrix, axis=-1, keepdims=True)
    centred = matrix - average
    spread = jnp.mean(centred * centred, axis=-1, keepdims=True)
    scaled = centred * lax.rsqrt(spread + EPSILON)
    inner = grad * weights
    back = lax.rsqrt(spread + EPSILON) * (
        inner
        - jnp.mean(inner, axis=-1, keepdims=True)
        - scaled * jnp.mean(inner * scaled, axis=-1, keepdims=True)
    )
    return back, jnp.sum(grad * scaled, axis=0)


def tp_from(array, k):
    n = lax.axis_size("tp")
    return lax.ppermute(array, "tp", [((i + k) % n, i) for i in range(n)])


def tp_to(array, k):
    n = lax.axis_size("tp")
    return lax.ppermute(array, "tp", [(i, (i + k) % n) for i in range(n)])


def far_first(n):
    return sorted(range(1, n), key=lambda k: -min(k, n - k))


def tp_gather(piece):
    n = lax.axis_size("tp")
    found = {k: tp_from(piece, k) for k in far_first(n)}
    return [piece] + [found[k] for k in range(1, n)]


def tp_scatter(parts):
    n = lax.axis_size("tp")
    total = parts[0]
    for k in far_first(n):
        total = total + tp_to(parts[k].astype(LOW), k).astype(HIGH)
    return total


def tp_total(part):
    low = part.astype(LOW)
    total = part
    for k in far_first(lax.axis_size("tp")):
        total = total + tp_to(low, k).astype(HIGH)
    return total


def split_rows(matrix, n):
    size = matrix.shape[0] // n
    return [matrix[k * size : (k + 1) * size] for k in range(n)]


def swap(array, k):
    n = lax.axis_size("seq")
    return lax.ppermute(array, "seq", [(s, s ^ k) for s in range(n)])


def pos_gather(piece):
    beside, across = swap(piece, 1), swap(piece, 2)
    return [piece, beside, across, swap(across, 1)]


def pos_scatter(parts):
    low = jnp.concatenate([parts[1], parts[3]]).astype(LOW)
    here, there = split_rows(swap(low, 1), 2)
    across = swap((parts[2] + there.astype(HIGH)).astype(LOW), 2)
    return parts[0] + here.astype(HIGH) + across.astype(HIGH)


def choose(stacked, index):
    return lax.dynamic_index_in_dim(stacked, index, 0, keepdims=False)


def turned(array, start):
    twice = jnp.concatenate([array, array])
    return lax.dynamic_slice_in_dim(twice, start, array.shape[0], 0)


def weight_grads(pairs, extra=None):
    n_seq = lax.axis_size("seq")
    depth = pairs[0][0][0].shape[1]
    unit = depth // n_seq
    block = max(256, CORES * unit)
    widths = [latter[0].shape[1] for _, latter in pairs]
    total = sum(widths) + (0 if extra is None else extra.shape[1])
    counts = [(len(former), len(latter)) for former, latter in pairs]
    operands, specs = [], []
    for former, latter in pairs:
        for piece in former:
            operands.append(piece)
            specs.append(pl.BlockSpec((piece.shape[0], block), lambda i: (0, i)))
        for piece in latter:
            operands.append(piece)
            specs.append(pl.BlockSpec(piece.shape, lambda i: (0, 0)))

    if extra is not None:
        operands.append(extra)
        specs.append(pl.BlockSpec((block, extra.shape[1]), lambda i: (i, 0)))

    def kernel(core_ref, *refs):
        mine_ref, other_ref = refs[-2:]
        first = core_ref[0] == 0

        def keep(product, column):
            columns = slice(column, column + product.shape[1])
            for g in range(block // (CORES * unit)):
                low = product[g * CORES * unit : g * CORES * unit + unit]
                high = product[g * CORES * unit + unit : (g + 1) * CORES * unit]
                rows = slice(g * unit, (g + 1) * unit)
                mine_ref[rows, columns] = jnp.where(first, low, high)
                other_ref[rows, columns] = jnp.where(first, high, low)

        at, column = 0, 0
        for (n_former, n_latter), width in zip(counts, widths):
            former = [ref[...] for ref in refs[at : at + n_former]]
            latter = [ref[...] for ref in refs[at + n_former : at + n_former + n_latter]]
            at += n_former + n_latter
            former = jnp.concatenate(former) if n_former > 1 else former[0]
            latter = jnp.concatenate(latter) if n_latter > 1 else latter[0]
            keep(dot_first(former, latter).astype(LOW), column)
            column += width
        if extra is not None:
            keep(refs[at][...], column)

    shape = jax.ShapeDtypeStruct((depth // CORES, total), LOW)
    out_spec = pl.BlockSpec((block // CORES, total), lambda i: (i, 0))
    rows = sum(piece.shape[0] for piece in pairs[0][0])
    core = (lax.axis_index("seq") % CORES).astype(jnp.int32).reshape(1)
    return pl.pallas_call(
        kernel,
        out_shape=(shape, shape),
        grid=(depth // block,),
        in_specs=[pl.BlockSpec(memory_space=pltpu.SMEM)] + specs,
        out_specs=(out_spec, out_spec),
        compiler_params=pltpu.CompilerParams(vmem_limit_bytes=32 * 1024 * 1024),
        cost_estimate=pl.CostEstimate(
            flops=2 * rows * depth * total,
            bytes_accessed=2 * (rows * (depth + total) + depth * total),
            transcendentals=0,
        ),
    )(core, *operands)


class SeqSum:
    def __init__(self, halves):
        n = lax.axis_size("seq")
        self.z_size = 4 if n % 8 == 0 else n // CORES
        self.x_size = n // (self.z_size * CORES)
        here = lax.axis_index("seq")
        self.z_at = here // CORES % self.z_size
        self.x_at = here // (CORES * self.z_size)
        self.mine, self.other = halves

    def pairs(self, dx, dz):
        def place(x, z, c):
            return (x % self.x_size * self.z_size + z % self.z_size) * CORES + c

        return [
            (place(x, z, c), place(x + dx, z + dz, c))
            for x in range(self.x_size)
            for z in range(self.z_size)
            for c in range(CORES)
        ]

    def over_z(self, array, dim):
        return self.stage(array, dim, self.z_at, self.z_size, lambda k: (0, k))

    def over_x(self, array, dim):
        return self.stage(array, dim, self.x_at, self.x_size, lambda k: (k, 0))

    def stage(self, array, dim, at, size, step):
        total = lax.dynamic_index_in_dim(array, at, dim, False).astype(HIGH)
        for k in far_first(size):
            sent = lax.dynamic_index_in_dim(array, (at + k) % size, dim, False)
            total = total + lax.ppermute(sent, "seq", self.pairs(*step(k))).astype(HIGH)
        return total.astype(LOW)

    def cores(self):
        width = self.mine.shape[1]
        array = (self.mine.astype(HIGH) + swap(self.other, 1).astype(HIGH)).astype(LOW)
        array = array.reshape(self.x_size, self.z_size, -1, width)
        half = width // 256 * 128
        self.one, self.two = array[..., :half], array[..., half:]
        return self.one, self.two

    def first(self):
        self.one, self.two = self.over_z(self.one, 1), self.over_x(self.two, 0)
        return self.one, self.two

    def second(self):
        one, two = self.over_x(self.one, 0), self.over_z(self.two, 0)
        self.total = jnp.concatenate([one, two], axis=1)
        return self.total


def heads_of(matrix):
    return [matrix[:, h * E : (h + 1) * E] for h in range(matrix.shape[1] // E)]


def full_attend(queries, key_rows, value_rows):
    results, logs = [], []
    for q, k, v in zip(heads_of(queries), heads_of(key_rows), heads_of(value_rows)):
        scores = dot_second(q, k) * E ** (-0.5)
        row_max = jnp.max(scores, axis=-1, keepdims=True)
        powers = jnp.exp(scores - row_max)
        totals = jnp.sum(powers, axis=-1, keepdims=True)
        results.append(plain_dot((powers / totals).astype(LOW), v).astype(LOW))
        logs.append(row_max + jnp.log(totals))
    return jnp.concatenate(results, axis=1), logs


def full_attend_back(queries, key_rows, value_rows, logs, grad_result):
    grads = ([], [], [])
    for q, k, v, log, g in zip(
        heads_of(queries), heads_of(key_rows), heads_of(value_rows), logs, heads_of(grad_result)
    ):
        chances = jnp.exp(dot_second(q, k) * E ** (-0.5) - log)
        grad_chances = dot_second(g, v)
        inner = jnp.sum(chances * grad_chances, axis=-1, keepdims=True)
        grad_scores = (chances * (grad_chances - inner) * E ** (-0.5)).astype(LOW)
        grads[0].append(plain_dot(grad_scores, k))
        grads[1].append(dot_first(grad_scores, q))
        grads[2].append(dot_first(chances.astype(LOW), g))
    return [jnp.concatenate(each, axis=1) for each in grads]


def band_scores(q, k, k_prev, below, starts_here):
    current = dot_second(q, k) * E ** (-0.5)
    before = jnp.where(starts_here, MASKED, dot_second(q, k_prev) * E ** (-0.5))
    return jnp.where(below, current, before)


def band_attend(queries, pair, pair_prev, below, starts_here):
    width = queries.shape[1]
    results, logs = [], []
    for q, k, v, kp, vp in zip(
        heads_of(queries),
        heads_of(pair[:, :width]),
        heads_of(pair[:, width:]),
        heads_of(pair_prev[:, :width]),
        heads_of(pair_prev[:, width:]),
    ):
        scores = band_scores(q, k, kp, below, starts_here)
        row_max = jnp.max(scores, axis=-1, keepdims=True)
        powers = jnp.exp(scores - row_max)
        totals = jnp.sum(powers, axis=-1, keepdims=True)
        chances = (powers / totals).astype(LOW)
        none = jnp.zeros_like(chances)
        result = plain_dot(jnp.where(below, chances, none), v) + plain_dot(
            jnp.where(below, none, chances), vp
        )
        results.append(result.astype(LOW))
        logs.append(row_max + jnp.log(totals))
    return jnp.concatenate(results, axis=1), logs


def band_attend_back(queries, pair, pair_prev, below, starts_here, logs, grad_result):
    width = queries.shape[1]
    grads = ([], [], [], [], [])
    for q, k, v, kp, vp, log, g in zip(
        heads_of(queries),
        heads_of(pair[:, :width]),
        heads_of(pair[:, width:]),
        heads_of(pair_prev[:, :width]),
        heads_of(pair_prev[:, width:]),
        logs,
        heads_of(grad_result),
    ):
        chances = jnp.exp(band_scores(q, k, kp, below, starts_here) - log)
        grad_chances = jnp.where(below, dot_second(g, v), dot_second(g, vp))
        inner = jnp.sum(chances * grad_chances, axis=-1, keepdims=True)
        grad_scores = (chances * (grad_chances - inner) * E ** (-0.5)).astype(LOW)
        low_chances = chances.astype(LOW)
        none = jnp.zeros_like(low_chances)
        scores_now = jnp.where(below, grad_scores, none)
        scores_prev = jnp.where(below, none, grad_scores)
        grads[0].append(plain_dot(scores_now, k) + plain_dot(scores_prev, kp))
        grads[1].append(dot_first(scores_now, q))
        grads[2].append(dot_first(jnp.where(below, low_chances, none), g))
        grads[3].append(dot_first(scores_prev, q))
        grads[4].append(dot_first(jnp.where(below, none, low_chances), g))
    query_grad = jnp.concatenate(grads[0], axis=1)
    pair_grad = jnp.concatenate(grads[1] + grads[2], axis=1)
    prev_grad = jnp.concatenate(grads[3] + grads[4], axis=1)
    return query_grad, pair_grad, prev_grad


def body(
    tokens,
    segment_start,
    norm_win,
    qkv_win,
    out_win,
    norm_wffn,
    up_win,
    down_win,
    norm_tok,
    qkv_tok,
    out_tok,
    norm_ffn,
    up_tok,
    down_tok,
    norm_state,
    qkv_state,
    out_state,
    gate_bias,
    norm_sffn,
    up_state,
    down_state,
    init_state,
    cotangent,
):
    seq_index = lax.axis_index("seq")
    tp_index = lax.axis_index("tp")
    n_tp = lax.axis_size("tp")
    position = seq_index % CHAIN
    flags = choose(segment_start, seq_index // CHAIN) == 1
    starts_here = choose(flags, position)
    block_rows, model_width = tokens.shape
    piece_rows = block_rows // n_tp
    state_rows = init_state.shape[0]
    slab_rows = state_rows // CHAIN
    thin_rows = slab_rows // n_tp
    width = qkv_tok.shape[2]
    qkv_win_flat = qkv_win.reshape(model_width, 3 * width)
    qkv_tok_flat = qkv_tok.reshape(model_width, 3 * width)
    out_tok_flat = out_tok.reshape(2 * width, model_width)
    qkv_state_flat = qkv_state.reshape(model_width, 3 * width)
    out_state_flat = out_state.reshape(2 * width, model_width)
    keep_one, keep_two = jax.nn.sigmoid(gate_bias)

    row_ids = (jnp.arange(block_rows) + tp_index * piece_rows) % block_rows
    below = row_ids[None, :] <= row_ids[:, None]
    token_rows = turned(tokens, tp_index * piece_rows)
    cotangent_rows = turned(cotangent, tp_index * piece_rows)

    def natural(pieces):
        whole = jnp.concatenate(pieces)
        return turned(whole, (n_tp - tp_index) % n_tp * piece_rows)

    input_rows = token_rows.astype(HIGH)
    win_normed = layer_norm(input_rows, norm_win).astype(LOW)
    win_qkv = plain_dot(win_normed, qkv_win_flat).astype(LOW)
    win_queries, win_pair = win_qkv[:, :width], win_qkv[:, width:]
    onward = [(s, s + 1) for s in range(lax.axis_size("seq")) if (s + 1) % CHAIN]
    win_prev = lax.ppermute(win_pair, "seq", onward)
    win_heads, win_logs = band_attend(win_queries, win_pair, win_prev, below, starts_here)
    own_input = input_rows[:piece_rows]
    win_mixed = own_input + tp_scatter(
        [plain_dot(part, out_win) for part in split_rows(win_heads, n_tp)]
    )
    win_ffn_in = tp_gather(layer_norm(win_mixed, norm_wffn).astype(LOW))
    win_hidden = [plain_dot(part, up_win) for part in win_ffn_in]
    win_active = [gelu_exact(part).astype(LOW) for part in win_hidden]

    init_slab = lax.dynamic_slice_in_dim(init_state, position * slab_rows, slab_rows, 0)

    def own_rows(slab):
        return lax.dynamic_slice_in_dim(slab, tp_index * thin_rows, thin_rows, 0)

    def state_start(slab):
        state_normed = layer_norm(slab.astype(HIGH), norm_state).astype(LOW)
        state_qkv = plain_dot(state_normed, qkv_state_flat).astype(LOW)
        state_queries = state_qkv[:, :width]
        state_pair = jnp.concatenate(pos_gather(state_qkv[:, width:]))
        own, own_logs = full_attend(state_queries, state_pair[:, :width], state_pair[:, width:])
        return state_normed, state_queries, state_pair, own, own_logs

    started = state_start(tied(init_slab, win_ffn_in[1]))
    layer_one = win_mixed + tp_scatter([plain_dot(part, down_win) for part in win_active])
    layer_one = tied(layer_one, started[3])

    normed_pieces = tp_gather(layer_norm(layer_one, norm_tok).astype(LOW))
    normed = jnp.concatenate(normed_pieces)
    token_qkv = plain_dot(normed, qkv_tok_flat).astype(LOW)
    queries, pair = token_qkv[:, :width], token_qkv[:, width:]
    pairs_all = pos_gather(pair)
    pair_prev = jnp.where(position % 2 == 1, pairs_all[1], pairs_all[3])
    pairs_stack = jnp.stack(pairs_all)

    state_slab = init_slab
    turns = []
    states_out = []
    for turn in range(CHAIN):
        state_slab = jnp.where(flags[turn], init_slab, state_slab)
        incoming = state_slab.astype(HIGH)
        if turn:
            started = state_start(state_slab)
        state_normed, state_queries, state_pair, own, own_logs = started
        token_pair = choose(pairs_stack, position ^ turn)
        cross, cross_logs = full_attend(
            state_queries, token_pair[:, :width], token_pair[:, width:]
        )
        state_heads = jnp.concatenate([own, cross], axis=1)
        update = tp_total(plain_dot(state_heads, out_state_flat))
        if turn == 1:
            own_heads, own_token_logs = band_attend(
                tied(queries, state_heads), pair, pair_prev, below, starts_here
            )
            update = tied(update, own_heads)
        mid_state = keep_one * incoming + (1.0 - keep_one) * update
        state_ffn_in = layer_norm(mid_state, norm_sffn).astype(LOW)
        state_hidden = plain_dot(state_ffn_in, up_state)
        state_active = gelu_exact(state_hidden).astype(LOW)
        state_mlp = tp_total(plain_dot(state_active, down_state))
        state_slab = (keep_two * mid_state + (1.0 - keep_two) * state_mlp).astype(LOW)
        states_out.append(own_rows(state_slab))
        turns.append(
            (
                incoming,
                state_normed,
                state_queries,
                state_pair,
                token_pair,
                cross_logs,
                own_logs,
                state_heads,
                update,
                mid_state,
                state_ffn_in,
                state_hidden,
                state_active,
                state_mlp,
            )
        )
    my_state_pair = turns[0][3]
    for turn in range(1, CHAIN):
        my_state_pair = jnp.where(position == turn, turns[turn][3], my_state_pair)

    cross_heads, cross_token_logs = full_attend(
        queries, my_state_pair[:, :width], my_state_pair[:, width:]
    )
    token_heads = jnp.concatenate([own_heads, cross_heads], axis=1)
    mixed_one = layer_one + tp_scatter(
        [plain_dot(part, out_tok_flat) for part in split_rows(token_heads, n_tp)]
    )
    ffn_in = tp_gather(layer_norm(mixed_one, norm_ffn).astype(LOW))
    hidden = [plain_dot(part, up_tok) for part in ffn_in]

    cotangents = split_rows(cotangent_rows, n_tp)
    grad_hidden = [
        gelu_slope(part, dot_second(grad, down_tok)).astype(LOW)
        for part, grad in zip(hidden, cotangents)
    ]
    grad_ffn_in = tp_scatter([dot_second(part, up_tok) for part in grad_hidden])
    active = [gelu_exact(part).astype(LOW) for part in hidden]
    back_mixed, grad_norm_ffn = norm_back(mixed_one, norm_ffn, grad_ffn_in)
    grad_mixed = cotangents[0].astype(HIGH) + back_mixed
    grad_proj_pieces = tp_gather(grad_mixed.astype(LOW))
    grad_proj = jnp.concatenate(grad_proj_pieces)
    grad_heads = dot_second(grad_proj, out_tok_flat).astype(LOW)
    cross_query_grad, cross_key_grad, cross_value_grad = full_attend_back(
        queries,
        my_state_pair[:, :width],
        my_state_pair[:, width:],
        cross_token_logs,
        grad_heads[:, width:],
    )
    cross_pair_grad = split_rows(
        jnp.concatenate([cross_key_grad, cross_value_grad], axis=1), CHAIN
    )
    cross_pieces = jnp.stack(
        [cross_pair_grad[0]]
        + [swap(cross_pair_grad[k].astype(LOW), k).astype(HIGH) for k in range(1, CHAIN)]
    )
    homeward = [(s, s - 1) for s in range(lax.axis_size("seq")) if s % CHAIN]

    def own_back():
        query_grad, pair_grad, prev_grad = band_attend_back(
            queries,
            pair,
            pair_prev,
            below,
            starts_here,
            own_token_logs,
            tied(grad_heads[:, :width], cross_pieces),
        )
        returned = lax.ppermute(prev_grad.astype(LOW), "seq", homeward)
        return query_grad + cross_query_grad, pair_grad + returned.astype(HIGH)

    def states_between():
        states_stack = jnp.stack(states_out)
        pieces = [choose(states_stack, position)]
        pieces += [swap(choose(states_stack, position ^ k), k) for k in range(1, CHAIN)]
        pieces = jnp.stack(pieces)
        return jnp.stack([choose(pieces, position ^ q) for q in range(CHAIN)])

    init_grad = jnp.zeros((thin_rows, model_width), HIGH)
    bias_one = bias_two = grad_norm_sffn = grad_norm_state = jnp.zeros((model_width,), HIGH)
    kept_qkv, kept_rest = [], []
    token_pair_grads = [None] * CHAIN
    grad_state = None
    for turn in reversed(range(CHAIN)):
        (
            incoming,
            state_normed,
            state_queries,
            state_pair,
            token_pair,
            cross_logs,
            own_logs,
            state_heads,
            update,
            mid_state,
            state_ffn_in,
            state_hidden,
            state_active,
            state_mlp,
        ) = turns[turn]
        pair_total = choose(cross_pieces, position ^ turn)
        if turn == CHAIN - 1:
            query_total = jnp.zeros((slab_rows, width), HIGH)
        else:
            grad_mlp = ((1.0 - keep_two) * grad_state).astype(LOW)
            bias_two = bias_two + jnp.sum(grad_state * (mid_state - state_mlp), axis=0)
            grad_state_hidden = gelu_slope(
                state_hidden, dot_second(grad_mlp, down_state)
            ).astype(LOW)
            grad_sffn_in = tp_total(dot_second(grad_state_hidden, up_state))
            if turn == CHAIN - 2:
                token_grads = SeqSum(
                    weight_grads(
                        [
                            (tied(tuple(ffn_in), grad_state_hidden), grad_hidden),
                            ([cotangent_rows], active),
                            (grad_proj_pieces, [token_heads]),
                        ]
                    )
                )
                grad_sffn_in = tied(grad_sffn_in, token_grads.other)
            if turn == CHAIN - 3:
                grad_sffn_in = tied(grad_sffn_in, *token_grads.first())
            back_mid, norm_part = norm_back(mid_state, norm_sffn, grad_sffn_in)
            grad_norm_sffn = grad_norm_sffn + norm_part
            grad_mid = keep_two * grad_state + back_mid
            bias_one = bias_one + jnp.sum(grad_mid * (incoming - update), axis=0)
            grad_update = ((1.0 - keep_one) * grad_mid).astype(LOW)
            grad_state_heads = dot_second(grad_update, out_state_flat).astype(LOW)
            own_q, own_k, own_v = full_attend_back(
                state_queries,
                state_pair[:, :width],
                state_pair[:, width:],
                own_logs,
                grad_state_heads[:, :width],
            )
            pair_total = pair_total + pos_scatter(
                split_rows(jnp.concatenate([own_k, own_v], axis=1), CHAIN)
            )
            cross_q, cross_k, cross_v = full_attend_back(
                state_queries,
                token_pair[:, :width],
                token_pair[:, width:],
                cross_logs,
                grad_state_heads[:, width:],
            )
            token_pair_grads[turn] = jnp.concatenate([cross_k, cross_v], axis=1)
            query_total = own_q + cross_q
            if turn == CHAIN - 3:
                slabs = states_between()
                pair_total = tied(pair_total, slabs)
            if turn == CHAIN - 4:
                by_tp = turned(jnp.stack(tp_gather(slabs)), (n_tp - tp_index) % n_tp)
                state_rows_out = jnp.transpose(by_tp, (1, 0, 2, 3)).reshape(
                    state_rows, model_width
                )
                pair_total = tied(pair_total, state_rows_out)
            kept_rest.append(
                (state_heads, grad_update, state_ffn_in, grad_state_hidden, state_active, grad_mlp)
            )
        grad_state_qkv = jnp.concatenate([query_total, pair_total], axis=1).astype(LOW)
        kept_qkv.append((state_normed, grad_state_qkv))
        grad_state_normed = tp_total(dot_second(grad_state_qkv, qkv_state_flat))
        if turn == CHAIN - 1:
            query_grad, pair_grad = own_back()
            grad_state_normed = tied(grad_state_normed, query_grad)
        if turn == CHAIN - 2:
            grad_state_normed = tied(grad_state_normed, *token_grads.cores())
        if turn == CHAIN - 3:
            grad_state_normed = tied(grad_state_normed, token_grads.second())
        back_state, norm_part = norm_back(incoming, norm_state, grad_state_normed)
        grad_norm_state = grad_norm_state + norm_part
        grad_incoming = back_state
        if grad_state is not None:
            grad_incoming = keep_one * grad_mid + back_state
        init_grad = init_grad + jnp.where(flags[turn], own_rows(grad_incoming), 0.0)
        grad_state = jnp.where(flags[turn], 0.0, grad_incoming)
    bias_one = bias_one * keep_one * (1.0 - keep_one) / n_tp
    bias_two = bias_two * keep_two * (1.0 - keep_two) / n_tp
    grad_norm_sffn = grad_norm_sffn / n_tp
    grad_norm_state = grad_norm_state / n_tp
    sum_token = token_grads.total

    token_pair_grads[CHAIN - 1] = jnp.zeros_like(token_pair_grads[0])
    pair_stack = jnp.stack(token_pair_grads)
    pair_grad = pair_grad + pos_scatter([choose(pair_stack, position ^ k) for k in range(CHAIN)])
    grad_qkv = jnp.concatenate([query_grad, pair_grad], axis=1).astype(LOW)
    grad_normed = tp_scatter(
        [dot_second(part, qkv_tok_flat) for part in split_rows(grad_qkv, n_tp)]
    )
    qkv_parts = list(zip(*kept_qkv))
    rest_parts = list(zip(*kept_rest))
    state_grads = SeqSum(
        weight_grads(
            [
                (qkv_parts[0], qkv_parts[1]),
                (rest_parts[1], rest_parts[0]),
                (rest_parts[2], rest_parts[3]),
                (rest_parts[5], rest_parts[4]),
            ]
        )
    )
    grad_normed = tied(grad_normed, state_grads.other)
    back_tokens, grad_norm_tok = norm_back(layer_one, norm_tok, grad_normed)
    grad_layer_one = grad_mixed + back_tokens

    grad_win_out = tp_gather(grad_layer_one.astype(LOW))
    grad_win_hidden = [
        gelu_slope(part, dot_second(grad, down_win)).astype(LOW)
        for part, grad in zip(win_hidden, grad_win_out)
    ]
    grad_win_ffn_in = tp_scatter([dot_second(part, up_win) for part in grad_win_hidden])
    grad_win_ffn_in = tied(grad_win_ffn_in, *state_grads.cores())
    back_win, grad_norm_wffn = norm_back(win_mixed, norm_wffn, grad_win_ffn_in)
    grad_win_mixed = grad_layer_one + back_win
    grad_win_pieces = tp_gather(grad_win_mixed.astype(LOW))
    middle_grads = SeqSum(
        weight_grads(
            [
                (normed_pieces, [grad_qkv]),
                (win_ffn_in, grad_win_hidden),
                (grad_win_out, win_active),
            ]
        )
    )
    grad_win_proj = jnp.concatenate(tied(tuple(grad_win_pieces), middle_grads.other))
    grad_win_heads = dot_second(grad_win_proj, out_win).astype(LOW)
    win_query_grad, win_pair_grad, win_prev_grad = band_attend_back(
        win_queries, win_pair, win_prev, below, starts_here, win_logs, grad_win_heads
    )
    win_returned = lax.ppermute(win_prev_grad.astype(LOW), "seq", homeward)
    win_pair_grad = win_pair_grad + tied(win_returned, *state_grads.first()).astype(HIGH)
    grad_win_qkv = jnp.concatenate([win_query_grad, win_pair_grad], axis=1).astype(LOW)
    sum_state = state_grads.second()
    middle_grads.cores()
    grad_win_normed = tp_scatter(
        [dot_second(part, qkv_win_flat) for part in split_rows(grad_win_qkv, n_tp)]
    )
    back_input, grad_norm_win = norm_back(own_input, norm_win, grad_win_normed)
    grad_token_rows = natural(tp_gather((grad_win_mixed + back_input).astype(LOW)))

    layer_output = mixed_one + tp_scatter([plain_dot(part, down_tok) for part in active])
    output_rows = natural(tp_gather(layer_output.astype(LOW)))

    init_columns = jnp.concatenate(
        [jnp.where(position == p, init_grad.T, 0.0) for p in range(CHAIN)], axis=1
    )
    vectors = [
        grad_norm_win,
        grad_norm_wffn,
        grad_norm_tok,
        grad_norm_ffn,
        grad_norm_state,
        grad_norm_sffn,
        bias_one,
        bias_two,
    ]
    small = jnp.concatenate([init_columns, jnp.stack(vectors, axis=1)], axis=1)
    small_width = small.shape[1]
    small = jnp.pad(small, ((0, 0), (0, -small_width % 256))).astype(LOW)
    last_grads = SeqSum(
        weight_grads(
            [([win_normed], [grad_win_qkv]), ([grad_win_proj], [win_heads])], small
        )
    )
    middle_grads.first()
    sum_middle = middle_grads.second()
    last_grads.cores()
    last_grads.first()
    sum_last = last_grads.second()
    own_columns = model_width // lax.axis_size("seq")
    small_sums = tp_gather(sum_last[:, 4 * width : 4 * width + small_width])
    init_part = turned(
        jnp.stack([part[:, : CHAIN * thin_rows] for part in small_sums]),
        (n_tp - tp_index) % n_tp,
    ).reshape(n_tp, own_columns, CHAIN, thin_rows)
    sum_init = jnp.transpose(init_part, (2, 0, 3, 1)).reshape(state_rows, own_columns)
    vector_sums = sum(part[:, CHAIN * thin_rows :].astype(HIGH) for part in small_sums)

    def columns(sums, at, count):
        return sums[:, at : at + count].astype(HIGH)

    def qkv_of(sums, at):
        return columns(sums, at, 3 * width).reshape(own_columns, 3, width)

    def out_of(sums, at):
        return columns(sums, at, 2 * width).T.reshape(2, width, own_columns)

    inner_width = up_tok.shape[1]
    return (
        output_rows,
        state_rows_out,
        grad_token_rows,
        vector_sums[:, 0],
        qkv_of(sum_last, 0),
        columns(sum_last, 3 * width, width).T,
        vector_sums[:, 1],
        columns(sum_middle, 3 * width, inner_width),
        columns(sum_middle, 3 * width + inner_width, inner_width).T,
        vector_sums[:, 2],
        qkv_of(sum_middle, 0),
        out_of(sum_token, 2 * inner_width),
        vector_sums[:, 3],
        columns(sum_token, 0, inner_width),
        columns(sum_token, inner_width, inner_width).T,
        vector_sums[:, 4],
        qkv_of(sum_state, 0),
        out_of(sum_state, 3 * width),
        vector_sums[:, 6:8].T,
        vector_sums[:, 5],
        columns(sum_state, 5 * width, inner_width),
        columns(sum_state, 5 * width + inner_width, inner_width).T,
        sum_init.astype(HIGH),
    )

def solution(mesh):
    placed = (
        P("seq", None),
        P(),
        P(),
        P(None, None, "tp"),
        P("tp", None),
        P(),
        P(None, "tp"),
        P("tp", None),
        P(),
        P(None, None, "tp"),
        P(None, "tp", None),
        P(),
        P(None, "tp"),
        P("tp", None),
        P(),
        P(None, None, "tp"),
        P(None, "tp", None),
        P(),
        P(),
        P(None, "tp"),
        P("tp", None),
        P(),
        P("seq", None),
    )
    return jax.shard_map(
        body,
        mesh=mesh,
        in_specs=placed,
        out_specs=(
            P("seq", None),
            P("seq", None),
            P("seq", None),
            P("seq"),
            P("seq", None, "tp"),
            P("tp", "seq"),
            P("seq"),
            P("seq", "tp"),
            P("tp", "seq"),
            P("seq"),
            P("seq", None, "tp"),
            P(None, "tp", "seq"),
            P("seq"),
            P("seq", "tp"),
            P("tp", "seq"),
            P("seq"),
            P("seq", None, "tp"),
            P(None, "tp", "seq"),
            P(None, "seq"),
            P("seq"),
            P("seq", "tp"),
            P("tp", "seq"),
            P(None, "seq"),
        ),
        check_vma=False,
    )
```

```python
import jax
import jax.numpy as jnp
from jax import lax
from jax.experimental import pallas as pl
from jax.experimental.pallas import tpu as pltpu
from jax.sharding import PartitionSpec as P

E = 128
CHAIN = 4
CORES = 2

EPSILON = 1e-05
MASKED = -1e30
LOW = jnp.bfloat16
HIGH = jnp.float32


def layer_norm(matrix, weights):
    average = jnp.mean(matrix, axis=-1, keepdims=True)
    centred = matrix - average
    spread = jnp.mean(centred * centred, axis=-1, keepdims=True)
    return centred * lax.rsqrt(spread + EPSILON) * weights


def gelu_exact(matrix):
    return jax.nn.gelu(matrix, approximate=False)


def gelu_slope(matrix, grad):
    return jax.vjp(gelu_exact, matrix)[1](grad)[0]


def plain_dot(former, latter):
    return jnp.dot(former, latter, preferred_element_type=HIGH)


def dot_first(former, latter):
    return lax.dot_general(
        former, latter, (((0,), (0,)), ((), ())), preferred_element_type=HIGH
    )


def dot_second(former, latter):
    return lax.dot_general(
        former, latter, (((1,), (1,)), ((), ())), preferred_element_type=HIGH
    )


def tied(value, *others):
    return lax.optimization_barrier((value,) + others)[0]


def norm_back(matrix, weights, grad):
    average = jnp.mean(matrix, axis=-1, keepdims=True)
    centred = matrix - average
    spread = jnp.mean(centred * centred, axis=-1, keepdims=True)
    scaled = centred * lax.rsqrt(spread + EPSILON)
    inner = grad * weights
    back = lax.rsqrt(spread + EPSILON) * (
        inner
        - jnp.mean(inner, axis=-1, keepdims=True)
        - scaled * jnp.mean(inner * scaled, axis=-1, keepdims=True)
    )
    return back, jnp.sum(grad * scaled, axis=0)


def tp_from(array, k):
    n = lax.axis_size("tp")
    return lax.ppermute(array, "tp", [((i + k) % n, i) for i in range(n)])


def tp_to(array, k):
    n = lax.axis_size("tp")
    return lax.ppermute(array, "tp", [(i, (i + k) % n) for i in range(n)])


def far_first(n):
    return sorted(range(1, n), key=lambda k: -min(k, n - k))


def tp_gather(piece):
    n = lax.axis_size("tp")
    found = {k: tp_from(piece, k) for k in far_first(n)}
    return [piece] + [found[k] for k in range(1, n)]


def tp_scatter(parts):
    n = lax.axis_size("tp")
    total = parts[0]
    for k in far_first(n):
        total = total + tp_to(parts[k].astype(LOW), k).astype(HIGH)
    return total


def tp_total(part):
    low = part.astype(LOW)
    total = part
    for k in far_first(lax.axis_size("tp")):
        total = total + tp_to(low, k).astype(HIGH)
    return total


def split_rows(matrix, n):
    size = matrix.shape[0] // n
    return [matrix[k * size : (k + 1) * size] for k in range(n)]


def swap(array, k):
    n = lax.axis_size("seq")
    return lax.ppermute(array, "seq", [(s, s ^ k) for s in range(n)])


def pos_gather(piece):
    beside, across = swap(piece, 1), swap(piece, 2)
    return [piece, beside, across, swap(across, 1)]


def pos_scatter(parts):
    low = jnp.concatenate([parts[1], parts[3]]).astype(LOW)
    here, there = split_rows(swap(low, 1), 2)
    across = swap((parts[2] + there.astype(HIGH)).astype(LOW), 2)
    return parts[0] + here.astype(HIGH) + across.astype(HIGH)


def choose(stacked, index):
    return lax.dynamic_index_in_dim(stacked, index, 0, keepdims=False)


def turned(array, start):
    twice = jnp.concatenate([array, array])
    return lax.dynamic_slice_in_dim(twice, start, array.shape[0], 0)


def weight_grads(pairs):
    n_seq = lax.axis_size("seq")
    depth = pairs[0][0][0].shape[1]
    unit = depth // n_seq
    block = max(256, CORES * unit)
    widths = [latter[0].shape[1] for _, latter in pairs]
    total = sum(widths)
    counts = [(len(former), len(latter)) for former, latter in pairs]
    operands, specs = [], []
    for former, latter in pairs:
        for piece in former:
            operands.append(piece)
            specs.append(pl.BlockSpec((piece.shape[0], block), lambda i: (0, i)))
        for piece in latter:
            operands.append(piece)
            specs.append(pl.BlockSpec(piece.shape, lambda i: (0, 0)))

    def kernel(core_ref, *refs):
        mine_ref, other_ref = refs[-2:]
        first = core_ref[0] == 0

        def keep(product, column):
            columns = slice(column, column + product.shape[1])
            for g in range(block // (CORES * unit)):
                low = product[g * CORES * unit : g * CORES * unit + unit]
                high = product[g * CORES * unit + unit : (g + 1) * CORES * unit]
                rows = slice(g * unit, (g + 1) * unit)
                mine_ref[rows, columns] = jnp.where(first, low, high)
                other_ref[rows, columns] = jnp.where(first, high, low)

        at, column = 0, 0
        for (n_former, n_latter), width in zip(counts, widths):
            former = [ref[...] for ref in refs[at : at + n_former]]
            latter = [ref[...] for ref in refs[at + n_former : at + n_former + n_latter]]
            at += n_former + n_latter
            former = jnp.concatenate(former) if n_former > 1 else former[0]
            latter = jnp.concatenate(latter) if n_latter > 1 else latter[0]
            keep(dot_first(former, latter).astype(LOW), column)
            column += width

    shape = jax.ShapeDtypeStruct((depth // CORES, total), LOW)
    out_spec = pl.BlockSpec((block // CORES, total), lambda i: (i, 0))
    rows = sum(piece.shape[0] for piece in pairs[0][0])
    core = (lax.axis_index("seq") % CORES).astype(jnp.int32).reshape(1)
    return pl.pallas_call(
        kernel,
        out_shape=(shape, shape),
        grid=(depth // block,),
        in_specs=[pl.BlockSpec(memory_space=pltpu.SMEM)] + specs,
        out_specs=(out_spec, out_spec),
        compiler_params=pltpu.CompilerParams(vmem_limit_bytes=32 * 1024 * 1024),
        cost_estimate=pl.CostEstimate(
            flops=2 * rows * depth * total,
            bytes_accessed=2 * (rows * (depth + total) + depth * total),
            transcendentals=0,
        ),
    )(core, *operands)


class SeqSum:
    def __init__(self, halves):
        n = lax.axis_size("seq")
        self.z_size = 4 if n % 8 == 0 else n // CORES
        self.x_size = n // (self.z_size * CORES)
        here = lax.axis_index("seq")
        self.z_at = here // CORES % self.z_size
        self.x_at = here // (CORES * self.z_size)
        self.mine, self.other = halves

    def pairs(self, dx, dz):
        def place(x, z, c):
            return (x % self.x_size * self.z_size + z % self.z_size) * CORES + c

        return [
            (place(x, z, c), place(x + dx, z + dz, c))
            for x in range(self.x_size)
            for z in range(self.z_size)
            for c in range(CORES)
        ]

    def over_z(self, array, dim):
        return self.stage(array, dim, self.z_at, self.z_size, lambda k: (0, k))

    def over_x(self, array, dim):
        return self.stage(array, dim, self.x_at, self.x_size, lambda k: (k, 0))

    def stage(self, array, dim, at, size, step):
        total = lax.dynamic_index_in_dim(array, at, dim, False).astype(HIGH)
        for k in far_first(size):
            sent = lax.dynamic_index_in_dim(array, (at + k) % size, dim, False)
            total = total + lax.ppermute(sent, "seq", self.pairs(*step(k))).astype(HIGH)
        return total.astype(LOW)

    def cores(self):
        width = self.mine.shape[1]
        array = (self.mine.astype(HIGH) + swap(self.other, 1).astype(HIGH)).astype(LOW)
        array = array.reshape(self.x_size, self.z_size, -1, width)
        half = width // 256 * 128
        self.one, self.two = array[..., :half], array[..., half:]
        return self.one, self.two

    def first(self):
        self.one, self.two = self.over_z(self.one, 1), self.over_x(self.two, 0)
        return self.one, self.two

    def second(self):
        one, two = self.over_x(self.one, 0), self.over_z(self.two, 0)
        self.total = jnp.concatenate([one, two], axis=1)
        return self.total


def heads_of(matrix):
    return [matrix[:, h * E : (h + 1) * E] for h in range(matrix.shape[1] // E)]


def full_attend(queries, key_rows, value_rows):
    results, logs = [], []
    for q, k, v in zip(heads_of(queries), heads_of(key_rows), heads_of(value_rows)):
        scores = dot_second(q, k) * E ** (-0.5)
        row_max = jnp.max(scores, axis=-1, keepdims=True)
        powers = jnp.exp(scores - row_max)
        totals = jnp.sum(powers, axis=-1, keepdims=True)
        results.append(plain_dot((powers / totals).astype(LOW), v).astype(LOW))
        logs.append(row_max + jnp.log(totals))
    return jnp.concatenate(results, axis=1), logs


def full_attend_back(queries, key_rows, value_rows, logs, grad_result):
    grads = ([], [], [])
    for q, k, v, log, g in zip(
        heads_of(queries), heads_of(key_rows), heads_of(value_rows), logs, heads_of(grad_result)
    ):
        chances = jnp.exp(dot_second(q, k) * E ** (-0.5) - log)
        grad_chances = dot_second(g, v)
        inner = jnp.sum(chances * grad_chances, axis=-1, keepdims=True)
        grad_scores = (chances * (grad_chances - inner) * E ** (-0.5)).astype(LOW)
        grads[0].append(plain_dot(grad_scores, k))
        grads[1].append(dot_first(grad_scores, q))
        grads[2].append(dot_first(chances.astype(LOW), g))
    return [jnp.concatenate(each, axis=1) for each in grads]


def band_scores(q, k, k_prev, below, starts_here):
    current = dot_second(q, k) * E ** (-0.5)
    before = jnp.where(starts_here, MASKED, dot_second(q, k_prev) * E ** (-0.5))
    return jnp.where(below, current, before)


def band_attend(queries, pair, pair_prev, below, starts_here):
    width = queries.shape[1]
    results, logs = [], []
    for q, k, v, kp, vp in zip(
        heads_of(queries),
        heads_of(pair[:, :width]),
        heads_of(pair[:, width:]),
        heads_of(pair_prev[:, :width]),
        heads_of(pair_prev[:, width:]),
    ):
        scores = band_scores(q, k, kp, below, starts_here)
        row_max = jnp.max(scores, axis=-1, keepdims=True)
        powers = jnp.exp(scores - row_max)
        totals = jnp.sum(powers, axis=-1, keepdims=True)
        chances = (powers / totals).astype(LOW)
        none = jnp.zeros_like(chances)
        result = plain_dot(jnp.where(below, chances, none), v) + plain_dot(
            jnp.where(below, none, chances), vp
        )
        results.append(result.astype(LOW))
        logs.append(row_max + jnp.log(totals))
    return jnp.concatenate(results, axis=1), logs


def band_attend_back(queries, pair, pair_prev, below, starts_here, logs, grad_result):
    width = queries.shape[1]
    grads = ([], [], [], [], [])
    for q, k, v, kp, vp, log, g in zip(
        heads_of(queries),
        heads_of(pair[:, :width]),
        heads_of(pair[:, width:]),
        heads_of(pair_prev[:, :width]),
        heads_of(pair_prev[:, width:]),
        logs,
        heads_of(grad_result),
    ):
        chances = jnp.exp(band_scores(q, k, kp, below, starts_here) - log)
        grad_chances = jnp.where(below, dot_second(g, v), dot_second(g, vp))
        inner = jnp.sum(chances * grad_chances, axis=-1, keepdims=True)
        grad_scores = (chances * (grad_chances - inner) * E ** (-0.5)).astype(LOW)
        low_chances = chances.astype(LOW)
        none = jnp.zeros_like(low_chances)
        scores_now = jnp.where(below, grad_scores, none)
        scores_prev = jnp.where(below, none, grad_scores)
        grads[0].append(plain_dot(scores_now, k) + plain_dot(scores_prev, kp))
        grads[1].append(dot_first(scores_now, q))
        grads[2].append(dot_first(jnp.where(below, low_chances, none), g))
        grads[3].append(dot_first(scores_prev, q))
        grads[4].append(dot_first(jnp.where(below, none, low_chances), g))
    query_grad = jnp.concatenate(grads[0], axis=1)
    pair_grad = jnp.concatenate(grads[1] + grads[2], axis=1)
    prev_grad = jnp.concatenate(grads[3] + grads[4], axis=1)
    return query_grad, pair_grad, prev_grad


def body(
    tokens,
    segment_start,
    norm_win,
    qkv_win,
    out_win,
    norm_wffn,
    up_win,
    down_win,
    norm_tok,
    qkv_tok,
    out_tok,
    norm_ffn,
    up_tok,
    down_tok,
    norm_state,
    qkv_state,
    out_state,
    gate_bias,
    norm_sffn,
    up_state,
    down_state,
    init_state,
    cotangent,
):
    seq_index = lax.axis_index("seq")
    tp_index = lax.axis_index("tp")
    n_tp = lax.axis_size("tp")
    position = seq_index % CHAIN
    flags = choose(segment_start, seq_index // CHAIN) == 1
    starts_here = choose(flags, position)
    block_rows, model_width = tokens.shape
    piece_rows = block_rows // n_tp
    state_rows = init_state.shape[0]
    slab_rows = state_rows // CHAIN
    thin_rows = slab_rows // n_tp
    width = qkv_tok.shape[2]
    qkv_win_flat = qkv_win.reshape(model_width, 3 * width)
    out_tok_flat = out_tok.reshape(2 * width, model_width)
    out_state_flat = out_state.reshape(2 * width, model_width)

    row_ids = (jnp.arange(block_rows) + tp_index * piece_rows) % block_rows
    below = row_ids[None, :] <= row_ids[:, None]
    token_rows = turned(tokens, tp_index * piece_rows)

    def natural(pieces):
        whole = jnp.concatenate(pieces)
        return turned(whole, (n_tp - tp_index) % n_tp * piece_rows)

    input_rows = token_rows.astype(HIGH)
    win_normed = layer_norm(input_rows, norm_win).astype(LOW)
    win_qkv = plain_dot(win_normed, qkv_win_flat).astype(LOW)
    win_queries, win_pair = win_qkv[:, :width], win_qkv[:, width:]
    onward = [(s, s + 1) for s in range(lax.axis_size("seq")) if (s + 1) % CHAIN]
    win_prev = lax.ppermute(win_pair, "seq", onward)
    win_heads, win_logs = band_attend(win_queries, win_pair, win_prev, below, starts_here)
    cotangent, qkv_tok, qkv_state, gate_bias, init_state, _ = lax.optimization_barrier(
        (cotangent, qkv_tok, qkv_state, gate_bias, init_state, win_heads)
    )
    qkv_tok_flat = qkv_tok.reshape(model_width, 3 * width)
    qkv_state_flat = qkv_state.reshape(model_width, 3 * width)
    keep_one, keep_two = jax.nn.sigmoid(gate_bias)
    cotangent_rows = turned(cotangent, tp_index * piece_rows)
    own_input = input_rows[:piece_rows]
    win_mixed = own_input + tp_scatter(
        [plain_dot(part, out_win) for part in split_rows(win_heads, n_tp)]
    )
    win_ffn_in = tp_gather(layer_norm(win_mixed, norm_wffn).astype(LOW))
    win_hidden = [plain_dot(part, up_win) for part in win_ffn_in]
    win_active = [gelu_exact(part).astype(LOW) for part in win_hidden]

    init_slab = lax.dynamic_slice_in_dim(init_state, position * slab_rows, slab_rows, 0)

    def own_rows(slab):
        return lax.dynamic_slice_in_dim(slab, tp_index * thin_rows, thin_rows, 0)

    def state_start(slab):
        state_normed = layer_norm(slab.astype(HIGH), norm_state).astype(LOW)
        state_qkv = plain_dot(state_normed, qkv_state_flat).astype(LOW)
        state_queries = state_qkv[:, :width]
        state_pair = jnp.concatenate(pos_gather(state_qkv[:, width:]))
        own, own_logs = full_attend(state_queries, state_pair[:, :width], state_pair[:, width:])
        return state_normed, state_queries, state_pair, own, own_logs

    started = state_start(tied(init_slab, win_ffn_in[1]))
    layer_one = win_mixed + tp_scatter([plain_dot(part, down_win) for part in win_active])
    layer_one = tied(layer_one, started[3])

    normed_pieces = tp_gather(layer_norm(layer_one, norm_tok).astype(LOW))
    normed = jnp.concatenate(normed_pieces)
    token_qkv = plain_dot(normed, qkv_tok_flat).astype(LOW)
    queries, pair = token_qkv[:, :width], token_qkv[:, width:]
    pairs_all = pos_gather(pair)
    pair_prev = jnp.where(position % 2 == 1, pairs_all[1], pairs_all[3])
    pairs_stack = jnp.stack(pairs_all)

    state_slab = init_slab
    turns = []
    states_out = []
    for turn in range(CHAIN):
        state_slab = jnp.where(flags[turn], init_slab, state_slab)
        incoming = state_slab.astype(HIGH)
        if turn:
            started = state_start(state_slab)
        state_normed, state_queries, state_pair, own, own_logs = started
        token_pair = choose(pairs_stack, position ^ turn)
        cross, cross_logs = full_attend(
            state_queries, token_pair[:, :width], token_pair[:, width:]
        )
        state_heads = jnp.concatenate([own, cross], axis=1)
        update = tp_total(plain_dot(state_heads, out_state_flat))
        if turn == 1:
            own_heads, own_token_logs = band_attend(
                tied(queries, state_heads), pair, pair_prev, below, starts_here
            )
            update = tied(update, own_heads)
        mid_state = keep_one * incoming + (1.0 - keep_one) * update
        state_ffn_in = layer_norm(mid_state, norm_sffn).astype(LOW)
        state_hidden = plain_dot(state_ffn_in, up_state)
        state_active = gelu_exact(state_hidden).astype(LOW)
        state_mlp = tp_total(plain_dot(state_active, down_state))
        state_slab = (keep_two * mid_state + (1.0 - keep_two) * state_mlp).astype(LOW)
        states_out.append(own_rows(state_slab))
        turns.append(
            (
                incoming,
                state_normed,
                state_queries,
                state_pair,
                token_pair,
                cross_logs,
                own_logs,
                state_heads,
                update,
                mid_state,
                state_ffn_in,
                state_hidden,
                state_active,
                state_mlp,
            )
        )
    my_state_pair = turns[0][3]
    for turn in range(1, CHAIN):
        my_state_pair = jnp.where(position == turn, turns[turn][3], my_state_pair)

    cross_heads, cross_token_logs = full_attend(
        queries, my_state_pair[:, :width], my_state_pair[:, width:]
    )
    token_heads = jnp.concatenate([own_heads, cross_heads], axis=1)
    proj_total = tp_scatter(
        [plain_dot(part, out_tok_flat) for part in split_rows(token_heads, n_tp)]
    )
    cotangents = split_rows(tied(cotangent_rows, token_heads), n_tp)
    grad_active = [dot_second(part, down_tok) for part in cotangents]
    mixed_one = layer_one + tied(proj_total, *grad_active)
    ffn_in = tp_gather(layer_norm(mixed_one, norm_ffn).astype(LOW))
    hidden = [plain_dot(part, up_tok) for part in ffn_in]

    grad_hidden = [
        gelu_slope(part, grad).astype(LOW) for part, grad in zip(hidden, grad_active)
    ]
    grad_ffn_in = tp_scatter([dot_second(part, up_tok) for part in grad_hidden])
    active = [gelu_exact(part).astype(LOW) for part in hidden]
    back_mixed, grad_norm_ffn = norm_back(mixed_one, norm_ffn, grad_ffn_in)
    grad_mixed = cotangents[0].astype(HIGH) + back_mixed
    grad_proj_pieces = tp_gather(grad_mixed.astype(LOW))
    grad_proj = jnp.concatenate(grad_proj_pieces)
    grad_heads = dot_second(grad_proj, out_tok_flat).astype(LOW)
    cross_query_grad, cross_key_grad, cross_value_grad = full_attend_back(
        queries,
        my_state_pair[:, :width],
        my_state_pair[:, width:],
        cross_token_logs,
        grad_heads[:, width:],
    )
    cross_pair_grad = split_rows(
        jnp.concatenate([cross_key_grad, cross_value_grad], axis=1), CHAIN
    )
    cross_pieces = jnp.stack(
        [cross_pair_grad[0]]
        + [swap(cross_pair_grad[k].astype(LOW), k).astype(HIGH) for k in range(1, CHAIN)]
    )
    homeward = [(s, s - 1) for s in range(lax.axis_size("seq")) if s % CHAIN]

    def own_back():
        query_grad, pair_grad, prev_grad = band_attend_back(
            queries,
            pair,
            pair_prev,
            below,
            starts_here,
            own_token_logs,
            tied(grad_heads[:, :width], cross_pieces),
        )
        returned = lax.ppermute(prev_grad.astype(LOW), "seq", homeward)
        return query_grad + cross_query_grad, pair_grad + returned.astype(HIGH)

    def states_between():
        states_stack = jnp.stack(states_out)
        pieces = [choose(states_stack, position)]
        pieces += [swap(choose(states_stack, position ^ k), k) for k in range(1, CHAIN)]
        pieces = jnp.stack(pieces)
        return jnp.stack([choose(pieces, position ^ q) for q in range(CHAIN)])

    init_grad = jnp.zeros((thin_rows, model_width), HIGH)
    bias_one = bias_two = grad_norm_sffn = grad_norm_state = jnp.zeros((model_width,), HIGH)
    kept_qkv, kept_rest = [], []
    token_pair_grads = [None] * CHAIN
    grad_state = None
    for turn in reversed(range(CHAIN)):
        (
            incoming,
            state_normed,
            state_queries,
            state_pair,
            token_pair,
            cross_logs,
            own_logs,
            state_heads,
            update,
            mid_state,
            state_ffn_in,
            state_hidden,
            state_active,
            state_mlp,
        ) = turns[turn]
        pair_total = choose(cross_pieces, position ^ turn)
        if turn == CHAIN - 1:
            query_total = jnp.zeros((slab_rows, width), HIGH)
        else:
            grad_mlp = ((1.0 - keep_two) * grad_state).astype(LOW)
            bias_two = bias_two + jnp.sum(grad_state * (mid_state - state_mlp), axis=0)
            grad_state_hidden = gelu_slope(
                state_hidden, dot_second(grad_mlp, down_state)
            ).astype(LOW)
            grad_sffn_in = tp_total(dot_second(grad_state_hidden, up_state))
            if turn == CHAIN - 2:
                token_grads = SeqSum(
                    weight_grads(
                        [
                            (tied(tuple(ffn_in), grad_state_hidden), grad_hidden),
                            ([cotangent_rows], active),
                            (grad_proj_pieces, [token_heads]),
                        ]
                    )
                )
                grad_sffn_in = tied(grad_sffn_in, token_grads.other)
            if turn == CHAIN - 3:
                grad_sffn_in = tied(grad_sffn_in, *token_grads.first())
            back_mid, norm_part = norm_back(mid_state, norm_sffn, grad_sffn_in)
            grad_norm_sffn = grad_norm_sffn + norm_part
            grad_mid = keep_two * grad_state + back_mid
            bias_one = bias_one + jnp.sum(grad_mid * (incoming - update), axis=0)
            grad_update = ((1.0 - keep_one) * grad_mid).astype(LOW)
            grad_state_heads = dot_second(grad_update, out_state_flat).astype(LOW)
            own_q, own_k, own_v = full_attend_back(
                state_queries,
                state_pair[:, :width],
                state_pair[:, width:],
                own_logs,
                grad_state_heads[:, :width],
            )
            pair_total = pair_total + pos_scatter(
                split_rows(jnp.concatenate([own_k, own_v], axis=1), CHAIN)
            )
            cross_q, cross_k, cross_v = full_attend_back(
                state_queries,
                token_pair[:, :width],
                token_pair[:, width:],
                cross_logs,
                grad_state_heads[:, width:],
            )
            token_pair_grads[turn] = jnp.concatenate([cross_k, cross_v], axis=1)
            query_total = own_q + cross_q
            if turn == CHAIN - 3:
                slabs = states_between()
                pair_total = tied(pair_total, slabs)
            if turn == CHAIN - 4:
                by_tp = turned(jnp.stack(tp_gather(slabs)), (n_tp - tp_index) % n_tp)
                state_rows_out = jnp.transpose(by_tp, (1, 0, 2, 3)).reshape(
                    state_rows, model_width
                )
                pair_total = tied(pair_total, state_rows_out)
            kept_rest.append(
                (state_heads, grad_update, state_ffn_in, grad_state_hidden, state_active, grad_mlp)
            )
        grad_state_qkv = jnp.concatenate([query_total, pair_total], axis=1).astype(LOW)
        kept_qkv.append((state_normed, grad_state_qkv))
        grad_state_normed = tp_total(dot_second(grad_state_qkv, qkv_state_flat))
        if turn == CHAIN - 1:
            query_grad, pair_grad = own_back()
            grad_state_normed = tied(grad_state_normed, query_grad)
        if turn == CHAIN - 2:
            grad_state_normed = tied(grad_state_normed, *token_grads.cores())
        if turn == CHAIN - 3:
            grad_state_normed = tied(grad_state_normed, token_grads.second())
        back_state, norm_part = norm_back(incoming, norm_state, grad_state_normed)
        grad_norm_state = grad_norm_state + norm_part
        grad_incoming = back_state
        if grad_state is not None:
            grad_incoming = keep_one * grad_mid + back_state
        init_grad = init_grad + jnp.where(flags[turn], own_rows(grad_incoming), 0.0)
        grad_state = jnp.where(flags[turn], 0.0, grad_incoming)
    bias_one = bias_one * keep_one * (1.0 - keep_one) / n_tp
    bias_two = bias_two * keep_two * (1.0 - keep_two) / n_tp
    grad_norm_sffn = grad_norm_sffn / n_tp
    grad_norm_state = grad_norm_state / n_tp
    sum_token = token_grads.total

    token_pair_grads[CHAIN - 1] = jnp.zeros_like(token_pair_grads[0])
    pair_stack = jnp.stack(token_pair_grads)
    pair_grad = pair_grad + pos_scatter([choose(pair_stack, position ^ k) for k in range(CHAIN)])
    grad_qkv = jnp.concatenate([query_grad, pair_grad], axis=1).astype(LOW)
    grad_normed = tp_scatter(
        [dot_second(part, qkv_tok_flat) for part in split_rows(grad_qkv, n_tp)]
    )
    qkv_parts = list(zip(*kept_qkv))
    rest_parts = list(zip(*kept_rest))
    state_grads = SeqSum(
        weight_grads(
            [
                (qkv_parts[0], qkv_parts[1]),
                (rest_parts[1], rest_parts[0]),
                (rest_parts[2], rest_parts[3]),
                (rest_parts[5], rest_parts[4]),
            ]
        )
    )
    grad_normed = tied(grad_normed, state_grads.other)
    back_tokens, grad_norm_tok = norm_back(layer_one, norm_tok, grad_normed)
    grad_layer_one = grad_mixed + back_tokens

    grad_win_out = tp_gather(grad_layer_one.astype(LOW))
    grad_win_hidden = [
        gelu_slope(part, dot_second(grad, down_win)).astype(LOW)
        for part, grad in zip(win_hidden, grad_win_out)
    ]
    grad_win_ffn_in = tp_scatter([dot_second(part, up_win) for part in grad_win_hidden])
    grad_win_ffn_in = tied(grad_win_ffn_in, *state_grads.cores())
    back_win, grad_norm_wffn = norm_back(win_mixed, norm_wffn, grad_win_ffn_in)
    grad_win_mixed = grad_layer_one + back_win
    grad_win_pieces = tp_gather(grad_win_mixed.astype(LOW))
    middle_grads = SeqSum(
        weight_grads(
            [
                (normed_pieces, [grad_qkv]),
                (win_ffn_in, grad_win_hidden),
                (grad_win_out, win_active),
            ]
        )
    )
    grad_win_proj = jnp.concatenate(tied(tuple(grad_win_pieces), middle_grads.other))
    grad_win_heads = dot_second(grad_win_proj, out_win).astype(LOW)
    win_query_grad, win_pair_grad, win_prev_grad = band_attend_back(
        win_queries, win_pair, win_prev, below, starts_here, win_logs, grad_win_heads
    )
    win_returned = lax.ppermute(win_prev_grad.astype(LOW), "seq", homeward)
    win_pair_grad = win_pair_grad + tied(win_returned, *state_grads.first()).astype(HIGH)
    grad_win_qkv = jnp.concatenate([win_query_grad, win_pair_grad], axis=1).astype(LOW)
    sum_state = state_grads.second()
    middle_grads.cores()
    grad_win_normed = tp_scatter(
        [dot_second(part, qkv_win_flat) for part in split_rows(grad_win_qkv, n_tp)]
    )
    back_input, grad_norm_win = norm_back(own_input, norm_win, grad_win_normed)
    grad_token_rows = natural(tp_gather((grad_win_mixed + back_input).astype(LOW)))

    layer_output = mixed_one + tp_scatter([plain_dot(part, down_tok) for part in active])
    output_rows = natural(tp_gather(layer_output.astype(LOW)))

    vectors = [
        grad_norm_win,
        grad_norm_wffn,
        grad_norm_tok,
        grad_norm_ffn,
        grad_norm_state,
        grad_norm_sffn,
        bias_one,
        bias_two,
    ]
    small_rows = jnp.concatenate(
        [init_grad, jnp.stack(vectors), jnp.zeros((8, model_width), HIGH)]
    ).astype(LOW)
    small_width = CHAIN * thin_rows + len(vectors)
    small_padded = small_width + -small_width % 256
    row_of = lax.broadcasted_iota(jnp.int32, (small_rows.shape[0], small_padded), 0)
    column_of = lax.broadcasted_iota(jnp.int32, (small_rows.shape[0], small_padded), 1)
    column_for = jnp.where(
        row_of < thin_rows,
        position * thin_rows + row_of,
        (CHAIN - 1) * thin_rows + row_of,
    )
    selector = (column_of == column_for).astype(LOW)
    last_grads = SeqSum(
        weight_grads(
            [
                ([win_normed], [grad_win_qkv]),
                ([grad_win_proj], [win_heads]),
                ([small_rows], [selector]),
            ]
        )
    )
    middle_grads.first()
    sum_middle = middle_grads.second()
    last_grads.cores()
    last_grads.first()
    sum_last = last_grads.second()
    own_columns = model_width // lax.axis_size("seq")
    small_sums = tp_gather(sum_last[:, 4 * width : 4 * width + small_width])
    init_part = turned(
        jnp.stack([part[:, : CHAIN * thin_rows] for part in small_sums]),
        (n_tp - tp_index) % n_tp,
    ).reshape(n_tp, own_columns, CHAIN, thin_rows)
    sum_init = jnp.transpose(init_part, (2, 0, 3, 1)).reshape(state_rows, own_columns)
    vector_sums = sum(part[:, CHAIN * thin_rows :].astype(HIGH) for part in small_sums)

    def columns(sums, at, count):
        return sums[:, at : at + count].astype(HIGH)

    def qkv_of(sums, at):
        return columns(sums, at, 3 * width).reshape(own_columns, 3, width)

    def out_of(sums, at):
        return columns(sums, at, 2 * width).T.reshape(2, width, own_columns)

    inner_width = up_tok.shape[1]
    return (
        output_rows,
        state_rows_out,
        grad_token_rows,
        vector_sums[:, 0],
        qkv_of(sum_last, 0),
        columns(sum_last, 3 * width, width).T,
        vector_sums[:, 1],
        columns(sum_middle, 3 * width, inner_width),
        columns(sum_middle, 3 * width + inner_width, inner_width).T,
        vector_sums[:, 2],
        qkv_of(sum_middle, 0),
        out_of(sum_token, 2 * inner_width),
        vector_sums[:, 3],
        columns(sum_token, 0, inner_width),
        columns(sum_token, inner_width, inner_width).T,
        vector_sums[:, 4],
        qkv_of(sum_state, 0),
        out_of(sum_state, 3 * width),
        vector_sums[:, 6:8].T,
        vector_sums[:, 5],
        columns(sum_state, 5 * width, inner_width),
        columns(sum_state, 5 * width + inner_width, inner_width).T,
        sum_init.astype(HIGH),
    )

def solution(mesh):
    placed = (
        P("seq", None),
        P(),
        P(),
        P(None, None, "tp"),
        P("tp", None),
        P(),
        P(None, "tp"),
        P("tp", None),
        P(),
        P(None, None, "tp"),
        P(None, "tp", None),
        P(),
        P(None, "tp"),
        P("tp", None),
        P(),
        P(None, None, "tp"),
        P(None, "tp", None),
        P(),
        P(),
        P(None, "tp"),
        P("tp", None),
        P(),
        P("seq", None),
    )
    return jax.shard_map(
        body,
        mesh=mesh,
        in_specs=placed,
        out_specs=(
            P("seq", None),
            P("seq", None),
            P("seq", None),
            P("seq"),
            P("seq", None, "tp"),
            P("tp", "seq"),
            P("seq"),
            P("seq", "tp"),
            P("tp", "seq"),
            P("seq"),
            P("seq", None, "tp"),
            P(None, "tp", "seq"),
            P("seq"),
            P("seq", "tp"),
            P("tp", "seq"),
            P("seq"),
            P("seq", None, "tp"),
            P(None, "tp", "seq"),
            P(None, "seq"),
            P("seq"),
            P("seq", "tp"),
            P("tp", "seq"),
            P(None, "seq"),
        ),
        check_vma=False,
    )
```

```python
import jax
import jax.numpy as jnp
from jax import lax
from jax.experimental import pallas as pl
from jax.experimental.pallas import tpu as pltpu
from jax.sharding import PartitionSpec as P

E = 128
CHAIN = 4
CORES = 2

EPSILON = 1e-05
MASKED = -1e30
LOW = jnp.bfloat16
HIGH = jnp.float32


def layer_norm(matrix, weights):
    average = jnp.mean(matrix, axis=-1, keepdims=True)
    centred = matrix - average
    spread = jnp.mean(centred * centred, axis=-1, keepdims=True)
    return centred * lax.rsqrt(spread + EPSILON) * weights


def gelu_exact(matrix):
    return jax.nn.gelu(matrix, approximate=False)


def gelu_slope(matrix, grad):
    return jax.vjp(gelu_exact, matrix)[1](grad)[0]


def plain_dot(former, latter):
    return jnp.dot(former, latter, preferred_element_type=HIGH)


def dot_first(former, latter):
    return lax.dot_general(
        former, latter, (((0,), (0,)), ((), ())), preferred_element_type=HIGH
    )


def dot_second(former, latter):
    return lax.dot_general(
        former, latter, (((1,), (1,)), ((), ())), preferred_element_type=HIGH
    )


def tied(value, *others):
    return lax.optimization_barrier((value,) + others)[0]


def norm_back(matrix, weights, grad):
    average = jnp.mean(matrix, axis=-1, keepdims=True)
    centred = matrix - average
    spread = jnp.mean(centred * centred, axis=-1, keepdims=True)
    scaled = centred * lax.rsqrt(spread + EPSILON)
    inner = grad * weights
    return lax.rsqrt(spread + EPSILON) * (
        inner
        - jnp.mean(inner, axis=-1, keepdims=True)
        - scaled * jnp.mean(inner * scaled, axis=-1, keepdims=True)
    )


def gain_grad(weights, grads, gain, first):
    rows = lax.dynamic_slice_in_dim(weights, first, grads.shape[0], 0).astype(HIGH)
    gains = lax.dynamic_slice_in_dim(gain, first, grads.shape[0], 0)
    return jnp.sum(rows * grads, axis=1) / gains


def tp_from(array, k):
    n = lax.axis_size("tp")
    return lax.ppermute(array, "tp", [((i + k) % n, i) for i in range(n)])


def tp_to(array, k):
    n = lax.axis_size("tp")
    return lax.ppermute(array, "tp", [(i, (i + k) % n) for i in range(n)])


def far_first(n):
    return sorted(range(1, n), key=lambda k: -min(k, n - k))


def tp_gather(piece):
    n = lax.axis_size("tp")
    found = {k: tp_from(piece, k) for k in far_first(n)}
    return [piece] + [found[k] for k in range(1, n)]


def tp_scatter(parts):
    n = lax.axis_size("tp")
    total = parts[0]
    for k in far_first(n):
        total = total + tp_to(parts[k].astype(LOW), k).astype(HIGH)
    return total


def tp_total(part):
    low = part.astype(LOW)
    total = part
    for k in far_first(lax.axis_size("tp")):
        total = total + tp_to(low, k).astype(HIGH)
    return total


def split_rows(matrix, n):
    size = matrix.shape[0] // n
    return [matrix[k * size : (k + 1) * size] for k in range(n)]


def swap(array, k):
    n = lax.axis_size("seq")
    return lax.ppermute(array, "seq", [(s, s ^ k) for s in range(n)])


def pos_gather(piece):
    beside, across = swap(piece, 1), swap(piece, 2)
    return [piece, beside, across, swap(across, 1)]


def pos_scatter(parts):
    low = jnp.concatenate([parts[1], parts[3]]).astype(LOW)
    here, there = split_rows(swap(low, 1), 2)
    across = swap((parts[2] + there.astype(HIGH)).astype(LOW), 2)
    return parts[0] + here.astype(HIGH) + across.astype(HIGH)


def choose(stacked, index):
    return lax.dynamic_index_in_dim(stacked, index, 0, keepdims=False)


def turned(array, start):
    twice = jnp.concatenate([array, array])
    return lax.dynamic_slice_in_dim(twice, start, array.shape[0], 0)


def weight_grads(pairs):
    n_seq = lax.axis_size("seq")
    depth = pairs[0][0][0].shape[1]
    unit = depth // n_seq
    block = max(256, CORES * unit)
    widths = [latter[0].shape[1] for _, latter in pairs]
    total = sum(widths)
    counts = [(len(former), len(latter)) for former, latter in pairs]
    operands, specs = [], []
    for former, latter in pairs:
        for piece in former:
            operands.append(piece)
            specs.append(pl.BlockSpec((piece.shape[0], block), lambda i: (0, i)))
        for piece in latter:
            operands.append(piece)
            specs.append(pl.BlockSpec(piece.shape, lambda i: (0, 0), pipeline_mode=pl.Buffered(1)))

    def kernel(core_ref, *refs):
        mine_ref, other_ref = refs[-2:]
        first = core_ref[0] == 0

        def keep(product, column):
            columns = slice(column, column + product.shape[1])
            for g in range(block // (CORES * unit)):
                low = product[g * CORES * unit : g * CORES * unit + unit]
                high = product[g * CORES * unit + unit : (g + 1) * CORES * unit]
                rows = slice(g * unit, (g + 1) * unit)
                mine_ref[rows, columns] = jnp.where(first, low, high)
                other_ref[rows, columns] = jnp.where(first, high, low)

        at, column = 0, 0
        for (n_former, n_latter), width in zip(counts, widths):
            former = [ref[...] for ref in refs[at : at + n_former]]
            latter = [ref[...] for ref in refs[at + n_former : at + n_former + n_latter]]
            at += n_former + n_latter
            former = jnp.concatenate(former) if n_former > 1 else former[0]
            latter = jnp.concatenate(latter) if n_latter > 1 else latter[0]
            keep(dot_first(former, latter).astype(LOW), column)
            column += width

    shape = jax.ShapeDtypeStruct((depth // CORES, total), LOW)
    out_spec = pl.BlockSpec((block // CORES, total), lambda i: (i, 0))
    rows = sum(piece.shape[0] for piece in pairs[0][0])
    core = (lax.axis_index("seq") % CORES).astype(jnp.int32).reshape(1)
    return pl.pallas_call(
        kernel,
        out_shape=(shape, shape),
        grid=(depth // block,),
        in_specs=[pl.BlockSpec(memory_space=pltpu.SMEM)] + specs,
        out_specs=(out_spec, out_spec),
        compiler_params=pltpu.CompilerParams(vmem_limit_bytes=20 * 1024 * 1024),
        cost_estimate=pl.CostEstimate(
            flops=2 * rows * depth * total,
            bytes_accessed=2 * (rows * (depth + total) + depth * total),
            transcendentals=0,
        ),
    )(core, *operands)


class SeqSum:
    def __init__(self, halves):
        n = lax.axis_size("seq")
        self.z_size = 4 if n % 8 == 0 else n // CORES
        self.x_size = n // (self.z_size * CORES)
        here = lax.axis_index("seq")
        self.z_at = here // CORES % self.z_size
        self.x_at = here // (CORES * self.z_size)
        self.mine, self.other = halves

    def pairs(self, dx, dz):
        def place(x, z, c):
            return (x % self.x_size * self.z_size + z % self.z_size) * CORES + c

        return [
            (place(x, z, c), place(x + dx, z + dz, c))
            for x in range(self.x_size)
            for z in range(self.z_size)
            for c in range(CORES)
        ]

    def over_z(self, array, dim):
        return self.stage(array, dim, self.z_at, self.z_size, lambda k: (0, k))

    def over_x(self, array, dim):
        return self.stage(array, dim, self.x_at, self.x_size, lambda k: (k, 0))

    def stage(self, array, dim, at, size, step):
        total = lax.dynamic_index_in_dim(array, at, dim, False).astype(HIGH)
        for k in far_first(size):
            sent = lax.dynamic_index_in_dim(array, (at + k) % size, dim, False)
            total = total + lax.ppermute(sent, "seq", self.pairs(*step(k))).astype(HIGH)
        return total

    def cores(self, after):
        width = self.mine.shape[1]
        sent = swap(tied(self.other, after), 1)
        array = (self.mine.astype(HIGH) + sent.astype(HIGH)).astype(LOW)
        array = array.reshape(self.x_size, self.z_size, -1, width)
        half = width // 256 * 128
        self.one, self.two = array[..., :half], array[..., half:]
        return array

    def one_first(self, after):
        self.one = self.over_z(tied(self.one, after), 1).astype(LOW)
        return self.one

    def two_first(self, after):
        self.two = self.over_x(tied(self.two, after), 0).astype(LOW)
        return self.two

    def one_last(self, after):
        self.one = self.over_x(tied(self.one, after), 0)
        return self.one

    def two_last(self, after):
        self.two = self.over_z(tied(self.two, after), 0)
        return self.two

    def columns(self, at, count):
        half = self.one.shape[1]
        if at + count <= half:
            return self.one[:, at : at + count]
        if at >= half:
            return self.two[:, at - half : at - half + count]
        return jnp.concatenate([self.one[:, at:], self.two[:, : at + count - half]], axis=1)


def heads_of(matrix):
    return [matrix[:, h * E : (h + 1) * E] for h in range(matrix.shape[1] // E)]


def full_attend(queries, key_rows, value_rows):
    results, logs = [], []
    for q, k, v in zip(heads_of(queries), heads_of(key_rows), heads_of(value_rows)):
        scores = dot_second(q, k) * E ** (-0.5)
        row_max = jnp.max(scores, axis=-1, keepdims=True)
        powers = jnp.exp(scores - row_max)
        totals = jnp.sum(powers, axis=-1, keepdims=True)
        results.append(plain_dot((powers / totals).astype(LOW), v).astype(LOW))
        logs.append(row_max + jnp.log(totals))
    return jnp.concatenate(results, axis=1), logs


def full_attend_back(queries, key_rows, value_rows, logs, grad_result):
    grads = ([], [], [])
    for q, k, v, log, g in zip(
        heads_of(queries), heads_of(key_rows), heads_of(value_rows), logs, heads_of(grad_result)
    ):
        chances = jnp.exp(dot_second(q, k) * E ** (-0.5) - log)
        grad_chances = dot_second(g, v)
        inner = jnp.sum(chances * grad_chances, axis=-1, keepdims=True)
        grad_scores = (chances * (grad_chances - inner) * E ** (-0.5)).astype(LOW)
        grads[0].append(plain_dot(grad_scores, k))
        grads[1].append(dot_first(grad_scores, q))
        grads[2].append(dot_first(chances.astype(LOW), g))
    return [jnp.concatenate(each, axis=1) for each in grads]


def band_scores(q, k, k_prev, below, starts_here):
    current = dot_second(q, k) * E ** (-0.5)
    before = jnp.where(starts_here, MASKED, dot_second(q, k_prev) * E ** (-0.5))
    return jnp.where(below, current, before)


def band_attend(queries, pair, pair_prev, below, starts_here):
    width = queries.shape[1]
    results, logs = [], []
    for q, k, v, kp, vp in zip(
        heads_of(queries),
        heads_of(pair[:, :width]),
        heads_of(pair[:, width:]),
        heads_of(pair_prev[:, :width]),
        heads_of(pair_prev[:, width:]),
    ):
        scores = band_scores(q, k, kp, below, starts_here)
        row_max = jnp.max(scores, axis=-1, keepdims=True)
        powers = jnp.exp(scores - row_max)
        totals = jnp.sum(powers, axis=-1, keepdims=True)
        chances = (powers / totals).astype(LOW)
        none = jnp.zeros_like(chances)
        result = plain_dot(jnp.where(below, chances, none), v) + plain_dot(
            jnp.where(below, none, chances), vp
        )
        results.append(result.astype(LOW))
        logs.append(row_max + jnp.log(totals))
    return jnp.concatenate(results, axis=1), logs


def band_attend_back(queries, pair, pair_prev, below, starts_here, logs, grad_result):
    width = queries.shape[1]
    grads = ([], [], [], [], [])
    for q, k, v, kp, vp, log, g in zip(
        heads_of(queries),
        heads_of(pair[:, :width]),
        heads_of(pair[:, width:]),
        heads_of(pair_prev[:, :width]),
        heads_of(pair_prev[:, width:]),
        logs,
        heads_of(grad_result),
    ):
        chances = jnp.exp(band_scores(q, k, kp, below, starts_here) - log)
        grad_chances = jnp.where(below, dot_second(g, v), dot_second(g, vp))
        inner = jnp.sum(chances * grad_chances, axis=-1, keepdims=True)
        grad_scores = (chances * (grad_chances - inner) * E ** (-0.5)).astype(LOW)
        low_chances = chances.astype(LOW)
        none = jnp.zeros_like(low_chances)
        scores_now = jnp.where(below, grad_scores, none)
        scores_prev = jnp.where(below, none, grad_scores)
        grads[0].append(plain_dot(scores_now, k) + plain_dot(scores_prev, kp))
        grads[1].append(dot_first(scores_now, q))
        grads[2].append(dot_first(jnp.where(below, low_chances, none), g))
        grads[3].append(dot_first(scores_prev, q))
        grads[4].append(dot_first(jnp.where(below, none, low_chances), g))
    query_grad = jnp.concatenate(grads[0], axis=1)
    pair_grad = jnp.concatenate(grads[1] + grads[2], axis=1)
    prev_grad = jnp.concatenate(grads[3] + grads[4], axis=1)
    return query_grad, pair_grad, prev_grad


def body(
    tokens,
    segment_start,
    norm_win,
    qkv_win,
    out_win,
    norm_wffn,
    up_win,
    down_win,
    norm_tok,
    qkv_tok,
    out_tok,
    norm_ffn,
    up_tok,
    down_tok,
    norm_state,
    qkv_state,
    out_state,
    gate_bias,
    norm_sffn,
    up_state,
    down_state,
    init_state,
    cotangent,
):
    seq_index = lax.axis_index("seq")
    tp_index = lax.axis_index("tp")
    n_tp = lax.axis_size("tp")
    position = seq_index % CHAIN
    flags = choose(segment_start, seq_index // CHAIN) == 1
    starts_here = choose(flags, position)
    block_rows, model_width = tokens.shape
    piece_rows = block_rows // n_tp
    state_rows = init_state.shape[0]
    slab_rows = state_rows // CHAIN
    thin_rows = slab_rows // n_tp
    width = qkv_tok.shape[2]
    qkv_win_flat = qkv_win.reshape(model_width, 3 * width)
    out_tok_flat = out_tok.reshape(2 * width, model_width)
    out_state_flat = out_state.reshape(2 * width, model_width)

    row_ids = (jnp.arange(block_rows) + tp_index * piece_rows) % block_rows
    below = row_ids[None, :] <= row_ids[:, None]
    token_rows = turned(tokens, tp_index * piece_rows)

    def natural(pieces):
        whole = jnp.concatenate(pieces)
        return turned(whole, (n_tp - tp_index) % n_tp * piece_rows)

    input_rows = token_rows.astype(HIGH)
    win_normed = layer_norm(input_rows, norm_win).astype(LOW)
    win_qkv = plain_dot(win_normed, qkv_win_flat).astype(LOW)
    win_queries, win_pair = win_qkv[:, :width], win_qkv[:, width:]
    onward = [(s, s + 1) for s in range(lax.axis_size("seq")) if (s + 1) % CHAIN]
    win_prev = lax.ppermute(win_pair, "seq", onward)
    win_heads, win_logs = band_attend(win_queries, win_pair, win_prev, below, starts_here)
    cotangent, qkv_tok, qkv_state, gate_bias, init_state, _ = lax.optimization_barrier(
        (cotangent, qkv_tok, qkv_state, gate_bias, init_state, win_heads)
    )
    qkv_tok_flat = qkv_tok.reshape(model_width, 3 * width)
    qkv_state_flat = qkv_state.reshape(model_width, 3 * width)
    keep_one, keep_two = jax.nn.sigmoid(gate_bias)
    cotangent_rows = turned(cotangent, tp_index * piece_rows)
    own_input = input_rows[:piece_rows]
    win_mixed = own_input + tp_scatter(
        [plain_dot(part, out_win) for part in split_rows(win_heads, n_tp)]
    )
    win_ffn_in = tp_gather(layer_norm(win_mixed, norm_wffn).astype(LOW))
    win_hidden = [plain_dot(part, up_win) for part in win_ffn_in]
    win_active = [gelu_exact(part).astype(LOW) for part in win_hidden]

    init_slab = lax.dynamic_slice_in_dim(init_state, position * slab_rows, slab_rows, 0)

    def own_rows(slab):
        return lax.dynamic_slice_in_dim(slab, tp_index * thin_rows, thin_rows, 0)

    def state_start(slab):
        state_normed = layer_norm(slab.astype(HIGH), norm_state).astype(LOW)
        state_qkv = plain_dot(state_normed, qkv_state_flat).astype(LOW)
        state_queries = state_qkv[:, :width]
        state_pair = jnp.concatenate(pos_gather(state_qkv[:, width:]))
        own, own_logs = full_attend(state_queries, state_pair[:, :width], state_pair[:, width:])
        return state_normed, state_queries, state_pair, own, own_logs

    started = state_start(tied(init_slab, win_ffn_in[1]))
    layer_one = win_mixed + tp_scatter([plain_dot(part, down_win) for part in win_active])
    layer_one = tied(layer_one, started[3])

    normed_pieces = tp_gather(layer_norm(layer_one, norm_tok).astype(LOW))
    normed = jnp.concatenate(normed_pieces)
    token_qkv = plain_dot(normed, qkv_tok_flat).astype(LOW)
    queries, pair = token_qkv[:, :width], token_qkv[:, width:]
    pairs_all = pos_gather(pair)
    pair_prev = jnp.where(position % 2 == 1, pairs_all[1], pairs_all[3])
    pairs_stack = jnp.stack(pairs_all)

    def state_rest(incoming, state_heads, meanwhile=lambda heads: ()):
        update = tp_total(plain_dot(state_heads, out_state_flat))
        update = tied(update, *meanwhile(state_heads))
        mid_state = keep_one * incoming + (1.0 - keep_one) * update
        state_ffn_in = layer_norm(mid_state, norm_sffn).astype(LOW)
        state_hidden = plain_dot(state_ffn_in, up_state)
        state_active = gelu_exact(state_hidden).astype(LOW)
        state_mlp = tp_total(plain_dot(state_active, down_state))
        slab = (keep_two * mid_state + (1.0 - keep_two) * state_mlp).astype(LOW)
        return slab, (update, mid_state, state_ffn_in, state_hidden, state_active, state_mlp)

    own_done = []

    def own_attention(after):
        own_done.extend(band_attend(tied(queries, after), pair, pair_prev, below, starts_here))
        return own_done[:1]

    state_slab = init_slab
    turns = []
    states_out = []
    for turn in range(CHAIN):
        state_slab = jnp.where(flags[turn], init_slab, state_slab)
        incoming = state_slab.astype(HIGH)
        if turn:
            started = state_start(state_slab)
        state_normed, state_queries, state_pair, own, own_logs = started
        if turn == CHAIN - 1:
            turns.append((incoming, state_normed, state_queries, state_pair, own))
            break
        token_pair = choose(pairs_stack, position ^ turn)
        cross, cross_logs = full_attend(
            state_queries, token_pair[:, :width], token_pair[:, width:]
        )
        state_heads = jnp.concatenate([own, cross], axis=1)
        first = (incoming, state_normed, state_queries, state_pair)
        if turn == 1:
            state_slab, rest = state_rest(incoming, state_heads, own_attention)
        else:
            state_slab, rest = state_rest(incoming, state_heads)
        states_out.append(own_rows(state_slab))
        turns.append(first + (token_pair, cross_logs, own_logs, state_heads) + rest)
    own_heads, own_token_logs = own_done
    my_state_pair = turns[0][3]
    for turn in range(1, CHAIN):
        my_state_pair = jnp.where(position == turn, turns[turn][3], my_state_pair)

    cross_heads, cross_token_logs = full_attend(
        queries, my_state_pair[:, :width], my_state_pair[:, width:]
    )
    token_heads = jnp.concatenate([own_heads, cross_heads], axis=1)
    proj_total = tp_scatter(
        [plain_dot(part, out_tok_flat) for part in split_rows(token_heads, n_tp)]
    )
    cotangents = split_rows(tied(cotangent_rows, token_heads), n_tp)
    grad_active = [dot_second(part, down_tok) for part in cotangents]
    mixed_one = layer_one + tied(proj_total, *grad_active)
    ffn_in = tp_gather(layer_norm(mixed_one, norm_ffn).astype(LOW))
    hidden = [plain_dot(part, up_tok) for part in ffn_in]

    grad_hidden = [
        gelu_slope(part, grad).astype(LOW) for part, grad in zip(hidden, grad_active)
    ]
    active = [gelu_exact(part).astype(LOW) for part in hidden]
    grad_ffn_in = tp_scatter([dot_second(part, up_tok) for part in grad_hidden])
    grad_mixed = cotangents[0].astype(HIGH) + norm_back(mixed_one, norm_ffn, grad_ffn_in)
    grad_proj_pieces = tp_gather(grad_mixed.astype(LOW))
    grad_proj = jnp.concatenate(grad_proj_pieces)
    grad_heads = dot_second(grad_proj, out_tok_flat).astype(LOW)
    cross_query_grad, cross_key_grad, cross_value_grad = full_attend_back(
        queries,
        my_state_pair[:, :width],
        my_state_pair[:, width:],
        cross_token_logs,
        grad_heads[:, width:],
    )
    cross_pair_grad = split_rows(
        jnp.concatenate([cross_key_grad, cross_value_grad], axis=1), CHAIN
    )
    cross_pieces = jnp.stack(
        [cross_pair_grad[0]]
        + [swap(cross_pair_grad[k].astype(LOW), k).astype(HIGH) for k in range(1, CHAIN)]
    )
    homeward = [(s, s - 1) for s in range(lax.axis_size("seq")) if s % CHAIN]

    def own_back():
        query_grad, pair_grad, prev_grad = band_attend_back(
            queries,
            pair,
            pair_prev,
            below,
            starts_here,
            own_token_logs,
            tied(grad_heads[:, :width], cross_pieces),
        )
        returned = lax.ppermute(prev_grad.astype(LOW), "seq", homeward)
        return query_grad + cross_query_grad, pair_grad + returned.astype(HIGH)

    init_grad = jnp.zeros((thin_rows, model_width), HIGH)
    bias_one = bias_two = jnp.zeros((model_width,), HIGH)
    kept_qkv, kept_rest = [], []
    token_pair_grads = [None] * CHAIN
    grad_state = None
    for turn in reversed(range(CHAIN)):
        incoming, state_normed, state_queries, state_pair = turns[turn][:4]
        pair_total = choose(cross_pieces, position ^ turn)
        if turn == CHAIN - 1:
            query_total = jnp.zeros((slab_rows, width), HIGH)
        else:
            (
                token_pair,
                cross_logs,
                own_logs,
                state_heads,
                update,
                mid_state,
                state_ffn_in,
                state_hidden,
                state_active,
                state_mlp,
            ) = turns[turn][4:]
            grad_mlp = ((1.0 - keep_two) * grad_state).astype(LOW)
            bias_two = bias_two + jnp.sum(grad_state * (mid_state - state_mlp), axis=0)
            grad_state_hidden = gelu_slope(
                state_hidden, dot_second(grad_mlp, down_state)
            ).astype(LOW)
            grad_sffn_in = tp_total(dot_second(grad_state_hidden, up_state))
            if turn == CHAIN - 2:
                token_grads = SeqSum(
                    weight_grads(
                        [
                            (tied(tuple(ffn_in), grad_state_hidden), grad_hidden),
                            ([cotangent_rows], active),
                            (grad_proj_pieces, [token_heads]),
                        ]
                    )
                )
                grad_sffn_in = tied(grad_sffn_in, token_grads.other)
            if turn == CHAIN - 3:
                step = token_grads.one_first(grad_state_hidden)
            if turn == CHAIN - 4:
                grad_sffn_in = tied(grad_sffn_in, step)
                step = token_grads.one_last(grad_state_hidden)
            grad_mid = keep_two * grad_state + norm_back(mid_state, norm_sffn, grad_sffn_in)
            bias_one = bias_one + jnp.sum(grad_mid * (incoming - update), axis=0)
            grad_update = ((1.0 - keep_one) * grad_mid).astype(LOW)
            grad_state_heads = dot_second(grad_update, out_state_flat).astype(LOW)
            own_q, own_k, own_v = full_attend_back(
                state_queries,
                state_pair[:, :width],
                state_pair[:, width:],
                own_logs,
                grad_state_heads[:, :width],
            )
            pair_total = pair_total + pos_scatter(
                split_rows(jnp.concatenate([own_k, own_v], axis=1), CHAIN)
            )
            cross_q, cross_k, cross_v = full_attend_back(
                state_queries,
                token_pair[:, :width],
                token_pair[:, width:],
                cross_logs,
                grad_state_heads[:, width:],
            )
            token_pair_grads[turn] = jnp.concatenate([cross_k, cross_v], axis=1)
            query_total = own_q + cross_q
            kept_rest.append(
                (state_heads, grad_update, state_ffn_in, grad_state_hidden, state_active, grad_mlp)
            )
        if turn == CHAIN - 3:
            pair_total = tied(pair_total, step)
        grad_state_qkv = jnp.concatenate([query_total, pair_total], axis=1).astype(LOW)
        kept_qkv.append((state_normed, grad_state_qkv))
        grad_state_normed = tp_total(dot_second(grad_state_qkv, qkv_state_flat))
        if turn == CHAIN - 1:
            query_grad, pair_grad = own_back()
            grad_state_normed = tied(grad_state_normed, query_grad)
        if turn == CHAIN - 2:
            grad_state_normed = tied(grad_state_normed, token_grads.cores(grad_state_qkv))
        if turn == CHAIN - 3:
            step = token_grads.two_first(grad_state_qkv)
        grad_incoming = norm_back(incoming, norm_state, grad_state_normed)
        if grad_state is not None:
            grad_incoming = keep_one * grad_mid + grad_incoming
        init_grad = init_grad + jnp.where(flags[turn], own_rows(grad_incoming), 0.0)
        grad_state = jnp.where(flags[turn], 0.0, grad_incoming)
    bias_one = bias_one * keep_one * (1.0 - keep_one) / n_tp
    bias_two = bias_two * keep_two * (1.0 - keep_two) / n_tp

    token_pair_grads[CHAIN - 1] = jnp.zeros_like(token_pair_grads[0])
    pair_stack = jnp.stack(token_pair_grads)
    pair_grad = pair_grad + pos_scatter([choose(pair_stack, position ^ k) for k in range(CHAIN)])
    layer_output = mixed_one + tp_scatter(
        [plain_dot(part, down_tok) for part in tied(tuple(active), pair_stack)]
    )
    qkv_parts = list(zip(*kept_qkv))
    rest_parts = list(zip(*kept_rest))
    state_grads = SeqSum(
        weight_grads(
            [
                (qkv_parts[0], qkv_parts[1]),
                (rest_parts[1], rest_parts[0]),
                (rest_parts[2], rest_parts[3]),
                (rest_parts[5], rest_parts[4]),
            ]
        )
    )
    pair_grad = tied(pair_grad, step, layer_output, state_grads.other)
    grad_qkv = jnp.concatenate([query_grad, pair_grad], axis=1).astype(LOW)
    grad_normed = tp_scatter(
        [dot_second(part, qkv_tok_flat) for part in split_rows(grad_qkv, n_tp)]
    )
    grad_normed = tied(grad_normed, state_grads.cores(grad_qkv))
    grad_layer_one = grad_mixed + norm_back(layer_one, norm_tok, grad_normed)

    step = token_grads.two_last(grad_layer_one)
    grad_win_out = tp_gather(grad_layer_one.astype(LOW))
    grad_win_hidden = [
        gelu_slope(part, dot_second(grad, down_win)).astype(LOW)
        for part, grad in zip(win_hidden, grad_win_out)
    ]
    grad_win_ffn_in = tp_scatter([dot_second(part, up_win) for part in grad_win_hidden])
    step = state_grads.one_first(step), state_grads.two_first(step)

    small_rows = jnp.concatenate(
        [init_grad, jnp.stack([bias_one, bias_two]), jnp.zeros((14, model_width), HIGH)]
    ).astype(LOW)
    row_of = lax.broadcasted_iota(jnp.int32, (small_rows.shape[0], 256), 0)
    column_of = lax.broadcasted_iota(jnp.int32, (small_rows.shape[0], 256), 1)
    column_for = jnp.where(
        row_of < thin_rows,
        position * thin_rows + row_of,
        (CHAIN - 1) * thin_rows + row_of,
    )
    selector = (column_of == column_for).astype(LOW)
    middle_grads = SeqSum(
        weight_grads(
            [
                (normed_pieces, [grad_qkv]),
                (win_ffn_in, grad_win_hidden),
                (grad_win_out, win_active),
                ([small_rows], [selector]),
            ]
        )
    )
    grad_win_ffn_in = tied(grad_win_ffn_in, *step, middle_grads.other)
    grad_win_mixed = grad_layer_one + norm_back(win_mixed, norm_wffn, grad_win_ffn_in)
    grad_win_pieces = tp_gather(grad_win_mixed.astype(LOW))
    step = middle_grads.cores(grad_win_mixed), state_grads.one_last(grad_win_mixed)
    grad_win_proj = tied(jnp.concatenate(grad_win_pieces), *step)
    grad_win_heads = dot_second(grad_win_proj, out_win).astype(LOW)
    win_query_grad, win_pair_grad, win_prev_grad = band_attend_back(
        win_queries, win_pair, win_prev, below, starts_here, win_logs, grad_win_heads
    )
    step = (
        state_grads.two_last(grad_win_heads),
        middle_grads.one_first(grad_win_heads),
        middle_grads.two_first(grad_win_heads),
    )
    win_returned = lax.ppermute(win_prev_grad.astype(LOW), "seq", homeward)
    win_pair_grad = win_pair_grad + tied(win_returned, *step).astype(HIGH)
    grad_win_qkv = jnp.concatenate([win_query_grad, win_pair_grad], axis=1).astype(LOW)
    last_grads = SeqSum(
        weight_grads([([win_normed], [grad_win_qkv]), ([grad_win_proj], [win_heads])])
    )
    grad_win_normed = tp_scatter(
        [dot_second(part, qkv_win_flat) for part in split_rows(grad_win_qkv, n_tp)]
    )
    step = last_grads.cores(grad_win_qkv)
    step = middle_grads.one_last(step), middle_grads.two_last(step)
    last_grads.one_first(step[0])
    last_grads.two_first(step[1])
    last_grads.one_last(last_grads.two)
    last_grads.two_last(last_grads.two)
    back_input = norm_back(own_input, norm_win, grad_win_normed)
    grad_token_rows = natural(tp_gather((grad_win_mixed + back_input).astype(LOW)))
    output_rows = natural(tp_gather(tied(layer_output.astype(LOW), grad_win_heads)))

    incoming, _, state_queries, _, own = turns[CHAIN - 1]
    token_pair = choose(tied(pairs_stack, grad_win_heads), position ^ (CHAIN - 1))
    cross, _ = full_attend(state_queries, token_pair[:, :width], token_pair[:, width:])
    state_slab, _ = state_rest(incoming, jnp.concatenate([own, cross], axis=1))
    states_out.append(own_rows(state_slab))
    states_stack = jnp.stack(states_out)
    pieces = [choose(states_stack, position)]
    pieces += [swap(choose(states_stack, position ^ k), k) for k in range(1, CHAIN)]
    pieces = jnp.stack(pieces)
    slabs = jnp.stack([choose(pieces, position ^ q) for q in range(CHAIN)])
    by_tp = turned(jnp.stack(tp_gather(slabs)), (n_tp - tp_index) % n_tp)
    state_rows_out = jnp.transpose(by_tp, (1, 0, 2, 3)).reshape(state_rows, model_width)

    own_columns = model_width // lax.axis_size("seq")
    inner_width = up_tok.shape[1]
    sum_qkv_win = last_grads.columns(0, 3 * width)
    sum_qkv_tok = middle_grads.columns(0, 3 * width)
    sum_qkv_state = state_grads.columns(0, 3 * width)
    sum_up_win = middle_grads.columns(3 * width, inner_width)
    sum_up_tok = token_grads.columns(0, inner_width)
    sum_up_state = state_grads.columns(5 * width, inner_width)
    small_sums = middle_grads.columns(3 * width + 2 * inner_width, CHAIN * thin_rows + 2)
    first_row = seq_index * own_columns
    vectors = [
        gain_grad(qkv_win_flat, sum_qkv_win, norm_win, first_row),
        gain_grad(up_win, sum_up_win, norm_wffn, first_row),
        gain_grad(qkv_tok_flat, sum_qkv_tok, norm_tok, first_row),
        gain_grad(up_tok, sum_up_tok, norm_ffn, first_row),
        gain_grad(qkv_state_flat, sum_qkv_state, norm_state, first_row),
        gain_grad(up_state, sum_up_state, norm_sffn, first_row),
    ]
    small_sums = jnp.concatenate([small_sums, jnp.stack(vectors, axis=1)], axis=1)
    small_sums = tp_gather(small_sums)
    init_part = turned(
        jnp.stack([part[:, : CHAIN * thin_rows] for part in small_sums]),
        (n_tp - tp_index) % n_tp,
    ).reshape(n_tp, own_columns, CHAIN, thin_rows)
    sum_init = jnp.transpose(init_part, (2, 0, 3, 1)).reshape(state_rows, own_columns)
    vector_sums = sum(part[:, CHAIN * thin_rows :] for part in small_sums)

    def qkv_of(columns):
        return columns.reshape(own_columns, 3, width)

    def out_of(columns):
        return columns.T.reshape(2, width, own_columns)

    return (
        output_rows,
        state_rows_out,
        grad_token_rows,
        vector_sums[:, 2],
        qkv_of(sum_qkv_win),
        last_grads.columns(3 * width, width).T,
        vector_sums[:, 3],
        sum_up_win,
        middle_grads.columns(3 * width + inner_width, inner_width).T,
        vector_sums[:, 4],
        qkv_of(sum_qkv_tok),
        out_of(token_grads.columns(2 * inner_width, 2 * width)),
        vector_sums[:, 5],
        sum_up_tok,
        token_grads.columns(inner_width, inner_width).T,
        vector_sums[:, 6],
        qkv_of(sum_qkv_state),
        out_of(state_grads.columns(3 * width, 2 * width)),
        vector_sums[:, 0:2].T,
        vector_sums[:, 7],
        sum_up_state,
        state_grads.columns(5 * width + inner_width, inner_width).T,
        sum_init,
    )


def solution(mesh):
    placed = (
        P("seq", None),
        P(),
        P(),
        P(None, None, "tp"),
        P("tp", None),
        P(),
        P(None, "tp"),
        P("tp", None),
        P(),
        P(None, None, "tp"),
        P(None, "tp", None),
        P(),
        P(None, "tp"),
        P("tp", None),
        P(),
        P(None, None, "tp"),
        P(None, "tp", None),
        P(),
        P(),
        P(None, "tp"),
        P("tp", None),
        P(),
        P("seq", None),
    )
    return jax.shard_map(
        body,
        mesh=mesh,
        in_specs=placed,
        out_specs=(
            P("seq", None),
            P("seq", None),
            P("seq", None),
            P("seq"),
            P("seq", None, "tp"),
            P("tp", "seq"),
            P("seq"),
            P("seq", "tp"),
            P("tp", "seq"),
            P("seq"),
            P("seq", None, "tp"),
            P(None, "tp", "seq"),
            P("seq"),
            P("seq", "tp"),
            P("tp", "seq"),
            P("seq"),
            P("seq", None, "tp"),
            P(None, "tp", "seq"),
            P(None, "seq"),
            P("seq"),
            P("seq", "tp"),
            P("tp", "seq"),
            P(None, "seq"),
        ),
        check_vma=False,
    )
```

```python
import jax
import jax.numpy as jnp
from jax import lax
from jax.experimental import pallas as pl
from jax.experimental.layout import Layout, with_layout_constraint
from jax.experimental.pallas import tpu as pltpu
from jax.sharding import PartitionSpec as P

E = 128
CHAIN = 4
CORES = 2

EPSILON = 1e-05
MASKED = -1e30
LOW = jnp.bfloat16
HIGH = jnp.float32


def layer_norm(matrix, weights):
    average = jnp.mean(matrix, axis=-1, keepdims=True)
    centred = matrix - average
    spread = jnp.mean(centred * centred, axis=-1, keepdims=True)
    return centred * lax.rsqrt(spread + EPSILON) * weights


def gelu_exact(matrix):
    return jax.nn.gelu(matrix, approximate=False)


def gelu_slope(matrix, grad):
    return jax.vjp(gelu_exact, matrix)[1](grad)[0]


def plain_dot(former, latter):
    return jnp.dot(former, latter, preferred_element_type=HIGH)


def dot_first(former, latter):
    return lax.dot_general(
        former, latter, (((0,), (0,)), ((), ())), preferred_element_type=HIGH
    )


def dot_second(former, latter):
    return lax.dot_general(
        former, latter, (((1,), (1,)), ((), ())), preferred_element_type=HIGH
    )


def row_major(array):
    return with_layout_constraint(array, Layout(major_to_minor=tuple(range(array.ndim))))


def tied(value, *others):
    return lax.optimization_barrier((value, others))[0]


def norm_back(matrix, weights, grad):
    average = jnp.mean(matrix, axis=-1, keepdims=True)
    centred = matrix - average
    spread = jnp.mean(centred * centred, axis=-1, keepdims=True)
    scaled = centred * lax.rsqrt(spread + EPSILON)
    inner = grad * weights
    return lax.rsqrt(spread + EPSILON) * (
        inner
        - jnp.mean(inner, axis=-1, keepdims=True)
        - scaled * jnp.mean(inner * scaled, axis=-1, keepdims=True)
    )


def gain_grad(weights, grads, gain, first):
    rows = lax.dynamic_slice_in_dim(weights, first, grads.shape[0], 0).astype(HIGH)
    gains = lax.dynamic_slice_in_dim(gain, first, grads.shape[0], 0)
    return jnp.sum(rows * grads, axis=1) / gains


def tp_from(array, k):
    n = lax.axis_size("tp")
    return lax.ppermute(array, "tp", [((i + k) % n, i) for i in range(n)])


def tp_to(array, k):
    n = lax.axis_size("tp")
    return lax.ppermute(array, "tp", [(i, (i + k) % n) for i in range(n)])


def far_first(n):
    return sorted(range(1, n), key=lambda k: -min(k, n - k))


def tp_gather(piece):
    n = lax.axis_size("tp")
    found = {k: tp_from(piece, k) for k in far_first(n)}
    return [piece] + [found[k] for k in range(1, n)]


def tp_scatter(parts):
    n = lax.axis_size("tp")
    total = parts[0]
    for k in far_first(n):
        total = total + tp_to(parts[k].astype(LOW), k).astype(HIGH)
    return total


def tp_total(part):
    low = part.astype(LOW)
    total = part
    for k in far_first(lax.axis_size("tp")):
        total = total + tp_to(low, k).astype(HIGH)
    return total


def split_rows(matrix, n):
    size = matrix.shape[0] // n
    return [matrix[k * size : (k + 1) * size] for k in range(n)]


def swap(array, k):
    n = lax.axis_size("seq")
    return lax.ppermute(array, "seq", [(s, s ^ k) for s in range(n)])


def pos_gather(piece):
    beside, across = swap(piece, 1), swap(piece, 2)
    return [piece, beside, across, swap(across, 1)]


def pos_scatter(parts):
    low = jnp.concatenate([parts[1], parts[3]]).astype(LOW)
    here, there = split_rows(swap(low, 1), 2)
    across = swap((parts[2] + there.astype(HIGH)).astype(LOW), 2)
    return parts[0] + here.astype(HIGH) + across.astype(HIGH)


def choose(stacked, index):
    return lax.dynamic_index_in_dim(stacked, index, 0, keepdims=False)


def turned(array, start):
    twice = jnp.concatenate([array, array])
    return lax.dynamic_slice_in_dim(twice, start, array.shape[0], 0)


def weight_grads(pairs):
    n_seq = lax.axis_size("seq")
    depth = pairs[0][0][0].shape[1]
    unit = depth // n_seq
    block = max(256, CORES * unit)
    widths = [latter[0].shape[1] for _, latter in pairs]
    total = sum(widths)
    counts = [(len(former), len(latter)) for former, latter in pairs]
    operands, specs = [], []
    for former, latter in pairs:
        for piece in former:
            operands.append(piece)
            specs.append(pl.BlockSpec((piece.shape[0], block), lambda i: (0, i)))
        for piece in latter:
            operands.append(piece)
            specs.append(pl.BlockSpec(piece.shape, lambda i: (0, 0), pipeline_mode=pl.Buffered(1)))

    def kernel(core_ref, *refs):
        mine_ref, other_ref = refs[-2:]
        first = core_ref[0] == 0

        def keep(product, column):
            columns = slice(column, column + product.shape[1])
            for g in range(block // (CORES * unit)):
                low = product[g * CORES * unit : g * CORES * unit + unit]
                high = product[g * CORES * unit + unit : (g + 1) * CORES * unit]
                rows = slice(g * unit, (g + 1) * unit)
                mine_ref[rows, columns] = jnp.where(first, low, high)
                other_ref[rows, columns] = jnp.where(first, high, low)

        at, column = 0, 0
        for (n_former, n_latter), width in zip(counts, widths):
            former = [ref[...] for ref in refs[at : at + n_former]]
            latter = [ref[...] for ref in refs[at + n_former : at + n_former + n_latter]]
            at += n_former + n_latter
            former = jnp.concatenate(former) if n_former > 1 else former[0]
            latter = jnp.concatenate(latter) if n_latter > 1 else latter[0]
            keep(dot_first(former, latter).astype(LOW), column)
            column += width

    shape = jax.ShapeDtypeStruct((depth // CORES, total), LOW)
    out_spec = pl.BlockSpec((block // CORES, total), lambda i: (i, 0))
    rows = sum(piece.shape[0] for piece in pairs[0][0])
    core = (lax.axis_index("seq") % CORES).astype(jnp.int32).reshape(1)
    return pl.pallas_call(
        kernel,
        out_shape=(shape, shape),
        grid=(depth // block,),
        in_specs=[pl.BlockSpec(memory_space=pltpu.SMEM)] + specs,
        out_specs=(out_spec, out_spec),
        compiler_params=pltpu.CompilerParams(vmem_limit_bytes=20 * 1024 * 1024),
        cost_estimate=pl.CostEstimate(
            flops=2 * rows * depth * total,
            bytes_accessed=2 * (rows * (depth + total) + depth * total),
            transcendentals=0,
        ),
    )(core, *operands)


class SeqSum:
    def __init__(self, halves):
        n = lax.axis_size("seq")
        self.z_size = 4 if n % 8 == 0 else n // CORES
        self.x_size = n // (self.z_size * CORES)
        here = lax.axis_index("seq")
        self.z_at = here // CORES % self.z_size
        self.x_at = here // (CORES * self.z_size)
        self.mine, self.other = halves

    def pairs(self, dx, dz):
        def place(x, z, c):
            return (x % self.x_size * self.z_size + z % self.z_size) * CORES + c

        return [
            (place(x, z, c), place(x + dx, z + dz, c))
            for x in range(self.x_size)
            for z in range(self.z_size)
            for c in range(CORES)
        ]

    def over_z(self, array, dim):
        return self.stage(array, dim, self.z_at, self.z_size, lambda k: (0, k))

    def over_x(self, array, dim):
        return self.stage(array, dim, self.x_at, self.x_size, lambda k: (k, 0))

    def stage(self, array, dim, at, size, step):
        total = lax.dynamic_index_in_dim(array, at, dim, False).astype(HIGH)
        for k in far_first(size):
            sent = lax.dynamic_index_in_dim(array, (at + k) % size, dim, False)
            total = total + lax.ppermute(sent, "seq", self.pairs(*step(k))).astype(HIGH)
        return row_major(total)

    def cores(self, after):
        width = self.mine.shape[1]
        sent = swap(tied(self.other, after), 1)
        half = width // 256 * 128

        def total(columns):
            part = self.mine[:, columns].astype(HIGH) + sent[:, columns].astype(HIGH)
            return part.astype(LOW).reshape(self.x_size, self.z_size, -1, part.shape[1])

        self.one, self.two = total(slice(0, half)), total(slice(half, width))
        return self.one, self.two

    def one_first(self, after):
        self.one = self.over_z(tied(self.one, after), 1).astype(LOW)
        return self.one

    def two_first(self, after):
        self.two = self.over_x(tied(self.two, after), 0).astype(LOW)
        return self.two

    def one_last(self, after):
        self.one = self.over_x(tied(self.one, after), 0)
        return self.one

    def two_last(self, after):
        self.two = self.over_z(tied(self.two, after), 0)
        return self.two

    def columns(self, at, count):
        half = self.one.shape[1]
        if at + count <= half:
            return self.one[:, at : at + count]
        if at >= half:
            return self.two[:, at - half : at - half + count]
        return jnp.concatenate([self.one[:, at:], self.two[:, : at + count - half]], axis=1)


def heads_of(matrix):
    return [matrix[:, h * E : (h + 1) * E] for h in range(matrix.shape[1] // E)]


def full_attend(queries, key_rows, value_rows):
    results, logs = [], []
    for q, k, v in zip(heads_of(queries), heads_of(key_rows), heads_of(value_rows)):
        scores = dot_second(q, k) * E ** (-0.5)
        row_max = jnp.max(scores, axis=-1, keepdims=True)
        powers = jnp.exp(scores - row_max)
        totals = jnp.sum(powers, axis=-1, keepdims=True)
        results.append(plain_dot((powers / totals).astype(LOW), v).astype(LOW))
        logs.append(row_max + jnp.log(totals))
    return jnp.concatenate(results, axis=1), logs


def full_attend_back(queries, key_rows, value_rows, logs, grad_result):
    grads = ([], [], [])
    for q, k, v, log, g in zip(
        heads_of(queries), heads_of(key_rows), heads_of(value_rows), logs, heads_of(grad_result)
    ):
        chances = jnp.exp(dot_second(q, k) * E ** (-0.5) - log)
        grad_chances = dot_second(g, v)
        inner = jnp.sum(chances * grad_chances, axis=-1, keepdims=True)
        grad_scores = (chances * (grad_chances - inner) * E ** (-0.5)).astype(LOW)
        grads[0].append(plain_dot(grad_scores, k))
        grads[1].append(dot_first(grad_scores, q))
        grads[2].append(dot_first(chances.astype(LOW), g))
    return [jnp.concatenate(each, axis=1) for each in grads]


def band_scores(q, k, k_prev, below, starts_here):
    current = dot_second(q, k) * E ** (-0.5)
    before = jnp.where(starts_here, MASKED, dot_second(q, k_prev) * E ** (-0.5))
    return jnp.where(below, current, before)


def band_attend(queries, pair, pair_prev, below, starts_here):
    width = queries.shape[1]
    results, logs = [], []
    for q, k, v, kp, vp in zip(
        heads_of(queries),
        heads_of(pair[:, :width]),
        heads_of(pair[:, width:]),
        heads_of(pair_prev[:, :width]),
        heads_of(pair_prev[:, width:]),
    ):
        scores = band_scores(q, k, kp, below, starts_here)
        row_max = jnp.max(scores, axis=-1, keepdims=True)
        powers = jnp.exp(scores - row_max)
        totals = jnp.sum(powers, axis=-1, keepdims=True)
        chances = (powers / totals).astype(LOW)
        none = jnp.zeros_like(chances)
        result = plain_dot(jnp.where(below, chances, none), v) + plain_dot(
            jnp.where(below, none, chances), vp
        )
        results.append(result.astype(LOW))
        logs.append(row_max + jnp.log(totals))
    return jnp.concatenate(results, axis=1), logs


def band_attend_back(queries, pair, pair_prev, below, starts_here, logs, grad_result):
    width = queries.shape[1]
    grads, kept = ([], [], [], [], []), []
    for q, k, v, kp, vp, log, g in zip(
        heads_of(queries),
        heads_of(pair[:, :width]),
        heads_of(pair[:, width:]),
        heads_of(pair_prev[:, :width]),
        heads_of(pair_prev[:, width:]),
        logs,
        heads_of(grad_result),
    ):
        chances = jnp.exp(band_scores(q, k, kp, below, starts_here) - log)
        grad_chances = jnp.where(below, dot_second(g, v), dot_second(g, vp))
        inner = jnp.sum(chances * grad_chances, axis=-1, keepdims=True)
        grad_scores = (chances * (grad_chances - inner) * E ** (-0.5)).astype(LOW)
        low_chances = chances.astype(LOW)
        none = jnp.zeros_like(low_chances)
        scores_prev = jnp.where(below, none, grad_scores)
        grads[3].append(dot_first(scores_prev, q))
        grads[4].append(dot_first(jnp.where(below, none, low_chances), g))
        kept.append((q, k, kp, g, scores_prev, grad_scores, low_chances))
    prev_grad = jnp.concatenate(grads[3] + grads[4], axis=1).astype(LOW)
    for q, k, kp, g, scores_prev, grad_scores, low_chances in tied(kept, prev_grad):
        none = jnp.zeros_like(low_chances)
        scores_now = jnp.where(below, grad_scores, none)
        grads[0].append(plain_dot(scores_now, k) + plain_dot(scores_prev, kp))
        grads[1].append(dot_first(scores_now, q))
        grads[2].append(dot_first(jnp.where(below, low_chances, none), g))
    query_grad = jnp.concatenate(grads[0], axis=1)
    pair_grad = jnp.concatenate(grads[1] + grads[2], axis=1)
    return query_grad, pair_grad, prev_grad


def body(
    tokens,
    segment_start,
    norm_win,
    qkv_win,
    out_win,
    norm_wffn,
    up_win,
    down_win,
    norm_tok,
    qkv_tok,
    out_tok,
    norm_ffn,
    up_tok,
    down_tok,
    norm_state,
    qkv_state,
    out_state,
    gate_bias,
    norm_sffn,
    up_state,
    down_state,
    init_state,
    cotangent,
):
    seq_index = lax.axis_index("seq")
    tp_index = lax.axis_index("tp")
    n_tp = lax.axis_size("tp")
    position = seq_index % CHAIN
    flags = choose(segment_start, seq_index // CHAIN) == 1
    starts_here = choose(flags, position)
    block_rows, model_width = tokens.shape
    piece_rows = block_rows // n_tp
    state_rows = init_state.shape[0]
    slab_rows = state_rows // CHAIN
    thin_rows = slab_rows // n_tp
    width = qkv_tok.shape[2]
    qkv_win_flat = qkv_win.reshape(model_width, 3 * width)
    out_tok_flat = out_tok.reshape(2 * width, model_width)
    out_state_flat = out_state.reshape(2 * width, model_width)

    row_ids = (jnp.arange(block_rows) + tp_index * piece_rows) % block_rows
    below = row_ids[None, :] <= row_ids[:, None]
    token_rows = turned(tokens, tp_index * piece_rows)

    def natural(pieces):
        whole = jnp.concatenate(pieces)
        return turned(whole, (n_tp - tp_index) % n_tp * piece_rows)

    input_rows = token_rows.astype(HIGH)
    win_normed = layer_norm(input_rows, norm_win).astype(LOW)
    win_qkv = plain_dot(win_normed, qkv_win_flat).astype(LOW)
    win_queries, win_pair = win_qkv[:, :width], win_qkv[:, width:]
    onward = [(s, s + 1) for s in range(lax.axis_size("seq")) if (s + 1) % CHAIN]
    win_prev = lax.ppermute(win_pair, "seq", onward)
    win_heads, win_logs = band_attend(win_queries, win_pair, win_prev, below, starts_here)
    cotangent, qkv_tok, qkv_state, gate_bias, init_state, _ = lax.optimization_barrier(
        (cotangent, qkv_tok, qkv_state, gate_bias, init_state, win_heads)
    )
    qkv_tok_flat = qkv_tok.reshape(model_width, 3 * width)
    qkv_state_flat = qkv_state.reshape(model_width, 3 * width)
    keep_one, keep_two = jax.nn.sigmoid(gate_bias)
    cotangent_rows = turned(cotangent, tp_index * piece_rows)
    own_input = input_rows[:piece_rows]
    win_mixed = own_input + tp_scatter(
        [plain_dot(part, out_win) for part in split_rows(win_heads, n_tp)]
    )
    win_ffn_in = tp_gather(layer_norm(win_mixed, norm_wffn).astype(LOW))
    win_hidden = [plain_dot(part, up_win) for part in win_ffn_in]
    win_active = [gelu_exact(part).astype(LOW) for part in win_hidden]

    init_slab = lax.dynamic_slice_in_dim(init_state, position * slab_rows, slab_rows, 0)

    def own_rows(slab):
        return lax.dynamic_slice_in_dim(slab, tp_index * thin_rows, thin_rows, 0)

    def state_start(slab):
        state_normed = layer_norm(slab.astype(HIGH), norm_state).astype(LOW)
        state_qkv = plain_dot(state_normed, qkv_state_flat).astype(LOW)
        state_queries = state_qkv[:, :width]
        state_pair = jnp.concatenate(pos_gather(state_qkv[:, width:]))
        own, own_logs = full_attend(state_queries, state_pair[:, :width], state_pair[:, width:])
        return state_normed, state_queries, state_pair, own, own_logs

    started = state_start(tied(init_slab, win_ffn_in[1]))
    layer_one = win_mixed + tp_scatter([plain_dot(part, down_win) for part in win_active])
    layer_one = tied(layer_one, started[3])

    normed_pieces = tp_gather(layer_norm(layer_one, norm_tok).astype(LOW))
    normed = jnp.concatenate(normed_pieces)
    token_qkv = plain_dot(normed, qkv_tok_flat).astype(LOW)
    queries, pair = token_qkv[:, :width], token_qkv[:, width:]
    pairs_all = pos_gather(pair)
    pair_prev = jnp.where(position % 2 == 1, pairs_all[1], pairs_all[3])
    pairs_stack = jnp.stack(pairs_all)

    def state_rest(incoming, state_heads, meanwhile=lambda heads: ()):
        update = tp_total(plain_dot(state_heads, out_state_flat))
        return state_end(incoming, tied(update, *meanwhile(state_heads)))

    def state_end(incoming, update):
        mid_state = keep_one * incoming + (1.0 - keep_one) * update
        state_ffn_in = layer_norm(mid_state, norm_sffn).astype(LOW)
        state_hidden = plain_dot(state_ffn_in, up_state)
        state_active = gelu_exact(state_hidden).astype(LOW)
        state_mlp = tp_total(plain_dot(state_active, down_state))
        slab = (keep_two * mid_state + (1.0 - keep_two) * state_mlp).astype(LOW)
        return slab, (update, mid_state, state_ffn_in, state_hidden, state_active, state_mlp)

    own_done = []

    def own_attention(after):
        own_done.extend(band_attend(tied(queries, after), pair, pair_prev, below, starts_here))
        return own_done[:1]

    state_slab = init_slab
    turns = []
    states_out = []
    for turn in range(CHAIN):
        state_slab = jnp.where(flags[turn], init_slab, state_slab)
        incoming = state_slab.astype(HIGH)
        if turn:
            started = state_start(state_slab)
        state_normed, state_queries, state_pair, own, own_logs = started
        if turn == CHAIN - 1:
            turns.append((incoming, state_normed, state_queries, state_pair, own))
            break
        token_pair = choose(pairs_stack, position ^ turn)
        cross, cross_logs = full_attend(
            state_queries, token_pair[:, :width], token_pair[:, width:]
        )
        state_heads = jnp.concatenate([own, cross], axis=1)
        first = (incoming, state_normed, state_queries, state_pair)
        if turn == 1:
            state_slab, rest = state_rest(incoming, state_heads, own_attention)
        else:
            state_slab, rest = state_rest(incoming, state_heads)
        states_out.append(own_rows(state_slab))
        turns.append(first + (token_pair, cross_logs, own_logs, state_heads) + rest)
    own_heads, own_token_logs = own_done
    my_state_pair = turns[0][3]
    for turn in range(1, CHAIN):
        my_state_pair = jnp.where(position == turn, turns[turn][3], my_state_pair)

    cross_heads, cross_token_logs = full_attend(
        queries, my_state_pair[:, :width], my_state_pair[:, width:]
    )
    token_heads = jnp.concatenate([own_heads, cross_heads], axis=1)
    proj_total = tp_scatter(
        [plain_dot(part, out_tok_flat) for part in split_rows(token_heads, n_tp)]
    )
    cotangents = split_rows(tied(cotangent_rows, token_heads), n_tp)
    grad_active = [dot_second(part, down_tok) for part in cotangents]
    mixed_one = layer_one + tied(proj_total, *grad_active)
    ffn_in = tp_gather(layer_norm(mixed_one, norm_ffn).astype(LOW))
    hidden = [plain_dot(part, up_tok) for part in ffn_in]

    grad_hidden = [
        gelu_slope(part, grad).astype(LOW) for part, grad in zip(hidden, grad_active)
    ]
    active = [gelu_exact(part).astype(LOW) for part in hidden]
    grad_ffn_in = tp_scatter([dot_second(part, up_tok) for part in grad_hidden])
    grad_mixed = cotangents[0].astype(HIGH) + norm_back(mixed_one, norm_ffn, grad_ffn_in)
    grad_proj_pieces = tp_gather(grad_mixed.astype(LOW))
    grad_proj = jnp.concatenate(grad_proj_pieces)
    grad_heads = dot_second(grad_proj, out_tok_flat).astype(LOW)
    cross_query_grad, cross_key_grad, cross_value_grad = full_attend_back(
        queries,
        my_state_pair[:, :width],
        my_state_pair[:, width:],
        cross_token_logs,
        grad_heads[:, width:],
    )
    cross_pair_grad = split_rows(
        jnp.concatenate([cross_key_grad, cross_value_grad], axis=1), CHAIN
    )
    cross_pieces = jnp.stack(
        [cross_pair_grad[0]]
        + [swap(cross_pair_grad[k].astype(LOW), k).astype(HIGH) for k in range(1, CHAIN)]
    )
    homeward = [(s, s - 1) for s in range(lax.axis_size("seq")) if s % CHAIN]

    def own_back():
        query_grad, pair_grad, prev_grad = band_attend_back(
            queries,
            pair,
            pair_prev,
            below,
            starts_here,
            own_token_logs,
            tied(grad_heads[:, :width], cross_pieces),
        )
        returned = lax.ppermute(prev_grad, "seq", homeward)
        return query_grad + cross_query_grad, pair_grad + returned.astype(HIGH)

    incoming, _, state_queries, _, own = turns[CHAIN - 1]
    token_pair = choose(pairs_stack, position ^ (CHAIN - 1))
    cross, _ = full_attend(
        tied(state_queries, grad_heads), token_pair[:, :width], token_pair[:, width:]
    )
    last_heads = jnp.concatenate([own, cross], axis=1)
    last_update = tp_total(plain_dot(last_heads, out_state_flat))

    def last_state(after):
        state_slab, _ = state_end(incoming_last, tied(last_update, after))
        states_stack = jnp.stack(states_out + [own_rows(state_slab)])
        pieces = [choose(states_stack, position)]
        pieces += [swap(choose(states_stack, position ^ k), k) for k in range(1, CHAIN)]
        pieces = jnp.stack(pieces)
        return jnp.stack([choose(pieces, position ^ q) for q in range(CHAIN)])

    def states_whole(slabs):
        by_tp = turned(jnp.stack(tp_gather(slabs)), (n_tp - tp_index) % n_tp)
        return jnp.transpose(by_tp, (1, 0, 2, 3)).reshape(state_rows, model_width)

    incoming_last = incoming

    init_grad = jnp.zeros((thin_rows, model_width), HIGH)
    bias_one = bias_two = jnp.zeros((model_width,), HIGH)
    kept_qkv, kept_rest = [], []
    token_pair_grads = [None] * CHAIN
    grad_state = None
    for turn in reversed(range(CHAIN)):
        incoming, state_normed, state_queries, state_pair = turns[turn][:4]
        pair_total = choose(cross_pieces, position ^ turn)
        if turn == CHAIN - 1:
            query_total = jnp.zeros((slab_rows, width), HIGH)
        else:
            (
                token_pair,
                cross_logs,
                own_logs,
                state_heads,
                update,
                mid_state,
                state_ffn_in,
                state_hidden,
                state_active,
                state_mlp,
            ) = turns[turn][4:]
            grad_mlp = ((1.0 - keep_two) * grad_state).astype(LOW)
            bias_two = bias_two + jnp.sum(grad_state * (mid_state - state_mlp), axis=0)
            grad_state_hidden = gelu_slope(
                state_hidden, dot_second(grad_mlp, down_state)
            ).astype(LOW)
            grad_sffn_in = tp_total(dot_second(grad_state_hidden, up_state))
            if turn == CHAIN - 2:
                token_grads = SeqSum(
                    weight_grads(
                        [
                            (tied(tuple(ffn_in), grad_state_hidden), grad_hidden),
                            ([cotangent_rows], active),
                            (grad_proj_pieces, [token_heads]),
                        ]
                    )
                )
                grad_sffn_in = tied(grad_sffn_in, token_grads.other)
            if turn == CHAIN - 3:
                step = token_grads.one_first(grad_state_hidden)
            if turn == CHAIN - 4:
                grad_sffn_in = tied(grad_sffn_in, step)
                step = token_grads.one_last(grad_state_hidden)
            grad_mid = keep_two * grad_state + norm_back(mid_state, norm_sffn, grad_sffn_in)
            bias_one = bias_one + jnp.sum(grad_mid * (incoming - update), axis=0)
            grad_update = ((1.0 - keep_one) * grad_mid).astype(LOW)
            grad_state_heads = dot_second(grad_update, out_state_flat).astype(LOW)
            own_q, own_k, own_v = full_attend_back(
                state_queries,
                state_pair[:, :width],
                state_pair[:, width:],
                own_logs,
                grad_state_heads[:, :width],
            )
            pair_total = pair_total + pos_scatter(
                split_rows(jnp.concatenate([own_k, own_v], axis=1), CHAIN)
            )
            cross_q, cross_k, cross_v = full_attend_back(
                state_queries,
                token_pair[:, :width],
                token_pair[:, width:],
                cross_logs,
                grad_state_heads[:, width:],
            )
            token_pair_grads[turn] = jnp.concatenate([cross_k, cross_v], axis=1)
            query_total = own_q + cross_q
            kept_rest.append(
                (state_heads, grad_update, state_ffn_in, grad_state_hidden, state_active, grad_mlp)
            )
        if turn == CHAIN - 2:
            slabs = last_state(grad_mid)
            pair_total = tied(pair_total, slabs)
        if turn == CHAIN - 3:
            pair_total = tied(pair_total, step)
        if turn == CHAIN - 4:
            state_rows_out = states_whole(tied(slabs, grad_mid))
            pair_total = tied(pair_total, state_rows_out)
        grad_state_qkv = jnp.concatenate([query_total, pair_total], axis=1).astype(LOW)
        kept_qkv.append((state_normed, grad_state_qkv))
        if turn == 0:
            break
        grad_state_normed = tp_total(dot_second(grad_state_qkv, qkv_state_flat))
        if turn == CHAIN - 1:
            query_grad, pair_grad = own_back()
            grad_state_normed = tied(grad_state_normed, query_grad)
        if turn == CHAIN - 2:
            grad_state_normed = tied(grad_state_normed, token_grads.cores(grad_state_qkv))
        if turn == CHAIN - 3:
            step = token_grads.two_first(grad_state_qkv)
        grad_incoming = norm_back(incoming, norm_state, grad_state_normed)
        if grad_state is not None:
            grad_incoming = keep_one * grad_mid + grad_incoming
        init_grad = init_grad + jnp.where(flags[turn], own_rows(grad_incoming), 0.0)
        grad_state = jnp.where(flags[turn], 0.0, grad_incoming)
    grad_mid_first, grad_qkv_first = grad_mid, grad_state_qkv

    def first_incoming_grad(after):
        normed_grad = tp_total(dot_second(tied(grad_qkv_first, after), qkv_state_flat))
        incoming = turns[0][0]
        return keep_one * grad_mid_first + norm_back(incoming, norm_state, normed_grad)

    bias_one = bias_one * keep_one * (1.0 - keep_one) / n_tp
    bias_two = bias_two * keep_two * (1.0 - keep_two) / n_tp

    token_pair_grads[CHAIN - 1] = jnp.zeros_like(token_pair_grads[0])
    pair_stack = jnp.stack(token_pair_grads)
    pair_grad = pair_grad + pos_scatter([choose(pair_stack, position ^ k) for k in range(CHAIN)])
    layer_output = mixed_one + tp_scatter(
        [plain_dot(part, down_tok) for part in tied(tuple(active), pair_stack)]
    )
    qkv_parts = list(zip(*kept_qkv))
    rest_parts = list(zip(*kept_rest))
    state_grads = SeqSum(
        weight_grads(
            [
                (qkv_parts[0], qkv_parts[1]),
                (rest_parts[1], rest_parts[0]),
                (rest_parts[2], rest_parts[3]),
                (rest_parts[5], rest_parts[4]),
            ]
        )
    )
    pair_grad = tied(pair_grad, step, layer_output, state_grads.other)
    grad_qkv = jnp.concatenate([query_grad, pair_grad], axis=1).astype(LOW)
    grad_normed = tp_scatter(
        [dot_second(part, qkv_tok_flat) for part in split_rows(grad_qkv, n_tp)]
    )
    grad_normed = tied(grad_normed, state_grads.cores(grad_qkv))
    grad_layer_one = grad_mixed + norm_back(layer_one, norm_tok, grad_normed)

    step = token_grads.two_last(grad_layer_one)
    grad_win_out = tp_gather(grad_layer_one.astype(LOW))
    grad_win_hidden = [
        gelu_slope(part, dot_second(grad, down_win)).astype(LOW)
        for part, grad in zip(win_hidden, grad_win_out)
    ]
    parts = [dot_second(part, up_win) for part in grad_win_hidden]
    grad_win_ffn_in = tp_scatter(parts)
    step = step, parts
    step = state_grads.one_first(step), state_grads.two_first(step)

    middle_grads = SeqSum(
        weight_grads(
            [
                (normed_pieces, [grad_qkv]),
                (win_ffn_in, grad_win_hidden),
                (grad_win_out, win_active),
            ]
        )
    )
    grad_win_ffn_in = tied(grad_win_ffn_in, *step, middle_grads.other)
    grad_win_mixed = grad_layer_one + norm_back(win_mixed, norm_wffn, grad_win_ffn_in)
    grad_win_pieces = tp_gather(grad_win_mixed.astype(LOW))
    step = middle_grads.cores(grad_win_mixed), state_grads.one_last(grad_win_mixed)
    grad_win_proj = tied(jnp.concatenate(grad_win_pieces), *step)
    grad_win_heads = dot_second(grad_win_proj, out_win).astype(LOW)
    win_query_grad, win_pair_grad, win_prev_grad = band_attend_back(
        win_queries, win_pair, win_prev, below, starts_here, win_logs, grad_win_heads
    )
    win_returned = lax.ppermute(win_prev_grad, "seq", homeward)
    after = win_query_grad, win_pair_grad
    step = state_grads.two_last(after)
    middle_grads.one_first(after)
    middle_grads.two_first(after)
    first_grad = own_rows(first_incoming_grad(after))
    init_grad = init_grad + jnp.where(flags[0], first_grad, 0.0)
    win_pair_grad = win_pair_grad + tied(win_returned, step).astype(HIGH)
    grad_win_qkv = jnp.concatenate([win_query_grad, win_pair_grad], axis=1).astype(LOW)

    small_rows = jnp.concatenate(
        [init_grad, jnp.stack([bias_one, bias_two]), jnp.zeros((14, model_width), HIGH)]
    ).astype(LOW)
    row_of = lax.broadcasted_iota(jnp.int32, (small_rows.shape[0], 256), 0)
    column_of = lax.broadcasted_iota(jnp.int32, (small_rows.shape[0], 256), 1)
    column_for = jnp.where(
        row_of < thin_rows,
        position * thin_rows + row_of,
        (CHAIN - 1) * thin_rows + row_of,
    )
    selector = (column_of == column_for).astype(LOW)
    last_grads = SeqSum(
        weight_grads(
            [
                ([win_normed], [grad_win_qkv]),
                ([grad_win_proj], [win_heads]),
                ([small_rows], [selector]),
            ]
        )
    )
    grad_win_normed = tp_scatter(
        [dot_second(part, qkv_win_flat) for part in split_rows(grad_win_qkv, n_tp)]
    )
    step = last_grads.cores(last_grads.other)
    step = middle_grads.one_last(step), middle_grads.two_last(step)
    last_grads.one_first(step)
    last_grads.two_first(step)
    step = last_grads.one, last_grads.two
    last_grads.one_last(step)
    last_grads.two_last(step)
    back_input = norm_back(own_input, norm_win, grad_win_normed)
    grad_token_rows = natural(tp_gather((grad_win_mixed + back_input).astype(LOW)))
    output_rows = natural(tp_gather(tied(layer_output.astype(LOW), after)))

    own_columns = model_width // lax.axis_size("seq")
    inner_width = up_tok.shape[1]
    sum_qkv_win = last_grads.columns(0, 3 * width)
    sum_qkv_tok = middle_grads.columns(0, 3 * width)
    sum_qkv_state = state_grads.columns(0, 3 * width)
    sum_up_win = middle_grads.columns(3 * width, inner_width)
    sum_up_tok = token_grads.columns(0, inner_width)
    sum_up_state = state_grads.columns(5 * width, inner_width)
    small_sums = last_grads.columns(4 * width, CHAIN * thin_rows + 2)
    first_row = seq_index * own_columns
    vectors = [
        gain_grad(qkv_win_flat, sum_qkv_win, norm_win, first_row),
        gain_grad(up_win, sum_up_win, norm_wffn, first_row),
        gain_grad(qkv_tok_flat, sum_qkv_tok, norm_tok, first_row),
        gain_grad(up_tok, sum_up_tok, norm_ffn, first_row),
        gain_grad(qkv_state_flat, sum_qkv_state, norm_state, first_row),
        gain_grad(up_state, sum_up_state, norm_sffn, first_row),
    ]
    small_sums = jnp.concatenate([small_sums, jnp.stack(vectors, axis=1)], axis=1)
    small_sums = tp_gather(small_sums)
    init_part = turned(
        jnp.stack([part[:, : CHAIN * thin_rows] for part in small_sums]),
        (n_tp - tp_index) % n_tp,
    ).reshape(n_tp, own_columns, CHAIN, thin_rows)
    sum_init = jnp.transpose(init_part, (2, 0, 3, 1)).reshape(state_rows, own_columns)
    vector_sums = sum(part[:, CHAIN * thin_rows :] for part in small_sums)

    def qkv_of(columns):
        return columns.reshape(own_columns, 3, width)

    def out_of(columns):
        return columns.T.reshape(2, width, own_columns)

    return (
        output_rows,
        state_rows_out,
        grad_token_rows,
        vector_sums[:, 2],
        qkv_of(sum_qkv_win),
        last_grads.columns(3 * width, width).T,
        vector_sums[:, 3],
        sum_up_win,
        middle_grads.columns(3 * width + inner_width, inner_width).T,
        vector_sums[:, 4],
        qkv_of(sum_qkv_tok),
        out_of(token_grads.columns(2 * inner_width, 2 * width)),
        vector_sums[:, 5],
        sum_up_tok,
        token_grads.columns(inner_width, inner_width).T,
        vector_sums[:, 6],
        qkv_of(sum_qkv_state),
        out_of(state_grads.columns(3 * width, 2 * width)),
        vector_sums[:, 0:2].T,
        vector_sums[:, 7],
        sum_up_state,
        state_grads.columns(5 * width + inner_width, inner_width).T,
        sum_init,
    )


def solution(mesh):
    placed = (
        P("seq", None),
        P(),
        P(),
        P(None, None, "tp"),
        P("tp", None),
        P(),
        P(None, "tp"),
        P("tp", None),
        P(),
        P(None, None, "tp"),
        P(None, "tp", None),
        P(),
        P(None, "tp"),
        P("tp", None),
        P(),
        P(None, None, "tp"),
        P(None, "tp", None),
        P(),
        P(),
        P(None, "tp"),
        P("tp", None),
        P(),
        P("seq", None),
    )
    return jax.shard_map(
        body,
        mesh=mesh,
        in_specs=placed,
        out_specs=(
            P("seq", None),
            P("seq", None),
            P("seq", None),
            P("seq"),
            P("seq", None, "tp"),
            P("tp", "seq"),
            P("seq"),
            P("seq", "tp"),
            P("tp", "seq"),
            P("seq"),
            P("seq", None, "tp"),
            P(None, "tp", "seq"),
            P("seq"),
            P("seq", "tp"),
            P("tp", "seq"),
            P("seq"),
            P("seq", None, "tp"),
            P(None, "tp", "seq"),
            P(None, "seq"),
            P("seq"),
            P("seq", "tp"),
            P("tp", "seq"),
            P(None, "seq"),
        ),
        check_vma=False,
    )
```

```python
import jax
import jax.numpy as jnp
from jax import lax
from jax.experimental import pallas as pl
from jax.experimental.layout import Layout, with_layout_constraint
from jax.experimental.pallas import tpu as pltpu
from jax.sharding import PartitionSpec as P

E = 128
CHAIN = 4
CORES = 2

EPSILON = 1e-05
MASKED = -1e30
LOW = jnp.bfloat16
HIGH = jnp.float32


def layer_norm(matrix, weights):
    average = jnp.mean(matrix, axis=-1, keepdims=True)
    centred = matrix - average
    spread = jnp.mean(centred * centred, axis=-1, keepdims=True)
    return centred * lax.rsqrt(spread + EPSILON) * weights


def gelu_exact(matrix):
    return jax.nn.gelu(matrix, approximate=False)


def gelu_slope(matrix, grad):
    return jax.vjp(gelu_exact, matrix)[1](grad)[0]


def plain_dot(former, latter):
    return jnp.dot(former, latter, preferred_element_type=HIGH)


def dot_first(former, latter):
    return lax.dot_general(
        former, latter, (((0,), (0,)), ((), ())), preferred_element_type=HIGH
    )


def dot_second(former, latter):
    return lax.dot_general(
        former, latter, (((1,), (1,)), ((), ())), preferred_element_type=HIGH
    )


def row_major(array):
    return with_layout_constraint(array, Layout(major_to_minor=tuple(range(array.ndim))))


def tied(value, *others):
    return lax.optimization_barrier((value, others))[0]


def norm_back(matrix, weights, grad):
    average = jnp.mean(matrix, axis=-1, keepdims=True)
    centred = matrix - average
    spread = jnp.mean(centred * centred, axis=-1, keepdims=True)
    scaled = centred * lax.rsqrt(spread + EPSILON)
    inner = grad * weights
    return lax.rsqrt(spread + EPSILON) * (
        inner
        - jnp.mean(inner, axis=-1, keepdims=True)
        - scaled * jnp.mean(inner * scaled, axis=-1, keepdims=True)
    )


def gain_grad(weights, grads, gain, first):
    rows = lax.dynamic_slice_in_dim(weights, first, grads.shape[0], 0).astype(HIGH)
    gains = lax.dynamic_slice_in_dim(gain, first, grads.shape[0], 0)
    return jnp.sum(rows * grads, axis=1) / gains


def tp_from(array, k):
    n = lax.axis_size("tp")
    return lax.ppermute(array, "tp", [((i + k) % n, i) for i in range(n)])


def tp_to(array, k):
    n = lax.axis_size("tp")
    return lax.ppermute(array, "tp", [(i, (i + k) % n) for i in range(n)])


def far_first(n):
    return sorted(range(1, n), key=lambda k: -min(k, n - k))


def tp_gather(piece):
    n = lax.axis_size("tp")
    found = {k: tp_from(piece, k) for k in far_first(n)}
    return [piece] + [found[k] for k in range(1, n)]


def tp_scatter(parts):
    n = lax.axis_size("tp")
    total = parts[0]
    for k in far_first(n):
        total = total + tp_to(parts[k].astype(LOW), k).astype(HIGH)
    return total


def tp_total(part):
    low = part.astype(LOW)
    total = part
    for k in far_first(lax.axis_size("tp")):
        total = total + tp_to(low, k).astype(HIGH)
    return total


def split_rows(matrix, n):
    size = matrix.shape[0] // n
    return [matrix[k * size : (k + 1) * size] for k in range(n)]


def swap(array, k):
    n = lax.axis_size("seq")
    return lax.ppermute(array, "seq", [(s, s ^ k) for s in range(n)])


def pos_gather(piece):
    beside, across = swap(piece, 1), swap(piece, 2)
    return [piece, beside, across, swap(across, 1)]


def pos_scatter(parts):
    low = jnp.concatenate([parts[1], parts[3]]).astype(LOW)
    here, there = split_rows(swap(low, 1), 2)
    across = swap((parts[2] + there.astype(HIGH)).astype(LOW), 2)
    return parts[0] + here.astype(HIGH) + across.astype(HIGH)


def choose(stacked, index):
    return lax.dynamic_index_in_dim(stacked, index, 0, keepdims=False)


def turned(array, start):
    twice = jnp.concatenate([array, array])
    return lax.dynamic_slice_in_dim(twice, start, array.shape[0], 0)


def weight_grads(pairs, split=True):
    n_seq = lax.axis_size("seq")
    depth = pairs[0][0][0].shape[1]
    unit = depth // n_seq
    block = max(256, CORES * unit)
    widths = [latter[0].shape[1] for _, latter in pairs]
    total = sum(widths)
    counts = [(len(former), len(latter)) for former, latter in pairs]
    operands, specs = [], []
    for former, latter in pairs:
        for piece in former:
            operands.append(piece)
            specs.append(pl.BlockSpec((piece.shape[0], block), lambda i: (0, i)))
        for piece in latter:
            operands.append(piece)
            specs.append(pl.BlockSpec(piece.shape, lambda i: (0, 0), pipeline_mode=pl.Buffered(1)))

    def kernel(core_ref, *refs):
        mine_ref, other_ref = refs[-2:]
        first = core_ref[0] == 0

        def keep(product, column):
            columns = slice(column, column + product.shape[1])
            if not split:
                other_ref[:, columns] = product
                return
            for g in range(block // (CORES * unit)):
                low = product[g * CORES * unit : g * CORES * unit + unit]
                high = product[g * CORES * unit + unit : (g + 1) * CORES * unit]
                rows = slice(g * unit, (g + 1) * unit)
                mine_ref[rows, columns] = jnp.where(first, low, high)
                other_ref[rows, columns] = jnp.where(first, high, low)

        at, column = 0, 0
        for (n_former, n_latter), width in zip(counts, widths):
            former = [ref[...] for ref in refs[at : at + n_former]]
            latter = [ref[...] for ref in refs[at + n_former : at + n_former + n_latter]]
            at += n_former + n_latter
            former = jnp.concatenate(former) if n_former > 1 else former[0]
            latter = jnp.concatenate(latter) if n_latter > 1 else latter[0]
            keep(dot_first(former, latter).astype(LOW), column)
            column += width

    shapes = [jax.ShapeDtypeStruct((depth // CORES, total), LOW)] * 2
    out_specs = [pl.BlockSpec((block // CORES, total), lambda i: (i, 0))] * 2
    if not split:
        shapes = [jax.ShapeDtypeStruct((depth, total), LOW)]
        out_specs = [pl.BlockSpec((block, total), lambda i: (i, 0))]
    rows = sum(piece.shape[0] for piece in pairs[0][0])
    core = (lax.axis_index("seq") % CORES).astype(jnp.int32).reshape(1)
    return pl.pallas_call(
        kernel,
        out_shape=shapes,
        grid=(depth // block,),
        in_specs=[pl.BlockSpec(memory_space=pltpu.SMEM)] + specs,
        out_specs=out_specs,
        compiler_params=pltpu.CompilerParams(vmem_limit_bytes=20 * 1024 * 1024),
        cost_estimate=pl.CostEstimate(
            flops=2 * rows * depth * total,
            bytes_accessed=2 * (rows * (depth + total) + depth * total),
            transcendentals=0,
        ),
    )(core, *operands)


class ScatterSum:
    def __init__(self, grads):
        self.grads = grads[0]
        self.total = lax.psum_scatter(self.grads, "seq", scatter_dimension=0, tiled=True)

    def columns(self, at, count):
        return self.total[:, at : at + count].astype(HIGH)


class SeqSum:
    def __init__(self, halves):
        n = lax.axis_size("seq")
        self.z_size = 4 if n % 8 == 0 else n // CORES
        self.x_size = n // (self.z_size * CORES)
        here = lax.axis_index("seq")
        self.z_at = here // CORES % self.z_size
        self.x_at = here // (CORES * self.z_size)
        self.mine, self.other = halves

    def pairs(self, dx, dz):
        def place(x, z, c):
            return (x % self.x_size * self.z_size + z % self.z_size) * CORES + c

        return [
            (place(x, z, c), place(x + dx, z + dz, c))
            for x in range(self.x_size)
            for z in range(self.z_size)
            for c in range(CORES)
        ]

    def over_z(self, array, dim):
        return self.stage(array, dim, self.z_at, self.z_size, lambda k: (0, k))

    def over_x(self, array, dim):
        return self.stage(array, dim, self.x_at, self.x_size, lambda k: (k, 0))

    def stage(self, array, dim, at, size, step):
        total = lax.dynamic_index_in_dim(array, at, dim, False).astype(HIGH)
        for k in far_first(size):
            sent = lax.dynamic_index_in_dim(array, (at + k) % size, dim, False)
            total = total + lax.ppermute(sent, "seq", self.pairs(*step(k))).astype(HIGH)
        return row_major(total)

    def cores(self, after):
        width = self.mine.shape[1]
        sent = swap(tied(self.other, after), 1)
        half = width // 256 * 128

        def total(columns):
            part = self.mine[:, columns].astype(HIGH) + sent[:, columns].astype(HIGH)
            return part.astype(LOW).reshape(self.x_size, self.z_size, -1, part.shape[1])

        self.one, self.two = total(slice(0, half)), total(slice(half, width))
        return self.one, self.two

    def one_first(self, after):
        self.one = self.over_z(tied(self.one, after), 1).astype(LOW)
        return self.one

    def two_first(self, after):
        self.two = self.over_x(tied(self.two, after), 0).astype(LOW)
        return self.two

    def one_last(self, after):
        self.one = self.over_x(tied(self.one, after), 0)
        return self.one

    def two_last(self, after):
        self.two = self.over_z(tied(self.two, after), 0)
        return self.two

    def columns(self, at, count):
        half = self.one.shape[1]
        if at + count <= half:
            return self.one[:, at : at + count]
        if at >= half:
            return self.two[:, at - half : at - half + count]
        return jnp.concatenate([self.one[:, at:], self.two[:, : at + count - half]], axis=1)


ATTEND_STEP = 256


def attention_kernel(kernel, shapes, scratch, operands, scalars, work):
    in_vmem = pl.BlockSpec(memory_space=pltpu.VMEM)
    in_smem = pl.BlockSpec(memory_space=pltpu.SMEM)
    products, exps = work
    return pl.pallas_call(
        kernel,
        out_shape=shapes,
        in_specs=[in_smem] * len(scalars) + [in_vmem] * len(operands),
        out_specs=tuple([in_vmem] * len(shapes)),
        scratch_shapes=scratch,
        compiler_params=pltpu.CompilerParams(vmem_limit_bytes=16 * 1024 * 1024),
        cost_estimate=pl.CostEstimate(
            flops=2 * products * E,
            bytes_accessed=sum(2 * operand.size for operand in operands),
            transcendentals=exps,
        ),
    )(*scalars, *operands)


def head_columns(head, width, part):
    return slice(part * width + head * E, part * width + (head + 1) * E)


def score_parts(query, key, before, spot):
    if before is None:
        return dot_second(key, query) * E ** (-0.5), None
    key_before, shift, start, rows = before
    count = key.shape[0]
    key_ids = (lax.broadcasted_iota(jnp.int32, (count, rows), 0) + shift) % count
    query_ids = (lax.broadcasted_iota(jnp.int32, (count, rows), 1) + shift + spot) % count
    below = key_ids <= query_ids
    scores = jnp.where(below, dot_second(key, query), dot_second(key_before, query))
    return jnp.where(below | (start == 0), scores * E ** (-0.5), MASKED), below


def attend(queries, pair, before=None):
    count, width = queries.shape
    heads = width // E
    rows = min(count, ATTEND_STEP)
    scalars = [] if before is None else [part.reshape(1) for part in before[1:]]
    operands = [queries, pair] + ([] if before is None else [before[0]])

    def kernel(*refs):
        scalar_refs, refs = refs[: len(scalars)], refs[len(scalars) :]
        query_ref, pair_ref = refs[:2]
        result_ref, log_ref = refs[-2:]
        for h in range(heads):
            own = slice(h * E, (h + 1) * E)
            key = pair_ref[:, head_columns(h, width, 0)]
            value = pair_ref[:, head_columns(h, width, 1)]
            if before is not None:
                key_before = refs[2][:, head_columns(h, width, 0)]
                value_before = refs[2][:, head_columns(h, width, 1)]
            for spot in range(0, count, rows):
                here = slice(spot, spot + rows)
                mask = None
                if before is not None:
                    mask = key_before, scalar_refs[0][0], scalar_refs[1][0], rows
                scores, below = score_parts(query_ref[here, own], key, mask, spot)
                top = jnp.max(scores, axis=0, keepdims=True)
                powers = jnp.exp(scores - top)
                total = jnp.sum(powers, axis=0, keepdims=True)
                chances = (powers * (1.0 / total)).astype(LOW)
                if before is None:
                    result = dot_first(value, chances)
                else:
                    none = jnp.zeros_like(chances)
                    result = dot_first(value, jnp.where(below, chances, none)) + dot_first(
                        value_before, jnp.where(below, none, chances)
                    )
                result_ref[here, own] = result.T.astype(LOW)
                log_ref[h : h + 1, here] = top + jnp.log(total)

    shapes = (
        jax.ShapeDtypeStruct((count, width), LOW),
        jax.ShapeDtypeStruct((heads, count), HIGH),
    )
    scores_count = heads * count * pair.shape[0]
    return attention_kernel(
        kernel, shapes, [], operands, scalars, (scores_count * len(operands), scores_count)
    )


def attend_back(queries, pair, logs, grad_result, before=None):
    count, width = queries.shape
    heads = width // E
    rows = min(count, ATTEND_STEP)
    keys = pair.shape[0]
    scalars = [] if before is None else [part.reshape(1) for part in before[1:]]
    operands = [queries, logs, grad_result, pair] + ([] if before is None else [before[0]])

    def kernel(*refs):
        scalar_refs, refs = refs[: len(scalars)], refs[len(scalars) :]
        query_ref, log_ref, grad_ref, pair_ref = refs[:4]
        outs = refs[len(operands) :]
        query_out, pair_out = outs[:2]
        for h in range(heads):
            own = slice(h * E, (h + 1) * E)
            key_at, value_at = head_columns(h, width, 0), head_columns(h, width, 1)
            key, value = pair_ref[:, key_at], pair_ref[:, value_at]
            if before is not None:
                key_before, value_before = refs[4][:, key_at], refs[4][:, value_at]
            sums = [jnp.zeros((keys, E), HIGH)] * 4
            for spot in range(0, count, rows):
                here = slice(spot, spot + rows)
                query, grad = query_ref[here, own], grad_ref[here, own]
                mask = None
                if before is not None:
                    mask = key_before, scalar_refs[0][0], scalar_refs[1][0], rows
                scores, below = score_parts(query, key, mask, spot)
                chances = jnp.exp(scores - log_ref[h : h + 1, here])
                grad_chances = dot_second(value, grad)
                if before is not None:
                    grad_chances = jnp.where(below, grad_chances, dot_second(value_before, grad))
                inner = jnp.sum(chances * grad_chances, axis=0, keepdims=True)
                grad_scores = (chances * (grad_chances - inner) * E ** (-0.5)).astype(LOW)
                chances = chances.astype(LOW)
                if before is None:
                    query_grad = dot_first(key, grad_scores)
                    terms = [plain_dot(grad_scores, query), plain_dot(chances, grad)]
                else:
                    none = jnp.zeros_like(chances)
                    scores_now = jnp.where(below, grad_scores, none)
                    scores_before = jnp.where(below, none, grad_scores)
                    query_grad = dot_first(key, scores_now) + dot_first(key_before, scores_before)
                    terms = [
                        plain_dot(scores_now, query),
                        plain_dot(jnp.where(below, chances, none), grad),
                        plain_dot(scores_before, query),
                        plain_dot(jnp.where(below, none, chances), grad),
                    ]
                query_out[here, own] = query_grad.T
                sums = [one + two for one, two in zip(sums, terms)]
            pair_out[:, key_at] = sums[0]
            pair_out[:, value_at] = sums[1]
            if before is not None:
                outs[2][:, key_at] = sums[2].astype(LOW)
                outs[2][:, value_at] = sums[3].astype(LOW)

    shapes = [
        jax.ShapeDtypeStruct((count, width), HIGH),
        jax.ShapeDtypeStruct((keys, 2 * width), HIGH),
    ]
    if before is not None:
        shapes.append(jax.ShapeDtypeStruct((keys, 2 * width), LOW))
    scores_count = heads * count * keys
    return attention_kernel(
        kernel,
        tuple(shapes),
        [],
        operands,
        scalars,
        (scores_count * (5 if before is None else 10), scores_count),
    )


def body(
    tokens,
    segment_start,
    norm_win,
    qkv_win,
    out_win,
    norm_wffn,
    up_win,
    down_win,
    norm_tok,
    qkv_tok,
    out_tok,
    norm_ffn,
    up_tok,
    down_tok,
    norm_state,
    qkv_state,
    out_state,
    gate_bias,
    norm_sffn,
    up_state,
    down_state,
    init_state,
    cotangent,
):
    seq_index = lax.axis_index("seq")
    tp_index = lax.axis_index("tp")
    n_tp = lax.axis_size("tp")
    position = seq_index % CHAIN
    flags = choose(segment_start, seq_index // CHAIN) == 1
    starts_here = choose(flags, position)
    block_rows, model_width = tokens.shape
    piece_rows = block_rows // n_tp
    state_rows = init_state.shape[0]
    slab_rows = state_rows // CHAIN
    thin_rows = slab_rows // n_tp
    width = qkv_tok.shape[2]
    qkv_win_flat = qkv_win.reshape(model_width, 3 * width)
    out_tok_flat = out_tok.reshape(2 * width, model_width)
    out_state_flat = out_state.reshape(2 * width, model_width)

    shift = (tp_index * piece_rows).astype(jnp.int32)
    start_flag = starts_here.astype(jnp.int32)
    token_rows = turned(tokens, tp_index * piece_rows)

    def natural(pieces):
        whole = jnp.concatenate(pieces)
        return turned(whole, (n_tp - tp_index) % n_tp * piece_rows)

    input_rows = token_rows.astype(HIGH)
    win_normed = layer_norm(input_rows, norm_win).astype(LOW)
    win_qkv = plain_dot(win_normed, qkv_win_flat).astype(LOW)
    win_queries, win_pair = win_qkv[:, :width], win_qkv[:, width:]
    onward = [(s, s + 1) for s in range(lax.axis_size("seq")) if (s + 1) % CHAIN]
    win_prev = lax.ppermute(win_pair, "seq", onward)
    win_before = win_prev, shift, start_flag
    win_heads, win_logs = attend(win_queries, win_pair, win_before)
    cotangent, qkv_tok, qkv_state, gate_bias, init_state, _ = lax.optimization_barrier(
        (cotangent, qkv_tok, qkv_state, gate_bias, init_state, win_heads)
    )
    qkv_tok_flat = qkv_tok.reshape(model_width, 3 * width)
    qkv_state_flat = qkv_state.reshape(model_width, 3 * width)
    keep_one, keep_two = jax.nn.sigmoid(gate_bias)
    cotangent_rows = turned(cotangent, tp_index * piece_rows)
    own_input = input_rows[:piece_rows]
    win_mixed = own_input + tp_scatter(
        [plain_dot(part, out_win) for part in split_rows(win_heads, n_tp)]
    )
    win_ffn_in = tp_gather(layer_norm(win_mixed, norm_wffn).astype(LOW))
    win_hidden = [plain_dot(part, up_win) for part in win_ffn_in]
    win_active = [gelu_exact(part).astype(LOW) for part in win_hidden]

    init_slab = lax.dynamic_slice_in_dim(init_state, position * slab_rows, slab_rows, 0)

    def own_rows(slab):
        return lax.dynamic_slice_in_dim(slab, tp_index * thin_rows, thin_rows, 0)

    def state_start(slab):
        state_normed = layer_norm(slab.astype(HIGH), norm_state).astype(LOW)
        state_qkv = plain_dot(state_normed, qkv_state_flat).astype(LOW)
        state_queries = state_qkv[:, :width]
        state_pair = jnp.concatenate(pos_gather(state_qkv[:, width:]))
        own, own_logs = attend(state_queries, state_pair)
        return state_normed, state_queries, state_pair, own, own_logs

    started = state_start(tied(init_slab, win_ffn_in[1]))
    layer_one = win_mixed + tp_scatter([plain_dot(part, down_win) for part in win_active])
    layer_one = tied(layer_one, started[3])

    normed_pieces = tp_gather(layer_norm(layer_one, norm_tok).astype(LOW))
    normed = jnp.concatenate(normed_pieces)
    token_qkv = plain_dot(normed, qkv_tok_flat).astype(LOW)
    queries, pair = token_qkv[:, :width], token_qkv[:, width:]
    pairs_all = pos_gather(pair)
    pair_prev = jnp.where(position % 2 == 1, pairs_all[1], pairs_all[3])
    pairs_stack = jnp.stack(pairs_all)
    before = pair_prev, shift, start_flag

    def state_rest(incoming, state_heads, meanwhile=lambda heads: ()):
        update = tp_total(plain_dot(state_heads, out_state_flat))
        return state_end(incoming, tied(update, *meanwhile(state_heads)))

    def state_end(incoming, update):
        mid_state = keep_one * incoming + (1.0 - keep_one) * update
        state_ffn_in = layer_norm(mid_state, norm_sffn).astype(LOW)
        state_hidden = plain_dot(state_ffn_in, up_state)
        state_active = gelu_exact(state_hidden).astype(LOW)
        state_mlp = tp_total(plain_dot(state_active, down_state))
        slab = (keep_two * mid_state + (1.0 - keep_two) * state_mlp).astype(LOW)
        return slab, (update, mid_state, state_ffn_in, state_hidden, state_active, state_mlp)

    own_done = []

    def own_attention(after):
        own_done.extend(attend(tied(queries, after), pair, before))
        return own_done[:1]

    state_slab = init_slab
    turns = []
    states_out = []
    for turn in range(CHAIN):
        state_slab = jnp.where(flags[turn], init_slab, state_slab)
        incoming = state_slab.astype(HIGH)
        if turn:
            started = state_start(state_slab)
        state_normed, state_queries, state_pair, own, own_logs = started
        if turn == CHAIN - 1:
            turns.append((incoming, state_normed, state_queries, state_pair, own))
            break
        token_pair = choose(pairs_stack, position ^ turn)
        cross, cross_logs = attend(state_queries, token_pair)
        state_heads = jnp.concatenate([own, cross], axis=1)
        first = (incoming, state_normed, state_queries, state_pair)
        if turn == 1:
            state_slab, rest = state_rest(incoming, state_heads, own_attention)
        else:
            state_slab, rest = state_rest(incoming, state_heads)
        states_out.append(own_rows(state_slab))
        turns.append(first + (token_pair, cross_logs, own_logs, state_heads) + rest)
    own_heads, own_token_logs = own_done
    my_state_pair = turns[0][3]
    for turn in range(1, CHAIN):
        my_state_pair = jnp.where(position == turn, turns[turn][3], my_state_pair)

    cross_heads, cross_token_logs = attend(queries, my_state_pair)
    token_heads = jnp.concatenate([own_heads, cross_heads], axis=1)
    proj_total = tp_scatter(
        [plain_dot(part, out_tok_flat) for part in split_rows(token_heads, n_tp)]
    )
    cotangents = split_rows(tied(cotangent_rows, token_heads), n_tp)
    grad_active = [dot_second(part, down_tok) for part in cotangents]
    mixed_one = layer_one + tied(proj_total, *grad_active)
    ffn_in = tp_gather(layer_norm(mixed_one, norm_ffn).astype(LOW))
    hidden = [plain_dot(part, up_tok) for part in ffn_in]

    grad_hidden = [
        gelu_slope(part, grad).astype(LOW) for part, grad in zip(hidden, grad_active)
    ]
    active = [gelu_exact(part).astype(LOW) for part in hidden]
    grad_ffn_in = tp_scatter([dot_second(part, up_tok) for part in grad_hidden])
    grad_mixed = cotangents[0].astype(HIGH) + norm_back(mixed_one, norm_ffn, grad_ffn_in)
    grad_proj_pieces = tp_gather(grad_mixed.astype(LOW))
    grad_proj = jnp.concatenate(grad_proj_pieces)
    grad_heads = dot_second(grad_proj, out_tok_flat).astype(LOW)
    cross_query_grad, cross_pair_grad = attend_back(
        queries, my_state_pair, cross_token_logs, grad_heads[:, width:]
    )
    cross_pair_grad = split_rows(cross_pair_grad, CHAIN)
    cross_pieces = jnp.stack(
        [cross_pair_grad[0]]
        + [swap(cross_pair_grad[k].astype(LOW), k).astype(HIGH) for k in range(1, CHAIN)]
    )
    homeward = [(s, s - 1) for s in range(lax.axis_size("seq")) if s % CHAIN]

    def own_back():
        query_grad, pair_grad, prev_grad = attend_back(
            queries, pair, own_token_logs, tied(grad_heads[:, :width], cross_pieces), before
        )
        returned = lax.ppermute(prev_grad, "seq", homeward)
        return query_grad + cross_query_grad, pair_grad + returned.astype(HIGH)

    incoming, _, state_queries, _, own = turns[CHAIN - 1]
    token_pair = choose(pairs_stack, position ^ (CHAIN - 1))
    cross, _ = attend(tied(state_queries, grad_heads), token_pair)
    last_heads = jnp.concatenate([own, cross], axis=1)
    last_update = tp_total(plain_dot(last_heads, out_state_flat))

    def last_state(after):
        return state_end(incoming_last, tied(last_update, after))[0]

    def states_between(state_slab):
        states_stack = jnp.stack(states_out + [own_rows(state_slab)])
        pieces = [choose(states_stack, position)]
        pieces += [swap(choose(states_stack, position ^ k), k) for k in range(1, CHAIN)]
        pieces = jnp.stack(pieces)
        return jnp.stack([choose(pieces, position ^ q) for q in range(CHAIN)])

    def states_whole(slabs):
        by_tp = turned(jnp.stack(tp_gather(slabs)), (n_tp - tp_index) % n_tp)
        return jnp.transpose(by_tp, (1, 0, 2, 3)).reshape(state_rows, model_width)

    incoming_last = incoming

    init_grad = jnp.zeros((thin_rows, model_width), HIGH)
    bias_one = bias_two = jnp.zeros((model_width,), HIGH)
    kept_qkv, kept_rest = [], []
    token_pair_grads = [None] * CHAIN
    grad_state = None
    for turn in reversed(range(CHAIN)):
        incoming, state_normed, state_queries, state_pair = turns[turn][:4]
        pair_total = choose(cross_pieces, position ^ turn)
        if turn == CHAIN - 1:
            query_total = jnp.zeros((slab_rows, width), HIGH)
        else:
            (
                token_pair,
                cross_logs,
                own_logs,
                state_heads,
                update,
                mid_state,
                state_ffn_in,
                state_hidden,
                state_active,
                state_mlp,
            ) = turns[turn][4:]
            grad_mlp = ((1.0 - keep_two) * grad_state).astype(LOW)
            bias_two = bias_two + jnp.sum(grad_state * (mid_state - state_mlp), axis=0)
            grad_state_hidden = gelu_slope(
                state_hidden, dot_second(grad_mlp, down_state)
            ).astype(LOW)
            grad_sffn_in = tp_total(dot_second(grad_state_hidden, up_state))
            if turn == CHAIN - 2:
                token_grads = ScatterSum(
                    weight_grads(
                        [
                            (tied(tuple(ffn_in), grad_state_hidden), grad_hidden),
                            ([cotangent_rows], active),
                            (grad_proj_pieces, [token_heads]),
                        ],
                        False,
                    )
                )
                grad_sffn_in = tied(grad_sffn_in, token_grads.grads)
            grad_mid = keep_two * grad_state + norm_back(mid_state, norm_sffn, grad_sffn_in)
            bias_one = bias_one + jnp.sum(grad_mid * (incoming - update), axis=0)
            grad_update = ((1.0 - keep_one) * grad_mid).astype(LOW)
            grad_state_heads = dot_second(grad_update, out_state_flat).astype(LOW)
            own_q, own_pair = attend_back(
                state_queries, state_pair, own_logs, grad_state_heads[:, :width]
            )
            pair_total = pair_total + pos_scatter(split_rows(own_pair, CHAIN))
            cross_q, token_pair_grads[turn] = attend_back(
                state_queries, token_pair, cross_logs, grad_state_heads[:, width:]
            )
            query_total = own_q + cross_q
            kept_rest.append(
                (state_heads, grad_update, state_ffn_in, grad_state_hidden, state_active, grad_mlp)
            )
        if turn == CHAIN - 2:
            last_slab = last_state(grad_mid)
            pair_total = tied(pair_total, last_slab)
        if turn == CHAIN - 3:
            slabs = states_between(tied(last_slab, grad_mid))
            pair_total = tied(pair_total, slabs)
        if turn == CHAIN - 4:
            state_rows_out = states_whole(tied(slabs, grad_mid))
            pair_total = tied(pair_total, state_rows_out)
        grad_state_qkv = jnp.concatenate([query_total, pair_total], axis=1).astype(LOW)
        kept_qkv.append((state_normed, grad_state_qkv))
        if turn == 0:
            break
        grad_state_normed = tp_total(dot_second(grad_state_qkv, qkv_state_flat))
        if turn == CHAIN - 1:
            query_grad, pair_grad = own_back()
            grad_state_normed = tied(grad_state_normed, query_grad)
        grad_incoming = norm_back(incoming, norm_state, grad_state_normed)
        if grad_state is not None:
            grad_incoming = keep_one * grad_mid + grad_incoming
        init_grad = init_grad + jnp.where(flags[turn], own_rows(grad_incoming), 0.0)
        grad_state = jnp.where(flags[turn], 0.0, grad_incoming)
    grad_mid_first, grad_qkv_first = grad_mid, grad_state_qkv

    def first_incoming_grad(after):
        normed_grad = tp_total(dot_second(tied(grad_qkv_first, after), qkv_state_flat))
        incoming = turns[0][0]
        return keep_one * grad_mid_first + norm_back(incoming, norm_state, normed_grad)

    bias_one = bias_one * keep_one * (1.0 - keep_one) / n_tp
    bias_two = bias_two * keep_two * (1.0 - keep_two) / n_tp

    token_pair_grads[CHAIN - 1] = jnp.zeros_like(token_pair_grads[0])
    pair_stack = jnp.stack(token_pair_grads)
    pair_grad = pair_grad + pos_scatter([choose(pair_stack, position ^ k) for k in range(CHAIN)])
    layer_output = mixed_one + tp_scatter(
        [plain_dot(part, down_tok) for part in tied(tuple(active), pair_stack)]
    )
    qkv_parts = list(zip(*kept_qkv))
    rest_parts = list(zip(*kept_rest))
    state_grads = ScatterSum(
        weight_grads(
            [
                (qkv_parts[0], qkv_parts[1]),
                (rest_parts[1], rest_parts[0]),
                (rest_parts[2], rest_parts[3]),
                (rest_parts[5], rest_parts[4]),
            ],
            False,
        )
    )
    pair_grad = tied(pair_grad, layer_output, state_grads.grads)
    grad_qkv = jnp.concatenate([query_grad, pair_grad], axis=1).astype(LOW)
    grad_normed = tp_scatter(
        [dot_second(part, qkv_tok_flat) for part in split_rows(grad_qkv, n_tp)]
    )
    grad_layer_one = grad_mixed + norm_back(layer_one, norm_tok, grad_normed)

    grad_win_out = tp_gather(grad_layer_one.astype(LOW))
    grad_win_hidden = [
        gelu_slope(part, dot_second(grad, down_win)).astype(LOW)
        for part, grad in zip(win_hidden, grad_win_out)
    ]
    grad_win_ffn_in = tp_scatter([dot_second(part, up_win) for part in grad_win_hidden])

    middle_grads = SeqSum(
        weight_grads(
            [
                (normed_pieces, [grad_qkv]),
                (win_ffn_in, grad_win_hidden),
                (grad_win_out, win_active),
            ]
        )
    )
    grad_win_ffn_in = tied(grad_win_ffn_in, middle_grads.other)
    grad_win_mixed = grad_layer_one + norm_back(win_mixed, norm_wffn, grad_win_ffn_in)
    grad_win_pieces = tp_gather(grad_win_mixed.astype(LOW))
    step = middle_grads.cores(grad_win_mixed)
    grad_win_proj = tied(jnp.concatenate(grad_win_pieces), step)
    grad_win_heads = dot_second(grad_win_proj, out_win).astype(LOW)
    win_query_grad, win_pair_grad, win_prev_grad = attend_back(
        win_queries, win_pair, win_logs, grad_win_heads, win_before
    )
    win_returned = lax.ppermute(win_prev_grad, "seq", homeward)
    after = win_query_grad, win_pair_grad
    step = middle_grads.one_first(grad_win_heads), middle_grads.two_first(grad_win_heads)
    first_grad = own_rows(first_incoming_grad(after))
    init_grad = init_grad + jnp.where(flags[0], first_grad, 0.0)
    win_pair_grad = win_pair_grad + tied(win_returned, step).astype(HIGH)
    grad_win_qkv = jnp.concatenate([win_query_grad, win_pair_grad], axis=1).astype(LOW)

    small_rows = jnp.concatenate(
        [init_grad, jnp.stack([bias_one, bias_two]), jnp.zeros((14, model_width), HIGH)]
    ).astype(LOW)
    row_of = lax.broadcasted_iota(jnp.int32, (small_rows.shape[0], 256), 0)
    column_of = lax.broadcasted_iota(jnp.int32, (small_rows.shape[0], 256), 1)
    column_for = jnp.where(
        row_of < thin_rows,
        position * thin_rows + row_of,
        (CHAIN - 1) * thin_rows + row_of,
    )
    selector = (column_of == column_for).astype(LOW)
    last_grads = SeqSum(
        weight_grads(
            [
                ([win_normed], [grad_win_qkv]),
                ([grad_win_proj], [win_heads]),
                ([small_rows], [selector]),
            ]
        )
    )
    grad_win_normed = tp_scatter(
        [dot_second(part, qkv_win_flat) for part in split_rows(grad_win_qkv, n_tp)]
    )
    step = last_grads.cores(last_grads.other)
    step = middle_grads.one_last(step), middle_grads.two_last(step)
    last_grads.one_first(step)
    last_grads.two_first(step)
    step = last_grads.one, last_grads.two
    last_grads.one_last(step)
    last_grads.two_last(step)
    back_input = norm_back(own_input, norm_win, grad_win_normed)
    grad_token_rows = natural(tp_gather((grad_win_mixed + back_input).astype(LOW)))
    output_rows = natural(tp_gather(tied(layer_output.astype(LOW), after)))

    own_columns = model_width // lax.axis_size("seq")
    inner_width = up_tok.shape[1]
    sum_qkv_win = last_grads.columns(0, 3 * width)
    sum_qkv_tok = middle_grads.columns(0, 3 * width)
    sum_qkv_state = state_grads.columns(0, 3 * width)
    sum_up_win = middle_grads.columns(3 * width, inner_width)
    sum_up_tok = token_grads.columns(0, inner_width)
    sum_up_state = state_grads.columns(5 * width, inner_width)
    small_sums = last_grads.columns(4 * width, CHAIN * thin_rows + 2)
    first_row = seq_index * own_columns
    vectors = [
        gain_grad(qkv_win_flat, sum_qkv_win, norm_win, first_row),
        gain_grad(up_win, sum_up_win, norm_wffn, first_row),
        gain_grad(qkv_tok_flat, sum_qkv_tok, norm_tok, first_row),
        gain_grad(up_tok, sum_up_tok, norm_ffn, first_row),
        gain_grad(qkv_state_flat, sum_qkv_state, norm_state, first_row),
        gain_grad(up_state, sum_up_state, norm_sffn, first_row),
    ]
    small_sums = jnp.concatenate([small_sums, jnp.stack(vectors, axis=1)], axis=1)
    small_sums = tp_gather(small_sums)
    init_part = turned(
        jnp.stack([part[:, : CHAIN * thin_rows] for part in small_sums]),
        (n_tp - tp_index) % n_tp,
    ).reshape(n_tp, own_columns, CHAIN, thin_rows)
    sum_init = jnp.transpose(init_part, (2, 0, 3, 1)).reshape(state_rows, own_columns)
    vector_sums = sum(part[:, CHAIN * thin_rows :] for part in small_sums)

    def qkv_of(columns):
        return columns.reshape(own_columns, 3, width)

    def out_of(columns):
        return columns.T.reshape(2, width, own_columns)

    return (
        output_rows,
        state_rows_out,
        grad_token_rows,
        vector_sums[:, 2],
        qkv_of(sum_qkv_win),
        last_grads.columns(3 * width, width).T,
        vector_sums[:, 3],
        sum_up_win,
        middle_grads.columns(3 * width + inner_width, inner_width).T,
        vector_sums[:, 4],
        qkv_of(sum_qkv_tok),
        out_of(token_grads.columns(2 * inner_width, 2 * width)),
        vector_sums[:, 5],
        sum_up_tok,
        token_grads.columns(inner_width, inner_width).T,
        vector_sums[:, 6],
        qkv_of(sum_qkv_state),
        out_of(state_grads.columns(3 * width, 2 * width)),
        vector_sums[:, 0:2].T,
        vector_sums[:, 7],
        sum_up_state,
        state_grads.columns(5 * width + inner_width, inner_width).T,
        sum_init,
    )


def solution(mesh):
    placed = (
        P("seq", None),
        P(),
        P(),
        P(None, None, "tp"),
        P("tp", None),
        P(),
        P(None, "tp"),
        P("tp", None),
        P(),
        P(None, None, "tp"),
        P(None, "tp", None),
        P(),
        P(None, "tp"),
        P("tp", None),
        P(),
        P(None, None, "tp"),
        P(None, "tp", None),
        P(),
        P(),
        P(None, "tp"),
        P("tp", None),
        P(),
        P("seq", None),
    )
    return jax.shard_map(
        body,
        mesh=mesh,
        in_specs=placed,
        out_specs=(
            P("seq", None),
            P("seq", None),
            P("seq", None),
            P("seq"),
            P("seq", None, "tp"),
            P("tp", "seq"),
            P("seq"),
            P("seq", "tp"),
            P("tp", "seq"),
            P("seq"),
            P("seq", None, "tp"),
            P(None, "tp", "seq"),
            P("seq"),
            P("seq", "tp"),
            P("tp", "seq"),
            P("seq"),
            P("seq", None, "tp"),
            P(None, "tp", "seq"),
            P(None, "seq"),
            P("seq"),
            P("seq", "tp"),
            P("tp", "seq"),
            P(None, "seq"),
        ),
        check_vma=False,
    )
```

```python
import jax
import jax.numpy as jnp
from jax import lax
from jax.experimental import pallas as pl
from jax.experimental.layout import Layout, with_layout_constraint
from jax.experimental.pallas import tpu as pltpu
from jax.sharding import PartitionSpec as P

E = 128
CHAIN = 4
CORES = 2

EPSILON = 1e-05
MASKED = -1e30
LOW = jnp.bfloat16
HIGH = jnp.float32


def layer_norm(matrix, weights):
    average = jnp.mean(matrix, axis=-1, keepdims=True)
    centred = matrix - average
    spread = jnp.mean(centred * centred, axis=-1, keepdims=True)
    return centred * lax.rsqrt(spread + EPSILON) * weights


def gelu_exact(matrix):
    return jax.nn.gelu(matrix, approximate=False)


def gelu_slope(matrix, grad):
    return jax.vjp(gelu_exact, matrix)[1](grad)[0]


def plain_dot(former, latter):
    return jnp.dot(former, latter, preferred_element_type=HIGH)


def dot_first(former, latter):
    return lax.dot_general(
        former, latter, (((0,), (0,)), ((), ())), preferred_element_type=HIGH
    )


def dot_second(former, latter):
    return lax.dot_general(
        former, latter, (((1,), (1,)), ((), ())), preferred_element_type=HIGH
    )


def row_major(array):
    return with_layout_constraint(array, Layout(major_to_minor=tuple(range(array.ndim))))


def tied(value, *others):
    return lax.optimization_barrier((value, others))[0]


def norm_back(matrix, weights, grad):
    average = jnp.mean(matrix, axis=-1, keepdims=True)
    centred = matrix - average
    spread = jnp.mean(centred * centred, axis=-1, keepdims=True)
    scaled = centred * lax.rsqrt(spread + EPSILON)
    inner = grad * weights
    return lax.rsqrt(spread + EPSILON) * (
        inner
        - jnp.mean(inner, axis=-1, keepdims=True)
        - scaled * jnp.mean(inner * scaled, axis=-1, keepdims=True)
    )


def gain_grad(weights, grads, gain, first):
    rows = lax.dynamic_slice_in_dim(weights, first, grads.shape[0], 0).astype(HIGH)
    gains = lax.dynamic_slice_in_dim(gain, first, grads.shape[0], 0)
    return jnp.sum(rows * grads, axis=1) / gains


def tp_from(array, k):
    n = lax.axis_size("tp")
    return lax.ppermute(array, "tp", [((i + k) % n, i) for i in range(n)])


def tp_to(array, k):
    n = lax.axis_size("tp")
    return lax.ppermute(array, "tp", [(i, (i + k) % n) for i in range(n)])


def far_first(n):
    return sorted(range(1, n), key=lambda k: -min(k, n - k))


def tp_gather(piece):
    n = lax.axis_size("tp")
    found = {k: tp_from(piece, k) for k in far_first(n)}
    return [piece] + [found[k] for k in range(1, n)]


def tp_scatter(parts):
    n = lax.axis_size("tp")
    total = parts[0]
    for k in far_first(n):
        total = total + tp_to(parts[k].astype(LOW), k).astype(HIGH)
    return total


def tp_total(part):
    low = part.astype(LOW)
    total = part
    for k in far_first(lax.axis_size("tp")):
        total = total + tp_to(low, k).astype(HIGH)
    return total


def split_rows(matrix, n):
    size = matrix.shape[0] // n
    return [matrix[k * size : (k + 1) * size] for k in range(n)]


def swap(array, k):
    n = lax.axis_size("seq")
    return lax.ppermute(array, "seq", [(s, s ^ k) for s in range(n)])


def pos_gather(piece):
    beside, across = swap(piece, 1), swap(piece, 2)
    return [piece, beside, across, swap(across, 1)]


def pos_scatter(parts):
    low = jnp.concatenate([parts[1], parts[3]]).astype(LOW)
    here, there = split_rows(swap(low, 1), 2)
    across = swap((parts[2] + there.astype(HIGH)).astype(LOW), 2)
    return parts[0] + here.astype(HIGH) + across.astype(HIGH)


def choose(stacked, index):
    return lax.dynamic_index_in_dim(stacked, index, 0, keepdims=False)


def turned(array, start):
    twice = jnp.concatenate([array, array])
    return lax.dynamic_slice_in_dim(twice, start, array.shape[0], 0)


def weight_grads(pairs, split=True):
    n_seq = lax.axis_size("seq")
    depth = pairs[0][0][0].shape[1]
    unit = depth // n_seq
    block = max(256, CORES * unit)
    widths = [latter[0].shape[1] for _, latter in pairs]
    total = sum(widths)
    counts = [(len(former), len(latter)) for former, latter in pairs]
    operands, specs = [], []
    for former, latter in pairs:
        for piece in former:
            operands.append(piece)
            specs.append(pl.BlockSpec((piece.shape[0], block), lambda i: (0, i)))
        for piece in latter:
            operands.append(piece)
            specs.append(pl.BlockSpec(piece.shape, lambda i: (0, 0), pipeline_mode=pl.Buffered(1)))

    def kernel(core_ref, *refs):
        mine_ref, other_ref = refs[-2:]
        first = core_ref[0] == 0

        def keep(product, column):
            columns = slice(column, column + product.shape[1])
            if not split:
                other_ref[:, columns] = product
                return
            for g in range(block // (CORES * unit)):
                low = product[g * CORES * unit : g * CORES * unit + unit]
                high = product[g * CORES * unit + unit : (g + 1) * CORES * unit]
                rows = slice(g * unit, (g + 1) * unit)
                mine_ref[rows, columns] = jnp.where(first, low, high)
                other_ref[rows, columns] = jnp.where(first, high, low)

        at, column = 0, 0
        for (n_former, n_latter), width in zip(counts, widths):
            former = [ref[...] for ref in refs[at : at + n_former]]
            latter = [ref[...] for ref in refs[at + n_former : at + n_former + n_latter]]
            at += n_former + n_latter
            former = jnp.concatenate(former) if n_former > 1 else former[0]
            latter = jnp.concatenate(latter) if n_latter > 1 else latter[0]
            keep(dot_first(former, latter).astype(LOW), column)
            column += width

    shapes = [jax.ShapeDtypeStruct((depth // CORES, total), LOW)] * 2
    out_specs = [pl.BlockSpec((block // CORES, total), lambda i: (i, 0))] * 2
    if not split:
        shapes = [jax.ShapeDtypeStruct((depth, total), LOW)]
        out_specs = [pl.BlockSpec((block, total), lambda i: (i, 0))]
    rows = sum(piece.shape[0] for piece in pairs[0][0])
    core = (lax.axis_index("seq") % CORES).astype(jnp.int32).reshape(1)
    return pl.pallas_call(
        kernel,
        out_shape=shapes,
        grid=(depth // block,),
        in_specs=[pl.BlockSpec(memory_space=pltpu.SMEM)] + specs,
        out_specs=out_specs,
        compiler_params=pltpu.CompilerParams(vmem_limit_bytes=20 * 1024 * 1024),
        cost_estimate=pl.CostEstimate(
            flops=2 * rows * depth * total,
            bytes_accessed=2 * (rows * (depth + total) + depth * total),
            transcendentals=0,
        ),
    )(core, *operands)


class ScatterSum:
    def __init__(self, grads):
        self.grads = grads[0]
        self.total = lax.psum_scatter(self.grads, "seq", scatter_dimension=0, tiled=True)

    def columns(self, at, count):
        return self.total[:, at : at + count].astype(HIGH)


class SeqSum:
    def __init__(self, halves):
        n = lax.axis_size("seq")
        self.z_size = 4 if n % 8 == 0 else n // CORES
        self.x_size = n // (self.z_size * CORES)
        here = lax.axis_index("seq")
        self.z_at = here // CORES % self.z_size
        self.x_at = here // (CORES * self.z_size)
        self.mine, self.other = halves

    def pairs(self, dx, dz):
        def place(x, z, c):
            return (x % self.x_size * self.z_size + z % self.z_size) * CORES + c

        return [
            (place(x, z, c), place(x + dx, z + dz, c))
            for x in range(self.x_size)
            for z in range(self.z_size)
            for c in range(CORES)
        ]

    def over_z(self, array, dim):
        return self.stage(array, dim, self.z_at, self.z_size, lambda k: (0, k))

    def over_x(self, array, dim):
        return self.stage(array, dim, self.x_at, self.x_size, lambda k: (k, 0))

    def stage(self, array, dim, at, size, step):
        total = lax.dynamic_index_in_dim(array, at, dim, False).astype(HIGH)
        for k in far_first(size):
            sent = lax.dynamic_index_in_dim(array, (at + k) % size, dim, False)
            total = total + lax.ppermute(sent, "seq", self.pairs(*step(k))).astype(HIGH)
        return row_major(total)

    def cores(self, after):
        width = self.mine.shape[1]
        sent = swap(tied(self.other, after), 1)
        half = width // 256 * 128

        def total(columns):
            part = self.mine[:, columns].astype(HIGH) + sent[:, columns].astype(HIGH)
            return part.astype(LOW).reshape(self.x_size, self.z_size, -1, part.shape[1])

        self.one, self.two = total(slice(0, half)), total(slice(half, width))
        return self.one, self.two

    def one_first(self, after):
        self.one = self.over_z(tied(self.one, after), 1).astype(LOW)
        return self.one

    def two_first(self, after):
        self.two = self.over_x(tied(self.two, after), 0).astype(LOW)
        return self.two

    def one_last(self, after):
        self.one = self.over_x(tied(self.one, after), 0)
        return self.one

    def two_last(self, after):
        self.two = self.over_z(tied(self.two, after), 0)
        return self.two

    def columns(self, at, count):
        half = self.one.shape[1]
        if at + count <= half:
            return self.one[:, at : at + count]
        if at >= half:
            return self.two[:, at - half : at - half + count]
        return jnp.concatenate([self.one[:, at:], self.two[:, : at + count - half]], axis=1)


ATTEND_STEP = 256


def fused(kernel, outs, operands, products, scalars=(), exps=0):
    in_vmem = pl.BlockSpec(memory_space=pltpu.VMEM)
    in_smem = pl.BlockSpec(memory_space=pltpu.SMEM)
    scalars = [jnp.asarray(scalar, jnp.int32).reshape(1) for scalar in scalars]
    return pl.pallas_call(
        kernel,
        out_shape=[jax.ShapeDtypeStruct(shape, kind) for shape, kind in outs],
        in_specs=[in_smem] * len(scalars) + [in_vmem] * len(operands),
        out_specs=[in_vmem] * len(outs),
        compiler_params=pltpu.CompilerParams(vmem_limit_bytes=20 * 1024 * 1024),
        cost_estimate=pl.CostEstimate(
            flops=2 * products,
            bytes_accessed=sum(2 * operand.size for operand in operands),
            transcendentals=exps,
        ),
    )(*scalars, *operands)


def score_parts(query, key, before, spot):
    if before is None:
        return dot_second(key, query) * E ** (-0.5), None
    key_before, _, shift, start = before
    shape = key.shape[0], query.shape[0]
    key_ids = (lax.broadcasted_iota(jnp.int32, shape, 0) + shift) % shape[0]
    query_ids = (lax.broadcasted_iota(jnp.int32, shape, 1) + shift + spot) % shape[0]
    below = key_ids <= query_ids
    scores = jnp.where(below, dot_second(key, query), dot_second(key_before, query))
    return jnp.where(below | (start == 0), scores * E ** (-0.5), MASKED), below


def head_attend(query, key, value, before=None, spot=0):
    scores, below = score_parts(query, key, before, spot)
    top = jnp.max(scores, axis=0, keepdims=True)
    powers = jnp.exp(scores - top)
    total = jnp.sum(powers, axis=0, keepdims=True)
    chances = (powers * (1.0 / total)).astype(LOW)
    if before is None:
        result = dot_first(value, chances)
    else:
        none = jnp.zeros_like(chances)
        result = dot_first(value, jnp.where(below, chances, none)) + dot_first(
            before[1], jnp.where(below, none, chances)
        )
    return result.T.astype(LOW), top + jnp.log(total)


def head_back(query, key, value, log, grad, before=None, spot=0):
    scores, below = score_parts(query, key, before, spot)
    chances = jnp.exp(scores - log)
    grad_chances = dot_second(value, grad)
    if before is not None:
        grad_chances = jnp.where(below, grad_chances, dot_second(before[1], grad))
    inner = jnp.sum(chances * grad_chances, axis=0, keepdims=True)
    grad_scores = (chances * (grad_chances - inner) * E ** (-0.5)).astype(LOW)
    chances = chances.astype(LOW)
    if before is None:
        terms = [plain_dot(grad_scores, query), plain_dot(chances, grad)]
        return dot_first(key, grad_scores).T, terms
    none = jnp.zeros_like(chances)
    scores_now = jnp.where(below, grad_scores, none)
    scores_before = jnp.where(below, none, grad_scores)
    terms = [
        plain_dot(scores_now, query),
        plain_dot(jnp.where(below, chances, none), grad),
        plain_dot(scores_before, query),
        plain_dot(jnp.where(below, none, chances), grad),
    ]
    query_grad = dot_first(key, scores_now) + dot_first(before[0], scores_before)
    return query_grad.T, terms


def head_columns(head, width, part):
    return slice(part * width + head * E, part * width + (head + 1) * E)


def attend(queries, pair, before=None):
    count, width = queries.shape
    heads = width // E
    rows = min(count, ATTEND_STEP)
    scalars = [] if before is None else before[1:]
    operands = [queries, pair] + ([] if before is None else [before[0]])

    def kernel(*refs):
        scalar_refs, refs = refs[: len(scalars)], refs[len(scalars) :]
        query_ref, pair_ref = refs[:2]
        result_ref, log_ref = refs[-2:]
        for h in range(heads):
            own = slice(h * E, (h + 1) * E)
            key_at, value_at = head_columns(h, width, 0), head_columns(h, width, 1)
            mask = None
            if before is not None:
                mask = (refs[2][:, key_at], refs[2][:, value_at]) + tuple(
                    ref[0] for ref in scalar_refs
                )
            for spot in range(0, count, rows):
                here = slice(spot, spot + rows)
                result_ref[here, own], log_ref[h : h + 1, here] = head_attend(
                    query_ref[here, own], pair_ref[:, key_at], pair_ref[:, value_at], mask, spot
                )

    scores_count = heads * count * pair.shape[0]
    outs = [((count, width), LOW), ((heads, count), HIGH)]
    products = scores_count * E * len(operands)
    return fused(kernel, outs, operands, products, scalars, scores_count)


def attend_back(queries, pair, logs, grad_result, before=None):
    count, width = queries.shape
    heads = width // E
    rows = min(count, ATTEND_STEP)
    keys = pair.shape[0]
    scalars = [] if before is None else before[1:]
    operands = [queries, logs, grad_result, pair] + ([] if before is None else [before[0]])

    def kernel(*refs):
        scalar_refs, refs = refs[: len(scalars)], refs[len(scalars) :]
        query_ref, log_ref, grad_ref, pair_ref = refs[:4]
        outs = refs[len(operands) :]
        for h in range(heads):
            own = slice(h * E, (h + 1) * E)
            key_at, value_at = head_columns(h, width, 0), head_columns(h, width, 1)
            mask = None
            if before is not None:
                mask = (refs[4][:, key_at], refs[4][:, value_at]) + tuple(
                    ref[0] for ref in scalar_refs
                )
            sums = None
            for spot in range(0, count, rows):
                here = slice(spot, spot + rows)
                outs[0][here, own], terms = head_back(
                    query_ref[here, own],
                    pair_ref[:, key_at],
                    pair_ref[:, value_at],
                    log_ref[h : h + 1, here],
                    grad_ref[here, own],
                    mask,
                    spot,
                )
                sums = terms if sums is None else [one + two for one, two in zip(sums, terms)]
            outs[1][:, key_at], outs[1][:, value_at] = sums[:2]
            if before is not None:
                outs[2][:, key_at], outs[2][:, value_at] = sums[2].astype(LOW), sums[3].astype(LOW)

    outs = [((count, width), HIGH), ((keys, 2 * width), HIGH)]
    if before is not None:
        outs.append(((keys, 2 * width), LOW))
    scores_count = heads * count * keys
    products = scores_count * E * (5 if before is None else 10)
    return fused(kernel, outs, operands, products, scalars, scores_count)


def gelu_of(matrix):
    return 0.5 * matrix * (1.0 + lax.erf(matrix * 0.5**0.5))


def gelu_slope_of(matrix):
    density = jnp.exp(-0.5 * matrix * matrix) * (2.0 * jnp.pi) ** (-0.5)
    return 0.5 * (1.0 + lax.erf(matrix * 0.5**0.5)) + matrix * density


def sent_around(low):
    return [tp_to(low, k) for k in far_first(lax.axis_size("tp"))]


def added(refs):
    total = refs[0][...]
    for ref in refs[1:]:
        total = total + ref[...].astype(HIGH)
    return total


def chain_attend(queries, pieces, stack, index, out_flat):
    count, width = queries.shape
    n, keys = len(pieces), stack.shape[1]

    def kernel(index_ref, query_ref, *refs):
        pieces_refs, (stack_ref, out_ref) = refs[:n], refs[n : n + 2]
        pair_ref, own_ref, cross_ref, heads_ref, part_ref, low_ref = refs[n + 2 :]
        for k, ref in enumerate(pieces_refs):
            pair_ref[k * (keys // n) : (k + 1) * (keys // n), :] = ref[...]
        token = stack_ref[index_ref[0]]
        for h in range(width // E):
            own = slice(h * E, (h + 1) * E)
            key_at, value_at = head_columns(h, width, 0), head_columns(h, width, 1)
            row = slice(h, h + 1)
            heads_ref[:, width + h * E : width + (h + 1) * E], cross_ref[row, :] = head_attend(
                query_ref[:, own], token[:, key_at], token[:, value_at]
            )
            heads_ref[:, own], own_ref[row, :] = head_attend(
                query_ref[:, own], pair_ref[:, key_at], pair_ref[:, value_at]
            )
        part = plain_dot(heads_ref[...], out_ref[...])
        part_ref[...] = part
        low_ref[...] = part.astype(LOW)

    depth = out_flat.shape[1]
    logs = ((width // E, count), HIGH)
    outs = [((keys, 2 * width), LOW), logs, logs, ((count, 2 * width), LOW)]
    outs += [((count, depth), HIGH), ((count, depth), LOW)]
    products = count * width * (4 * keys + 2 * depth)
    operands = [queries, *pieces, stack, out_flat]
    return fused(kernel, outs, operands, products, [index], 2 * count * keys)


def chain_mlp(parts, incoming, keeps, gain, up, down):
    n = len(parts)

    def kernel(*refs):
        incoming_ref, keep_ref, gain_ref, up_ref, down_ref = refs[n : n + 5]
        update_ref, mid_ref, normed_ref, hidden_ref, active_ref, part_ref, low_ref = refs[n + 5 :]
        update = added(refs[:n])
        keep = keep_ref[0:1, :]
        mid = keep * incoming_ref[...] + (1.0 - keep) * update
        normed = layer_norm(mid, gain_ref[...]).astype(LOW)
        hidden = plain_dot(normed, up_ref[...])
        active = gelu_of(hidden).astype(LOW)
        part = plain_dot(active, down_ref[...])
        update_ref[...], mid_ref[...], normed_ref[...] = update, mid, normed
        hidden_ref[...], active_ref[...] = hidden, active
        part_ref[...], low_ref[...] = part, part.astype(LOW)

    count, depth = incoming.shape
    inner = up.shape[1]
    outs = [((count, depth), HIGH), ((count, depth), HIGH), ((count, depth), LOW)]
    outs += [((count, inner), HIGH), ((count, inner), LOW)]
    outs += [((count, depth), HIGH), ((count, depth), LOW)]
    operands = [*parts, incoming, keeps, gain, up, down]
    return fused(kernel, outs, operands, 2 * count * depth * inner, (), count * inner)


def chain_start(parts, mid, keeps, init_slab, flag, gain, qkv_flat):
    n = len(parts)
    width = qkv_flat.shape[1] // 3

    def kernel(flag_ref, *refs):
        mid_ref, keep_ref, init_ref, gain_ref, qkv_ref = refs[n : n + 5]
        mlp_ref, slab_ref, incoming_ref, normed_ref, query_ref, pair_ref = refs[n + 5 :]
        mlp = added(refs[:n])
        keep = keep_ref[1:2, :]
        slab = (keep * mid_ref[...] + (1.0 - keep) * mlp).astype(LOW)
        incoming = jnp.where(
            flag_ref[0] == 1, init_ref[...].astype(HIGH), slab.astype(HIGH)
        )
        normed = layer_norm(incoming, gain_ref[...]).astype(LOW)
        qkv = plain_dot(normed, qkv_ref[...]).astype(LOW)
        mlp_ref[...], slab_ref[...], incoming_ref[...] = mlp, slab, incoming
        normed_ref[...], query_ref[...], pair_ref[...] = normed, qkv[:, :width], qkv[:, width:]

    count, depth = mid.shape
    outs = [((count, depth), HIGH), ((count, depth), LOW), ((count, depth), HIGH)]
    outs += [((count, depth), LOW), ((count, width), LOW), ((count, 2 * width), LOW)]
    operands = [*parts, mid, keeps, init_slab, gain, qkv_flat]
    return fused(kernel, outs, operands, 3 * count * depth * width, [flag])


def chain_back_mlp(parts, incoming, grad_mid, flag, keeps, gain, mid, mlp, hidden, up, down):
    n = len(parts)
    operands = [*parts, incoming, keeps, gain, mid, mlp, hidden, up, down]
    operands += [] if grad_mid is None else [grad_mid]

    def kernel(flag_ref, *refs):
        incoming_ref, keep_ref, gain_ref, mid_ref, mlp_ref, hidden_ref, up_ref, down_ref = refs[
            n : n + 8
        ]
        grad_ref, state_ref, low_mlp_ref, low_hidden_ref, bias_ref, part_ref, low_ref = refs[-7:]
        grad = norm_back(incoming_ref[...], gain_ref[...], added(refs[:n]))
        if grad_mid is not None:
            grad = keep_ref[0:1, :] * refs[n + 8][...] + grad
        state = jnp.where(flag_ref[0] == 1, 0.0, grad)
        low_mlp = ((1.0 - keep_ref[1:2, :]) * state).astype(LOW)
        grad_active = dot_second(low_mlp, down_ref[...])
        low_hidden = (gelu_slope_of(hidden_ref[...]) * grad_active).astype(LOW)
        part = dot_second(low_hidden, up_ref[...])
        grad_ref[...], state_ref[...] = grad, state
        low_mlp_ref[...], low_hidden_ref[...] = low_mlp, low_hidden
        bias_ref[...] = jnp.sum(state * (mid_ref[...] - mlp_ref[...]), axis=0, keepdims=True)
        part_ref[...], low_ref[...] = part, part.astype(LOW)

    count, depth = mid.shape
    inner = up.shape[1]
    outs = [((count, depth), HIGH), ((count, depth), HIGH), ((count, depth), LOW)]
    outs += [((count, inner), LOW), ((1, depth), HIGH)]
    outs += [((count, depth), HIGH), ((count, depth), LOW)]
    return fused(kernel, outs, operands, 2 * count * depth * inner, [flag], count * inner)


def chain_back_heads(
    parts, mid, gain, keeps, grad_state, incoming, update, out_flat, queries, pair, logs, stack, index
):
    n = len(parts)
    count, width = queries.shape
    keys = pair.shape[0]
    slab = keys // CHAIN

    def kernel(index_ref, *refs):
        mid_ref, gain_ref, keep_ref, state_ref, incoming_ref, update_ref, out_ref = refs[n : n + 7]
        query_ref, pair_ref, own_log_ref, cross_log_ref, stack_ref = refs[n + 7 : n + 12]
        outs = refs[n + 12 :]
        mid_out, low_out, bias_out, query_out, here_out, across_out, sent_out, token_out = outs
        grad_mid = keep_ref[1:2, :] * state_ref[...] + norm_back(
            mid_ref[...], gain_ref[...], added(refs[:n])
        )
        mid_out[...] = grad_mid
        low = ((1.0 - keep_ref[0:1, :]) * grad_mid).astype(LOW)
        low_out[...] = low
        bias_out[...] = jnp.sum(
            grad_mid * (incoming_ref[...] - update_ref[...]), axis=0, keepdims=True
        )
        grad_heads = dot_second(low, out_ref[...]).astype(LOW)
        token = stack_ref[index_ref[0]]
        for h in range(width // E):
            own = slice(h * E, (h + 1) * E)
            row = slice(h, h + 1)
            own_query, own_terms = head_back(
                query_ref[:, own],
                pair_ref[:, head_columns(h, width, 0)],
                pair_ref[:, head_columns(h, width, 1)],
                own_log_ref[row, :],
                grad_heads[:, own],
            )
            cross_query, cross_terms = head_back(
                query_ref[:, own],
                token[:, head_columns(h, width, 0)],
                token[:, head_columns(h, width, 1)],
                cross_log_ref[row, :],
                grad_heads[:, head_columns(h, width, 1)],
            )
            query_out[:, own] = own_query + cross_query
            for part in range(2):
                at = head_columns(h, width, part)
                here_out[:, at] = own_terms[part][:slab]
                across_out[:, at] = own_terms[part][2 * slab : 3 * slab]
                sent_out[:slab, at] = own_terms[part][slab : 2 * slab].astype(LOW)
                sent_out[slab:, at] = own_terms[part][3 * slab :].astype(LOW)
                token_out[:, at] = cross_terms[part]

    depth = mid.shape[1]
    outs = [((count, depth), HIGH), ((count, depth), LOW), ((1, depth), HIGH)]
    outs += [((count, width), HIGH), ((slab, 2 * width), HIGH), ((slab, 2 * width), HIGH)]
    outs += [((2 * slab, 2 * width), LOW), ((keys, 2 * width), HIGH)]
    operands = [*parts, mid, gain, keeps, grad_state, incoming, update, out_flat]
    operands += [queries, pair, *logs, stack]
    products = count * width * (10 * keys + 2 * depth)
    return fused(kernel, outs, operands, products, [index], 2 * count * keys)


def chain_back_inputs(query_grad, terms, stack, index, qkv_flat):
    rows, depth = stack.shape[1], qkv_flat.shape[0]
    width = qkv_flat.shape[1] // 3
    first = [] if query_grad is None else [query_grad]

    def kernel(index_ref, *refs):
        stack_ref, qkv_ref = refs[len(first) + len(terms) : len(first) + len(terms) + 2]
        grad_ref, part_ref, low_ref = refs[-3:]
        pair = stack_ref[index_ref[0]]
        for ref in refs[len(first) : len(first) + len(terms)]:
            pair = pair + ref[...].astype(HIGH)
        if first:
            grad_ref[:, :width] = refs[0][...].astype(LOW)
        else:
            grad_ref[:, :width] = jnp.zeros((rows, width), LOW)
        grad_ref[:, width:] = pair.astype(LOW)
        part = dot_second(grad_ref[...], qkv_ref[...])
        part_ref[...], low_ref[...] = part, part.astype(LOW)

    outs = [((rows, 3 * width), LOW), ((rows, depth), HIGH), ((rows, depth), LOW)]
    operands = [*first, *terms, stack, qkv_flat]
    return fused(kernel, outs, operands, 3 * rows * depth * width, [index])


def body(
    tokens,
    segment_start,
    norm_win,
    qkv_win,
    out_win,
    norm_wffn,
    up_win,
    down_win,
    norm_tok,
    qkv_tok,
    out_tok,
    norm_ffn,
    up_tok,
    down_tok,
    norm_state,
    qkv_state,
    out_state,
    gate_bias,
    norm_sffn,
    up_state,
    down_state,
    init_state,
    cotangent,
):
    seq_index = lax.axis_index("seq")
    tp_index = lax.axis_index("tp")
    n_tp = lax.axis_size("tp")
    position = seq_index % CHAIN
    flags = choose(segment_start, seq_index // CHAIN) == 1
    starts_here = choose(flags, position)
    block_rows, model_width = tokens.shape
    piece_rows = block_rows // n_tp
    state_rows = init_state.shape[0]
    slab_rows = state_rows // CHAIN
    thin_rows = slab_rows // n_tp
    width = qkv_tok.shape[2]
    qkv_win_flat = qkv_win.reshape(model_width, 3 * width)
    out_tok_flat = out_tok.reshape(2 * width, model_width)
    out_state_flat = out_state.reshape(2 * width, model_width)

    shift = (tp_index * piece_rows).astype(jnp.int32)
    start_flag = starts_here.astype(jnp.int32)
    token_rows = turned(tokens, tp_index * piece_rows)

    def natural(pieces):
        whole = jnp.zeros((block_rows, model_width), pieces[0].dtype)
        for k, piece in enumerate(pieces):
            at = (tp_index + k) % n_tp * piece_rows
            whole = lax.dynamic_update_slice_in_dim(whole, piece, at, 0)
        return whole

    input_rows = token_rows.astype(HIGH)
    win_normed = layer_norm(input_rows, norm_win).astype(LOW)
    win_qkv = plain_dot(win_normed, qkv_win_flat).astype(LOW)
    win_queries, win_pair = win_qkv[:, :width], win_qkv[:, width:]
    onward = [(s, s + 1) for s in range(lax.axis_size("seq")) if (s + 1) % CHAIN]
    win_prev = lax.ppermute(win_pair, "seq", onward)
    win_before = win_prev, shift, start_flag
    win_heads, win_logs = attend(win_queries, win_pair, win_before)
    cotangent, qkv_tok, qkv_state, gate_bias, init_state, _ = lax.optimization_barrier(
        (cotangent, qkv_tok, qkv_state, gate_bias, init_state, win_heads)
    )
    qkv_tok_flat = qkv_tok.reshape(model_width, 3 * width)
    qkv_state_flat = qkv_state.reshape(model_width, 3 * width)
    keep_one, keep_two = jax.nn.sigmoid(gate_bias)
    cotangent_rows = turned(cotangent, tp_index * piece_rows)
    own_input = input_rows[:piece_rows]
    win_mixed = own_input + tp_scatter(
        [plain_dot(part, out_win) for part in split_rows(win_heads, n_tp)]
    )
    win_ffn_in = tp_gather(layer_norm(win_mixed, norm_wffn).astype(LOW))
    win_hidden = [plain_dot(part, up_win) for part in win_ffn_in]
    win_active = [gelu_exact(part).astype(LOW) for part in win_hidden]

    init_slab = lax.dynamic_slice_in_dim(init_state, position * slab_rows, slab_rows, 0)

    def own_rows(slab):
        return lax.dynamic_slice_in_dim(slab, tp_index * thin_rows, thin_rows, 0)

    init_late = tied(init_slab, win_ffn_in[1])
    state_incoming = init_late.astype(HIGH)
    state_normed = layer_norm(state_incoming, norm_state).astype(LOW)
    state_qkv = plain_dot(state_normed, qkv_state_flat).astype(LOW)
    state_queries = state_qkv[:, :width]
    state_pieces = pos_gather(state_qkv[:, width:])
    layer_one = win_mixed + tp_scatter([plain_dot(part, down_win) for part in win_active])
    layer_one = tied(layer_one, state_pieces)

    normed_pieces = tp_gather(layer_norm(layer_one, norm_tok).astype(LOW))
    normed = jnp.concatenate(normed_pieces)
    token_qkv = plain_dot(normed, qkv_tok_flat).astype(LOW)
    queries, pair = token_qkv[:, :width], token_qkv[:, width:]
    pairs_all = pos_gather(pair)
    pair_prev = jnp.where(position % 2 == 1, pairs_all[1], pairs_all[3])
    pairs_stack = jnp.stack(pairs_all)
    before = pair_prev, shift, start_flag

    keeps = jnp.stack([keep_one, keep_two])
    gain_state, gain_sffn = norm_state.reshape(1, -1), norm_sffn.reshape(1, -1)
    turns = []
    slabs_out = []
    for turn in range(CHAIN - 1):
        state_pair, own_logs, cross_logs, state_heads, part, low = chain_attend(
            state_queries, state_pieces, pairs_stack, position ^ turn, out_state_flat
        )
        parts = [part] + sent_around(low)
        if turn == 1:
            own_heads, own_token_logs = attend(tied(queries, part), pair, before)
            parts = tied(parts, own_heads)
        update, mid_state, state_ffn_in, state_hidden, state_active, part, low = chain_mlp(
            parts, state_incoming, keeps, gain_sffn, up_state, down_state
        )
        parts = [part] + sent_around(low)
        state_mlp, slab, incoming_next, normed_next, queries_next, pair_next = chain_start(
            parts, mid_state, keeps, init_slab, flags[turn + 1], gain_state, qkv_state_flat
        )
        slabs_out.append(slab)
        turns.append(
            (
                state_incoming,
                state_normed,
                state_queries,
                state_pair,
                (own_logs, cross_logs),
                state_heads,
                update,
                mid_state,
                state_ffn_in,
                state_hidden,
                state_active,
                state_mlp,
            )
        )
        state_incoming, state_normed, state_queries = incoming_next, normed_next, queries_next
        state_pieces = pos_gather(pair_next)
    turns.append((state_incoming, state_normed))
    my_state_pair = jnp.concatenate(state_pieces)
    for turn in range(CHAIN - 1):
        my_state_pair = jnp.where(position == turn, turns[turn][3], my_state_pair)

    cross_heads, cross_token_logs = attend(queries, my_state_pair)
    token_heads = jnp.concatenate([own_heads, cross_heads], axis=1)
    proj_total = tp_scatter(
        [plain_dot(part, out_tok_flat) for part in split_rows(token_heads, n_tp)]
    )
    cotangents = split_rows(tied(cotangent_rows, token_heads), n_tp)
    grad_active = [dot_second(part, down_tok) for part in cotangents]
    mixed_one = layer_one + tied(proj_total, *grad_active)
    ffn_in = tp_gather(layer_norm(mixed_one, norm_ffn).astype(LOW))
    hidden = [plain_dot(part, up_tok) for part in ffn_in]

    grad_hidden = [
        gelu_slope(part, grad).astype(LOW) for part, grad in zip(hidden, grad_active)
    ]
    active = [gelu_exact(part).astype(LOW) for part in hidden]
    grad_ffn_in = tp_scatter([dot_second(part, up_tok) for part in grad_hidden])
    grad_mixed = cotangents[0].astype(HIGH) + norm_back(mixed_one, norm_ffn, grad_ffn_in)
    grad_proj_pieces = tp_gather(grad_mixed.astype(LOW))
    grad_proj = jnp.concatenate(grad_proj_pieces)
    grad_heads = dot_second(grad_proj, out_tok_flat).astype(LOW)
    cross_query_grad, cross_pair_grad = attend_back(
        queries, my_state_pair, cross_token_logs, grad_heads[:, width:]
    )
    cross_pair_grad = split_rows(cross_pair_grad, CHAIN)
    cross_pieces = jnp.stack(
        [cross_pair_grad[0]]
        + [swap(cross_pair_grad[k].astype(LOW), k).astype(HIGH) for k in range(1, CHAIN)]
    )
    homeward = [(s, s - 1) for s in range(lax.axis_size("seq")) if s % CHAIN]

    def own_back():
        query_grad, pair_grad, prev_grad = attend_back(
            queries, pair, own_token_logs, tied(grad_heads[:, :width], cross_pieces), before
        )
        returned = lax.ppermute(prev_grad, "seq", homeward)
        return query_grad + cross_query_grad, pair_grad + returned.astype(HIGH)

    last_incoming = state_incoming
    _, _, _, _, part, low = chain_attend(
        tied(state_queries, grad_heads),
        state_pieces,
        pairs_stack,
        position ^ (CHAIN - 1),
        out_state_flat,
    )
    last_parts = [part] + sent_around(low)

    def last_state(after):
        _, mid_state, _, _, _, part, _ = chain_mlp(
            tied(last_parts, after), last_incoming, keeps, gain_sffn, up_state, down_state
        )
        state_mlp = tp_total(part)
        return (keep_two * mid_state + (1.0 - keep_two) * state_mlp).astype(LOW)

    def states_between(state_slab):
        states_stack = jnp.stack([own_rows(slab) for slab in slabs_out + [state_slab]])
        pieces = [choose(states_stack, position)]
        pieces += [swap(choose(states_stack, position ^ k), k) for k in range(1, CHAIN)]
        pieces = jnp.stack(pieces)
        return jnp.stack([choose(pieces, position ^ q) for q in range(CHAIN)])

    def states_whole(slabs):
        by_tp = turned(jnp.stack(tp_gather(slabs)), (n_tp - tp_index) % n_tp)
        return jnp.transpose(by_tp, (1, 0, 2, 3)).reshape(state_rows, model_width)

    grad_state_qkv, part, low = chain_back_inputs(
        None, [], cross_pieces, position ^ (CHAIN - 1), qkv_state_flat
    )
    parts = [part] + sent_around(low)
    query_grad, pair_grad = own_back()
    parts = tied(parts, query_grad)
    kept_qkv, kept_rest = [(state_normed, grad_state_qkv)], []
    token_pair_grads = [None] * CHAIN
    init_grad = jnp.zeros((thin_rows, model_width), HIGH)
    bias_one = bias_two = jnp.zeros((1, model_width), HIGH)
    grad_mid = None
    for turn in reversed(range(CHAIN - 1)):
        next_incoming = turns[turn + 1][0]
        (
            state_incoming,
            state_normed,
            state_queries,
            state_pair,
            logs,
            state_heads,
            update,
            mid_state,
            state_ffn_in,
            state_hidden,
            state_active,
            state_mlp,
        ) = turns[turn]
        grad_next, grad_state, grad_mlp, grad_state_hidden, sums, part, low = chain_back_mlp(
            parts,
            next_incoming,
            grad_mid,
            flags[turn + 1],
            keeps,
            gain_state,
            mid_state,
            state_mlp,
            state_hidden,
            up_state,
            down_state,
        )
        init_grad = init_grad + jnp.where(flags[turn + 1], own_rows(grad_next), 0.0)
        bias_two = bias_two + sums
        parts = [part] + sent_around(low)
        if turn == CHAIN - 2:
            token_grads = ScatterSum(
                weight_grads(
                    [
                        (tied(tuple(ffn_in), part), grad_hidden),
                        ([cotangent_rows], active),
                        (grad_proj_pieces, [token_heads]),
                    ],
                    False,
                )
            )
            parts = tied(parts, token_grads.grads)
        if turn == 0:
            parts = tied(parts, token_grads.total)
        grad_mid, grad_update, sums, query_total, here, across, sent, token_grad = chain_back_heads(
            parts,
            mid_state,
            gain_sffn,
            keeps,
            grad_state,
            state_incoming,
            update,
            out_state_flat,
            state_queries,
            state_pair,
            logs,
            pairs_stack,
            position ^ turn,
        )
        bias_one = bias_one + sums
        token_pair_grads[turn] = token_grad
        kept_rest.append(
            (state_heads, grad_update, state_ffn_in, grad_state_hidden, state_active, grad_mlp)
        )
        beside, there = split_rows(swap(sent, 1), 2)
        across = swap((across + there.astype(HIGH)).astype(LOW), 2)
        if turn == CHAIN - 2:
            last_slab = last_state(grad_mid)
            across = tied(across, last_slab)
        if turn == CHAIN - 3:
            slabs = states_between(tied(last_slab, grad_mid))
            across = tied(across, slabs)
        if turn == CHAIN - 4:
            state_rows_out = states_whole(tied(slabs, grad_mid))
            across = tied(across, state_rows_out)
        grad_state_qkv, part, low = chain_back_inputs(
            query_total, [here, beside, across], cross_pieces, position ^ turn, qkv_state_flat
        )
        kept_qkv.append((state_normed, grad_state_qkv))
        if turn:
            parts = [part] + sent_around(low)

    def first_incoming_grad(after):
        normed_grad = tp_total(tied(part, after))
        return keep_one * grad_mid + norm_back(turns[0][0], norm_state, normed_grad)

    bias_one = bias_one[0] * keep_one * (1.0 - keep_one) / n_tp
    bias_two = bias_two[0] * keep_two * (1.0 - keep_two) / n_tp

    token_pair_grads[CHAIN - 1] = jnp.zeros_like(token_pair_grads[0])
    pair_stack = jnp.stack(token_pair_grads)
    pair_grad = pair_grad + pos_scatter([choose(pair_stack, position ^ k) for k in range(CHAIN)])
    layer_output = mixed_one + tp_scatter(
        [plain_dot(part, down_tok) for part in tied(tuple(active), pair_stack)]
    )
    qkv_parts = list(zip(*kept_qkv))
    rest_parts = list(zip(*kept_rest))
    state_grads = ScatterSum(
        weight_grads(
            [
                (qkv_parts[0], qkv_parts[1]),
                (rest_parts[1], rest_parts[0]),
                (rest_parts[2], rest_parts[3]),
                (rest_parts[5], rest_parts[4]),
            ],
            False,
        )
    )
    pair_grad = tied(pair_grad, layer_output, state_grads.grads)
    grad_qkv = jnp.concatenate([query_grad, pair_grad], axis=1).astype(LOW)
    grad_normed = tp_scatter(
        [dot_second(part, qkv_tok_flat) for part in split_rows(grad_qkv, n_tp)]
    )
    grad_layer_one = grad_mixed + norm_back(layer_one, norm_tok, grad_normed)

    grad_win_out = tp_gather(grad_layer_one.astype(LOW))
    grad_win_hidden = [
        gelu_slope(part, dot_second(grad, down_win)).astype(LOW)
        for part, grad in zip(win_hidden, grad_win_out)
    ]
    grad_win_ffn_in = tp_scatter([dot_second(part, up_win) for part in grad_win_hidden])

    middle_grads = SeqSum(
        weight_grads(
            [
                (normed_pieces, [grad_qkv]),
                (win_ffn_in, grad_win_hidden),
                (grad_win_out, win_active),
            ]
        )
    )
    grad_win_ffn_in = tied(grad_win_ffn_in, middle_grads.other)
    grad_win_mixed = grad_layer_one + norm_back(win_mixed, norm_wffn, grad_win_ffn_in)
    grad_win_pieces = tp_gather(grad_win_mixed.astype(LOW))
    step = middle_grads.cores(grad_win_mixed)
    grad_win_proj = tied(jnp.concatenate(grad_win_pieces), step)
    grad_win_heads = dot_second(grad_win_proj, out_win).astype(LOW)
    win_query_grad, win_pair_grad, win_prev_grad = attend_back(
        win_queries, win_pair, win_logs, grad_win_heads, win_before
    )
    win_returned = lax.ppermute(win_prev_grad, "seq", homeward)
    after = win_query_grad, win_pair_grad
    middle_grads.one_first(grad_win_heads)
    middle_grads.two_first(grad_win_heads)
    first_grad = own_rows(first_incoming_grad(after))
    init_grad = init_grad + jnp.where(flags[0], first_grad, 0.0)
    win_pair_grad = win_pair_grad + tied(win_returned, state_grads.total).astype(HIGH)
    grad_win_qkv = jnp.concatenate([win_query_grad, win_pair_grad], axis=1).astype(LOW)

    small_rows = jnp.concatenate(
        [init_grad, jnp.stack([bias_one, bias_two]), jnp.zeros((14, model_width), HIGH)]
    ).astype(LOW)
    row_of = lax.broadcasted_iota(jnp.int32, (small_rows.shape[0], 256), 0)
    column_of = lax.broadcasted_iota(jnp.int32, (small_rows.shape[0], 256), 1)
    column_for = jnp.where(
        row_of < thin_rows,
        position * thin_rows + row_of,
        (CHAIN - 1) * thin_rows + row_of,
    )
    selector = (column_of == column_for).astype(LOW)
    last_grads = SeqSum(
        weight_grads(
            [
                ([win_normed], [grad_win_qkv]),
                ([grad_win_proj], [win_heads]),
                ([small_rows], [selector]),
            ]
        )
    )
    grad_win_normed = tp_scatter(
        [dot_second(part, qkv_win_flat) for part in split_rows(grad_win_qkv, n_tp)]
    )
    step = last_grads.cores(last_grads.other)
    step = middle_grads.one_last(step), middle_grads.two_last(step)
    last_grads.one_first(step)
    last_grads.two_first(step)
    step = last_grads.one, last_grads.two
    last_grads.one_last(step)
    last_grads.two_last(step)
    back_input = norm_back(own_input, norm_win, grad_win_normed)
    grad_token_rows = natural(tp_gather((grad_win_mixed + back_input).astype(LOW)))
    output_rows = natural(tp_gather(tied(layer_output.astype(LOW), after)))

    own_columns = model_width // lax.axis_size("seq")
    inner_width = up_tok.shape[1]
    sum_qkv_win = last_grads.columns(0, 3 * width)
    sum_qkv_tok = middle_grads.columns(0, 3 * width)
    sum_qkv_state = state_grads.columns(0, 3 * width)
    sum_up_win = middle_grads.columns(3 * width, inner_width)
    sum_up_tok = token_grads.columns(0, inner_width)
    sum_up_state = state_grads.columns(5 * width, inner_width)
    small_sums = last_grads.columns(4 * width, CHAIN * thin_rows + 2)
    first_row = seq_index * own_columns
    vectors = [
        gain_grad(qkv_win_flat, sum_qkv_win, norm_win, first_row),
        gain_grad(up_win, sum_up_win, norm_wffn, first_row),
        gain_grad(qkv_tok_flat, sum_qkv_tok, norm_tok, first_row),
        gain_grad(up_tok, sum_up_tok, norm_ffn, first_row),
        gain_grad(qkv_state_flat, sum_qkv_state, norm_state, first_row),
        gain_grad(up_state, sum_up_state, norm_sffn, first_row),
    ]
    small_sums = jnp.concatenate([small_sums, jnp.stack(vectors, axis=1)], axis=1)
    small_sums = tp_gather(small_sums)
    init_part = turned(
        jnp.stack([part[:, : CHAIN * thin_rows] for part in small_sums]),
        (n_tp - tp_index) % n_tp,
    ).reshape(n_tp, own_columns, CHAIN, thin_rows)
    sum_init = jnp.transpose(init_part, (2, 0, 3, 1)).reshape(state_rows, own_columns)
    vector_sums = sum(part[:, CHAIN * thin_rows :] for part in small_sums)

    def qkv_of(columns):
        return columns.reshape(own_columns, 3, width)

    def out_of(columns):
        return columns.T.reshape(2, width, own_columns)

    return (
        output_rows,
        state_rows_out,
        grad_token_rows,
        vector_sums[:, 2],
        qkv_of(sum_qkv_win),
        last_grads.columns(3 * width, width).T,
        vector_sums[:, 3],
        sum_up_win,
        middle_grads.columns(3 * width + inner_width, inner_width).T,
        vector_sums[:, 4],
        qkv_of(sum_qkv_tok),
        out_of(token_grads.columns(2 * inner_width, 2 * width)),
        vector_sums[:, 5],
        sum_up_tok,
        token_grads.columns(inner_width, inner_width).T,
        vector_sums[:, 6],
        qkv_of(sum_qkv_state),
        out_of(state_grads.columns(3 * width, 2 * width)),
        vector_sums[:, 0:2].T,
        vector_sums[:, 7],
        sum_up_state,
        state_grads.columns(5 * width + inner_width, inner_width).T,
        sum_init,
    )


def solution(mesh):
    placed = (
        P("seq", None),
        P(),
        P(),
        P(None, None, "tp"),
        P("tp", None),
        P(),
        P(None, "tp"),
        P("tp", None),
        P(),
        P(None, None, "tp"),
        P(None, "tp", None),
        P(),
        P(None, "tp"),
        P("tp", None),
        P(),
        P(None, None, "tp"),
        P(None, "tp", None),
        P(),
        P(),
        P(None, "tp"),
        P("tp", None),
        P(),
        P("seq", None),
    )
    return jax.shard_map(
        body,
        mesh=mesh,
        in_specs=placed,
        out_specs=(
            P("seq", None),
            P("seq", None),
            P("seq", None),
            P("seq"),
            P("seq", None, "tp"),
            P("tp", "seq"),
            P("seq"),
            P("seq", "tp"),
            P("tp", "seq"),
            P("seq"),
            P("seq", None, "tp"),
            P(None, "tp", "seq"),
            P("seq"),
            P("seq", "tp"),
            P("tp", "seq"),
            P("seq"),
            P("seq", None, "tp"),
            P(None, "tp", "seq"),
            P(None, "seq"),
            P("seq"),
            P("seq", "tp"),
            P("tp", "seq"),
            P(None, "seq"),
        ),
        check_vma=False,
    )
```

```python
import jax
import jax.numpy as jnp
from jax import lax
from jax.experimental import pallas as pl
from jax.experimental.layout import Layout, with_layout_constraint
from jax.experimental.pallas import tpu as pltpu
from jax.sharding import PartitionSpec as P

E = 128
CHAIN = 4
CORES = 2

EPSILON = 1e-05
MASKED = -1e30
LOW = jnp.bfloat16
HIGH = jnp.float32


def layer_norm(matrix, weights):
    average = jnp.mean(matrix, axis=-1, keepdims=True)
    centred = matrix - average
    spread = jnp.mean(centred * centred, axis=-1, keepdims=True)
    return centred * lax.rsqrt(spread + EPSILON) * weights


def gelu_exact(matrix):
    return jax.nn.gelu(matrix, approximate=False)


def gelu_slope(matrix, grad):
    return jax.vjp(gelu_exact, matrix)[1](grad)[0]


def plain_dot(former, latter):
    return jnp.dot(former, latter, preferred_element_type=HIGH)


def dot_first(former, latter):
    return lax.dot_general(
        former, latter, (((0,), (0,)), ((), ())), preferred_element_type=HIGH
    )


def dot_second(former, latter):
    return lax.dot_general(
        former, latter, (((1,), (1,)), ((), ())), preferred_element_type=HIGH
    )


def row_major(array):
    return with_layout_constraint(array, Layout(major_to_minor=tuple(range(array.ndim))))


def tied(value, *others):
    return lax.optimization_barrier((value, others))[0]


def norm_back(matrix, weights, grad):
    average = jnp.mean(matrix, axis=-1, keepdims=True)
    centred = matrix - average
    spread = jnp.mean(centred * centred, axis=-1, keepdims=True)
    scaled = centred * lax.rsqrt(spread + EPSILON)
    inner = grad * weights
    return lax.rsqrt(spread + EPSILON) * (
        inner
        - jnp.mean(inner, axis=-1, keepdims=True)
        - scaled * jnp.mean(inner * scaled, axis=-1, keepdims=True)
    )


def gain_grad(weights, grads, gain, first):
    rows = lax.dynamic_slice_in_dim(weights, first, grads.shape[0], 0).astype(HIGH)
    gains = lax.dynamic_slice_in_dim(gain.reshape(-1, 1), first, grads.shape[0], 0)
    return jnp.sum(rows * grads, axis=1, keepdims=True) / gains


def tp_from(array, k):
    n = lax.axis_size("tp")
    return lax.ppermute(array, "tp", [((i + k) % n, i) for i in range(n)])


def tp_to(array, k):
    n = lax.axis_size("tp")
    return lax.ppermute(array, "tp", [(i, (i + k) % n) for i in range(n)])


def far_first(n):
    return sorted(range(1, n), key=lambda k: -min(k, n - k))


def tp_gather(piece):
    n = lax.axis_size("tp")
    found = {k: tp_from(piece, k) for k in far_first(n)}
    return [piece] + [found[k] for k in range(1, n)]


def tp_scatter(parts):
    n = lax.axis_size("tp")
    total = parts[0]
    for k in far_first(n):
        total = total + tp_to(parts[k].astype(LOW), k).astype(HIGH)
    return total


def tp_total(part):
    low = part.astype(LOW)
    total = part
    for k in far_first(lax.axis_size("tp")):
        total = total + tp_to(low, k).astype(HIGH)
    return total


def split_rows(matrix, n):
    size = matrix.shape[0] // n
    return [matrix[k * size : (k + 1) * size] for k in range(n)]


def swap(array, k):
    n = lax.axis_size("seq")
    return lax.ppermute(array, "seq", [(s, s ^ k) for s in range(n)])


def pos_gather(piece):
    beside, across = swap(piece, 1), swap(piece, 2)
    return [piece, beside, across, swap(across, 1)]


def pos_scatter(parts):
    low = jnp.concatenate([parts[1], parts[3]]).astype(LOW)
    here, there = split_rows(swap(low, 1), 2)
    across = swap((parts[2] + there.astype(HIGH)).astype(LOW), 2)
    return parts[0] + here.astype(HIGH) + across.astype(HIGH)


def choose(stacked, index):
    return lax.dynamic_index_in_dim(stacked, index, 0, keepdims=False)


def turned(array, start):
    twice = jnp.concatenate([array, array])
    return lax.dynamic_slice_in_dim(twice, start, array.shape[0], 0)


def weight_grads(pairs, split=True):
    n_seq = lax.axis_size("seq")
    depth = pairs[0][0][0].shape[1]
    unit = depth // n_seq
    block = max(256, CORES * unit)
    widths = [latter[0].shape[1] for _, latter in pairs]
    total = sum(widths)
    counts = [(len(former), len(latter)) for former, latter in pairs]
    operands, specs = [], []
    for former, latter in pairs:
        for piece in former:
            operands.append(piece)
            specs.append(pl.BlockSpec((piece.shape[0], block), lambda i: (0, i)))
        for piece in latter:
            operands.append(piece)
            specs.append(pl.BlockSpec(piece.shape, lambda i: (0, 0), pipeline_mode=pl.Buffered(1)))

    def kernel(core_ref, *refs):
        mine_ref, other_ref = refs[-2:]
        first = core_ref[0] == 0

        def keep(product, column):
            columns = slice(column, column + product.shape[1])
            if not split:
                other_ref[:, columns] = product
                return
            for g in range(block // (CORES * unit)):
                low = product[g * CORES * unit : g * CORES * unit + unit]
                high = product[g * CORES * unit + unit : (g + 1) * CORES * unit]
                rows = slice(g * unit, (g + 1) * unit)
                mine_ref[rows, columns] = jnp.where(first, low, high)
                other_ref[rows, columns] = jnp.where(first, high, low)

        at, column = 0, 0
        for (n_former, n_latter), width in zip(counts, widths):
            former = [ref[...] for ref in refs[at : at + n_former]]
            latter = [ref[...] for ref in refs[at + n_former : at + n_former + n_latter]]
            at += n_former + n_latter
            former = jnp.concatenate(former) if n_former > 1 else former[0]
            latter = jnp.concatenate(latter) if n_latter > 1 else latter[0]
            keep(dot_first(former, latter).astype(LOW), column)
            column += width

    shapes = [jax.ShapeDtypeStruct((depth // CORES, total), LOW)] * 2
    out_specs = [pl.BlockSpec((block // CORES, total), lambda i: (i, 0))] * 2
    if not split:
        shapes = [jax.ShapeDtypeStruct((depth, total), LOW)]
        out_specs = [pl.BlockSpec((block, total), lambda i: (i, 0))]
    rows = sum(piece.shape[0] for piece in pairs[0][0])
    core = (lax.axis_index("seq") % CORES).astype(jnp.int32).reshape(1)
    return pl.pallas_call(
        kernel,
        out_shape=shapes,
        grid=(depth // block,),
        in_specs=[pl.BlockSpec(memory_space=pltpu.SMEM)] + specs,
        out_specs=out_specs,
        compiler_params=pltpu.CompilerParams(vmem_limit_bytes=20 * 1024 * 1024),
        cost_estimate=pl.CostEstimate(
            flops=2 * rows * depth * total,
            bytes_accessed=2 * (rows * (depth + total) + depth * total),
            transcendentals=0,
        ),
    )(core, *operands)


class ScatterSum:
    def __init__(self, grads):
        self.grads = grads[0]
        self.total = lax.psum_scatter(self.grads, "seq", scatter_dimension=0, tiled=True)

    def columns(self, at, count):
        return self.total[:, at : at + count].astype(HIGH)


class SeqSum:
    def __init__(self, halves):
        n = lax.axis_size("seq")
        self.z_size = 4 if n % 8 == 0 else n // CORES
        self.x_size = n // (self.z_size * CORES)
        here = lax.axis_index("seq")
        self.z_at = here // CORES % self.z_size
        self.x_at = here // (CORES * self.z_size)
        self.mine, self.other = halves

    def pairs(self, dx, dz):
        def place(x, z, c):
            return (x % self.x_size * self.z_size + z % self.z_size) * CORES + c

        return [
            (place(x, z, c), place(x + dx, z + dz, c))
            for x in range(self.x_size)
            for z in range(self.z_size)
            for c in range(CORES)
        ]

    def over_z(self, array, dim):
        return self.stage(array, dim, self.z_at, self.z_size, lambda k: (0, k))

    def over_x(self, array, dim):
        return self.stage(array, dim, self.x_at, self.x_size, lambda k: (k, 0))

    def stage(self, array, dim, at, size, step):
        total = lax.dynamic_index_in_dim(array, at, dim, False).astype(HIGH)
        for k in far_first(size):
            sent = lax.dynamic_index_in_dim(array, (at + k) % size, dim, False)
            total = total + lax.ppermute(sent, "seq", self.pairs(*step(k))).astype(HIGH)
        return row_major(total)

    def cores(self, after):
        width = self.mine.shape[1]
        sent = swap(tied(self.other, after), 1)
        half = width // 256 * 128

        def total(columns):
            part = self.mine[:, columns].astype(HIGH) + sent[:, columns].astype(HIGH)
            return part.astype(LOW).reshape(self.x_size, self.z_size, -1, part.shape[1])

        return total(slice(0, half)), total(slice(half, width))

    def across(self, one, two):
        one, two = self.over_z(one, 1).astype(LOW), self.over_x(two, 0).astype(LOW)
        return self.over_x(one, 0), self.over_z(two, 0)


def columns_of(halves, at, count):
    one, two = halves
    half = one.shape[1]
    if at + count <= half:
        return one[:, at : at + count]
    if at >= half:
        return two[:, at - half : at - half + count]
    return jnp.concatenate([one[:, at:], two[:, : at + count - half]], axis=1)


ATTEND_STEP = 256


def fused(kernel, outs, operands, products, scalars=(), exps=0):
    in_vmem = pl.BlockSpec(memory_space=pltpu.VMEM)
    in_smem = pl.BlockSpec(memory_space=pltpu.SMEM)
    scalars = [jnp.asarray(scalar, jnp.int32).reshape(1) for scalar in scalars]
    return pl.pallas_call(
        kernel,
        out_shape=[jax.ShapeDtypeStruct(shape, kind) for shape, kind in outs],
        in_specs=[in_smem] * len(scalars) + [in_vmem] * len(operands),
        out_specs=[in_vmem] * len(outs),
        compiler_params=pltpu.CompilerParams(vmem_limit_bytes=20 * 1024 * 1024),
        cost_estimate=pl.CostEstimate(
            flops=2 * products,
            bytes_accessed=sum(2 * operand.size for operand in operands),
            transcendentals=exps,
        ),
    )(*scalars, *operands)


def score_parts(query, key, before, spot):
    if before is None:
        return dot_second(key, query) * E ** (-0.5), None
    key_before, _, shift, start = before
    shape = key.shape[0], query.shape[0]
    key_ids = (lax.broadcasted_iota(jnp.int32, shape, 0) + shift) % shape[0]
    query_ids = (lax.broadcasted_iota(jnp.int32, shape, 1) + shift + spot) % shape[0]
    below = key_ids <= query_ids
    scores = jnp.where(below, dot_second(key, query), dot_second(key_before, query))
    return jnp.where(below | (start == 0), scores * E ** (-0.5), MASKED), below


def head_attend(query, key, value, before=None, spot=0):
    scores, below = score_parts(query, key, before, spot)
    top = jnp.max(scores, axis=0, keepdims=True)
    powers = jnp.exp(scores - top)
    total = jnp.sum(powers, axis=0, keepdims=True)
    chances = (powers * (1.0 / total)).astype(LOW)
    if before is None:
        result = dot_first(value, chances)
    else:
        none = jnp.zeros_like(chances)
        result = dot_first(value, jnp.where(below, chances, none)) + dot_first(
            before[1], jnp.where(below, none, chances)
        )
    return result.T.astype(LOW), top + jnp.log(total)


def head_back(query, key, value, log, grad, before=None, spot=0):
    scores, below = score_parts(query, key, before, spot)
    chances = jnp.exp(scores - log)
    grad_chances = dot_second(value, grad)
    if before is not None:
        grad_chances = jnp.where(below, grad_chances, dot_second(before[1], grad))
    inner = jnp.sum(chances * grad_chances, axis=0, keepdims=True)
    grad_scores = (chances * (grad_chances - inner) * E ** (-0.5)).astype(LOW)
    chances = chances.astype(LOW)
    if before is None:
        terms = [plain_dot(grad_scores, query), plain_dot(chances, grad)]
        return dot_first(key, grad_scores).T, terms
    none = jnp.zeros_like(chances)
    scores_now = jnp.where(below, grad_scores, none)
    scores_before = jnp.where(below, none, grad_scores)
    terms = [
        plain_dot(scores_now, query),
        plain_dot(jnp.where(below, chances, none), grad),
        plain_dot(scores_before, query),
        plain_dot(jnp.where(below, none, chances), grad),
    ]
    query_grad = dot_first(key, scores_now) + dot_first(before[0], scores_before)
    return query_grad.T, terms


def head_columns(head, width, part):
    return slice(part * width + head * E, part * width + (head + 1) * E)


def attend(queries, pair, before=None):
    count, width = queries.shape
    heads = width // E
    rows = min(count, ATTEND_STEP)
    scalars = [] if before is None else before[1:]
    operands = [queries, pair] + ([] if before is None else [before[0]])

    def kernel(*refs):
        scalar_refs, refs = refs[: len(scalars)], refs[len(scalars) :]
        query_ref, pair_ref = refs[:2]
        result_ref, log_ref = refs[-2:]
        for h in range(heads):
            own = slice(h * E, (h + 1) * E)
            key_at, value_at = head_columns(h, width, 0), head_columns(h, width, 1)
            mask = None
            if before is not None:
                mask = (refs[2][:, key_at], refs[2][:, value_at]) + tuple(
                    ref[0] for ref in scalar_refs
                )
            for spot in range(0, count, rows):
                here = slice(spot, spot + rows)
                result_ref[here, own], log_ref[h : h + 1, here] = head_attend(
                    query_ref[here, own], pair_ref[:, key_at], pair_ref[:, value_at], mask, spot
                )

    scores_count = heads * count * pair.shape[0]
    outs = [((count, width), LOW), ((heads, count), HIGH)]
    products = scores_count * E * len(operands)
    return fused(kernel, outs, operands, products, scalars, scores_count)


def attend_back(queries, pair, logs, grad_result, before=None):
    count, width = queries.shape
    heads = width // E
    rows = min(count, ATTEND_STEP)
    keys = pair.shape[0]
    scalars = [] if before is None else before[1:]
    operands = [queries, logs, grad_result, pair] + ([] if before is None else [before[0]])

    def kernel(*refs):
        scalar_refs, refs = refs[: len(scalars)], refs[len(scalars) :]
        query_ref, log_ref, grad_ref, pair_ref = refs[:4]
        outs = refs[len(operands) :]
        for h in range(heads):
            own = slice(h * E, (h + 1) * E)
            key_at, value_at = head_columns(h, width, 0), head_columns(h, width, 1)
            mask = None
            if before is not None:
                mask = (refs[4][:, key_at], refs[4][:, value_at]) + tuple(
                    ref[0] for ref in scalar_refs
                )
            sums = None
            for spot in range(0, count, rows):
                here = slice(spot, spot + rows)
                outs[0][here, own], terms = head_back(
                    query_ref[here, own],
                    pair_ref[:, key_at],
                    pair_ref[:, value_at],
                    log_ref[h : h + 1, here],
                    grad_ref[here, own],
                    mask,
                    spot,
                )
                sums = terms if sums is None else [one + two for one, two in zip(sums, terms)]
            outs[1][:, key_at], outs[1][:, value_at] = sums[:2]
            if before is not None:
                outs[2][:, key_at], outs[2][:, value_at] = sums[2].astype(LOW), sums[3].astype(LOW)

    outs = [((count, width), HIGH), ((keys, 2 * width), HIGH)]
    if before is not None:
        outs.append(((keys, 2 * width), LOW))
    scores_count = heads * count * keys
    products = scores_count * E * (5 if before is None else 10)
    return fused(kernel, outs, operands, products, scalars, scores_count)


def gelu_of(matrix):
    return 0.5 * matrix * (1.0 + lax.erf(matrix * 0.5**0.5))


def gelu_slope_of(matrix):
    density = jnp.exp(-0.5 * matrix * matrix) * (2.0 * jnp.pi) ** (-0.5)
    return 0.5 * (1.0 + lax.erf(matrix * 0.5**0.5)) + matrix * density


def sent_around(low):
    return [tp_to(low, k) for k in far_first(lax.axis_size("tp"))]


def added(refs):
    total = refs[0][...]
    for ref in refs[1:]:
        total = total + ref[...].astype(HIGH)
    return total


def chain_attend(queries, pieces, stack, index, out_flat):
    count, width = queries.shape
    n, keys = len(pieces), stack.shape[1]

    def kernel(index_ref, query_ref, *refs):
        pieces_refs, (stack_ref, out_ref) = refs[:n], refs[n : n + 2]
        pair_ref, own_ref, cross_ref, heads_ref, part_ref, low_ref = refs[n + 2 :]
        for k, ref in enumerate(pieces_refs):
            pair_ref[k * (keys // n) : (k + 1) * (keys // n), :] = ref[...]
        token = stack_ref[index_ref[0]]
        for h in range(width // E):
            own = slice(h * E, (h + 1) * E)
            key_at, value_at = head_columns(h, width, 0), head_columns(h, width, 1)
            row = slice(h, h + 1)
            heads_ref[:, width + h * E : width + (h + 1) * E], cross_ref[row, :] = head_attend(
                query_ref[:, own], token[:, key_at], token[:, value_at]
            )
            heads_ref[:, own], own_ref[row, :] = head_attend(
                query_ref[:, own], pair_ref[:, key_at], pair_ref[:, value_at]
            )
        part = plain_dot(heads_ref[...], out_ref[...])
        part_ref[...] = part
        low_ref[...] = part.astype(LOW)

    depth = out_flat.shape[1]
    logs = ((width // E, count), HIGH)
    outs = [((keys, 2 * width), LOW), logs, logs, ((count, 2 * width), LOW)]
    outs += [((count, depth), HIGH), ((count, depth), LOW)]
    products = count * width * (4 * keys + 2 * depth)
    operands = [queries, *pieces, stack, out_flat]
    return fused(kernel, outs, operands, products, [index], 2 * count * keys)


def chain_mlp(parts, incoming, keeps, gain, up, down):
    n = len(parts)

    def kernel(*refs):
        incoming_ref, keep_ref, gain_ref, up_ref, down_ref = refs[n : n + 5]
        mid_ref, normed_ref, slope_ref, active_ref, part_ref, low_ref = refs[n + 5 :]
        keep = keep_ref[0:1, :]
        mid = keep * incoming_ref[...].astype(HIGH) + (1.0 - keep) * added(refs[:n])
        normed = layer_norm(mid, gain_ref[...]).astype(LOW)
        hidden = plain_dot(normed, up_ref[...])
        active = gelu_of(hidden).astype(LOW)
        part = plain_dot(active, down_ref[...])
        mid_ref[...], normed_ref[...] = mid, normed
        slope_ref[...], active_ref[...] = gelu_slope_of(hidden).astype(LOW), active
        part_ref[...], low_ref[...] = part, part.astype(LOW)

    count, depth = incoming.shape
    inner = up.shape[1]
    outs = [((count, depth), HIGH), ((count, depth), LOW)]
    outs += [((count, inner), LOW), ((count, inner), LOW)]
    outs += [((count, depth), HIGH), ((count, depth), LOW)]
    operands = [*parts, incoming, keeps, gain, up, down]
    return fused(kernel, outs, operands, 2 * count * depth * inner, (), count * inner)


def chain_start(parts, mid, keeps, init_slab, flag, gain, qkv_flat):
    n = len(parts)
    width = qkv_flat.shape[1] // 3

    def kernel(flag_ref, *refs):
        mid_ref, keep_ref, init_ref, gain_ref, qkv_ref = refs[n : n + 5]
        mlp_ref, slab_ref, incoming_ref, normed_ref, query_ref, pair_ref = refs[n + 5 :]
        mlp = added(refs[:n])
        keep = keep_ref[1:2, :]
        slab = (keep * mid_ref[...] + (1.0 - keep) * mlp).astype(LOW)
        incoming = jnp.where(flag_ref[0] == 1, init_ref[...], slab)
        normed = layer_norm(incoming.astype(HIGH), gain_ref[...]).astype(LOW)
        qkv = plain_dot(normed, qkv_ref[...]).astype(LOW)
        mlp_ref[...], slab_ref[...], incoming_ref[...] = mlp.astype(LOW), slab, incoming
        normed_ref[...], query_ref[...], pair_ref[...] = normed, qkv[:, :width], qkv[:, width:]

    count, depth = mid.shape
    outs = [((count, depth), LOW)] * 4 + [((count, width), LOW), ((count, 2 * width), LOW)]
    operands = [*parts, mid, keeps, init_slab, gain, qkv_flat]
    return fused(kernel, outs, operands, 3 * count * depth * width, [flag])


def chain_back_mlp(parts, incoming, grad_mid, flag, keeps, gain, mid, mlp, slope, up, down):
    n = len(parts)
    operands = [*parts, incoming, keeps, gain, mid, mlp, slope, up, down]
    operands += [] if grad_mid is None else [grad_mid]

    def kernel(flag_ref, *refs):
        incoming_ref, keep_ref, gain_ref, mid_ref, mlp_ref, slope_ref, up_ref, down_ref = refs[
            n : n + 8
        ]
        grad_ref, state_ref, low_mlp_ref, low_hidden_ref, bias_ref, part_ref, low_ref = refs[-7:]
        grad = norm_back(incoming_ref[...].astype(HIGH), gain_ref[...], added(refs[:n]))
        if grad_mid is not None:
            grad = keep_ref[0:1, :] * refs[n + 8][...] + grad
        state = jnp.where(flag_ref[0] == 1, 0.0, grad)
        low_mlp = ((1.0 - keep_ref[1:2, :]) * state).astype(LOW)
        grad_active = dot_second(low_mlp, down_ref[...])
        low_hidden = (slope_ref[...].astype(HIGH) * grad_active).astype(LOW)
        part = dot_second(low_hidden, up_ref[...])
        grad_ref[...], state_ref[...] = grad, state
        low_mlp_ref[...], low_hidden_ref[...] = low_mlp, low_hidden
        change = mid_ref[...] - mlp_ref[...].astype(HIGH)
        bias_ref[...] = jnp.sum(state * change, axis=0, keepdims=True)
        part_ref[...], low_ref[...] = part, part.astype(LOW)

    count, depth = mid.shape
    inner = up.shape[1]
    outs = [((count, depth), HIGH), ((count, depth), HIGH), ((count, depth), LOW)]
    outs += [((count, inner), LOW), ((1, depth), HIGH)]
    outs += [((count, depth), HIGH), ((count, depth), LOW)]
    return fused(kernel, outs, operands, 2 * count * depth * inner, [flag], count * inner)


def chain_back_heads(
    parts, mid, gain, keeps, grad_state, incoming, out_flat, queries, pair, logs, stack, index
):
    n = len(parts)
    count, width = queries.shape
    keys = pair.shape[0]
    slab = keys // CHAIN

    def kernel(index_ref, *refs):
        mid_ref, gain_ref, keep_ref, state_ref, incoming_ref, out_ref = refs[n : n + 6]
        query_ref, pair_ref, own_log_ref, cross_log_ref, stack_ref = refs[n + 6 : n + 11]
        outs = refs[n + 11 :]
        mid_out, low_out, bias_out, query_out, here_out, across_out, sent_out, token_out = outs
        grad_mid = keep_ref[1:2, :] * state_ref[...] + norm_back(
            mid_ref[...], gain_ref[...], added(refs[:n])
        )
        mid_out[...] = grad_mid
        low = ((1.0 - keep_ref[0:1, :]) * grad_mid).astype(LOW)
        low_out[...] = low
        change = incoming_ref[...].astype(HIGH) - mid_ref[...]
        bias_out[...] = jnp.sum(grad_mid * change, axis=0, keepdims=True)
        grad_heads = dot_second(low, out_ref[...]).astype(LOW)
        token = stack_ref[index_ref[0]]
        for h in range(width // E):
            own = slice(h * E, (h + 1) * E)
            row = slice(h, h + 1)
            own_query, own_terms = head_back(
                query_ref[:, own],
                pair_ref[:, head_columns(h, width, 0)],
                pair_ref[:, head_columns(h, width, 1)],
                own_log_ref[row, :],
                grad_heads[:, own],
            )
            cross_query, cross_terms = head_back(
                query_ref[:, own],
                token[:, head_columns(h, width, 0)],
                token[:, head_columns(h, width, 1)],
                cross_log_ref[row, :],
                grad_heads[:, head_columns(h, width, 1)],
            )
            query_out[:, own] = own_query + cross_query
            for part in range(2):
                at = head_columns(h, width, part)
                here_out[:, at] = own_terms[part][:slab]
                across_out[:, at] = own_terms[part][2 * slab : 3 * slab]
                sent_out[:slab, at] = own_terms[part][slab : 2 * slab].astype(LOW)
                sent_out[slab:, at] = own_terms[part][3 * slab :].astype(LOW)
                token_out[:, at] = cross_terms[part]

    depth = mid.shape[1]
    outs = [((count, depth), HIGH), ((count, depth), LOW), ((1, depth), HIGH)]
    outs += [((count, width), HIGH), ((slab, 2 * width), HIGH), ((slab, 2 * width), HIGH)]
    outs += [((2 * slab, 2 * width), LOW), ((keys, 2 * width), HIGH)]
    operands = [*parts, mid, gain, keeps, grad_state, incoming, out_flat]
    operands += [queries, pair, *logs, stack]
    products = count * width * (10 * keys + 2 * depth)
    return fused(kernel, outs, operands, products, [index], 2 * count * keys)


def chain_back_inputs(query_grad, terms, stack, index, qkv_flat):
    rows, depth = stack.shape[1], qkv_flat.shape[0]
    width = qkv_flat.shape[1] // 3
    first = [] if query_grad is None else [query_grad]

    def kernel(index_ref, *refs):
        stack_ref, qkv_ref = refs[len(first) + len(terms) : len(first) + len(terms) + 2]
        grad_ref, part_ref, low_ref = refs[-3:]
        pair = stack_ref[index_ref[0]]
        for ref in refs[len(first) : len(first) + len(terms)]:
            pair = pair + ref[...].astype(HIGH)
        if first:
            grad_ref[:, :width] = refs[0][...].astype(LOW)
        else:
            grad_ref[:, :width] = jnp.zeros((rows, width), LOW)
        grad_ref[:, width:] = pair.astype(LOW)
        part = dot_second(grad_ref[...], qkv_ref[...])
        part_ref[...], low_ref[...] = part, part.astype(LOW)

    outs = [((rows, 3 * width), LOW), ((rows, depth), HIGH), ((rows, depth), LOW)]
    operands = [*first, *terms, stack, qkv_flat]
    return fused(kernel, outs, operands, 3 * rows * depth * width, [index])


def body(
    tokens,
    segment_start,
    norm_win,
    qkv_win,
    out_win,
    norm_wffn,
    up_win,
    down_win,
    norm_tok,
    qkv_tok,
    out_tok,
    norm_ffn,
    up_tok,
    down_tok,
    norm_state,
    qkv_state,
    out_state,
    gate_bias,
    norm_sffn,
    up_state,
    down_state,
    init_state,
    cotangent,
):
    seq_index = lax.axis_index("seq")
    tp_index = lax.axis_index("tp")
    n_tp = lax.axis_size("tp")
    position = seq_index % CHAIN
    flags = choose(segment_start, seq_index // CHAIN) == 1
    starts_here = choose(flags, position)
    block_rows, model_width = tokens.shape
    piece_rows = block_rows // n_tp
    state_rows = init_state.shape[0]
    slab_rows = state_rows // CHAIN
    thin_rows = slab_rows // n_tp
    width = qkv_tok.shape[2]
    qkv_win_flat = qkv_win.reshape(model_width, 3 * width)
    out_tok_flat = out_tok.reshape(2 * width, model_width)
    out_state_flat = out_state.reshape(2 * width, model_width)

    shift = (tp_index * piece_rows).astype(jnp.int32)
    start_flag = starts_here.astype(jnp.int32)
    token_rows = turned(tokens, tp_index * piece_rows)

    def natural(pieces):
        whole = jnp.zeros((block_rows, model_width), pieces[0].dtype)
        for k, piece in enumerate(pieces):
            at = (tp_index + k) % n_tp * piece_rows
            whole = lax.dynamic_update_slice_in_dim(whole, piece, at, 0)
        return whole

    input_rows = token_rows.astype(HIGH)
    win_normed = layer_norm(input_rows, norm_win).astype(LOW)
    win_qkv = plain_dot(win_normed, qkv_win_flat).astype(LOW)
    win_queries, win_pair = win_qkv[:, :width], win_qkv[:, width:]
    onward = [(s, s + 1) for s in range(lax.axis_size("seq")) if (s + 1) % CHAIN]
    win_prev = lax.ppermute(win_pair, "seq", onward)
    win_before = win_prev, shift, start_flag
    win_heads, win_logs = attend(win_queries, win_pair, win_before)
    cotangent, qkv_tok, qkv_state, gate_bias, init_state, _ = lax.optimization_barrier(
        (cotangent, qkv_tok, qkv_state, gate_bias, init_state, win_heads)
    )
    qkv_tok_flat = qkv_tok.reshape(model_width, 3 * width)
    qkv_state_flat = qkv_state.reshape(model_width, 3 * width)
    keep_one, keep_two = jax.nn.sigmoid(gate_bias)
    cotangent_rows = turned(cotangent, tp_index * piece_rows)
    own_input = input_rows[:piece_rows]
    win_mixed = own_input + tp_scatter(
        [plain_dot(part, out_win) for part in split_rows(win_heads, n_tp)]
    )
    win_ffn_in = tp_gather(layer_norm(win_mixed, norm_wffn).astype(LOW))
    win_hidden = [plain_dot(part, up_win) for part in win_ffn_in]
    win_active = [gelu_exact(part).astype(LOW) for part in win_hidden]

    init_slab = lax.dynamic_slice_in_dim(init_state, position * slab_rows, slab_rows, 0)

    def own_rows(slab):
        return lax.dynamic_slice_in_dim(slab, tp_index * thin_rows, thin_rows, 0)

    init_late = tied(init_slab, win_ffn_in[1])
    state_incoming = init_late
    state_normed = layer_norm(state_incoming.astype(HIGH), norm_state).astype(LOW)
    state_qkv = plain_dot(state_normed, qkv_state_flat).astype(LOW)
    state_queries = state_qkv[:, :width]
    state_pieces = pos_gather(state_qkv[:, width:])
    layer_one = win_mixed + tp_scatter([plain_dot(part, down_win) for part in win_active])
    layer_one = tied(layer_one, state_pieces)

    normed_pieces = tp_gather(layer_norm(layer_one, norm_tok).astype(LOW))
    normed = jnp.concatenate(normed_pieces)
    token_qkv = plain_dot(normed, qkv_tok_flat).astype(LOW)
    queries, pair = token_qkv[:, :width], token_qkv[:, width:]
    pairs_all = pos_gather(pair)
    pair_prev = jnp.where(position % 2 == 1, pairs_all[1], pairs_all[3])
    pairs_stack = jnp.stack(pairs_all)
    before = pair_prev, shift, start_flag

    keeps = jnp.stack([keep_one, keep_two])
    gain_state, gain_sffn = norm_state.reshape(1, -1), norm_sffn.reshape(1, -1)
    turns = []
    slabs_out = []
    for turn in range(CHAIN - 1):
        state_pair, own_logs, cross_logs, state_heads, part, low = chain_attend(
            state_queries, state_pieces, pairs_stack, position ^ turn, out_state_flat
        )
        parts = [part] + sent_around(low)
        if turn == 1:
            own_heads, own_token_logs = attend(tied(queries, part), pair, before)
            parts = tied(parts, own_heads)
        mid_state, state_ffn_in, state_slope, state_active, part, low = chain_mlp(
            parts, state_incoming, keeps, gain_sffn, up_state, down_state
        )
        parts = [part] + sent_around(low)
        state_mlp, slab, incoming_next, normed_next, queries_next, pair_next = chain_start(
            parts, mid_state, keeps, init_slab, flags[turn + 1], gain_state, qkv_state_flat
        )
        slabs_out.append(slab)
        turns.append(
            (
                state_incoming,
                state_normed,
                state_queries,
                state_pair,
                (own_logs, cross_logs),
                state_heads,
                mid_state,
                state_ffn_in,
                state_slope,
                state_active,
                state_mlp,
            )
        )
        state_incoming, state_normed, state_queries = incoming_next, normed_next, queries_next
        state_pieces = pos_gather(pair_next)
    turns.append((state_incoming, state_normed))
    my_state_pair = jnp.concatenate(state_pieces)
    for turn in range(CHAIN - 1):
        my_state_pair = jnp.where(position == turn, turns[turn][3], my_state_pair)

    cross_heads, cross_token_logs = attend(queries, my_state_pair)
    token_heads = jnp.concatenate([own_heads, cross_heads], axis=1)
    proj_total = tp_scatter(
        [plain_dot(part, out_tok_flat) for part in split_rows(token_heads, n_tp)]
    )
    cotangents = split_rows(tied(cotangent_rows, token_heads), n_tp)
    grad_active = [dot_second(part, down_tok) for part in cotangents]
    mixed_one = layer_one + tied(proj_total, *grad_active)
    ffn_in = tp_gather(layer_norm(mixed_one, norm_ffn).astype(LOW))
    hidden = [plain_dot(part, up_tok) for part in ffn_in]

    grad_hidden = [
        gelu_slope(part, grad).astype(LOW) for part, grad in zip(hidden, grad_active)
    ]
    active = [gelu_exact(part).astype(LOW) for part in hidden]
    grad_ffn_in = tp_scatter([dot_second(part, up_tok) for part in grad_hidden])
    grad_mixed = cotangents[0].astype(HIGH) + norm_back(mixed_one, norm_ffn, grad_ffn_in)
    grad_proj_pieces = tp_gather(grad_mixed.astype(LOW))
    grad_proj = jnp.concatenate(grad_proj_pieces)
    grad_heads = dot_second(grad_proj, out_tok_flat).astype(LOW)
    cross_query_grad, cross_pair_grad = attend_back(
        queries, my_state_pair, cross_token_logs, grad_heads[:, width:]
    )
    cross_pair_grad = split_rows(cross_pair_grad, CHAIN)
    cross_pieces = jnp.stack(
        [cross_pair_grad[0]]
        + [swap(cross_pair_grad[k].astype(LOW), k).astype(HIGH) for k in range(1, CHAIN)]
    )
    homeward = [(s, s - 1) for s in range(lax.axis_size("seq")) if s % CHAIN]

    def own_back():
        query_grad, pair_grad, prev_grad = attend_back(
            queries, pair, own_token_logs, tied(grad_heads[:, :width], cross_pieces), before
        )
        returned = lax.ppermute(prev_grad, "seq", homeward)
        return query_grad + cross_query_grad, pair_grad + returned.astype(HIGH)

    last_incoming = state_incoming
    _, _, _, _, part, low = chain_attend(
        tied(state_queries, grad_heads),
        state_pieces,
        pairs_stack,
        position ^ (CHAIN - 1),
        out_state_flat,
    )
    last_parts = [part] + sent_around(low)

    def last_state(after):
        mid_state, _, _, _, part, _ = chain_mlp(
            tied(last_parts, after), last_incoming, keeps, gain_sffn, up_state, down_state
        )
        state_mlp = tp_total(part)
        return (keep_two * mid_state + (1.0 - keep_two) * state_mlp).astype(LOW)

    def states_between(state_slab):
        states_stack = jnp.stack([own_rows(slab) for slab in slabs_out + [state_slab]])
        pieces = [choose(states_stack, position)]
        pieces += [swap(choose(states_stack, position ^ k), k) for k in range(1, CHAIN)]
        pieces = jnp.stack(pieces)
        return jnp.stack([choose(pieces, position ^ q) for q in range(CHAIN)])

    def states_whole(slabs):
        by_tp = turned(jnp.stack(tp_gather(slabs)), (n_tp - tp_index) % n_tp)
        return jnp.transpose(by_tp, (1, 0, 2, 3)).reshape(state_rows, model_width)

    grad_state_qkv, part, low = chain_back_inputs(
        None, [], cross_pieces, position ^ (CHAIN - 1), qkv_state_flat
    )
    parts = [part] + sent_around(low)
    query_grad, pair_grad = own_back()
    parts = tied(parts, query_grad)
    kept_qkv, kept_rest = [(state_normed, grad_state_qkv)], []
    token_pair_grads = [None] * CHAIN
    init_grad = jnp.zeros((slab_rows, model_width), HIGH)
    bias_one = bias_two = jnp.zeros((1, model_width), HIGH)
    grad_mid = None
    for turn in reversed(range(CHAIN - 1)):
        next_incoming = turns[turn + 1][0]
        (
            state_incoming,
            state_normed,
            state_queries,
            state_pair,
            logs,
            state_heads,
            mid_state,
            state_ffn_in,
            state_slope,
            state_active,
            state_mlp,
        ) = turns[turn]
        grad_next, grad_state, grad_mlp, grad_state_hidden, sums, part, low = chain_back_mlp(
            parts,
            next_incoming,
            grad_mid,
            flags[turn + 1],
            keeps,
            gain_state,
            mid_state,
            state_mlp,
            state_slope,
            up_state,
            down_state,
        )
        init_grad = init_grad + jnp.where(flags[turn + 1], grad_next, 0.0)
        bias_two = bias_two + sums
        parts = [part] + sent_around(low)
        if turn == CHAIN - 2:
            token_grads = ScatterSum(
                weight_grads(
                    [
                        (tied(tuple(ffn_in), part), grad_hidden),
                        ([cotangent_rows], active),
                        (grad_proj_pieces, [token_heads]),
                    ],
                    False,
                )
            )
            parts = tied(parts, token_grads.grads)
        if turn == 0:
            parts = tied(parts, token_grads.total)
        grad_mid, grad_update, sums, query_total, here, across, sent, token_grad = chain_back_heads(
            parts,
            mid_state,
            gain_sffn,
            keeps,
            grad_state,
            state_incoming,
            out_state_flat,
            state_queries,
            state_pair,
            logs,
            pairs_stack,
            position ^ turn,
        )
        bias_one = bias_one + sums
        token_pair_grads[turn] = token_grad
        kept_rest.append(
            (state_heads, grad_update, state_ffn_in, grad_state_hidden, state_active, grad_mlp)
        )
        beside, there = split_rows(swap(sent, 1), 2)
        across = swap((across + there.astype(HIGH)).astype(LOW), 2)
        if turn == CHAIN - 2:
            last_slab = last_state(grad_mid)
            across = tied(across, last_slab)
        if turn == CHAIN - 3:
            slabs = states_between(tied(last_slab, grad_mid))
            across = tied(across, slabs)
        if turn == CHAIN - 4:
            state_rows_out = states_whole(tied(slabs, grad_mid))
            across = tied(across, state_rows_out)
        grad_state_qkv, part, low = chain_back_inputs(
            query_total, [here, beside, across], cross_pieces, position ^ turn, qkv_state_flat
        )
        kept_qkv.append((state_normed, grad_state_qkv))
        if turn:
            parts = [part] + sent_around(low)

    init_grad = init_grad + jnp.where(flags[0], keep_one * grad_mid, 0.0)
    first_part = norm_back(turns[0][0].astype(HIGH), norm_state, part)
    init_grad = init_grad / n_tp + jnp.where(flags[0], first_part, 0.0)
    bias_one = bias_one[0] * keep_one / n_tp
    bias_two = bias_two[0] * keep_two * (1.0 - keep_two) / n_tp

    token_pair_grads[CHAIN - 1] = jnp.zeros_like(token_pair_grads[0])
    pair_stack = jnp.stack(token_pair_grads)
    pair_grad = pair_grad + pos_scatter([choose(pair_stack, position ^ k) for k in range(CHAIN)])
    layer_output = mixed_one + tp_scatter(
        [plain_dot(part, down_tok) for part in tied(tuple(active), pair_stack)]
    )
    qkv_parts = list(zip(*kept_qkv))
    rest_parts = list(zip(*kept_rest))
    state_grads = ScatterSum(
        weight_grads(
            [
                (qkv_parts[0], qkv_parts[1]),
                (rest_parts[1], rest_parts[0]),
                (rest_parts[2], rest_parts[3]),
                (rest_parts[5], rest_parts[4]),
            ],
            False,
        )
    )
    pair_grad = tied(pair_grad, layer_output, state_grads.grads)
    grad_qkv = jnp.concatenate([query_grad, pair_grad], axis=1).astype(LOW)
    grad_normed = tp_scatter(
        [dot_second(part, qkv_tok_flat) for part in split_rows(grad_qkv, n_tp)]
    )
    grad_layer_one = grad_mixed + norm_back(layer_one, norm_tok, grad_normed)

    grad_win_out = tp_gather(grad_layer_one.astype(LOW))
    grad_win_hidden = [
        gelu_slope(part, dot_second(grad, down_win)).astype(LOW)
        for part, grad in zip(win_hidden, grad_win_out)
    ]
    grad_win_ffn_in = tp_scatter([dot_second(part, up_win) for part in grad_win_hidden])

    middle_grads = SeqSum(
        weight_grads(
            [
                (normed_pieces, [grad_qkv]),
                (win_ffn_in, grad_win_hidden),
                (grad_win_out, win_active),
            ]
        )
    )
    grad_win_ffn_in = tied(grad_win_ffn_in, middle_grads.other)
    grad_win_mixed = grad_layer_one + norm_back(win_mixed, norm_wffn, grad_win_ffn_in)
    grad_win_pieces = tp_gather(grad_win_mixed.astype(LOW))
    middle_halves = middle_grads.cores(grad_win_mixed)
    grad_win_proj = jnp.concatenate(grad_win_pieces)
    grad_win_heads = dot_second(grad_win_proj, out_win).astype(LOW)
    win_query_grad, win_pair_grad, win_prev_grad = attend_back(
        win_queries, win_pair, win_logs, grad_win_heads, win_before
    )
    win_returned = lax.ppermute(win_prev_grad, "seq", homeward)
    win_pair_grad = win_pair_grad + tied(win_returned, state_grads.total).astype(HIGH)
    grad_win_qkv = jnp.concatenate([win_query_grad, win_pair_grad], axis=1).astype(LOW)

    small_rows = jnp.concatenate(
        [init_grad, jnp.stack([bias_one, bias_two]), jnp.zeros((14, model_width), HIGH)]
    ).astype(LOW)
    small_shape = small_rows.shape[0], state_rows + 128
    row_of = lax.broadcasted_iota(jnp.int32, small_shape, 0)
    column_of = lax.broadcasted_iota(jnp.int32, small_shape, 1)
    column_for = jnp.where(
        row_of < slab_rows,
        position * slab_rows + row_of,
        (CHAIN - 1) * slab_rows + row_of,
    )
    selector = (column_of == column_for).astype(LOW)
    last_grads = SeqSum(
        weight_grads(
            [
                ([win_normed], [grad_win_qkv]),
                ([grad_win_proj], [win_heads]),
                ([small_rows], [selector]),
            ]
        )
    )
    grad_win_normed = tp_scatter(
        [dot_second(part, qkv_win_flat) for part in split_rows(grad_win_qkv, n_tp)]
    )
    last_halves = last_grads.cores(last_grads.other)
    split_at = [half.shape[-1] for half in middle_halves]
    one, two = last_grads.across(
        *[jnp.concatenate(both, axis=-1) for both in zip(middle_halves, last_halves)]
    )
    middle_halves = one[:, : split_at[0]], two[:, : split_at[1]]
    last_halves = one[:, split_at[0] :], two[:, split_at[1] :]
    back_input = norm_back(own_input, norm_win, grad_win_normed)
    grad_token_rows = natural(tp_gather((grad_win_mixed + back_input).astype(LOW)))
    output_rows = natural(tp_gather(tied(layer_output.astype(LOW), win_returned)))

    own_columns = model_width // lax.axis_size("seq")
    inner_width = up_tok.shape[1]
    token_grads.total, state_grads.total = tied(
        (token_grads.total, state_grads.total), last_grads.other
    )
    sum_qkv_win = columns_of(last_halves, 0, 3 * width)
    sum_qkv_tok = columns_of(middle_halves, 0, 3 * width)
    sum_qkv_state = state_grads.columns(0, 3 * width)
    sum_up_win = columns_of(middle_halves, 3 * width, inner_width)
    sum_up_tok = token_grads.columns(0, inner_width)
    sum_up_state = state_grads.columns(5 * width, inner_width)
    small_sums = columns_of(last_halves, 4 * width, state_rows + 2)
    first_row = seq_index * own_columns
    vectors = [
        gain_grad(qkv_win_flat, sum_qkv_win, norm_win, first_row),
        gain_grad(up_win, sum_up_win, norm_wffn, first_row),
        gain_grad(qkv_tok_flat, sum_qkv_tok, norm_tok, first_row),
        gain_grad(up_tok, sum_up_tok, norm_ffn, first_row),
        gain_grad(qkv_state_flat, sum_qkv_state, norm_state, first_row),
        gain_grad(up_state, sum_up_state, norm_sffn, first_row),
    ]
    small_sums = sum(
        tp_gather(jnp.concatenate([small_sums] + vectors, axis=1))
    )
    sum_init, vector_sums = small_sums[:, :state_rows].T, small_sums[:, state_rows:]

    def qkv_of(columns):
        return columns.reshape(own_columns, 3, width)

    def out_of(columns):
        return columns.T.reshape(2, width, own_columns)

    return (
        output_rows,
        state_rows_out,
        grad_token_rows,
        vector_sums[:, 2],
        qkv_of(sum_qkv_win),
        columns_of(last_halves, 3 * width, width).T,
        vector_sums[:, 3],
        sum_up_win,
        columns_of(middle_halves, 3 * width + inner_width, inner_width).T,
        vector_sums[:, 4],
        qkv_of(sum_qkv_tok),
        out_of(token_grads.columns(2 * inner_width, 2 * width)),
        vector_sums[:, 5],
        sum_up_tok,
        token_grads.columns(inner_width, inner_width).T,
        vector_sums[:, 6],
        qkv_of(sum_qkv_state),
        out_of(state_grads.columns(3 * width, 2 * width)),
        vector_sums[:, 0:2].T,
        vector_sums[:, 7],
        sum_up_state,
        state_grads.columns(5 * width + inner_width, inner_width).T,
        sum_init,
    )


def solution(mesh):
    placed = (
        P("seq", None),
        P(),
        P(),
        P(None, None, "tp"),
        P("tp", None),
        P(),
        P(None, "tp"),
        P("tp", None),
        P(),
        P(None, None, "tp"),
        P(None, "tp", None),
        P(),
        P(None, "tp"),
        P("tp", None),
        P(),
        P(None, None, "tp"),
        P(None, "tp", None),
        P(),
        P(),
        P(None, "tp"),
        P("tp", None),
        P(),
        P("seq", None),
    )
    return jax.shard_map(
        body,
        mesh=mesh,
        in_specs=placed,
        out_specs=(
            P("seq", None),
            P("seq", None),
            P("seq", None),
            P("seq"),
            P("seq", None, "tp"),
            P("tp", "seq"),
            P("seq"),
            P("seq", "tp"),
            P("tp", "seq"),
            P("seq"),
            P("seq", None, "tp"),
            P(None, "tp", "seq"),
            P("seq"),
            P("seq", "tp"),
            P("tp", "seq"),
            P("seq"),
            P("seq", None, "tp"),
            P(None, "tp", "seq"),
            P(None, "seq"),
            P("seq"),
            P("seq", "tp"),
            P("tp", "seq"),
            P(None, "seq"),
        ),
        check_vma=False,
    )
```

```python
import jax
import jax.numpy as jnp
from jax import lax
from jax.experimental import pallas as pl
from jax.experimental.layout import Layout, with_layout_constraint
from jax.experimental.pallas import tpu as pltpu
from jax.sharding import PartitionSpec as P

E = 128
CHAIN = 4
CORES = 2

EPSILON = 1e-05
MASKED = -1e30
LOW = jnp.bfloat16
HIGH = jnp.float32


def layer_norm(matrix, weights):
    average = jnp.mean(matrix, axis=-1, keepdims=True)
    centred = matrix - average
    spread = jnp.mean(centred * centred, axis=-1, keepdims=True)
    return centred * lax.rsqrt(spread + EPSILON) * weights


def gelu_exact(matrix):
    return jax.nn.gelu(matrix, approximate=False)


def gelu_slope(matrix, grad):
    return jax.vjp(gelu_exact, matrix)[1](grad)[0]


def plain_dot(former, latter):
    return jnp.dot(former, latter, preferred_element_type=HIGH)


def dot_first(former, latter):
    return lax.dot_general(
        former, latter, (((0,), (0,)), ((), ())), preferred_element_type=HIGH
    )


def dot_second(former, latter):
    return lax.dot_general(
        former, latter, (((1,), (1,)), ((), ())), preferred_element_type=HIGH
    )


def row_major(array):
    return with_layout_constraint(array, Layout(major_to_minor=tuple(range(array.ndim))))


def tied(value, *others):
    return lax.optimization_barrier((value, others))[0]


def norm_back(matrix, weights, grad):
    average = jnp.mean(matrix, axis=-1, keepdims=True)
    centred = matrix - average
    spread = jnp.mean(centred * centred, axis=-1, keepdims=True)
    scaled = centred * lax.rsqrt(spread + EPSILON)
    inner = grad * weights
    return lax.rsqrt(spread + EPSILON) * (
        inner
        - jnp.mean(inner, axis=-1, keepdims=True)
        - scaled * jnp.mean(inner * scaled, axis=-1, keepdims=True)
    )


def gain_grad(weights, grads, gain, first):
    rows = lax.dynamic_slice_in_dim(weights, first, grads.shape[0], 0).astype(HIGH)
    gains = lax.dynamic_slice_in_dim(gain.reshape(-1, 1), first, grads.shape[0], 0)
    return jnp.sum(rows * grads, axis=1, keepdims=True) / gains


def tp_from(array, k):
    n = lax.axis_size("tp")
    return lax.ppermute(array, "tp", [((i + k) % n, i) for i in range(n)])


def tp_to(array, k):
    n = lax.axis_size("tp")
    return lax.ppermute(array, "tp", [(i, (i + k) % n) for i in range(n)])


def far_first(n):
    return sorted(range(1, n), key=lambda k: -min(k, n - k))


def tp_gather(piece):
    n = lax.axis_size("tp")
    found = {k: tp_from(piece, k) for k in far_first(n)}
    return [piece] + [found[k] for k in range(1, n)]


def tp_scatter(parts):
    n = lax.axis_size("tp")
    total = parts[0]
    for k in far_first(n):
        total = total + tp_to(parts[k].astype(LOW), k).astype(HIGH)
    return total


def tp_total(part):
    low = part.astype(LOW)
    total = part
    for k in far_first(lax.axis_size("tp")):
        total = total + tp_to(low, k).astype(HIGH)
    return total


def split_rows(matrix, n):
    size = matrix.shape[0] // n
    return [matrix[k * size : (k + 1) * size] for k in range(n)]


def swap(array, k):
    n = lax.axis_size("seq")
    return lax.ppermute(array, "seq", [(s, s ^ k) for s in range(n)])


def pos_gather(piece):
    beside, across = swap(piece, 1), swap(piece, 2)
    return [piece, beside, across, swap(across, 1)]


def pos_scatter(parts):
    low = jnp.concatenate([parts[1], parts[3]]).astype(LOW)
    here, there = split_rows(swap(low, 1), 2)
    across = swap((parts[2] + there.astype(HIGH)).astype(LOW), 2)
    return parts[0] + here.astype(HIGH) + across.astype(HIGH)


def choose(stacked, index):
    return lax.dynamic_index_in_dim(stacked, index, 0, keepdims=False)


def turned(array, start):
    twice = jnp.concatenate([array, array])
    return lax.dynamic_slice_in_dim(twice, start, array.shape[0], 0)


def weight_grads(pairs, split=True):
    n_seq = lax.axis_size("seq")
    depth = pairs[0][0][0].shape[1]
    unit = depth // n_seq
    block = max(256, CORES * unit)
    widths = [latter[0].shape[1] for _, latter in pairs]
    total = sum(widths)
    counts = [(len(former), len(latter)) for former, latter in pairs]
    operands, specs = [], []
    for former, latter in pairs:
        for piece in former:
            operands.append(piece)
            specs.append(pl.BlockSpec((piece.shape[0], block), lambda i: (0, i)))
        for piece in latter:
            operands.append(piece)
            specs.append(pl.BlockSpec(piece.shape, lambda i: (0, 0), pipeline_mode=pl.Buffered(1)))

    def kernel(core_ref, *refs):
        mine_ref, other_ref = refs[-2:]
        first = core_ref[0] == 0

        def keep(product, column):
            columns = slice(column, column + product.shape[1])
            if not split:
                other_ref[:, columns] = product
                return
            for g in range(block // (CORES * unit)):
                low = product[g * CORES * unit : g * CORES * unit + unit]
                high = product[g * CORES * unit + unit : (g + 1) * CORES * unit]
                rows = slice(g * unit, (g + 1) * unit)
                mine_ref[rows, columns] = jnp.where(first, low, high)
                other_ref[rows, columns] = jnp.where(first, high, low)

        at, column = 0, 0
        for (n_former, n_latter), width in zip(counts, widths):
            former = [ref[...] for ref in refs[at : at + n_former]]
            latter = [ref[...] for ref in refs[at + n_former : at + n_former + n_latter]]
            at += n_former + n_latter
            former = jnp.concatenate(former) if n_former > 1 else former[0]
            latter = jnp.concatenate(latter) if n_latter > 1 else latter[0]
            keep(dot_first(former, latter).astype(LOW), column)
            column += width

    shapes = [jax.ShapeDtypeStruct((depth // CORES, total), LOW)] * 2
    out_specs = [pl.BlockSpec((block // CORES, total), lambda i: (i, 0))] * 2
    if not split:
        shapes = [jax.ShapeDtypeStruct((depth, total), LOW)]
        out_specs = [pl.BlockSpec((block, total), lambda i: (i, 0))]
    rows = sum(piece.shape[0] for piece in pairs[0][0])
    core = (lax.axis_index("seq") % CORES).astype(jnp.int32).reshape(1)
    return pl.pallas_call(
        kernel,
        out_shape=shapes,
        grid=(depth // block,),
        in_specs=[pl.BlockSpec(memory_space=pltpu.SMEM)] + specs,
        out_specs=out_specs,
        compiler_params=pltpu.CompilerParams(vmem_limit_bytes=20 * 1024 * 1024),
        cost_estimate=pl.CostEstimate(
            flops=2 * rows * depth * total,
            bytes_accessed=2 * (rows * (depth + total) + depth * total),
            transcendentals=0,
        ),
    )(core, *operands)


class ScatterSum:
    def __init__(self, grads):
        self.grads = grads[0]
        self.total = lax.psum_scatter(self.grads, "seq", scatter_dimension=0, tiled=True)

    def columns(self, at, count):
        return self.total[:, at : at + count].astype(HIGH)


class SeqSum:
    def __init__(self, halves):
        n = lax.axis_size("seq")
        self.z_size = 4 if n % 8 == 0 else n // CORES
        self.x_size = n // (self.z_size * CORES)
        here = lax.axis_index("seq")
        self.z_at = here // CORES % self.z_size
        self.x_at = here // (CORES * self.z_size)
        self.mine, self.other = halves

    def pairs(self, dx, dz):
        def place(x, z, c):
            return (x % self.x_size * self.z_size + z % self.z_size) * CORES + c

        return [
            (place(x, z, c), place(x + dx, z + dz, c))
            for x in range(self.x_size)
            for z in range(self.z_size)
            for c in range(CORES)
        ]

    def over_z(self, array, dim):
        return self.stage(array, dim, self.z_at, self.z_size, lambda k: (0, k))

    def over_x(self, array, dim):
        return self.stage(array, dim, self.x_at, self.x_size, lambda k: (k, 0))

    def stage(self, array, dim, at, size, step):
        total = lax.dynamic_index_in_dim(array, at, dim, False).astype(HIGH)
        for k in far_first(size):
            sent = lax.dynamic_index_in_dim(array, (at + k) % size, dim, False)
            total = total + lax.ppermute(sent, "seq", self.pairs(*step(k))).astype(HIGH)
        return row_major(total)

    def cores(self, after):
        width = self.mine.shape[1]
        sent = swap(tied(self.other, after), 1)
        half = width // 256 * 128

        def total(columns):
            part = self.mine[:, columns].astype(HIGH) + sent[:, columns].astype(HIGH)
            return part.astype(LOW).reshape(self.x_size, self.z_size, -1, part.shape[1])

        return total(slice(0, half)), total(slice(half, width))

    def across(self, one, two):
        one, two = self.over_z(one, 1).astype(LOW), self.over_x(two, 0).astype(LOW)
        return self.over_x(one, 0), self.over_z(two, 0)


def columns_of(halves, at, count):
    one, two = halves
    half = one.shape[1]
    if at + count <= half:
        return one[:, at : at + count]
    if at >= half:
        return two[:, at - half : at - half + count]
    return jnp.concatenate([one[:, at:], two[:, : at + count - half]], axis=1)


ATTEND_STEP = 256


class Loaded:
    def __init__(self, source, buffer, semaphore):
        self.buffer, self.copy, self.waiting = buffer, None, True
        self.copy = pltpu.make_async_copy(source, buffer, semaphore)
        self.copy.start()

    def __getitem__(self, index):
        if self.waiting:
            self.copy.wait()
            self.waiting = False
        return self.buffer[index]


class Kept:
    def __init__(self, target, buffer, semaphore):
        self.buffer, self.started = buffer, False
        self.copy = pltpu.make_async_copy(buffer, target, semaphore)

    def __getitem__(self, index):
        return self.buffer[index]

    def __setitem__(self, index, value):
        self.buffer[index] = value
        if index is Ellipsis:
            self.start()

    def start(self):
        self.copy.start()
        self.started = True

    def finish(self):
        if not self.started:
            self.start()
        self.copy.wait()


def fused(kernel, outs, operands, products, scalars=(), exps=0, loaded=(), chosen=None, kept=()):
    in_vmem = pl.BlockSpec(memory_space=pltpu.VMEM)
    in_hbm = pl.BlockSpec(memory_space=pltpu.HBM)
    in_smem = pl.BlockSpec(memory_space=pltpu.SMEM)
    scalars = [jnp.asarray(scalar, jnp.int32).reshape(1) for scalar in scalars]
    loaded = list(loaded) + ([] if chosen is None else [chosen])
    n_scalars, n_in, n_out = len(scalars), len(operands), len(outs)
    scratch = []
    for k in loaded:
        shape = operands[k].shape
        scratch.append(pltpu.VMEM(shape[1:] if k == chosen else shape, operands[k].dtype))
    for k in kept:
        scratch.append(pltpu.VMEM(*outs[k]))
    moved = len(scratch)
    if moved:
        scratch.append(pltpu.SemaphoreType.DMA((moved,)))

    def whole(*refs):
        views = list(refs[: n_scalars + n_in + n_out])
        buffers = refs[n_scalars + n_in + n_out :]
        for spot, k in enumerate(loaded):
            source = views[n_scalars + k]
            if k == chosen:
                source = source.at[views[0][0]]
            views[n_scalars + k] = Loaded(source, buffers[spot], buffers[-1].at[spot])
        for spot, k in enumerate(kept, len(loaded)):
            at = n_scalars + n_in + k
            views[at] = Kept(views[at], buffers[spot], buffers[-1].at[spot])
        kernel(*views)
        for k in kept:
            views[n_scalars + n_in + k].finish()

    return pl.pallas_call(
        whole,
        out_shape=[jax.ShapeDtypeStruct(shape, kind) for shape, kind in outs],
        in_specs=[in_smem] * n_scalars + [in_hbm if k in loaded else in_vmem for k in range(n_in)],
        out_specs=[in_hbm if k in kept else in_vmem for k in range(n_out)],
        scratch_shapes=scratch,
        compiler_params=pltpu.CompilerParams(vmem_limit_bytes=20 * 1024 * 1024),
        cost_estimate=pl.CostEstimate(
            flops=2 * products,
            bytes_accessed=sum(2 * operand.size for operand in operands),
            transcendentals=exps,
        ),
    )(*scalars, *operands)


def score_parts(query, key, before, spot):
    if before is None:
        return dot_second(key, query) * E ** (-0.5), None
    key_before, _, shift, start = before
    shape = key.shape[0], query.shape[0]
    key_ids = (lax.broadcasted_iota(jnp.int32, shape, 0) + shift) % shape[0]
    query_ids = (lax.broadcasted_iota(jnp.int32, shape, 1) + shift + spot) % shape[0]
    below = key_ids <= query_ids
    scores = jnp.where(below, dot_second(key, query), dot_second(key_before, query))
    return jnp.where(below | (start == 0), scores * E ** (-0.5), MASKED), below


def head_attend(query, key, value, before=None, spot=0):
    scores, below = score_parts(query, key, before, spot)
    top = jnp.max(scores, axis=0, keepdims=True)
    powers = jnp.exp(scores - top)
    total = jnp.sum(powers, axis=0, keepdims=True)
    chances = (powers * (1.0 / total)).astype(LOW)
    if before is None:
        result = dot_first(value, chances)
    else:
        none = jnp.zeros_like(chances)
        result = dot_first(value, jnp.where(below, chances, none)) + dot_first(
            before[1], jnp.where(below, none, chances)
        )
    return result.T.astype(LOW), top + jnp.log(total)


def head_back(query, key, value, log, grad, before=None, spot=0):
    scores, below = score_parts(query, key, before, spot)
    chances = jnp.exp(scores - log)
    grad_chances = dot_second(value, grad)
    if before is not None:
        grad_chances = jnp.where(below, grad_chances, dot_second(before[1], grad))
    inner = jnp.sum(chances * grad_chances, axis=0, keepdims=True)
    grad_scores = (chances * (grad_chances - inner) * E ** (-0.5)).astype(LOW)
    chances = chances.astype(LOW)
    if before is None:
        terms = [plain_dot(grad_scores, query), plain_dot(chances, grad)]
        return dot_first(key, grad_scores).T, terms
    none = jnp.zeros_like(chances)
    scores_now = jnp.where(below, grad_scores, none)
    scores_before = jnp.where(below, none, grad_scores)
    terms = [
        plain_dot(scores_now, query),
        plain_dot(jnp.where(below, chances, none), grad),
        plain_dot(scores_before, query),
        plain_dot(jnp.where(below, none, chances), grad),
    ]
    query_grad = dot_first(key, scores_now) + dot_first(before[0], scores_before)
    return query_grad.T, terms


def head_columns(head, width, part):
    return slice(part * width + head * E, part * width + (head + 1) * E)


def attend(queries, pair, before=None):
    count, width = queries.shape
    heads = width // E
    rows = min(count, ATTEND_STEP)
    scalars = [] if before is None else before[1:]
    operands = [queries, pair] + ([] if before is None else [before[0]])

    def kernel(*refs):
        scalar_refs, refs = refs[: len(scalars)], refs[len(scalars) :]
        query_ref, pair_ref = refs[:2]
        result_ref, log_ref = refs[-2:]
        for h in range(heads):
            own = slice(h * E, (h + 1) * E)
            key_at, value_at = head_columns(h, width, 0), head_columns(h, width, 1)
            mask = None
            if before is not None:
                mask = (refs[2][:, key_at], refs[2][:, value_at]) + tuple(
                    ref[0] for ref in scalar_refs
                )
            for spot in range(0, count, rows):
                here = slice(spot, spot + rows)
                result_ref[here, own], log_ref[h : h + 1, here] = head_attend(
                    query_ref[here, own], pair_ref[:, key_at], pair_ref[:, value_at], mask, spot
                )

    scores_count = heads * count * pair.shape[0]
    outs = [((count, width), LOW), ((heads, count), HIGH)]
    products = scores_count * E * len(operands)
    return fused(kernel, outs, operands, products, scalars, scores_count)


def attend_back(queries, pair, logs, grad_result, before=None):
    count, width = queries.shape
    heads = width // E
    rows = min(count, ATTEND_STEP)
    keys = pair.shape[0]
    scalars = [] if before is None else before[1:]
    operands = [queries, logs, grad_result, pair] + ([] if before is None else [before[0]])

    def kernel(*refs):
        scalar_refs, refs = refs[: len(scalars)], refs[len(scalars) :]
        query_ref, log_ref, grad_ref, pair_ref = refs[:4]
        outs = refs[len(operands) :]
        for h in range(heads):
            own = slice(h * E, (h + 1) * E)
            key_at, value_at = head_columns(h, width, 0), head_columns(h, width, 1)
            mask = None
            if before is not None:
                mask = (refs[4][:, key_at], refs[4][:, value_at]) + tuple(
                    ref[0] for ref in scalar_refs
                )
            sums = None
            for spot in range(0, count, rows):
                here = slice(spot, spot + rows)
                outs[0][here, own], terms = head_back(
                    query_ref[here, own],
                    pair_ref[:, key_at],
                    pair_ref[:, value_at],
                    log_ref[h : h + 1, here],
                    grad_ref[here, own],
                    mask,
                    spot,
                )
                sums = terms if sums is None else [one + two for one, two in zip(sums, terms)]
            outs[1][:, key_at], outs[1][:, value_at] = sums[:2]
            if before is not None:
                outs[2][:, key_at], outs[2][:, value_at] = sums[2].astype(LOW), sums[3].astype(LOW)

    outs = [((count, width), HIGH), ((keys, 2 * width), HIGH)]
    if before is not None:
        outs.append(((keys, 2 * width), LOW))
    scores_count = heads * count * keys
    products = scores_count * E * (5 if before is None else 10)
    return fused(kernel, outs, operands, products, scalars, scores_count)


def gelu_of(matrix):
    return 0.5 * matrix * (1.0 + lax.erf(matrix * 0.5**0.5))


def gelu_slope_of(matrix):
    density = jnp.exp(-0.5 * matrix * matrix) * (2.0 * jnp.pi) ** (-0.5)
    return 0.5 * (1.0 + lax.erf(matrix * 0.5**0.5)) + matrix * density


def sent_around(low):
    return [tp_to(low, k) for k in far_first(lax.axis_size("tp"))]


def added(refs):
    total = refs[0][...]
    for ref in refs[1:]:
        total = total + ref[...].astype(HIGH)
    return total


def chain_attend(queries, pieces, stack, index, out_flat):
    count, width = queries.shape
    n, keys = len(pieces), stack.shape[1]

    def kernel(index_ref, query_ref, *refs):
        pieces_refs, (stack_ref, out_ref) = refs[:n], refs[n : n + 2]
        pair_ref, own_ref, cross_ref, heads_ref, part_ref, low_ref = refs[n + 2 :]
        for k, ref in enumerate(pieces_refs):
            pair_ref[k * (keys // n) : (k + 1) * (keys // n), :] = ref[...]
        for h in range(width // E):
            own = slice(h * E, (h + 1) * E)
            key_at, value_at = head_columns(h, width, 0), head_columns(h, width, 1)
            row = slice(h, h + 1)
            heads_ref[:, own], own_ref[row, :] = head_attend(
                query_ref[:, own], pair_ref[:, key_at], pair_ref[:, value_at]
            )
        for h in range(width // E):
            own = slice(h * E, (h + 1) * E)
            key_at, value_at = head_columns(h, width, 0), head_columns(h, width, 1)
            row = slice(h, h + 1)
            heads_ref[:, value_at], cross_ref[row, :] = head_attend(
                query_ref[:, own], stack_ref[:, key_at], stack_ref[:, value_at]
            )
        heads_ref.start()
        part = plain_dot(heads_ref[...], out_ref[...])
        part_ref[...] = part
        low_ref[...] = part.astype(LOW)

    depth = out_flat.shape[1]
    logs = ((width // E, count), HIGH)
    outs = [((keys, 2 * width), LOW), logs, logs, ((count, 2 * width), LOW)]
    outs += [((count, depth), HIGH), ((count, depth), LOW)]
    products = count * width * (4 * keys + 2 * depth)
    operands = [queries, *pieces, stack, out_flat]
    exps = 2 * count * keys
    return fused(kernel, outs, operands, products, [index], exps, chosen=n + 1, kept=(3,))


def chain_mlp(parts, incoming, keeps, gain, up, down):
    n = len(parts)

    def kernel(*refs):
        incoming_ref, keep_ref, gain_ref, up_ref, down_ref = refs[n : n + 5]
        mid_ref, normed_ref, slope_ref, active_ref, incoming_out, part_ref, low_ref = refs[n + 5 :]
        incoming_out[...] = incoming_ref[...]
        keep = keep_ref[0:1, :]
        mid = keep * incoming_ref[...].astype(HIGH) + (1.0 - keep) * added(refs[:n])
        normed = layer_norm(mid, gain_ref[...]).astype(LOW)
        mid_ref[...], normed_ref[...] = mid, normed
        hidden = plain_dot(normed, up_ref[...])
        active = gelu_of(hidden).astype(LOW)
        slope_ref[...], active_ref[...] = gelu_slope_of(hidden).astype(LOW), active
        part = plain_dot(active, down_ref[...])
        part_ref[...], low_ref[...] = part, part.astype(LOW)

    count, depth = incoming.shape
    inner = up.shape[1]
    outs = [((count, depth), HIGH), ((count, depth), LOW)]
    outs += [((count, inner), LOW), ((count, inner), LOW), ((count, depth), LOW)]
    outs += [((count, depth), HIGH), ((count, depth), LOW)]
    operands = [*parts, incoming, keeps, gain, up, down]
    products = 2 * count * depth * inner
    return fused(kernel, outs, operands, products, (), count * inner, kept=(1, 2, 3, 4))


def chain_start(parts, mid, keeps, init_slab, flag, gain, qkv_flat):
    n = len(parts)
    width = qkv_flat.shape[1] // 3

    def kernel(flag_ref, *refs):
        mid_ref, keep_ref, init_ref, gain_ref, qkv_ref = refs[n : n + 5]
        mlp_ref, slab_ref, incoming_ref, normed_ref, query_ref, pair_ref, mid_out = refs[n + 5 :]
        mid_out[...] = mid_ref[...]
        mlp = added(refs[:n])
        keep = keep_ref[1:2, :]
        slab = (keep * mid_ref[...] + (1.0 - keep) * mlp).astype(LOW)
        incoming = jnp.where(flag_ref[0] == 1, init_ref[...], slab)
        mlp_ref[...], slab_ref[...], incoming_ref[...] = mlp.astype(LOW), slab, incoming
        normed = layer_norm(incoming.astype(HIGH), gain_ref[...]).astype(LOW)
        normed_ref[...] = normed
        qkv = plain_dot(normed, qkv_ref[...]).astype(LOW)
        query_ref[...], pair_ref[...] = qkv[:, :width], qkv[:, width:]

    count, depth = mid.shape
    outs = [((count, depth), LOW)] * 4 + [((count, width), LOW), ((count, 2 * width), LOW)]
    outs += [((count, depth), HIGH)]
    operands = [*parts, mid, keeps, init_slab, gain, qkv_flat]
    return fused(kernel, outs, operands, 3 * count * depth * width, [flag], kept=(0, 1, 3, 6))


def chain_back_mlp(parts, incoming, grad_mid, flag, keeps, gain, mid, mlp, slope, up, down):
    n = len(parts)
    operands = [*parts, incoming, keeps, gain, mid, mlp, slope, up, down]
    operands += [] if grad_mid is None else [grad_mid]

    def kernel(flag_ref, *refs):
        incoming_ref, keep_ref, gain_ref, mid_ref, mlp_ref, slope_ref, up_ref, down_ref = refs[
            n : n + 8
        ]
        grad_ref, state_ref, low_mlp_ref, low_hidden_ref, bias_ref, part_ref, low_ref = refs[-7:]
        grad = norm_back(incoming_ref[...].astype(HIGH), gain_ref[...], added(refs[:n]))
        if grad_mid is not None:
            grad = keep_ref[0:1, :] * refs[n + 8][...] + grad
        state = jnp.where(flag_ref[0] == 1, 0.0, grad)
        low_mlp = ((1.0 - keep_ref[1:2, :]) * state).astype(LOW)
        grad_ref[...], state_ref[...], low_mlp_ref[...] = grad, state, low_mlp
        grad_active = dot_second(low_mlp, down_ref[...])
        low_hidden = (slope_ref[...].astype(HIGH) * grad_active).astype(LOW)
        low_hidden_ref[...] = low_hidden
        part = dot_second(low_hidden, up_ref[...])
        change = mid_ref[...] - mlp_ref[...].astype(HIGH)
        bias_ref[...] = jnp.sum(state * change, axis=0, keepdims=True)
        part_ref[...], low_ref[...] = part, part.astype(LOW)

    count, depth = mid.shape
    inner = up.shape[1]
    outs = [((count, depth), HIGH), ((count, depth), HIGH), ((count, depth), LOW)]
    outs += [((count, inner), LOW), ((1, depth), HIGH)]
    outs += [((count, depth), HIGH), ((count, depth), LOW)]
    loaded = (n, n + 3, n + 4, n + 5)
    products = 2 * count * depth * inner
    return fused(kernel, outs, operands, products, [flag], loaded=loaded, kept=(2, 3))


def chain_back_heads(
    parts, mid, gain, keeps, grad_state, incoming, out_flat, queries, pair, logs, stack, index
):
    n = len(parts)
    count, width = queries.shape
    keys = pair.shape[0]
    slab = keys // CHAIN

    def kernel(index_ref, *refs):
        mid_ref, gain_ref, keep_ref, state_ref, incoming_ref, out_ref = refs[n : n + 6]
        query_ref, pair_ref, own_log_ref, cross_log_ref, stack_ref = refs[n + 6 : n + 11]
        outs = refs[n + 11 :]
        mid_out, low_out, bias_out, query_out, here_out, across_out, sent_out, token_out = outs
        grad_mid = keep_ref[1:2, :] * state_ref[...] + norm_back(
            mid_ref[...], gain_ref[...], added(refs[:n])
        )
        mid_out[...] = grad_mid
        low = ((1.0 - keep_ref[0:1, :]) * grad_mid).astype(LOW)
        low_out[...] = low
        change = incoming_ref[...].astype(HIGH) - mid_ref[...]
        bias_out[...] = jnp.sum(grad_mid * change, axis=0, keepdims=True)
        grad_heads = dot_second(low, out_ref[...]).astype(LOW)
        for h in range(width // E):
            own = slice(h * E, (h + 1) * E)
            row = slice(h, h + 1)
            own_query, own_terms = head_back(
                query_ref[:, own],
                pair_ref[:, head_columns(h, width, 0)],
                pair_ref[:, head_columns(h, width, 1)],
                own_log_ref[row, :],
                grad_heads[:, own],
            )
            cross_query, cross_terms = head_back(
                query_ref[:, own],
                stack_ref[:, head_columns(h, width, 0)],
                stack_ref[:, head_columns(h, width, 1)],
                cross_log_ref[row, :],
                grad_heads[:, head_columns(h, width, 1)],
            )
            query_out[:, own] = own_query + cross_query
            for part in range(2):
                at = head_columns(h, width, part)
                here_out[:, at] = own_terms[part][:slab]
                across_out[:, at] = own_terms[part][2 * slab : 3 * slab]
                sent_out[:slab, at] = own_terms[part][slab : 2 * slab].astype(LOW)
                sent_out[slab:, at] = own_terms[part][3 * slab :].astype(LOW)
                token_out[:, at] = cross_terms[part]

    depth = mid.shape[1]
    outs = [((count, depth), HIGH), ((count, depth), LOW), ((1, depth), HIGH)]
    outs += [((count, width), HIGH), ((slab, 2 * width), HIGH), ((slab, 2 * width), HIGH)]
    outs += [((2 * slab, 2 * width), LOW), ((keys, 2 * width), HIGH)]
    operands = [*parts, mid, gain, keeps, grad_state, incoming, out_flat]
    operands += [queries, pair, *logs, stack]
    products = count * width * (10 * keys + 2 * depth)
    loaded = (n, n + 4, n + 6, n + 7)
    exps = 2 * count * keys
    return fused(kernel, outs, operands, products, [index], exps, loaded, n + 10, (1, 7))


def chain_back_inputs(query_grad, terms, stack, index, qkv_flat):
    rows, depth = stack.shape[1], qkv_flat.shape[0]
    width = qkv_flat.shape[1] // 3
    first = [] if query_grad is None else [query_grad]

    def kernel(index_ref, *refs):
        stack_ref, qkv_ref = refs[len(first) + len(terms) : len(first) + len(terms) + 2]
        grad_ref, part_ref, low_ref = refs[-3:]
        pair = stack_ref[...]
        for ref in refs[len(first) : len(first) + len(terms)]:
            pair = pair + ref[...].astype(HIGH)
        if first:
            grad_ref[:, :width] = refs[0][...].astype(LOW)
        else:
            grad_ref[:, :width] = jnp.zeros((rows, width), LOW)
        grad_ref[:, width:] = pair.astype(LOW)
        grad_ref.start()
        part = dot_second(grad_ref[...], qkv_ref[...])
        part_ref[...], low_ref[...] = part, part.astype(LOW)

    outs = [((rows, 3 * width), LOW), ((rows, depth), HIGH), ((rows, depth), LOW)]
    operands = [*first, *terms, stack, qkv_flat]
    chosen = len(first) + len(terms)
    products = 3 * rows * depth * width
    return fused(kernel, outs, operands, products, [index], chosen=chosen, kept=(0,))


def body(
    tokens,
    segment_start,
    norm_win,
    qkv_win,
    out_win,
    norm_wffn,
    up_win,
    down_win,
    norm_tok,
    qkv_tok,
    out_tok,
    norm_ffn,
    up_tok,
    down_tok,
    norm_state,
    qkv_state,
    out_state,
    gate_bias,
    norm_sffn,
    up_state,
    down_state,
    init_state,
    cotangent,
):
    seq_index = lax.axis_index("seq")
    tp_index = lax.axis_index("tp")
    n_tp = lax.axis_size("tp")
    position = seq_index % CHAIN
    flags = choose(segment_start, seq_index // CHAIN) == 1
    starts_here = choose(flags, position)
    block_rows, model_width = tokens.shape
    piece_rows = block_rows // n_tp
    state_rows = init_state.shape[0]
    slab_rows = state_rows // CHAIN
    thin_rows = slab_rows // n_tp
    width = qkv_tok.shape[2]
    qkv_win_flat = qkv_win.reshape(model_width, 3 * width)
    out_tok_flat = out_tok.reshape(2 * width, model_width)
    out_state_flat = out_state.reshape(2 * width, model_width)

    shift = (tp_index * piece_rows).astype(jnp.int32)
    start_flag = starts_here.astype(jnp.int32)
    token_rows = turned(tokens, tp_index * piece_rows)

    def natural(pieces):
        whole = jnp.zeros((block_rows, model_width), pieces[0].dtype)
        for k, piece in enumerate(pieces):
            at = (tp_index + k) % n_tp * piece_rows
            whole = lax.dynamic_update_slice_in_dim(whole, piece, at, 0)
        return whole

    input_rows = token_rows.astype(HIGH)
    win_normed = layer_norm(input_rows, norm_win).astype(LOW)
    win_qkv = plain_dot(win_normed, qkv_win_flat).astype(LOW)
    win_queries, win_pair = win_qkv[:, :width], win_qkv[:, width:]
    onward = [(s, s + 1) for s in range(lax.axis_size("seq")) if (s + 1) % CHAIN]
    win_prev = lax.ppermute(win_pair, "seq", onward)
    win_before = win_prev, shift, start_flag
    win_heads, win_logs = attend(win_queries, win_pair, win_before)
    cotangent, qkv_tok, qkv_state, gate_bias, init_state, _ = lax.optimization_barrier(
        (cotangent, qkv_tok, qkv_state, gate_bias, init_state, win_heads)
    )
    qkv_tok_flat = qkv_tok.reshape(model_width, 3 * width)
    qkv_state_flat = qkv_state.reshape(model_width, 3 * width)
    keep_one, keep_two = jax.nn.sigmoid(gate_bias)
    cotangent_rows = turned(cotangent, tp_index * piece_rows)
    own_input = input_rows[:piece_rows]
    win_mixed = own_input + tp_scatter(
        [plain_dot(part, out_win) for part in split_rows(win_heads, n_tp)]
    )
    win_ffn_in = tp_gather(layer_norm(win_mixed, norm_wffn).astype(LOW))
    win_hidden = [plain_dot(part, up_win) for part in win_ffn_in]
    win_active = [gelu_exact(part).astype(LOW) for part in win_hidden]

    init_slab = lax.dynamic_slice_in_dim(init_state, position * slab_rows, slab_rows, 0)

    def own_rows(slab):
        return lax.dynamic_slice_in_dim(slab, tp_index * thin_rows, thin_rows, 0)

    init_late = tied(init_slab, win_ffn_in[1])
    state_incoming = init_late
    state_normed = layer_norm(state_incoming.astype(HIGH), norm_state).astype(LOW)
    state_qkv = plain_dot(state_normed, qkv_state_flat).astype(LOW)
    state_queries = state_qkv[:, :width]
    state_pieces = pos_gather(state_qkv[:, width:])
    layer_one = win_mixed + tp_scatter([plain_dot(part, down_win) for part in win_active])
    layer_one = tied(layer_one, state_pieces)

    normed_pieces = tp_gather(layer_norm(layer_one, norm_tok).astype(LOW))
    normed = jnp.concatenate(normed_pieces)
    token_qkv = plain_dot(normed, qkv_tok_flat).astype(LOW)
    queries, pair = token_qkv[:, :width], token_qkv[:, width:]
    pairs_all = pos_gather(pair)
    pair_prev = jnp.where(position % 2 == 1, pairs_all[1], pairs_all[3])
    pairs_stack = jnp.stack(pairs_all)
    before = pair_prev, shift, start_flag

    keeps = jnp.stack([keep_one, keep_two])
    gain_state, gain_sffn = norm_state.reshape(1, -1), norm_sffn.reshape(1, -1)
    turns = []
    slabs_out = []
    for turn in range(CHAIN - 1):
        state_pair, own_logs, cross_logs, state_heads, part, low = chain_attend(
            state_queries, state_pieces, pairs_stack, position ^ turn, out_state_flat
        )
        parts = [part] + sent_around(low)
        if turn == 1:
            own_heads, own_token_logs = attend(tied(queries, part), pair, before)
            parts = tied(parts, own_heads)
        mid_state, state_ffn_in, state_slope, state_active, kept_incoming, part, low = chain_mlp(
            parts, state_incoming, keeps, gain_sffn, up_state, down_state
        )
        parts = [part] + sent_around(low)
        state_mlp, slab, incoming_next, normed_next, queries_next, pair_next, mid_state = chain_start(
            parts, mid_state, keeps, init_slab, flags[turn + 1], gain_state, qkv_state_flat
        )
        slabs_out.append(slab)
        turns.append(
            (
                kept_incoming,
                state_normed,
                state_queries,
                state_pair,
                (own_logs, cross_logs),
                state_heads,
                mid_state,
                state_ffn_in,
                state_slope,
                state_active,
                state_mlp,
            )
        )
        state_incoming, state_normed, state_queries = incoming_next, normed_next, queries_next
        state_pieces = pos_gather(pair_next)
    turns.append((state_incoming, state_normed))
    my_state_pair = jnp.concatenate(state_pieces)
    for turn in range(CHAIN - 1):
        my_state_pair = jnp.where(position == turn, turns[turn][3], my_state_pair)

    cross_heads, cross_token_logs = attend(queries, my_state_pair)
    token_heads = jnp.concatenate([own_heads, cross_heads], axis=1)
    proj_total = tp_scatter(
        [plain_dot(part, out_tok_flat) for part in split_rows(token_heads, n_tp)]
    )
    cotangents = split_rows(tied(cotangent_rows, token_heads), n_tp)
    grad_active = [dot_second(part, down_tok) for part in cotangents]
    mixed_one = layer_one + tied(proj_total, *grad_active)
    ffn_in = tp_gather(layer_norm(mixed_one, norm_ffn).astype(LOW))
    hidden = [plain_dot(part, up_tok) for part in ffn_in]

    grad_hidden = [
        gelu_slope(part, grad).astype(LOW) for part, grad in zip(hidden, grad_active)
    ]
    active = [gelu_exact(part).astype(LOW) for part in hidden]
    grad_ffn_in = tp_scatter([dot_second(part, up_tok) for part in grad_hidden])
    grad_mixed = cotangents[0].astype(HIGH) + norm_back(mixed_one, norm_ffn, grad_ffn_in)
    grad_proj_pieces = tp_gather(grad_mixed.astype(LOW))
    grad_proj = jnp.concatenate(grad_proj_pieces)
    grad_heads = dot_second(grad_proj, out_tok_flat).astype(LOW)
    cross_query_grad, cross_pair_grad = attend_back(
        queries, my_state_pair, cross_token_logs, grad_heads[:, width:]
    )
    cross_pair_grad = split_rows(cross_pair_grad, CHAIN)
    cross_pieces = jnp.stack(
        [cross_pair_grad[0]]
        + [swap(cross_pair_grad[k].astype(LOW), k).astype(HIGH) for k in range(1, CHAIN)]
    )
    homeward = [(s, s - 1) for s in range(lax.axis_size("seq")) if s % CHAIN]

    def own_back():
        query_grad, pair_grad, prev_grad = attend_back(
            queries, pair, own_token_logs, tied(grad_heads[:, :width], cross_pieces), before
        )
        returned = lax.ppermute(prev_grad, "seq", homeward)
        return query_grad + cross_query_grad, pair_grad + returned.astype(HIGH)

    last_incoming = state_incoming
    _, _, _, _, part, low = chain_attend(
        tied(state_queries, grad_heads),
        state_pieces,
        pairs_stack,
        position ^ (CHAIN - 1),
        out_state_flat,
    )
    last_parts = [part] + sent_around(low)

    def last_state(after):
        mid_state, _, _, _, _, part, _ = chain_mlp(
            tied(last_parts, after), last_incoming, keeps, gain_sffn, up_state, down_state
        )
        state_mlp = tp_total(part)
        return (keep_two * mid_state + (1.0 - keep_two) * state_mlp).astype(LOW)

    def states_between(state_slab):
        states_stack = jnp.stack([own_rows(slab) for slab in slabs_out + [state_slab]])
        pieces = [choose(states_stack, position)]
        pieces += [swap(choose(states_stack, position ^ k), k) for k in range(1, CHAIN)]
        pieces = jnp.stack(pieces)
        return jnp.stack([choose(pieces, position ^ q) for q in range(CHAIN)])

    def states_whole(slabs):
        by_tp = turned(jnp.stack(tp_gather(slabs)), (n_tp - tp_index) % n_tp)
        return jnp.transpose(by_tp, (1, 0, 2, 3)).reshape(state_rows, model_width)

    grad_state_qkv, part, low = chain_back_inputs(
        None, [], cross_pieces, position ^ (CHAIN - 1), qkv_state_flat
    )
    parts = [part] + sent_around(low)
    query_grad, pair_grad = own_back()
    token_grads = ScatterSum(
        weight_grads(
            [
                (tied(tuple(ffn_in), query_grad), grad_hidden),
                ([cotangent_rows], active),
                (grad_proj_pieces, [token_heads]),
            ],
            False,
        )
    )
    parts = tied(parts, token_grads.grads)
    kept_qkv, kept_rest = [(state_normed, grad_state_qkv)], []
    token_pair_grads = [None] * CHAIN
    init_grad = jnp.zeros((slab_rows, model_width), HIGH)
    bias_one = bias_two = jnp.zeros((1, model_width), HIGH)
    grad_mid = None
    for turn in reversed(range(CHAIN - 1)):
        next_incoming = turns[turn + 1][0]
        (
            state_incoming,
            state_normed,
            state_queries,
            state_pair,
            logs,
            state_heads,
            mid_state,
            state_ffn_in,
            state_slope,
            state_active,
            state_mlp,
        ) = turns[turn]
        grad_next, grad_state, grad_mlp, grad_state_hidden, sums, part, low = chain_back_mlp(
            parts,
            next_incoming,
            grad_mid,
            flags[turn + 1],
            keeps,
            gain_state,
            mid_state,
            state_mlp,
            state_slope,
            up_state,
            down_state,
        )
        init_grad = init_grad + jnp.where(flags[turn + 1], grad_next, 0.0)
        bias_two = bias_two + sums
        parts = [part] + sent_around(low)
        if turn == 0:
            parts = tied(parts, token_grads.total)
        grad_mid, grad_update, sums, query_total, here, across, sent, token_grad = chain_back_heads(
            parts,
            mid_state,
            gain_sffn,
            keeps,
            grad_state,
            state_incoming,
            out_state_flat,
            state_queries,
            state_pair,
            logs,
            pairs_stack,
            position ^ turn,
        )
        bias_one = bias_one + sums
        token_pair_grads[turn] = token_grad
        kept_rest.append(
            (state_heads, grad_update, state_ffn_in, grad_state_hidden, state_active, grad_mlp)
        )
        beside, there = split_rows(swap(sent, 1), 2)
        across = swap((across + there.astype(HIGH)).astype(LOW), 2)
        if turn == CHAIN - 2:
            last_slab = last_state(grad_mid)
            across = tied(across, last_slab)
        if turn == CHAIN - 3:
            slabs = states_between(tied(last_slab, grad_mid))
            across = tied(across, slabs)
        if turn == CHAIN - 4:
            state_rows_out = states_whole(tied(slabs, grad_mid))
            across = tied(across, state_rows_out)
        grad_state_qkv, part, low = chain_back_inputs(
            query_total, [here, beside, across], cross_pieces, position ^ turn, qkv_state_flat
        )
        kept_qkv.append((state_normed, grad_state_qkv))
        if turn:
            parts = [part] + sent_around(low)

    init_grad = init_grad + jnp.where(flags[0], keep_one * grad_mid, 0.0)
    first_part = norm_back(turns[0][0].astype(HIGH), norm_state, part)
    init_grad = init_grad / n_tp + jnp.where(flags[0], first_part, 0.0)
    bias_one = bias_one[0] * keep_one / n_tp
    bias_two = bias_two[0] * keep_two * (1.0 - keep_two) / n_tp

    token_pair_grads[CHAIN - 1] = jnp.zeros_like(token_pair_grads[0])
    pair_stack = jnp.stack(token_pair_grads)
    pair_grad = pair_grad + pos_scatter([choose(pair_stack, position ^ k) for k in range(CHAIN)])
    layer_output = mixed_one + tp_scatter(
        [plain_dot(part, down_tok) for part in tied(tuple(active), pair_stack)]
    )
    qkv_parts = list(zip(*kept_qkv))
    rest_parts = list(zip(*kept_rest))
    state_grads = ScatterSum(
        weight_grads(
            [
                (qkv_parts[0], qkv_parts[1]),
                (rest_parts[1], rest_parts[0]),
                (rest_parts[2], rest_parts[3]),
                (rest_parts[5], rest_parts[4]),
            ],
            False,
        )
    )
    pair_grad = tied(pair_grad, layer_output, state_grads.grads)
    grad_qkv = jnp.concatenate([query_grad, pair_grad], axis=1).astype(LOW)
    grad_normed = tp_scatter(
        [dot_second(part, qkv_tok_flat) for part in split_rows(grad_qkv, n_tp)]
    )
    grad_layer_one = grad_mixed + norm_back(layer_one, norm_tok, grad_normed)

    grad_win_out = tp_gather(grad_layer_one.astype(LOW))
    grad_win_hidden = [
        gelu_slope(part, dot_second(grad, down_win)).astype(LOW)
        for part, grad in zip(win_hidden, grad_win_out)
    ]
    grad_win_ffn_in = tp_scatter([dot_second(part, up_win) for part in grad_win_hidden])

    middle_grads = SeqSum(
        weight_grads(
            [
                (normed_pieces, [grad_qkv]),
                (win_ffn_in, grad_win_hidden),
                (grad_win_out, win_active),
            ]
        )
    )
    grad_win_ffn_in = tied(grad_win_ffn_in, middle_grads.other)
    grad_win_mixed = grad_layer_one + norm_back(win_mixed, norm_wffn, grad_win_ffn_in)
    grad_win_pieces = tp_gather(grad_win_mixed.astype(LOW))
    middle_halves = middle_grads.cores(grad_win_mixed)
    grad_win_proj = jnp.concatenate(grad_win_pieces)
    grad_win_heads = dot_second(grad_win_proj, out_win).astype(LOW)
    win_query_grad, win_pair_grad, win_prev_grad = attend_back(
        win_queries, win_pair, win_logs, grad_win_heads, win_before
    )
    win_returned = lax.ppermute(win_prev_grad, "seq", homeward)
    win_pair_grad = win_pair_grad + tied(win_returned, state_grads.total).astype(HIGH)
    grad_win_qkv = jnp.concatenate([win_query_grad, win_pair_grad], axis=1).astype(LOW)

    small_rows = jnp.concatenate(
        [init_grad, jnp.stack([bias_one, bias_two]), jnp.zeros((14, model_width), HIGH)]
    ).astype(LOW)
    small_shape = small_rows.shape[0], state_rows + 128
    row_of = lax.broadcasted_iota(jnp.int32, small_shape, 0)
    column_of = lax.broadcasted_iota(jnp.int32, small_shape, 1)
    column_for = jnp.where(
        row_of < slab_rows,
        position * slab_rows + row_of,
        (CHAIN - 1) * slab_rows + row_of,
    )
    selector = (column_of == column_for).astype(LOW)
    last_grads = SeqSum(
        weight_grads(
            [
                ([win_normed], [grad_win_qkv]),
                ([grad_win_proj], [win_heads]),
                ([small_rows], [selector]),
            ]
        )
    )
    last_halves = last_grads.cores(last_grads.other)
    split_at = [half.shape[-1] for half in middle_halves]
    halves = [jnp.concatenate(both, axis=-1) for both in zip(middle_halves, last_halves)]
    one, two = last_grads.across(*halves)
    grad_win_normed = tp_scatter(
        [dot_second(part, qkv_win_flat) for part in split_rows(tied(grad_win_qkv, halves), n_tp)]
    )
    middle_halves = one[:, : split_at[0]], two[:, : split_at[1]]
    last_halves = one[:, split_at[0] :], two[:, split_at[1] :]
    back_input = norm_back(own_input, norm_win, grad_win_normed)
    grad_token_rows = natural(tp_gather((grad_win_mixed + back_input).astype(LOW)))
    output_rows = natural(tp_gather(tied(layer_output.astype(LOW), halves)))

    own_columns = model_width // lax.axis_size("seq")
    inner_width = up_tok.shape[1]
    token_grads.total, state_grads.total = tied(
        (token_grads.total, state_grads.total), halves
    )
    sum_qkv_win = columns_of(last_halves, 0, 3 * width)
    sum_qkv_tok = columns_of(middle_halves, 0, 3 * width)
    sum_qkv_state = state_grads.columns(0, 3 * width)
    sum_up_win = columns_of(middle_halves, 3 * width, inner_width)
    sum_up_tok = token_grads.columns(0, inner_width)
    sum_up_state = state_grads.columns(5 * width, inner_width)
    small_sums = columns_of(last_halves, 4 * width, state_rows + 2)
    first_row = seq_index * own_columns
    vectors = [
        gain_grad(qkv_win_flat, sum_qkv_win, norm_win, first_row),
        gain_grad(up_win, sum_up_win, norm_wffn, first_row),
        gain_grad(qkv_tok_flat, sum_qkv_tok, norm_tok, first_row),
        gain_grad(up_tok, sum_up_tok, norm_ffn, first_row),
        gain_grad(qkv_state_flat, sum_qkv_state, norm_state, first_row),
        gain_grad(up_state, sum_up_state, norm_sffn, first_row),
    ]
    small_sums = sum(
        tp_gather(jnp.concatenate([small_sums] + vectors, axis=1))
    )
    sum_init, vector_sums = small_sums[:, :state_rows].T, small_sums[:, state_rows:]

    def qkv_of(columns):
        return columns.reshape(own_columns, 3, width)

    def out_of(columns):
        return columns.T.reshape(2, width, own_columns)

    return (
        output_rows,
        state_rows_out,
        grad_token_rows,
        vector_sums[:, 2],
        qkv_of(sum_qkv_win),
        columns_of(last_halves, 3 * width, width).T,
        vector_sums[:, 3],
        sum_up_win,
        columns_of(middle_halves, 3 * width + inner_width, inner_width).T,
        vector_sums[:, 4],
        qkv_of(sum_qkv_tok),
        out_of(token_grads.columns(2 * inner_width, 2 * width)),
        vector_sums[:, 5],
        sum_up_tok,
        token_grads.columns(inner_width, inner_width).T,
        vector_sums[:, 6],
        qkv_of(sum_qkv_state),
        out_of(state_grads.columns(3 * width, 2 * width)),
        vector_sums[:, 0:2].T,
        vector_sums[:, 7],
        sum_up_state,
        state_grads.columns(5 * width + inner_width, inner_width).T,
        sum_init,
    )


def solution(mesh):
    placed = (
        P("seq", None),
        P(),
        P(),
        P(None, None, "tp"),
        P("tp", None),
        P(),
        P(None, "tp"),
        P("tp", None),
        P(),
        P(None, None, "tp"),
        P(None, "tp", None),
        P(),
        P(None, "tp"),
        P("tp", None),
        P(),
        P(None, None, "tp"),
        P(None, "tp", None),
        P(),
        P(),
        P(None, "tp"),
        P("tp", None),
        P(),
        P("seq", None),
    )
    return jax.shard_map(
        body,
        mesh=mesh,
        in_specs=placed,
        out_specs=(
            P("seq", None),
            P("seq", None),
            P("seq", None),
            P("seq"),
            P("seq", None, "tp"),
            P("tp", "seq"),
            P("seq"),
            P("seq", "tp"),
            P("tp", "seq"),
            P("seq"),
            P("seq", None, "tp"),
            P(None, "tp", "seq"),
            P("seq"),
            P("seq", "tp"),
            P("tp", "seq"),
            P("seq"),
            P("seq", None, "tp"),
            P(None, "tp", "seq"),
            P(None, "seq"),
            P("seq"),
            P("seq", "tp"),
            P("tp", "seq"),
            P(None, "seq"),
        ),
        check_vma=False,
    )
```

```python
import jax
import jax.numpy as jnp
from jax import lax
from jax.experimental import pallas as pl
from jax.experimental.layout import Layout, with_layout_constraint
from jax.experimental.pallas import tpu as pltpu
from jax.sharding import PartitionSpec as P

E = 128
CHAIN = 4
CORES = 2

EPSILON = 1e-05
MASKED = -1e30
LOW = jnp.bfloat16
HIGH = jnp.float32


def layer_norm(matrix, weights):
    average = jnp.mean(matrix, axis=-1, keepdims=True)
    centred = matrix - average
    spread = jnp.mean(centred * centred, axis=-1, keepdims=True)
    return centred * lax.rsqrt(spread + EPSILON) * weights


def gelu_exact(matrix):
    return jax.nn.gelu(matrix, approximate=False)


def gelu_slope(matrix, grad):
    return jax.vjp(gelu_exact, matrix)[1](grad)[0]


def plain_dot(former, latter):
    return jnp.dot(former, latter, preferred_element_type=HIGH)


def dot_first(former, latter):
    return lax.dot_general(
        former, latter, (((0,), (0,)), ((), ())), preferred_element_type=HIGH
    )


def dot_second(former, latter):
    return lax.dot_general(
        former, latter, (((1,), (1,)), ((), ())), preferred_element_type=HIGH
    )


def row_major(array):
    return with_layout_constraint(array, Layout(major_to_minor=tuple(range(array.ndim))))


def tied(value, *others):
    return lax.optimization_barrier((value, others))[0]


def norm_back(matrix, weights, grad):
    average = jnp.mean(matrix, axis=-1, keepdims=True)
    centred = matrix - average
    spread = jnp.mean(centred * centred, axis=-1, keepdims=True)
    scaled = centred * lax.rsqrt(spread + EPSILON)
    inner = grad * weights
    return lax.rsqrt(spread + EPSILON) * (
        inner
        - jnp.mean(inner, axis=-1, keepdims=True)
        - scaled * jnp.mean(inner * scaled, axis=-1, keepdims=True)
    )


def gain_grad(weights, grads, gain, first):
    rows = lax.dynamic_slice_in_dim(weights, first, grads.shape[0], 0).astype(HIGH)
    gains = lax.dynamic_slice_in_dim(gain.reshape(-1, 1), first, grads.shape[0], 0)
    return jnp.sum(rows * grads, axis=1, keepdims=True) / gains


def tp_from(array, k):
    n = lax.axis_size("tp")
    return lax.ppermute(array, "tp", [((i + k) % n, i) for i in range(n)])


def tp_to(array, k):
    n = lax.axis_size("tp")
    return lax.ppermute(array, "tp", [(i, (i + k) % n) for i in range(n)])


def far_first(n):
    return sorted(range(1, n), key=lambda k: -min(k, n - k))


def tp_gather(piece):
    n = lax.axis_size("tp")
    found = {k: tp_from(piece, k) for k in far_first(n)}
    return [piece] + [found[k] for k in range(1, n)]


def tp_scatter(parts):
    n = lax.axis_size("tp")
    total = parts[0]
    for k in far_first(n):
        total = total + tp_to(parts[k].astype(LOW), k).astype(HIGH)
    return total


def tp_total(part):
    low = part.astype(LOW)
    total = part
    for k in far_first(lax.axis_size("tp")):
        total = total + tp_to(low, k).astype(HIGH)
    return total


def split_rows(matrix, n):
    size = matrix.shape[0] // n
    return [matrix[k * size : (k + 1) * size] for k in range(n)]


def swap(array, k):
    n = lax.axis_size("seq")
    return lax.ppermute(array, "seq", [(s, s ^ k) for s in range(n)])


def pos_gather(piece):
    beside, across = swap(piece, 1), swap(piece, 2)
    return [piece, beside, across, swap(across, 1)]


def pos_scatter(parts):
    low = jnp.concatenate([parts[1], parts[3]]).astype(LOW)
    here, there = split_rows(swap(low, 1), 2)
    across = swap((parts[2] + there.astype(HIGH)).astype(LOW), 2)
    return parts[0] + here.astype(HIGH) + across.astype(HIGH)


def choose(stacked, index):
    return lax.dynamic_index_in_dim(stacked, index, 0, keepdims=False)


def turned(array, start):
    twice = jnp.concatenate([array, array])
    return lax.dynamic_slice_in_dim(twice, start, array.shape[0], 0)


def weight_grads(pairs, split=True):
    n_seq = lax.axis_size("seq")
    depth = pairs[0][0][0].shape[1]
    unit = depth // n_seq
    block = max(256, CORES * unit)
    widths = [latter[0].shape[1] for _, latter in pairs]
    total = sum(widths)
    counts = [(len(former), len(latter)) for former, latter in pairs]
    operands, specs = [], []
    for former, latter in pairs:
        for piece in former:
            operands.append(piece)
            specs.append(pl.BlockSpec((piece.shape[0], block), lambda i: (0, i)))
        for piece in latter:
            operands.append(piece)
            specs.append(pl.BlockSpec(piece.shape, lambda i: (0, 0), pipeline_mode=pl.Buffered(1)))

    def kernel(core_ref, *refs):
        mine_ref, other_ref = refs[-2:]
        first = core_ref[0] == 0

        def keep(product, column):
            columns = slice(column, column + product.shape[1])
            if not split:
                other_ref[:, columns] = product
                return
            for g in range(block // (CORES * unit)):
                low = product[g * CORES * unit : g * CORES * unit + unit]
                high = product[g * CORES * unit + unit : (g + 1) * CORES * unit]
                rows = slice(g * unit, (g + 1) * unit)
                mine_ref[rows, columns] = jnp.where(first, low, high)
                other_ref[rows, columns] = jnp.where(first, high, low)

        at, column = 0, 0
        for (n_former, n_latter), width in zip(counts, widths):
            former = [ref[...] for ref in refs[at : at + n_former]]
            latter = [ref[...] for ref in refs[at + n_former : at + n_former + n_latter]]
            at += n_former + n_latter
            former = jnp.concatenate(former) if n_former > 1 else former[0]
            latter = jnp.concatenate(latter) if n_latter > 1 else latter[0]
            keep(dot_first(former, latter).astype(LOW), column)
            column += width

    shapes = [jax.ShapeDtypeStruct((depth // CORES, total), LOW)] * 2
    out_specs = [pl.BlockSpec((block // CORES, total), lambda i: (i, 0))] * 2
    if not split:
        shapes = [jax.ShapeDtypeStruct((depth, total), LOW)]
        out_specs = [pl.BlockSpec((block, total), lambda i: (i, 0))]
    rows = sum(piece.shape[0] for piece in pairs[0][0])
    core = (lax.axis_index("seq") % CORES).astype(jnp.int32).reshape(1)
    return pl.pallas_call(
        kernel,
        out_shape=shapes,
        grid=(depth // block,),
        in_specs=[pl.BlockSpec(memory_space=pltpu.SMEM)] + specs,
        out_specs=out_specs,
        compiler_params=pltpu.CompilerParams(vmem_limit_bytes=20 * 1024 * 1024),
        cost_estimate=pl.CostEstimate(
            flops=2 * rows * depth * total,
            bytes_accessed=2 * (rows * (depth + total) + depth * total),
            transcendentals=0,
        ),
    )(core, *operands)


class ScatterSum:
    def __init__(self, grads):
        self.grads = grads[0]
        self.total = lax.psum_scatter(self.grads, "seq", scatter_dimension=0, tiled=True)

    def columns(self, at, count):
        return self.total[:, at : at + count].astype(HIGH)


class SeqSum:
    def __init__(self, halves):
        n = lax.axis_size("seq")
        self.z_size = 4 if n % 8 == 0 else n // CORES
        self.x_size = n // (self.z_size * CORES)
        here = lax.axis_index("seq")
        self.z_at = here // CORES % self.z_size
        self.x_at = here // (CORES * self.z_size)
        self.mine, self.other = halves

    def pairs(self, dx, dz):
        def place(x, z, c):
            return (x % self.x_size * self.z_size + z % self.z_size) * CORES + c

        return [
            (place(x, z, c), place(x + dx, z + dz, c))
            for x in range(self.x_size)
            for z in range(self.z_size)
            for c in range(CORES)
        ]

    def over_z(self, array, dim):
        return self.stage(array, dim, self.z_at, self.z_size, lambda k: (0, k))

    def over_x(self, array, dim):
        return self.stage(array, dim, self.x_at, self.x_size, lambda k: (k, 0))

    def stage(self, array, dim, at, size, step):
        total = lax.dynamic_index_in_dim(array, at, dim, False).astype(HIGH)
        for k in far_first(size):
            sent = lax.dynamic_index_in_dim(array, (at + k) % size, dim, False)
            total = total + lax.ppermute(sent, "seq", self.pairs(*step(k))).astype(HIGH)
        return row_major(total)

    def cores(self, after):
        width = self.mine.shape[1]
        sent = swap(tied(self.other, after), 1)
        half = width // 256 * 128

        def total(columns):
            part = self.mine[:, columns].astype(HIGH) + sent[:, columns].astype(HIGH)
            return part.astype(LOW).reshape(self.x_size, self.z_size, -1, part.shape[1])

        return total(slice(0, half)), total(slice(half, width))

    def across(self, one, two):
        return self.over_z(one, 1).astype(LOW), self.over_x(two, 0).astype(LOW)

    def last(self, one, two):
        return self.over_x(one, 0), self.over_z(two, 0)


def columns_of(halves, at, count):
    one, two = halves
    half = one.shape[1]
    if at + count <= half:
        return one[:, at : at + count]
    if at >= half:
        return two[:, at - half : at - half + count]
    return jnp.concatenate([one[:, at:], two[:, : at + count - half]], axis=1)


ATTEND_STEP = 256


class Loaded:
    def __init__(self, source, buffer, semaphore):
        self.buffer, self.copy, self.waiting = buffer, None, True
        self.copy = pltpu.make_async_copy(source, buffer, semaphore)
        self.copy.start()

    def __getitem__(self, index):
        if self.waiting:
            self.copy.wait()
            self.waiting = False
        return self.buffer[index]


class Kept:
    def __init__(self, target, buffer, semaphore):
        self.buffer, self.started = buffer, False
        self.copy = pltpu.make_async_copy(buffer, target, semaphore)

    def __getitem__(self, index):
        return self.buffer[index]

    def __setitem__(self, index, value):
        self.buffer[index] = value
        if index is Ellipsis:
            self.start()

    def start(self):
        self.copy.start()
        self.started = True

    def finish(self):
        if not self.started:
            self.start()
        self.copy.wait()


def fused(kernel, outs, operands, products, scalars=(), exps=0, loaded=(), chosen=None, kept=()):
    in_vmem = pl.BlockSpec(memory_space=pltpu.VMEM)
    in_hbm = pl.BlockSpec(memory_space=pltpu.HBM)
    in_smem = pl.BlockSpec(memory_space=pltpu.SMEM)
    scalars = [jnp.asarray(scalar, jnp.int32).reshape(1) for scalar in scalars]
    loaded = list(loaded) + ([] if chosen is None else [chosen])
    n_scalars, n_in, n_out = len(scalars), len(operands), len(outs)
    scratch = []
    for k in loaded:
        shape = operands[k].shape
        scratch.append(pltpu.VMEM(shape[1:] if k == chosen else shape, operands[k].dtype))
    for k in kept:
        scratch.append(pltpu.VMEM(*outs[k]))
    moved = len(scratch)
    if moved:
        scratch.append(pltpu.SemaphoreType.DMA((moved,)))

    def whole(*refs):
        views = list(refs[: n_scalars + n_in + n_out])
        buffers = refs[n_scalars + n_in + n_out :]
        for spot, k in enumerate(loaded):
            source = views[n_scalars + k]
            if k == chosen:
                source = source.at[views[0][0]]
            views[n_scalars + k] = Loaded(source, buffers[spot], buffers[-1].at[spot])
        for spot, k in enumerate(kept, len(loaded)):
            at = n_scalars + n_in + k
            views[at] = Kept(views[at], buffers[spot], buffers[-1].at[spot])
        kernel(*views)
        for k in kept:
            views[n_scalars + n_in + k].finish()

    return pl.pallas_call(
        whole,
        out_shape=[jax.ShapeDtypeStruct(shape, kind) for shape, kind in outs],
        in_specs=[in_smem] * n_scalars + [in_hbm if k in loaded else in_vmem for k in range(n_in)],
        out_specs=[in_hbm if k in kept else in_vmem for k in range(n_out)],
        scratch_shapes=scratch,
        compiler_params=pltpu.CompilerParams(vmem_limit_bytes=20 * 1024 * 1024),
        cost_estimate=pl.CostEstimate(
            flops=2 * products,
            bytes_accessed=sum(2 * operand.size for operand in operands),
            transcendentals=exps,
        ),
    )(*scalars, *operands)


def score_parts(query, key, before, spot):
    if before is None:
        return dot_second(key, query) * E ** (-0.5), None
    key_before, _, shift, start = before
    shape = key.shape[0], query.shape[0]
    key_ids = (lax.broadcasted_iota(jnp.int32, shape, 0) + shift) % shape[0]
    query_ids = (lax.broadcasted_iota(jnp.int32, shape, 1) + shift + spot) % shape[0]
    below = key_ids <= query_ids
    scores = jnp.where(below, dot_second(key, query), dot_second(key_before, query))
    return jnp.where(below | (start == 0), scores * E ** (-0.5), MASKED), below


def head_attend(query, key, value, before=None, spot=0):
    scores, below = score_parts(query, key, before, spot)
    top = jnp.max(scores, axis=0, keepdims=True)
    powers = jnp.exp(scores - top)
    total = jnp.sum(powers, axis=0, keepdims=True)
    chances = (powers * (1.0 / total)).astype(LOW)
    if before is None:
        result = dot_first(value, chances)
    else:
        none = jnp.zeros_like(chances)
        result = dot_first(value, jnp.where(below, chances, none)) + dot_first(
            before[1], jnp.where(below, none, chances)
        )
    return result.T.astype(LOW), top + jnp.log(total)


def head_back(query, key, value, log, grad, before=None, spot=0):
    scores, below = score_parts(query, key, before, spot)
    chances = jnp.exp(scores - log)
    grad_chances = dot_second(value, grad)
    if before is not None:
        grad_chances = jnp.where(below, grad_chances, dot_second(before[1], grad))
    inner = jnp.sum(chances * grad_chances, axis=0, keepdims=True)
    grad_scores = (chances * (grad_chances - inner) * E ** (-0.5)).astype(LOW)
    chances = chances.astype(LOW)
    if before is None:
        terms = [plain_dot(grad_scores, query), plain_dot(chances, grad)]
        return dot_first(key, grad_scores).T, terms
    none = jnp.zeros_like(chances)
    scores_now = jnp.where(below, grad_scores, none)
    scores_before = jnp.where(below, none, grad_scores)
    terms = [
        plain_dot(scores_now, query),
        plain_dot(jnp.where(below, chances, none), grad),
        plain_dot(scores_before, query),
        plain_dot(jnp.where(below, none, chances), grad),
    ]
    query_grad = dot_first(key, scores_now) + dot_first(before[0], scores_before)
    return query_grad.T, terms


def head_columns(head, width, part):
    return slice(part * width + head * E, part * width + (head + 1) * E)


def attend(queries, pair, before=None):
    count, width = queries.shape
    heads = width // E
    rows = min(count, ATTEND_STEP)
    scalars = [] if before is None else before[1:]
    operands = [queries, pair] + ([] if before is None else [before[0]])

    def kernel(*refs):
        scalar_refs, refs = refs[: len(scalars)], refs[len(scalars) :]
        query_ref, pair_ref = refs[:2]
        result_ref, log_ref = refs[-2:]
        for h in range(heads):
            own = slice(h * E, (h + 1) * E)
            key_at, value_at = head_columns(h, width, 0), head_columns(h, width, 1)
            mask = None
            if before is not None:
                mask = (refs[2][:, key_at], refs[2][:, value_at]) + tuple(
                    ref[0] for ref in scalar_refs
                )
            for spot in range(0, count, rows):
                here = slice(spot, spot + rows)
                result_ref[here, own], log_ref[h : h + 1, here] = head_attend(
                    query_ref[here, own], pair_ref[:, key_at], pair_ref[:, value_at], mask, spot
                )

    scores_count = heads * count * pair.shape[0]
    outs = [((count, width), LOW), ((heads, count), HIGH)]
    products = scores_count * E * len(operands)
    return fused(kernel, outs, operands, products, scalars, scores_count)


def attend_back(queries, pair, logs, grad_result, before=None):
    count, width = queries.shape
    heads = width // E
    rows = min(count, ATTEND_STEP)
    keys = pair.shape[0]
    scalars = [] if before is None else before[1:]
    operands = [queries, logs, grad_result, pair] + ([] if before is None else [before[0]])

    def kernel(*refs):
        scalar_refs, refs = refs[: len(scalars)], refs[len(scalars) :]
        query_ref, log_ref, grad_ref, pair_ref = refs[:4]
        outs = refs[len(operands) :]
        for h in range(heads):
            own = slice(h * E, (h + 1) * E)
            key_at, value_at = head_columns(h, width, 0), head_columns(h, width, 1)
            mask = None
            if before is not None:
                mask = (refs[4][:, key_at], refs[4][:, value_at]) + tuple(
                    ref[0] for ref in scalar_refs
                )
            sums = None
            for spot in range(0, count, rows):
                here = slice(spot, spot + rows)
                outs[0][here, own], terms = head_back(
                    query_ref[here, own],
                    pair_ref[:, key_at],
                    pair_ref[:, value_at],
                    log_ref[h : h + 1, here],
                    grad_ref[here, own],
                    mask,
                    spot,
                )
                sums = terms if sums is None else [one + two for one, two in zip(sums, terms)]
            outs[1][:, key_at], outs[1][:, value_at] = sums[:2]
            if before is not None:
                outs[2][:, key_at], outs[2][:, value_at] = sums[2].astype(LOW), sums[3].astype(LOW)

    outs = [((count, width), HIGH), ((keys, 2 * width), HIGH)]
    if before is not None:
        outs.append(((keys, 2 * width), LOW))
    scores_count = heads * count * keys
    products = scores_count * E * (5 if before is None else 10)
    return fused(kernel, outs, operands, products, scalars, scores_count)


def gelu_of(matrix):
    return 0.5 * matrix * (1.0 + lax.erf(matrix * 0.5**0.5))


def gelu_slope_of(matrix):
    density = jnp.exp(-0.5 * matrix * matrix) * (2.0 * jnp.pi) ** (-0.5)
    return 0.5 * (1.0 + lax.erf(matrix * 0.5**0.5)) + matrix * density


def sent_around(low):
    return [tp_to(low, k) for k in far_first(lax.axis_size("tp"))]


def added(refs):
    total = refs[0][...].astype(HIGH)
    for ref in refs[1:]:
        total = total + ref[...].astype(HIGH)
    return total


def chain_attend(queries, pieces, stack, index, out_flat):
    count, width = queries.shape
    n, keys = len(pieces), stack.shape[1]

    def kernel(index_ref, query_ref, *refs):
        pieces_refs, (stack_ref, out_ref) = refs[:n], refs[n : n + 2]
        pair_ref, own_ref, cross_ref, heads_ref, low_ref = refs[n + 2 :]
        for k, ref in enumerate(pieces_refs):
            pair_ref[k * (keys // n) : (k + 1) * (keys // n), :] = ref[...]
        for h in range(width // E):
            own = slice(h * E, (h + 1) * E)
            key_at, value_at = head_columns(h, width, 0), head_columns(h, width, 1)
            row = slice(h, h + 1)
            heads_ref[:, own], own_ref[row, :] = head_attend(
                query_ref[:, own], pair_ref[:, key_at], pair_ref[:, value_at]
            )
        for h in range(width // E):
            own = slice(h * E, (h + 1) * E)
            key_at, value_at = head_columns(h, width, 0), head_columns(h, width, 1)
            row = slice(h, h + 1)
            heads_ref[:, value_at], cross_ref[row, :] = head_attend(
                query_ref[:, own], stack_ref[:, key_at], stack_ref[:, value_at]
            )
        heads_ref.start()
        low_ref[...] = plain_dot(heads_ref[...], out_ref[...]).astype(LOW)

    depth = out_flat.shape[1]
    logs = ((width // E, count), HIGH)
    outs = [((keys, 2 * width), LOW), logs, logs, ((count, 2 * width), LOW)]
    outs += [((count, depth), LOW)]
    products = count * width * (4 * keys + 2 * depth)
    operands = [queries, *pieces, stack, out_flat]
    exps = 2 * count * keys
    return fused(kernel, outs, operands, products, [index], exps, chosen=n + 1, kept=(3,))


def chain_mlp(parts, incoming, keeps, gain, up, down):
    n = len(parts)

    def kernel(*refs):
        incoming_ref, keep_ref, gain_ref, up_ref, down_ref = refs[n : n + 5]
        mid_ref, normed_ref, slope_ref, active_ref, low_ref = refs[n + 5 :]
        keep = keep_ref[0:1, :]
        mid = keep * incoming_ref[...].astype(HIGH) + (1.0 - keep) * added(refs[:n])
        normed = layer_norm(mid, gain_ref[...]).astype(LOW)
        mid_ref[...], normed_ref[...] = mid, normed
        hidden = plain_dot(normed, up_ref[...])
        active = gelu_of(hidden).astype(LOW)
        slope_ref[...], active_ref[...] = gelu_slope_of(hidden).astype(LOW), active
        low_ref[...] = plain_dot(active, down_ref[...]).astype(LOW)

    count, depth = incoming.shape
    inner = up.shape[1]
    outs = [((count, depth), HIGH), ((count, depth), LOW)]
    outs += [((count, inner), LOW), ((count, inner), LOW), ((count, depth), LOW)]
    operands = [*parts, incoming, keeps, gain, up, down]
    products = 2 * count * depth * inner
    exps = count * inner
    return fused(kernel, outs, operands, products, (), exps, (n,), kept=(0, 1, 2, 3))


def chain_start(parts, mid, keeps, init_slab, flag, gain, qkv_flat):
    n = len(parts)
    width = qkv_flat.shape[1] // 3

    def kernel(flag_ref, *refs):
        mid_ref, keep_ref, init_ref, gain_ref, qkv_ref = refs[n : n + 5]
        mlp_ref, slab_ref, incoming_ref, normed_ref, query_ref, pair_ref = refs[n + 5 :]
        mlp = added(refs[:n])
        keep = keep_ref[1:2, :]
        slab = (keep * mid_ref[...] + (1.0 - keep) * mlp).astype(LOW)
        incoming = jnp.where(flag_ref[0] == 1, init_ref[...], slab)
        mlp_ref[...], slab_ref[...], incoming_ref[...] = mlp.astype(LOW), slab, incoming
        normed = layer_norm(incoming.astype(HIGH), gain_ref[...]).astype(LOW)
        normed_ref[...] = normed
        qkv = plain_dot(normed, qkv_ref[...]).astype(LOW)
        query_ref[...], pair_ref[...] = qkv[:, :width], qkv[:, width:]

    count, depth = mid.shape
    outs = [((count, depth), LOW)] * 4 + [((count, width), LOW), ((count, 2 * width), LOW)]
    operands = [*parts, mid, keeps, init_slab, gain, qkv_flat]
    products = 3 * count * depth * width
    return fused(kernel, outs, operands, products, [flag], 0, (n,), kept=(0, 1, 2, 3))


def chain_back_mlp(parts, incoming, grad_mid, flag, keeps, gain, mid, mlp, slope, up, down):
    n = len(parts)
    operands = [*parts, incoming, keeps, gain, mid, mlp, slope, up, down]
    operands += [] if grad_mid is None else [grad_mid]
    n_ins = len(operands)

    def kernel(flag_ref, *refs):
        incoming_ref, keep_ref, gain_ref, mid_ref, mlp_ref, slope_ref, up_ref, down_ref = refs[
            n : n + 8
        ]
        grad_ref, state_ref, low_mlp_ref, low_hidden_ref, bias_ref, low_ref = refs[n_ins:]
        grad = norm_back(incoming_ref[...].astype(HIGH), gain_ref[...], added(refs[:n]))
        if grad_mid is not None:
            grad = keep_ref[0:1, :] * refs[n + 8][...] + grad
        state = jnp.where(flag_ref[0] == 1, 0.0, grad)
        low_mlp = ((1.0 - keep_ref[1:2, :]) * state).astype(LOW)
        grad_ref[...], state_ref[...], low_mlp_ref[...] = grad, state, low_mlp
        grad_active = dot_second(low_mlp, down_ref[...])
        low_hidden = (slope_ref[...].astype(HIGH) * grad_active).astype(LOW)
        low_hidden_ref[...] = low_hidden
        low_ref[...] = dot_second(low_hidden, up_ref[...]).astype(LOW)
        change = mid_ref[...] - mlp_ref[...].astype(HIGH)
        bias_ref[...] = jnp.sum(state * change, axis=0, keepdims=True)

    count, depth = mid.shape
    inner = up.shape[1]
    outs = [((count, depth), HIGH), ((count, depth), HIGH), ((count, depth), LOW)]
    outs += [((count, inner), LOW), ((1, depth), HIGH), ((count, depth), LOW)]
    loaded = (n, n + 3, n + 4, n + 5) + (() if grad_mid is None else (n + 8,))
    products = 2 * count * depth * inner
    return fused(kernel, outs, operands, products, [flag], loaded=loaded, kept=(0, 1, 2, 3))


def chain_back_heads(
    parts, mid, gain, keeps, grad_state, incoming, out_flat, queries, pair, logs, stack, index
):
    n = len(parts)
    count, width = queries.shape
    keys = pair.shape[0]
    slab = keys // CHAIN

    def kernel(index_ref, *refs):
        mid_ref, gain_ref, keep_ref, state_ref, incoming_ref, out_ref = refs[n : n + 6]
        query_ref, pair_ref, own_log_ref, cross_log_ref, stack_ref = refs[n + 6 : n + 11]
        outs = refs[n + 11 :]
        mid_out, low_out, bias_out, query_out, here_out, across_out, sent_out, token_out = outs
        grad_mid = keep_ref[1:2, :] * state_ref[...] + norm_back(
            mid_ref[...], gain_ref[...], added(refs[:n])
        )
        mid_out[...] = grad_mid
        low = ((1.0 - keep_ref[0:1, :]) * grad_mid).astype(LOW)
        low_out[...] = low
        change = incoming_ref[...].astype(HIGH) - mid_ref[...]
        bias_out[...] = jnp.sum(grad_mid * change, axis=0, keepdims=True)
        grad_heads = dot_second(low, out_ref[...]).astype(LOW)
        for h in range(width // E):
            own = slice(h * E, (h + 1) * E)
            row = slice(h, h + 1)
            own_query, own_terms = head_back(
                query_ref[:, own],
                pair_ref[:, head_columns(h, width, 0)],
                pair_ref[:, head_columns(h, width, 1)],
                own_log_ref[row, :],
                grad_heads[:, own],
            )
            cross_query, cross_terms = head_back(
                query_ref[:, own],
                stack_ref[:, head_columns(h, width, 0)],
                stack_ref[:, head_columns(h, width, 1)],
                cross_log_ref[row, :],
                grad_heads[:, head_columns(h, width, 1)],
            )
            query_out[:, own] = own_query + cross_query
            for part in range(2):
                at = head_columns(h, width, part)
                here_out[:, at] = own_terms[part][:slab]
                across_out[:, at] = own_terms[part][2 * slab : 3 * slab]
                sent_out[:slab, at] = own_terms[part][slab : 2 * slab].astype(LOW)
                sent_out[slab:, at] = own_terms[part][3 * slab :].astype(LOW)
                token_out[:, at] = cross_terms[part]

    depth = mid.shape[1]
    outs = [((count, depth), HIGH), ((count, depth), LOW), ((1, depth), HIGH)]
    outs += [((count, width), HIGH), ((slab, 2 * width), HIGH), ((slab, 2 * width), HIGH)]
    outs += [((2 * slab, 2 * width), LOW), ((keys, 2 * width), HIGH)]
    operands = [*parts, mid, gain, keeps, grad_state, incoming, out_flat]
    operands += [queries, pair, *logs, stack]
    products = count * width * (10 * keys + 2 * depth)
    loaded = (n, n + 3, n + 4, n + 6, n + 7)
    exps = 2 * count * keys
    return fused(kernel, outs, operands, products, [index], exps, loaded, n + 10, (0, 1, 7))


def chain_back_inputs(query_grad, terms, stack, index, qkv_flat):
    rows, depth = stack.shape[1], qkv_flat.shape[0]
    width = qkv_flat.shape[1] // 3
    first = [] if query_grad is None else [query_grad]

    def kernel(index_ref, *refs):
        stack_ref, qkv_ref = refs[len(first) + len(terms) : len(first) + len(terms) + 2]
        grad_ref, low_ref = refs[-2:]
        pair = stack_ref[...]
        for ref in refs[len(first) : len(first) + len(terms)]:
            pair = pair + ref[...].astype(HIGH)
        if first:
            grad_ref[:, :width] = refs[0][...].astype(LOW)
        else:
            grad_ref[:, :width] = jnp.zeros((rows, width), LOW)
        grad_ref[:, width:] = pair.astype(LOW)
        grad_ref.start()
        low_ref[...] = dot_second(grad_ref[...], qkv_ref[...]).astype(LOW)

    outs = [((rows, 3 * width), LOW), ((rows, depth), LOW)]
    operands = [*first, *terms, stack, qkv_flat]
    chosen = len(first) + len(terms)
    products = 3 * rows * depth * width
    return fused(kernel, outs, operands, products, [index], chosen=chosen, kept=(0,))


def body(
    tokens,
    segment_start,
    norm_win,
    qkv_win,
    out_win,
    norm_wffn,
    up_win,
    down_win,
    norm_tok,
    qkv_tok,
    out_tok,
    norm_ffn,
    up_tok,
    down_tok,
    norm_state,
    qkv_state,
    out_state,
    gate_bias,
    norm_sffn,
    up_state,
    down_state,
    init_state,
    cotangent,
):
    seq_index = lax.axis_index("seq")
    tp_index = lax.axis_index("tp")
    n_tp = lax.axis_size("tp")
    position = seq_index % CHAIN
    flags = choose(segment_start, seq_index // CHAIN) == 1
    starts_here = choose(flags, position)
    block_rows, model_width = tokens.shape
    piece_rows = block_rows // n_tp
    state_rows = init_state.shape[0]
    slab_rows = state_rows // CHAIN
    thin_rows = slab_rows // n_tp
    width = qkv_tok.shape[2]
    qkv_win_flat = qkv_win.reshape(model_width, 3 * width)
    out_tok_flat = out_tok.reshape(2 * width, model_width)
    out_state_flat = out_state.reshape(2 * width, model_width)

    shift = (tp_index * piece_rows).astype(jnp.int32)
    start_flag = starts_here.astype(jnp.int32)
    token_rows = turned(tokens, tp_index * piece_rows)

    def natural(pieces):
        whole = jnp.zeros((block_rows, model_width), pieces[0].dtype)
        for k, piece in enumerate(pieces):
            at = (tp_index + k) % n_tp * piece_rows
            whole = lax.dynamic_update_slice_in_dim(whole, piece, at, 0)
        return whole

    input_rows = token_rows.astype(HIGH)
    win_normed = layer_norm(input_rows, norm_win).astype(LOW)
    win_qkv = plain_dot(win_normed, qkv_win_flat).astype(LOW)
    win_queries, win_pair = win_qkv[:, :width], win_qkv[:, width:]
    onward = [(s, s + 1) for s in range(lax.axis_size("seq")) if (s + 1) % CHAIN]
    win_prev = lax.ppermute(win_pair, "seq", onward)
    win_before = win_prev, shift, start_flag
    win_heads, win_logs = attend(win_queries, win_pair, win_before)
    cotangent, qkv_tok, qkv_state, gate_bias, init_state, _ = lax.optimization_barrier(
        (cotangent, qkv_tok, qkv_state, gate_bias, init_state, win_heads)
    )
    qkv_tok_flat = qkv_tok.reshape(model_width, 3 * width)
    qkv_state_flat = qkv_state.reshape(model_width, 3 * width)
    keep_one, keep_two = jax.nn.sigmoid(gate_bias)
    cotangent_rows = turned(cotangent, tp_index * piece_rows)
    own_input = input_rows[:piece_rows]
    win_mixed = own_input + tp_scatter(
        [plain_dot(part, out_win) for part in split_rows(win_heads, n_tp)]
    )
    win_ffn_in = tp_gather(layer_norm(win_mixed, norm_wffn).astype(LOW))
    win_hidden = [plain_dot(part, up_win) for part in win_ffn_in]
    win_active = [gelu_exact(part).astype(LOW) for part in win_hidden]

    init_slab = lax.dynamic_slice_in_dim(init_state, position * slab_rows, slab_rows, 0)

    def own_rows(slab):
        return lax.dynamic_slice_in_dim(slab, tp_index * thin_rows, thin_rows, 0)

    init_late = tied(init_slab, win_ffn_in[1])
    state_incoming = init_late
    state_normed = layer_norm(state_incoming.astype(HIGH), norm_state).astype(LOW)
    state_qkv = plain_dot(state_normed, qkv_state_flat).astype(LOW)
    state_queries = state_qkv[:, :width]
    state_pieces = pos_gather(state_qkv[:, width:])
    layer_one = win_mixed + tp_scatter([plain_dot(part, down_win) for part in win_active])
    layer_one = tied(layer_one, state_pieces)

    normed_pieces = tp_gather(layer_norm(layer_one, norm_tok).astype(LOW))
    normed = jnp.concatenate(normed_pieces)
    token_qkv = plain_dot(normed, qkv_tok_flat).astype(LOW)
    queries, pair = token_qkv[:, :width], token_qkv[:, width:]
    pairs_all = pos_gather(pair)
    pair_prev = jnp.where(position % 2 == 1, pairs_all[1], pairs_all[3])
    pairs_stack = jnp.stack(pairs_all)
    before = pair_prev, shift, start_flag

    keeps = jnp.stack([keep_one, keep_two])
    gain_state, gain_sffn = norm_state.reshape(1, -1), norm_sffn.reshape(1, -1)
    turns = []
    slabs_out = []
    for turn in range(CHAIN - 1):
        state_pair, own_logs, cross_logs, state_heads, low = chain_attend(
            state_queries, state_pieces, pairs_stack, position ^ turn, out_state_flat
        )
        parts = [low] + sent_around(low)
        if turn == 1:
            own_heads, own_token_logs = attend(tied(queries, low), pair, before)
            parts = tied(parts, own_heads)
        mid_state, state_ffn_in, state_slope, state_active, low = chain_mlp(
            parts, state_incoming, keeps, gain_sffn, up_state, down_state
        )
        parts = [low] + sent_around(low)
        state_mlp, slab, incoming_next, normed_next, queries_next, pair_next = chain_start(
            parts, mid_state, keeps, init_slab, flags[turn + 1], gain_state, qkv_state_flat
        )
        slabs_out.append(slab)
        turns.append(
            (
                state_incoming,
                state_normed,
                state_queries,
                state_pair,
                (own_logs, cross_logs),
                state_heads,
                mid_state,
                state_ffn_in,
                state_slope,
                state_active,
                state_mlp,
            )
        )
        state_incoming, state_normed, state_queries = incoming_next, normed_next, queries_next
        state_pieces = pos_gather(pair_next)
    turns.append((state_incoming, state_normed))
    my_state_pair = jnp.concatenate(state_pieces)
    for turn in range(CHAIN - 1):
        my_state_pair = jnp.where(position == turn, turns[turn][3], my_state_pair)

    cross_heads, cross_token_logs = attend(queries, my_state_pair)
    token_heads = jnp.concatenate([own_heads, cross_heads], axis=1)
    proj_total = tp_scatter(
        [plain_dot(part, out_tok_flat) for part in split_rows(token_heads, n_tp)]
    )
    cotangents = split_rows(tied(cotangent_rows, token_heads), n_tp)
    grad_active = [dot_second(part, down_tok) for part in cotangents]
    mixed_one = layer_one + tied(proj_total, *grad_active)
    ffn_in = tp_gather(layer_norm(mixed_one, norm_ffn).astype(LOW))
    hidden = [plain_dot(part, up_tok) for part in ffn_in]

    grad_hidden = [
        gelu_slope(part, grad).astype(LOW) for part, grad in zip(hidden, grad_active)
    ]
    active = [gelu_exact(part).astype(LOW) for part in hidden]
    grad_ffn_in = tp_scatter([dot_second(part, up_tok) for part in grad_hidden])
    grad_mixed = cotangents[0].astype(HIGH) + norm_back(mixed_one, norm_ffn, grad_ffn_in)
    grad_proj_pieces = tp_gather(grad_mixed.astype(LOW))
    grad_proj = jnp.concatenate(grad_proj_pieces)
    grad_heads = dot_second(grad_proj, out_tok_flat).astype(LOW)
    cross_query_grad, cross_pair_grad = attend_back(
        queries, my_state_pair, cross_token_logs, grad_heads[:, width:]
    )
    cross_pair_grad = split_rows(cross_pair_grad, CHAIN)
    cross_pieces = jnp.stack(
        [cross_pair_grad[0]]
        + [swap(cross_pair_grad[k].astype(LOW), k).astype(HIGH) for k in range(1, CHAIN)]
    )
    homeward = [(s, s - 1) for s in range(lax.axis_size("seq")) if s % CHAIN]

    def own_back():
        query_grad, pair_grad, prev_grad = attend_back(
            queries, pair, own_token_logs, tied(grad_heads[:, :width], cross_pieces), before
        )
        returned = lax.ppermute(prev_grad, "seq", homeward)
        return query_grad + cross_query_grad, pair_grad + returned.astype(HIGH)

    last_incoming = state_incoming
    _, _, _, _, low = chain_attend(
        tied(state_queries, grad_heads),
        state_pieces,
        pairs_stack,
        position ^ (CHAIN - 1),
        out_state_flat,
    )
    last_parts = [low] + sent_around(low)

    def last_state(after):
        mid_state, _, _, _, low = chain_mlp(
            tied(last_parts, after), last_incoming, keeps, gain_sffn, up_state, down_state
        )
        state_mlp = low.astype(HIGH)
        for received in sent_around(low):
            state_mlp = state_mlp + received.astype(HIGH)
        return (keep_two * mid_state + (1.0 - keep_two) * state_mlp).astype(LOW)

    def states_between(state_slab):
        states_stack = jnp.stack([own_rows(slab) for slab in slabs_out + [state_slab]])
        pieces = [choose(states_stack, position)]
        pieces += [swap(choose(states_stack, position ^ k), k) for k in range(1, CHAIN)]
        pieces = jnp.stack(pieces)
        return jnp.stack([choose(pieces, position ^ q) for q in range(CHAIN)])

    def states_whole(slabs):
        by_tp = turned(jnp.stack(tp_gather(slabs)), (n_tp - tp_index) % n_tp)
        return jnp.transpose(by_tp, (1, 0, 2, 3)).reshape(state_rows, model_width)

    grad_state_qkv, low = chain_back_inputs(
        None, [], cross_pieces, position ^ (CHAIN - 1), qkv_state_flat
    )
    parts = [low] + sent_around(low)
    query_grad, pair_grad = own_back()
    token_grads = ScatterSum(
        weight_grads(
            [
                (tied(tuple(ffn_in), query_grad), grad_hidden),
                ([cotangent_rows], active),
                (grad_proj_pieces, [token_heads]),
            ],
            False,
        )
    )
    parts = tied(parts, token_grads.grads)
    kept_qkv, kept_rest = [(state_normed, grad_state_qkv)], []
    token_pair_grads = [None] * CHAIN
    init_grad = jnp.zeros((slab_rows, model_width), HIGH)
    bias_one = bias_two = jnp.zeros((1, model_width), HIGH)
    grad_mid = None
    for turn in reversed(range(CHAIN - 1)):
        next_incoming = turns[turn + 1][0]
        (
            state_incoming,
            state_normed,
            state_queries,
            state_pair,
            logs,
            state_heads,
            mid_state,
            state_ffn_in,
            state_slope,
            state_active,
            state_mlp,
        ) = turns[turn]
        grad_next, grad_state, grad_mlp, grad_state_hidden, sums, low = chain_back_mlp(
            parts,
            next_incoming,
            grad_mid,
            flags[turn + 1],
            keeps,
            gain_state,
            mid_state,
            state_mlp,
            state_slope,
            up_state,
            down_state,
        )
        init_grad = init_grad + jnp.where(flags[turn + 1], grad_next, 0.0)
        bias_two = bias_two + sums
        parts = [low] + sent_around(low)
        if turn == 0:
            parts = tied(parts, token_grads.total)
        grad_mid, grad_update, sums, query_total, here, across, sent, token_grad = chain_back_heads(
            parts,
            mid_state,
            gain_sffn,
            keeps,
            grad_state,
            state_incoming,
            out_state_flat,
            state_queries,
            state_pair,
            logs,
            pairs_stack,
            position ^ turn,
        )
        bias_one = bias_one + sums
        token_pair_grads[turn] = token_grad
        kept_rest.append(
            (state_heads, grad_update, state_ffn_in, grad_state_hidden, state_active, grad_mlp)
        )
        beside, there = split_rows(swap(sent, 1), 2)
        across = swap((across + there.astype(HIGH)).astype(LOW), 2)
        if turn == CHAIN - 2:
            last_slab = last_state(grad_mid)
            across = tied(across, last_slab)
        if turn == CHAIN - 3:
            slabs = states_between(tied(last_slab, grad_mid))
            across = tied(across, slabs)
        if turn == CHAIN - 4:
            state_rows_out = states_whole(tied(slabs, grad_mid))
            across = tied(across, state_rows_out)
        grad_state_qkv, low = chain_back_inputs(
            query_total, [here, beside, across], cross_pieces, position ^ turn, qkv_state_flat
        )
        kept_qkv.append((state_normed, grad_state_qkv))
        if turn:
            parts = [low] + sent_around(low)

    init_grad = init_grad + jnp.where(flags[0], keep_one * grad_mid, 0.0)
    first_part = norm_back(turns[0][0].astype(HIGH), norm_state, low.astype(HIGH))
    init_grad = init_grad / n_tp + jnp.where(flags[0], first_part, 0.0)
    bias_one = bias_one[0] * keep_one / n_tp
    bias_two = bias_two[0] * keep_two * (1.0 - keep_two) / n_tp

    token_pair_grads[CHAIN - 1] = jnp.zeros_like(token_pair_grads[0])
    pair_stack = jnp.stack(token_pair_grads)
    pair_grad = pair_grad + pos_scatter([choose(pair_stack, position ^ k) for k in range(CHAIN)])
    layer_output = mixed_one + tp_scatter(
        [plain_dot(part, down_tok) for part in tied(tuple(active), pair_stack)]
    )
    qkv_parts = list(zip(*kept_qkv))
    rest_parts = list(zip(*kept_rest))
    state_grads = ScatterSum(
        weight_grads(
            [
                (qkv_parts[0], qkv_parts[1]),
                (rest_parts[1], rest_parts[0]),
                (rest_parts[2], rest_parts[3]),
                (rest_parts[5], rest_parts[4]),
            ],
            False,
        )
    )
    pair_grad = tied(pair_grad, layer_output, state_grads.grads)
    grad_qkv = jnp.concatenate([query_grad, pair_grad], axis=1).astype(LOW)
    grad_normed = tp_scatter(
        [dot_second(part, qkv_tok_flat) for part in split_rows(grad_qkv, n_tp)]
    )
    grad_layer_one = grad_mixed + norm_back(layer_one, norm_tok, grad_normed)

    grad_win_out = tp_gather(grad_layer_one.astype(LOW))
    grad_win_hidden = [
        gelu_slope(part, dot_second(grad, down_win)).astype(LOW)
        for part, grad in zip(win_hidden, grad_win_out)
    ]
    grad_win_ffn_in = tp_scatter([dot_second(part, up_win) for part in grad_win_hidden])

    middle_grads = SeqSum(
        weight_grads(
            [
                (normed_pieces, [grad_qkv]),
                (win_ffn_in, grad_win_hidden),
                (grad_win_out, win_active),
            ]
        )
    )
    grad_win_ffn_in = tied(grad_win_ffn_in, middle_grads.other)
    grad_win_mixed = grad_layer_one + norm_back(win_mixed, norm_wffn, grad_win_ffn_in)
    grad_win_pieces = tp_gather(grad_win_mixed.astype(LOW))
    middle_halves = middle_grads.cores(grad_win_mixed)
    grad_win_proj = jnp.concatenate(grad_win_pieces)
    grad_win_heads = dot_second(grad_win_proj, out_win).astype(LOW)
    win_query_grad, win_pair_grad, win_prev_grad = attend_back(
        win_queries, win_pair, win_logs, grad_win_heads, win_before
    )
    win_returned = lax.ppermute(win_prev_grad, "seq", homeward)
    win_pair_grad = win_pair_grad + tied(win_returned, state_grads.total).astype(HIGH)
    grad_win_qkv = jnp.concatenate([win_query_grad, win_pair_grad], axis=1).astype(LOW)

    small_rows = jnp.concatenate(
        [init_grad, jnp.stack([bias_one, bias_two]), jnp.zeros((14, model_width), HIGH)]
    ).astype(LOW)
    small_shape = small_rows.shape[0], state_rows + 128
    row_of = lax.broadcasted_iota(jnp.int32, small_shape, 0)
    column_of = lax.broadcasted_iota(jnp.int32, small_shape, 1)
    column_for = jnp.where(
        row_of < slab_rows,
        position * slab_rows + row_of,
        (CHAIN - 1) * slab_rows + row_of,
    )
    selector = (column_of == column_for).astype(LOW)
    last_grads = SeqSum(
        weight_grads(
            [
                ([win_normed], [grad_win_qkv]),
                ([grad_win_proj], [win_heads]),
                ([small_rows], [selector]),
            ]
        )
    )
    last_halves = last_grads.cores(last_grads.other)
    split_at = [half.shape[-1] for half in middle_halves]
    halves = [jnp.concatenate(both, axis=-1) for both in zip(middle_halves, last_halves)]
    parts = [dot_second(part, qkv_win_flat) for part in split_rows(grad_win_qkv, n_tp)]
    grad_win_normed = tp_scatter(parts)
    firsts = last_grads.across(*tied(halves, parts))
    one, two = last_grads.last(*firsts)
    middle_halves = one[:, : split_at[0]], two[:, : split_at[1]]
    last_halves = one[:, split_at[0] :], two[:, split_at[1] :]
    back_input = norm_back(own_input, norm_win, tied(grad_win_normed, firsts))
    grad_token_rows = natural(tp_gather((grad_win_mixed + back_input).astype(LOW)))
    output_rows = natural(tp_gather(tied(layer_output.astype(LOW), grad_win_heads)))

    own_columns = model_width // lax.axis_size("seq")
    inner_width = up_tok.shape[1]
    token_grads.total, state_grads.total = tied(
        (token_grads.total, state_grads.total), firsts
    )
    sum_qkv_win = columns_of(last_halves, 0, 3 * width)
    sum_qkv_tok = columns_of(middle_halves, 0, 3 * width)
    sum_qkv_state = state_grads.columns(0, 3 * width)
    sum_up_win = columns_of(middle_halves, 3 * width, inner_width)
    sum_up_tok = token_grads.columns(0, inner_width)
    sum_up_state = state_grads.columns(5 * width, inner_width)
    small_sums = columns_of(last_halves, 4 * width, state_rows + 2)
    first_row = seq_index * own_columns
    vectors = [
        gain_grad(qkv_win_flat, sum_qkv_win, norm_win, first_row),
        gain_grad(up_win, sum_up_win, norm_wffn, first_row),
        gain_grad(qkv_tok_flat, sum_qkv_tok, norm_tok, first_row),
        gain_grad(up_tok, sum_up_tok, norm_ffn, first_row),
        gain_grad(qkv_state_flat, sum_qkv_state, norm_state, first_row),
        gain_grad(up_state, sum_up_state, norm_sffn, first_row),
    ]
    small_sums = sum(
        tp_gather(jnp.concatenate([small_sums] + vectors, axis=1))
    )
    sum_init, vector_sums = small_sums[:, :state_rows].T, small_sums[:, state_rows:]

    def qkv_of(columns):
        return columns.reshape(own_columns, 3, width)

    def out_of(columns):
        return columns.T.reshape(2, width, own_columns)

    return (
        output_rows,
        state_rows_out,
        grad_token_rows,
        vector_sums[:, 2],
        qkv_of(sum_qkv_win),
        columns_of(last_halves, 3 * width, width).T,
        vector_sums[:, 3],
        sum_up_win,
        columns_of(middle_halves, 3 * width + inner_width, inner_width).T,
        vector_sums[:, 4],
        qkv_of(sum_qkv_tok),
        out_of(token_grads.columns(2 * inner_width, 2 * width)),
        vector_sums[:, 5],
        sum_up_tok,
        token_grads.columns(inner_width, inner_width).T,
        vector_sums[:, 6],
        qkv_of(sum_qkv_state),
        out_of(state_grads.columns(3 * width, 2 * width)),
        vector_sums[:, 0:2].T,
        vector_sums[:, 7],
        sum_up_state,
        state_grads.columns(5 * width + inner_width, inner_width).T,
        sum_init,
    )


def solution(mesh):
    placed = (
        P("seq", None),
        P(),
        P(),
        P(None, None, "tp"),
        P("tp", None),
        P(),
        P(None, "tp"),
        P("tp", None),
        P(),
        P(None, None, "tp"),
        P(None, "tp", None),
        P(),
        P(None, "tp"),
        P("tp", None),
        P(),
        P(None, None, "tp"),
        P(None, "tp", None),
        P(),
        P(),
        P(None, "tp"),
        P("tp", None),
        P(),
        P("seq", None),
    )
    return jax.shard_map(
        body,
        mesh=mesh,
        in_specs=placed,
        out_specs=(
            P("seq", None),
            P("seq", None),
            P("seq", None),
            P("seq"),
            P("seq", None, "tp"),
            P("tp", "seq"),
            P("seq"),
            P("seq", "tp"),
            P("tp", "seq"),
            P("seq"),
            P("seq", None, "tp"),
            P(None, "tp", "seq"),
            P("seq"),
            P("seq", "tp"),
            P("tp", "seq"),
            P("seq"),
            P("seq", None, "tp"),
            P(None, "tp", "seq"),
            P(None, "seq"),
            P("seq"),
            P("seq", "tp"),
            P("tp", "seq"),
            P(None, "seq"),
        ),
        check_vma=False,
    )
```

```python
import jax
import jax.numpy as jnp
from jax import lax
from jax.experimental import pallas as pl
from jax.experimental.layout import Layout, with_layout_constraint
from jax.experimental.pallas import tpu as pltpu
from jax.sharding import PartitionSpec as P

E = 128
CHAIN = 4
CORES = 2

EPSILON = 1e-05
MASKED = -1e30
LOW = jnp.bfloat16
HIGH = jnp.float32


def layer_norm(matrix, weights):
    average = jnp.mean(matrix, axis=-1, keepdims=True)
    centred = matrix - average
    spread = jnp.mean(centred * centred, axis=-1, keepdims=True)
    return centred * lax.rsqrt(spread + EPSILON) * weights


def gelu_exact(matrix):
    return jax.nn.gelu(matrix, approximate=False)


def gelu_slope(matrix, grad):
    return jax.vjp(gelu_exact, matrix)[1](grad)[0]


def plain_dot(former, latter):
    return jnp.dot(former, latter, preferred_element_type=HIGH)


def dot_first(former, latter):
    return lax.dot_general(
        former, latter, (((0,), (0,)), ((), ())), preferred_element_type=HIGH
    )


def dot_second(former, latter):
    return lax.dot_general(
        former, latter, (((1,), (1,)), ((), ())), preferred_element_type=HIGH
    )


def row_major(array):
    return with_layout_constraint(array, Layout(major_to_minor=tuple(range(array.ndim))))


def tied(value, *others):
    return lax.optimization_barrier((value, others))[0]


def norm_back(matrix, weights, grad):
    average = jnp.mean(matrix, axis=-1, keepdims=True)
    centred = matrix - average
    spread = jnp.mean(centred * centred, axis=-1, keepdims=True)
    scaled = centred * lax.rsqrt(spread + EPSILON)
    inner = grad * weights
    return lax.rsqrt(spread + EPSILON) * (
        inner
        - jnp.mean(inner, axis=-1, keepdims=True)
        - scaled * jnp.mean(inner * scaled, axis=-1, keepdims=True)
    )


def gain_grad(weights, grads, gain, first):
    rows = lax.dynamic_slice_in_dim(weights, first, grads.shape[0], 0).astype(HIGH)
    gains = lax.dynamic_slice_in_dim(gain.reshape(-1, 1), first, grads.shape[0], 0)
    return jnp.sum(rows * grads, axis=1, keepdims=True) / gains


def tp_from(array, k):
    n = lax.axis_size("tp")
    return lax.ppermute(array, "tp", [((i + k) % n, i) for i in range(n)])


def tp_to(array, k):
    n = lax.axis_size("tp")
    return lax.ppermute(array, "tp", [(i, (i + k) % n) for i in range(n)])


def far_first(n):
    return sorted(range(1, n), key=lambda k: -min(k, n - k))


def tp_gather(piece):
    n = lax.axis_size("tp")
    found = {k: tp_from(piece, k) for k in far_first(n)}
    return [piece] + [found[k] for k in range(1, n)]


def tp_scatter(parts):
    n = lax.axis_size("tp")
    total = parts[0]
    for k in far_first(n):
        total = total + tp_to(parts[k].astype(LOW), k).astype(HIGH)
    return total


def tp_total(part):
    low = part.astype(LOW)
    total = part
    for k in far_first(lax.axis_size("tp")):
        total = total + tp_to(low, k).astype(HIGH)
    return total


def split_rows(matrix, n):
    size = matrix.shape[0] // n
    return [matrix[k * size : (k + 1) * size] for k in range(n)]


def swap(array, k):
    n = lax.axis_size("seq")
    return lax.ppermute(array, "seq", [(s, s ^ k) for s in range(n)])


def pos_gather(piece):
    beside, across = swap(piece, 1), swap(piece, 2)
    return [piece, beside, across, swap(across, 1)]


def pos_scatter(parts):
    low = jnp.concatenate([parts[1], parts[3]]).astype(LOW)
    here, there = split_rows(swap(low, 1), 2)
    across = swap((parts[2] + there.astype(HIGH)).astype(LOW), 2)
    return parts[0] + here.astype(HIGH) + across.astype(HIGH)


def choose(stacked, index):
    return lax.dynamic_index_in_dim(stacked, index, 0, keepdims=False)


def turned(array, start):
    twice = jnp.concatenate([array, array])
    return lax.dynamic_slice_in_dim(twice, start, array.shape[0], 0)


def weight_grads(pairs, split=True):
    n_seq = lax.axis_size("seq")
    depth = pairs[0][0][0].shape[1]
    unit = depth // n_seq
    block = max(256, CORES * unit)
    widths = [latter[0].shape[1] for _, latter in pairs]
    total = sum(widths)
    counts = [(len(former), len(latter)) for former, latter in pairs]
    operands, specs = [], []
    for former, latter in pairs:
        for piece in former:
            operands.append(piece)
            specs.append(pl.BlockSpec((piece.shape[0], block), lambda i: (0, i)))
        for piece in latter:
            operands.append(piece)
            specs.append(pl.BlockSpec(piece.shape, lambda i: (0, 0), pipeline_mode=pl.Buffered(1)))

    def kernel(core_ref, *refs):
        mine_ref, other_ref = refs[-2:]
        first = core_ref[0] == 0

        def keep(product, column):
            columns = slice(column, column + product.shape[1])
            if not split:
                other_ref[:, columns] = product
                return
            for g in range(block // (CORES * unit)):
                low = product[g * CORES * unit : g * CORES * unit + unit]
                high = product[g * CORES * unit + unit : (g + 1) * CORES * unit]
                rows = slice(g * unit, (g + 1) * unit)
                mine_ref[rows, columns] = jnp.where(first, low, high)
                other_ref[rows, columns] = jnp.where(first, high, low)

        at, column = 0, 0
        for (n_former, n_latter), width in zip(counts, widths):
            former = [ref[...] for ref in refs[at : at + n_former]]
            latter = [ref[...] for ref in refs[at + n_former : at + n_former + n_latter]]
            at += n_former + n_latter
            former = jnp.concatenate(former) if n_former > 1 else former[0]
            latter = jnp.concatenate(latter) if n_latter > 1 else latter[0]
            keep(dot_first(former, latter).astype(LOW), column)
            column += width

    shapes = [jax.ShapeDtypeStruct((depth // CORES, total), LOW)] * 2
    out_specs = [pl.BlockSpec((block // CORES, total), lambda i: (i, 0))] * 2
    if not split:
        shapes = [jax.ShapeDtypeStruct((depth, total), LOW)]
        out_specs = [pl.BlockSpec((block, total), lambda i: (i, 0))]
    rows = sum(piece.shape[0] for piece in pairs[0][0])
    core = (lax.axis_index("seq") % CORES).astype(jnp.int32).reshape(1)
    return pl.pallas_call(
        kernel,
        out_shape=shapes,
        grid=(depth // block,),
        in_specs=[pl.BlockSpec(memory_space=pltpu.SMEM)] + specs,
        out_specs=out_specs,
        compiler_params=pltpu.CompilerParams(vmem_limit_bytes=20 * 1024 * 1024),
        cost_estimate=pl.CostEstimate(
            flops=2 * rows * depth * total,
            bytes_accessed=2 * (rows * (depth + total) + depth * total),
            transcendentals=0,
        ),
    )(core, *operands)


class ScatterSum:
    def __init__(self, grads):
        self.grads = grads[0]
        self.total = lax.psum_scatter(self.grads, "seq", scatter_dimension=0, tiled=True)

    def columns(self, at, count):
        return self.total[:, at : at + count].astype(HIGH)


class SeqSum:
    def __init__(self, halves):
        n = lax.axis_size("seq")
        self.z_size = 4 if n % 8 == 0 else n // CORES
        self.x_size = n // (self.z_size * CORES)
        here = lax.axis_index("seq")
        self.z_at = here // CORES % self.z_size
        self.x_at = here // (CORES * self.z_size)
        self.mine, self.other = halves

    def pairs(self, dx, dz):
        def place(x, z, c):
            return (x % self.x_size * self.z_size + z % self.z_size) * CORES + c

        return [
            (place(x, z, c), place(x + dx, z + dz, c))
            for x in range(self.x_size)
            for z in range(self.z_size)
            for c in range(CORES)
        ]

    def over_z(self, array, dim):
        return self.stage(array, dim, self.z_at, self.z_size, lambda k: (0, k))

    def over_x(self, array, dim):
        return self.stage(array, dim, self.x_at, self.x_size, lambda k: (k, 0))

    def stage(self, array, dim, at, size, step):
        total = lax.dynamic_index_in_dim(array, at, dim, False).astype(HIGH)
        for k in far_first(size):
            sent = lax.dynamic_index_in_dim(array, (at + k) % size, dim, False)
            total = total + lax.ppermute(sent, "seq", self.pairs(*step(k))).astype(HIGH)
        return row_major(total)

    def cores(self, after):
        width = self.mine.shape[1]
        sent = swap(tied(self.other, after), 1)
        half = width // 256 * 128

        def total(columns):
            part = self.mine[:, columns].astype(HIGH) + sent[:, columns].astype(HIGH)
            return part.astype(LOW).reshape(self.x_size, self.z_size, -1, part.shape[1])

        return total(slice(0, half)), total(slice(half, width))

    def across(self, one, two):
        return self.over_z(one, 1).astype(LOW), self.over_x(two, 0).astype(LOW)

    def last(self, one, two):
        return self.over_x(one, 0), self.over_z(two, 0)


def columns_of(halves, at, count):
    one, two = halves
    half = one.shape[1]
    if at + count <= half:
        return one[:, at : at + count]
    if at >= half:
        return two[:, at - half : at - half + count]
    return jnp.concatenate([one[:, at:], two[:, : at + count - half]], axis=1)


ATTEND_STEP = 256


class Loaded:
    def __init__(self, source, buffer, semaphore):
        self.buffer, self.copy, self.waiting = buffer, None, True
        self.copy = pltpu.make_async_copy(source, buffer, semaphore)
        self.copy.start()

    def __getitem__(self, index):
        if self.waiting:
            self.copy.wait()
            self.waiting = False
        return self.buffer[index]


class Kept:
    def __init__(self, target, buffer, semaphore):
        self.buffer, self.started = buffer, False
        self.copy = pltpu.make_async_copy(buffer, target, semaphore)

    def __getitem__(self, index):
        return self.buffer[index]

    def __setitem__(self, index, value):
        self.buffer[index] = value
        if index is Ellipsis:
            self.start()

    def start(self):
        self.copy.start()
        self.started = True

    def finish(self):
        if not self.started:
            self.start()
        self.copy.wait()


def fused(kernel, outs, operands, products, scalars=(), exps=0, loaded=(), chosen=None, kept=()):
    in_vmem = pl.BlockSpec(memory_space=pltpu.VMEM)
    in_hbm = pl.BlockSpec(memory_space=pltpu.HBM)
    in_smem = pl.BlockSpec(memory_space=pltpu.SMEM)
    scalars = [jnp.asarray(scalar, jnp.int32).reshape(1) for scalar in scalars]
    loaded = list(loaded) + ([] if chosen is None else [chosen])
    n_scalars, n_in, n_out = len(scalars), len(operands), len(outs)
    scratch = []
    for k in loaded:
        shape = operands[k].shape
        scratch.append(pltpu.VMEM(shape[1:] if k == chosen else shape, operands[k].dtype))
    for k in kept:
        scratch.append(pltpu.VMEM(*outs[k]))
    moved = len(scratch)
    if moved:
        scratch.append(pltpu.SemaphoreType.DMA((moved,)))

    def whole(*refs):
        views = list(refs[: n_scalars + n_in + n_out])
        buffers = refs[n_scalars + n_in + n_out :]
        for spot, k in enumerate(loaded):
            source = views[n_scalars + k]
            if k == chosen:
                source = source.at[views[0][0]]
            views[n_scalars + k] = Loaded(source, buffers[spot], buffers[-1].at[spot])
        for spot, k in enumerate(kept, len(loaded)):
            at = n_scalars + n_in + k
            views[at] = Kept(views[at], buffers[spot], buffers[-1].at[spot])
        kernel(*views)
        for k in kept:
            views[n_scalars + n_in + k].finish()

    return pl.pallas_call(
        whole,
        out_shape=[jax.ShapeDtypeStruct(shape, kind) for shape, kind in outs],
        in_specs=[in_smem] * n_scalars + [in_hbm if k in loaded else in_vmem for k in range(n_in)],
        out_specs=[in_hbm if k in kept else in_vmem for k in range(n_out)],
        scratch_shapes=scratch,
        compiler_params=pltpu.CompilerParams(vmem_limit_bytes=20 * 1024 * 1024),
        cost_estimate=pl.CostEstimate(
            flops=2 * products,
            bytes_accessed=sum(2 * operand.size for operand in operands),
            transcendentals=exps,
        ),
    )(*scalars, *operands)


def score_parts(query, key, before, spot):
    if before is None:
        return dot_second(key, query) * E ** (-0.5), None
    key_before, _, shift, start = before
    shape = key.shape[0], query.shape[0]
    key_ids = (lax.broadcasted_iota(jnp.int32, shape, 0) + shift) % shape[0]
    query_ids = (lax.broadcasted_iota(jnp.int32, shape, 1) + shift + spot) % shape[0]
    below = key_ids <= query_ids
    scores = jnp.where(below, dot_second(key, query), dot_second(key_before, query))
    return jnp.where(below | (start == 0), scores * E ** (-0.5), MASKED), below


def head_attend(query, key, value, before=None, spot=0):
    scores, below = score_parts(query, key, before, spot)
    top = jnp.max(scores, axis=0, keepdims=True)
    powers = jnp.exp(scores - top)
    total = jnp.sum(powers, axis=0, keepdims=True)
    chances = (powers * (1.0 / total)).astype(LOW)
    if before is None:
        result = dot_first(value, chances)
    else:
        none = jnp.zeros_like(chances)
        result = dot_first(value, jnp.where(below, chances, none)) + dot_first(
            before[1], jnp.where(below, none, chances)
        )
    return result.T.astype(LOW), top + jnp.log(total)


def head_back(query, key, value, log, grad, before=None, spot=0):
    scores, below = score_parts(query, key, before, spot)
    chances = jnp.exp(scores - log)
    grad_chances = dot_second(value, grad)
    if before is not None:
        grad_chances = jnp.where(below, grad_chances, dot_second(before[1], grad))
    inner = jnp.sum(chances * grad_chances, axis=0, keepdims=True)
    grad_scores = (chances * (grad_chances - inner) * E ** (-0.5)).astype(LOW)
    chances = chances.astype(LOW)
    if before is None:
        terms = [plain_dot(grad_scores, query), plain_dot(chances, grad)]
        return dot_first(key, grad_scores).T, terms
    none = jnp.zeros_like(chances)
    scores_now = jnp.where(below, grad_scores, none)
    scores_before = jnp.where(below, none, grad_scores)
    terms = [
        plain_dot(scores_now, query),
        plain_dot(jnp.where(below, chances, none), grad),
        plain_dot(scores_before, query),
        plain_dot(jnp.where(below, none, chances), grad),
    ]
    query_grad = dot_first(key, scores_now) + dot_first(before[0], scores_before)
    return query_grad.T, terms


def head_columns(head, width, part):
    return slice(part * width + head * E, part * width + (head + 1) * E)


def attend(queries, pair, before=None):
    count, width = queries.shape
    heads = width // E
    rows = min(count, ATTEND_STEP)
    scalars = [] if before is None else before[1:]
    operands = [queries, pair] + ([] if before is None else [before[0]])

    def kernel(*refs):
        scalar_refs, refs = refs[: len(scalars)], refs[len(scalars) :]
        query_ref, pair_ref = refs[:2]
        result_ref, log_ref = refs[-2:]
        for h in range(heads):
            own = slice(h * E, (h + 1) * E)
            key_at, value_at = head_columns(h, width, 0), head_columns(h, width, 1)
            mask = None
            if before is not None:
                mask = (refs[2][:, key_at], refs[2][:, value_at]) + tuple(
                    ref[0] for ref in scalar_refs
                )
            for spot in range(0, count, rows):
                here = slice(spot, spot + rows)
                result_ref[here, own], log_ref[h : h + 1, here] = head_attend(
                    query_ref[here, own], pair_ref[:, key_at], pair_ref[:, value_at], mask, spot
                )

    scores_count = heads * count * pair.shape[0]
    outs = [((count, width), LOW), ((heads, count), HIGH)]
    products = scores_count * E * len(operands)
    return fused(kernel, outs, operands, products, scalars, scores_count)


def attend_back(queries, pair, logs, grad_result, before=None):
    count, width = queries.shape
    heads = width // E
    rows = min(count, ATTEND_STEP)
    keys = pair.shape[0]
    scalars = [] if before is None else before[1:]
    operands = [queries, logs, grad_result, pair] + ([] if before is None else [before[0]])

    def kernel(*refs):
        scalar_refs, refs = refs[: len(scalars)], refs[len(scalars) :]
        query_ref, log_ref, grad_ref, pair_ref = refs[:4]
        outs = refs[len(operands) :]
        for h in range(heads):
            own = slice(h * E, (h + 1) * E)
            key_at, value_at = head_columns(h, width, 0), head_columns(h, width, 1)
            mask = None
            if before is not None:
                mask = (refs[4][:, key_at], refs[4][:, value_at]) + tuple(
                    ref[0] for ref in scalar_refs
                )
            sums = None
            for spot in range(0, count, rows):
                here = slice(spot, spot + rows)
                outs[0][here, own], terms = head_back(
                    query_ref[here, own],
                    pair_ref[:, key_at],
                    pair_ref[:, value_at],
                    log_ref[h : h + 1, here],
                    grad_ref[here, own],
                    mask,
                    spot,
                )
                sums = terms if sums is None else [one + two for one, two in zip(sums, terms)]
            outs[1][:, key_at], outs[1][:, value_at] = sums[:2]
            if before is not None:
                outs[2][:, key_at], outs[2][:, value_at] = sums[2].astype(LOW), sums[3].astype(LOW)

    outs = [((count, width), HIGH), ((keys, 2 * width), HIGH)]
    if before is not None:
        outs.append(((keys, 2 * width), LOW))
    scores_count = heads * count * keys
    products = scores_count * E * (5 if before is None else 10)
    return fused(kernel, outs, operands, products, scalars, scores_count)


def gelu_of(matrix):
    return 0.5 * matrix * (1.0 + lax.erf(matrix * 0.5**0.5))


def gelu_slope_of(matrix):
    density = jnp.exp(-0.5 * matrix * matrix) * (2.0 * jnp.pi) ** (-0.5)
    return 0.5 * (1.0 + lax.erf(matrix * 0.5**0.5)) + matrix * density


def sent_around(low):
    return [tp_to(low, k) for k in far_first(lax.axis_size("tp"))]


def added(refs):
    total = refs[0][...].astype(HIGH)
    for ref in refs[1:]:
        total = total + ref[...].astype(HIGH)
    return total


def chain_attend(queries, pieces, stack, index, out_flat):
    count, width = queries.shape
    n, keys = len(pieces), stack.shape[1]

    def kernel(index_ref, query_ref, *refs):
        pieces_refs, (stack_ref, out_ref) = refs[:n], refs[n : n + 2]
        pair_ref, own_ref, cross_ref, heads_ref, low_ref = refs[n + 2 :]
        for k, ref in enumerate(pieces_refs):
            pair_ref[k * (keys // n) : (k + 1) * (keys // n), :] = ref[...]
        for h in range(width // E):
            own = slice(h * E, (h + 1) * E)
            key_at, value_at = head_columns(h, width, 0), head_columns(h, width, 1)
            row = slice(h, h + 1)
            heads_ref[:, own], own_ref[row, :] = head_attend(
                query_ref[:, own], pair_ref[:, key_at], pair_ref[:, value_at]
            )
        for h in range(width // E):
            own = slice(h * E, (h + 1) * E)
            key_at, value_at = head_columns(h, width, 0), head_columns(h, width, 1)
            row = slice(h, h + 1)
            heads_ref[:, value_at], cross_ref[row, :] = head_attend(
                query_ref[:, own], stack_ref[:, key_at], stack_ref[:, value_at]
            )
        heads_ref.start()
        low_ref[...] = plain_dot(heads_ref[...], out_ref[...]).astype(LOW)

    depth = out_flat.shape[1]
    logs = ((width // E, count), HIGH)
    outs = [((keys, 2 * width), LOW), logs, logs, ((count, 2 * width), LOW)]
    outs += [((count, depth), LOW)]
    products = count * width * (4 * keys + 2 * depth)
    operands = [queries, *pieces, stack, out_flat]
    exps = 2 * count * keys
    return fused(kernel, outs, operands, products, [index], exps, chosen=n + 1, kept=(3,))


def chain_mlp(parts, incoming, keeps, gain, up, down):
    n = len(parts)

    def kernel(*refs):
        incoming_ref, keep_ref, gain_ref, up_ref, down_ref = refs[n : n + 5]
        mid_ref, normed_ref, slope_ref, active_ref, low_ref = refs[n + 5 :]
        keep = keep_ref[0:1, :]
        mid = keep * incoming_ref[...].astype(HIGH) + (1.0 - keep) * added(refs[:n])
        normed = layer_norm(mid, gain_ref[...]).astype(LOW)
        mid_ref[...], normed_ref[...] = mid, normed
        hidden = plain_dot(normed, up_ref[...])
        active = gelu_of(hidden).astype(LOW)
        slope_ref[...], active_ref[...] = gelu_slope_of(hidden).astype(LOW), active
        low_ref[...] = plain_dot(active, down_ref[...]).astype(LOW)

    count, depth = incoming.shape
    inner = up.shape[1]
    outs = [((count, depth), HIGH), ((count, depth), LOW)]
    outs += [((count, inner), LOW), ((count, inner), LOW), ((count, depth), LOW)]
    operands = [*parts, incoming, keeps, gain, up, down]
    products = 2 * count * depth * inner
    exps = count * inner
    return fused(kernel, outs, operands, products, (), exps, (n,), kept=(0, 1, 2, 3))


def chain_start(parts, mid, keeps, init_slab, flag, gain, qkv_flat):
    n = len(parts)
    width = qkv_flat.shape[1] // 3

    def kernel(flag_ref, *refs):
        mid_ref, keep_ref, init_ref, gain_ref, qkv_ref = refs[n : n + 5]
        mlp_ref, slab_ref, incoming_ref, normed_ref, query_ref, pair_ref = refs[n + 5 :]
        mlp = added(refs[:n])
        keep = keep_ref[1:2, :]
        slab = (keep * mid_ref[...] + (1.0 - keep) * mlp).astype(LOW)
        incoming = jnp.where(flag_ref[0] == 1, init_ref[...], slab)
        mlp_ref[...], slab_ref[...], incoming_ref[...] = mlp.astype(LOW), slab, incoming
        normed = layer_norm(incoming.astype(HIGH), gain_ref[...]).astype(LOW)
        normed_ref[...] = normed
        qkv = plain_dot(normed, qkv_ref[...]).astype(LOW)
        query_ref[...], pair_ref[...] = qkv[:, :width], qkv[:, width:]

    count, depth = mid.shape
    outs = [((count, depth), LOW)] * 4 + [((count, width), LOW), ((count, 2 * width), LOW)]
    operands = [*parts, mid, keeps, init_slab, gain, qkv_flat]
    products = 3 * count * depth * width
    return fused(kernel, outs, operands, products, [flag], 0, (n,), kept=(0, 1, 2, 3))


def chain_back_mlp(parts, incoming, grad_mid, flag, keeps, gain, mid, mlp, slope, up, down):
    n = len(parts)
    operands = [*parts, incoming, keeps, gain, mid, mlp, slope, up, down]
    operands += [] if grad_mid is None else [grad_mid]
    n_ins = len(operands)

    def kernel(flag_ref, *refs):
        incoming_ref, keep_ref, gain_ref, mid_ref, mlp_ref, slope_ref, up_ref, down_ref = refs[
            n : n + 8
        ]
        grad_ref, state_ref, low_mlp_ref, low_hidden_ref, bias_ref, low_ref = refs[n_ins:]
        grad = norm_back(incoming_ref[...].astype(HIGH), gain_ref[...], added(refs[:n]))
        if grad_mid is not None:
            grad = keep_ref[0:1, :] * refs[n + 8][...] + grad
        state = jnp.where(flag_ref[0] == 1, 0.0, grad)
        low_mlp = ((1.0 - keep_ref[1:2, :]) * state).astype(LOW)
        grad_ref[...], state_ref[...], low_mlp_ref[...] = grad, state, low_mlp
        grad_active = dot_second(low_mlp, down_ref[...])
        low_hidden = (slope_ref[...].astype(HIGH) * grad_active).astype(LOW)
        low_hidden_ref[...] = low_hidden
        low_ref[...] = dot_second(low_hidden, up_ref[...]).astype(LOW)
        change = mid_ref[...] - mlp_ref[...].astype(HIGH)
        bias_ref[...] = jnp.sum(state * change, axis=0, keepdims=True)

    count, depth = mid.shape
    inner = up.shape[1]
    outs = [((count, depth), HIGH), ((count, depth), HIGH), ((count, depth), LOW)]
    outs += [((count, inner), LOW), ((1, depth), HIGH), ((count, depth), LOW)]
    loaded = (n, n + 3, n + 4, n + 5) + (() if grad_mid is None else (n + 8,))
    products = 2 * count * depth * inner
    return fused(kernel, outs, operands, products, [flag], loaded=loaded, kept=(0, 1, 2, 3))


def chain_back_heads(
    parts, mid, gain, keeps, grad_state, incoming, out_flat, queries, pair, logs, stack, index
):
    n = len(parts)
    count, width = queries.shape
    keys = pair.shape[0]
    slab = keys // CHAIN

    def kernel(index_ref, *refs):
        mid_ref, gain_ref, keep_ref, state_ref, incoming_ref, out_ref = refs[n : n + 6]
        query_ref, pair_ref, own_log_ref, cross_log_ref, stack_ref = refs[n + 6 : n + 11]
        outs = refs[n + 11 :]
        mid_out, low_out, bias_out, query_out, here_out, across_out, sent_out, token_out = outs
        grad_mid = keep_ref[1:2, :] * state_ref[...] + norm_back(
            mid_ref[...], gain_ref[...], added(refs[:n])
        )
        mid_out[...] = grad_mid
        low = ((1.0 - keep_ref[0:1, :]) * grad_mid).astype(LOW)
        low_out[...] = low
        change = incoming_ref[...].astype(HIGH) - mid_ref[...]
        bias_out[...] = jnp.sum(grad_mid * change, axis=0, keepdims=True)
        grad_heads = dot_second(low, out_ref[...]).astype(LOW)
        for h in range(width // E):
            own = slice(h * E, (h + 1) * E)
            row = slice(h, h + 1)
            own_query, own_terms = head_back(
                query_ref[:, own],
                pair_ref[:, head_columns(h, width, 0)],
                pair_ref[:, head_columns(h, width, 1)],
                own_log_ref[row, :],
                grad_heads[:, own],
            )
            cross_query, cross_terms = head_back(
                query_ref[:, own],
                stack_ref[:, head_columns(h, width, 0)],
                stack_ref[:, head_columns(h, width, 1)],
                cross_log_ref[row, :],
                grad_heads[:, head_columns(h, width, 1)],
            )
            query_out[:, own] = own_query + cross_query
            for part in range(2):
                at = head_columns(h, width, part)
                here_out[:, at] = own_terms[part][:slab]
                across_out[:, at] = own_terms[part][2 * slab : 3 * slab]
                sent_out[:slab, at] = own_terms[part][slab : 2 * slab].astype(LOW)
                sent_out[slab:, at] = own_terms[part][3 * slab :].astype(LOW)
                token_out[:, at] = cross_terms[part]

    depth = mid.shape[1]
    outs = [((count, depth), HIGH), ((count, depth), LOW), ((1, depth), HIGH)]
    outs += [((count, width), HIGH), ((slab, 2 * width), HIGH), ((slab, 2 * width), HIGH)]
    outs += [((2 * slab, 2 * width), LOW), ((keys, 2 * width), HIGH)]
    operands = [*parts, mid, gain, keeps, grad_state, incoming, out_flat]
    operands += [queries, pair, *logs, stack]
    products = count * width * (10 * keys + 2 * depth)
    loaded = (n, n + 3, n + 4, n + 6, n + 7)
    exps = 2 * count * keys
    return fused(kernel, outs, operands, products, [index], exps, loaded, n + 10, (0, 1, 7))


def chain_back_inputs(query_grad, terms, stack, index, qkv_flat):
    rows, depth = stack.shape[1], qkv_flat.shape[0]
    width = qkv_flat.shape[1] // 3
    first = [] if query_grad is None else [query_grad]

    def kernel(index_ref, *refs):
        stack_ref, qkv_ref = refs[len(first) + len(terms) : len(first) + len(terms) + 2]
        grad_ref, low_ref = refs[-2:]
        pair = stack_ref[...]
        for ref in refs[len(first) : len(first) + len(terms)]:
            pair = pair + ref[...].astype(HIGH)
        if first:
            grad_ref[:, :width] = refs[0][...].astype(LOW)
        else:
            grad_ref[:, :width] = jnp.zeros((rows, width), LOW)
        grad_ref[:, width:] = pair.astype(LOW)
        grad_ref.start()
        low_ref[...] = dot_second(grad_ref[...], qkv_ref[...]).astype(LOW)

    outs = [((rows, 3 * width), LOW), ((rows, depth), LOW)]
    operands = [*first, *terms, stack, qkv_flat]
    chosen = len(first) + len(terms)
    products = 3 * rows * depth * width
    return fused(kernel, outs, operands, products, [index], chosen=chosen, kept=(0,))


def body(
    tokens,
    segment_start,
    norm_win,
    qkv_win,
    out_win,
    norm_wffn,
    up_win,
    down_win,
    norm_tok,
    qkv_tok,
    out_tok,
    norm_ffn,
    up_tok,
    down_tok,
    norm_state,
    qkv_state,
    out_state,
    gate_bias,
    norm_sffn,
    up_state,
    down_state,
    init_state,
    cotangent,
):
    seq_index = lax.axis_index("seq")
    tp_index = lax.axis_index("tp")
    n_tp = lax.axis_size("tp")
    position = seq_index % CHAIN
    flags = choose(segment_start, seq_index // CHAIN) == 1
    starts_here = choose(flags, position)
    block_rows, model_width = tokens.shape
    piece_rows = block_rows // n_tp
    state_rows = init_state.shape[0]
    slab_rows = state_rows // CHAIN
    thin_rows = slab_rows // n_tp
    width = qkv_tok.shape[2]
    qkv_win_flat = qkv_win.reshape(model_width, 3 * width)
    out_tok_flat = out_tok.reshape(2 * width, model_width)
    out_state_flat = out_state.reshape(2 * width, model_width)

    shift = (tp_index * piece_rows).astype(jnp.int32)
    start_flag = starts_here.astype(jnp.int32)
    token_rows = turned(tokens, tp_index * piece_rows)

    def natural(pieces):
        whole = jnp.zeros((block_rows, model_width), pieces[0].dtype)
        for k, piece in enumerate(pieces):
            at = (tp_index + k) % n_tp * piece_rows
            whole = lax.dynamic_update_slice_in_dim(whole, piece, at, 0)
        return whole

    input_rows = token_rows.astype(HIGH)
    win_normed = layer_norm(input_rows, norm_win).astype(LOW)
    win_qkv = plain_dot(win_normed, qkv_win_flat).astype(LOW)
    win_queries, win_pair = win_qkv[:, :width], win_qkv[:, width:]
    onward = [(s, s + 1) for s in range(lax.axis_size("seq")) if (s + 1) % CHAIN]
    win_prev = lax.ppermute(win_pair, "seq", onward)
    win_before = win_prev, shift, start_flag
    win_heads, win_logs = attend(win_queries, win_pair, win_before)
    cotangent, qkv_tok, qkv_state, gate_bias, init_state, _ = lax.optimization_barrier(
        (cotangent, qkv_tok, qkv_state, gate_bias, init_state, win_heads)
    )
    qkv_tok_flat = qkv_tok.reshape(model_width, 3 * width)
    qkv_state_flat = qkv_state.reshape(model_width, 3 * width)
    keep_one, keep_two = jax.nn.sigmoid(gate_bias)
    cotangent_rows = turned(cotangent, tp_index * piece_rows)
    own_input = input_rows[:piece_rows]
    win_mixed = own_input + tp_scatter(
        [plain_dot(part, out_win) for part in split_rows(win_heads, n_tp)]
    )
    win_ffn_in = tp_gather(layer_norm(win_mixed, norm_wffn).astype(LOW))
    win_hidden = [plain_dot(part, up_win) for part in win_ffn_in]
    win_active = [gelu_exact(part).astype(LOW) for part in win_hidden]

    init_slab = lax.dynamic_slice_in_dim(init_state, position * slab_rows, slab_rows, 0)

    def own_rows(slab):
        return lax.dynamic_slice_in_dim(slab, tp_index * thin_rows, thin_rows, 0)

    init_late = tied(init_slab, win_ffn_in[1])
    state_incoming = init_late
    state_normed = layer_norm(state_incoming.astype(HIGH), norm_state).astype(LOW)
    state_qkv = plain_dot(state_normed, qkv_state_flat).astype(LOW)
    state_queries = state_qkv[:, :width]
    state_pieces = pos_gather(state_qkv[:, width:])
    layer_one = win_mixed + tp_scatter([plain_dot(part, down_win) for part in win_active])
    layer_one = tied(layer_one, state_pieces, cotangent_rows)

    normed_pieces = tp_gather(layer_norm(layer_one, norm_tok).astype(LOW))
    normed = jnp.concatenate(normed_pieces)
    token_qkv = plain_dot(normed, qkv_tok_flat).astype(LOW)
    queries, pair = token_qkv[:, :width], token_qkv[:, width:]
    pairs_all = pos_gather(pair)
    pair_prev = jnp.where(position % 2 == 1, pairs_all[1], pairs_all[3])
    pairs_stack = jnp.stack(pairs_all)
    before = pair_prev, shift, start_flag

    keeps = jnp.stack([keep_one, keep_two])
    gain_state, gain_sffn = norm_state.reshape(1, -1), norm_sffn.reshape(1, -1)
    turns = []
    slabs_out = []
    for turn in range(CHAIN - 1):
        state_pair, own_logs, cross_logs, state_heads, low = chain_attend(
            state_queries, state_pieces, pairs_stack, position ^ turn, out_state_flat
        )
        parts = [low] + sent_around(low)
        if turn == 1:
            own_heads, own_token_logs = attend(tied(queries, low), pair, before)
            parts = tied(parts, own_heads)
        mid_state, state_ffn_in, state_slope, state_active, low = chain_mlp(
            parts, state_incoming, keeps, gain_sffn, up_state, down_state
        )
        parts = [low] + sent_around(low)
        state_mlp, slab, incoming_next, normed_next, queries_next, pair_next = chain_start(
            parts, mid_state, keeps, init_slab, flags[turn + 1], gain_state, qkv_state_flat
        )
        slabs_out.append(slab)
        turns.append(
            (
                state_incoming,
                state_normed,
                state_queries,
                state_pair,
                (own_logs, cross_logs),
                state_heads,
                mid_state,
                state_ffn_in,
                state_slope,
                state_active,
                state_mlp,
            )
        )
        state_incoming, state_normed, state_queries = incoming_next, normed_next, queries_next
        state_pieces = pos_gather(pair_next)
    turns.append((state_incoming, state_normed))
    my_state_pair = jnp.concatenate(state_pieces)
    for turn in range(CHAIN - 1):
        my_state_pair = jnp.where(position == turn, turns[turn][3], my_state_pair)

    cross_heads, cross_token_logs = attend(queries, my_state_pair)
    token_heads = jnp.concatenate([own_heads, cross_heads], axis=1)
    proj_total = tp_scatter(
        [plain_dot(part, out_tok_flat) for part in split_rows(token_heads, n_tp)]
    )
    cotangents = split_rows(tied(cotangent_rows, token_heads), n_tp)
    grad_active = [dot_second(part, down_tok) for part in cotangents]
    mixed_one = layer_one + tied(proj_total, *grad_active)
    ffn_in = tp_gather(layer_norm(mixed_one, norm_ffn).astype(LOW))
    hidden = [plain_dot(part, up_tok) for part in ffn_in]

    grad_hidden = [
        gelu_slope(part, grad).astype(LOW) for part, grad in zip(hidden, grad_active)
    ]
    active = [gelu_exact(part).astype(LOW) for part in hidden]
    grad_ffn_in = tp_scatter([dot_second(part, up_tok) for part in grad_hidden])
    grad_mixed = cotangents[0].astype(HIGH) + norm_back(mixed_one, norm_ffn, grad_ffn_in)
    grad_proj_pieces = tp_gather(grad_mixed.astype(LOW))
    grad_proj = jnp.concatenate(grad_proj_pieces)
    grad_heads = dot_second(grad_proj, out_tok_flat).astype(LOW)
    cross_query_grad, cross_pair_grad = attend_back(
        queries, my_state_pair, cross_token_logs, grad_heads[:, width:]
    )
    cross_pair_grad = split_rows(cross_pair_grad, CHAIN)
    cross_pieces = jnp.stack(
        [cross_pair_grad[0]]
        + [swap(cross_pair_grad[k].astype(LOW), k).astype(HIGH) for k in range(1, CHAIN)]
    )
    homeward = [(s, s - 1) for s in range(lax.axis_size("seq")) if s % CHAIN]

    def own_back(after):
        query_grad, pair_grad, prev_grad = attend_back(
            queries, pair, own_token_logs, tied(grad_heads[:, :width], after), before
        )
        returned = lax.ppermute(prev_grad, "seq", homeward)
        return query_grad + cross_query_grad, pair_grad + returned.astype(HIGH)

    last_incoming = state_incoming
    _, _, _, _, low = chain_attend(
        tied(state_queries, grad_heads),
        state_pieces,
        pairs_stack,
        position ^ (CHAIN - 1),
        out_state_flat,
    )
    last_parts = [low] + sent_around(low)

    def last_state(after):
        mid_state, _, _, _, low = chain_mlp(
            tied(last_parts, after), last_incoming, keeps, gain_sffn, up_state, down_state
        )
        state_mlp = low.astype(HIGH)
        for received in sent_around(low):
            state_mlp = state_mlp + received.astype(HIGH)
        return (keep_two * mid_state + (1.0 - keep_two) * state_mlp).astype(LOW)

    def states_between(state_slab):
        states_stack = jnp.stack([own_rows(slab) for slab in slabs_out + [state_slab]])
        pieces = [choose(states_stack, position)]
        pieces += [swap(choose(states_stack, position ^ k), k) for k in range(1, CHAIN)]
        pieces = jnp.stack(pieces)
        return jnp.stack([choose(pieces, position ^ q) for q in range(CHAIN)])

    def states_whole(slabs):
        by_tp = turned(jnp.stack(tp_gather(slabs)), (n_tp - tp_index) % n_tp)
        return jnp.transpose(by_tp, (1, 0, 2, 3)).reshape(state_rows, model_width)

    grad_state_qkv, low = chain_back_inputs(
        None, [], cross_pieces, position ^ (CHAIN - 1), qkv_state_flat
    )
    parts = [low] + sent_around(low)
    query_grad, pair_grad = own_back(low)
    token_grads = ScatterSum(
        weight_grads(
            [
                (tied(tuple(ffn_in), query_grad), grad_hidden),
                ([cotangent_rows], active),
                (grad_proj_pieces, [token_heads]),
            ],
            False,
        )
    )
    parts = tied(parts, token_grads.grads)
    kept_qkv, kept_rest = [(state_normed, grad_state_qkv)], []
    token_pair_grads = [None] * CHAIN
    init_grad = jnp.zeros((slab_rows, model_width), HIGH)
    bias_one = bias_two = jnp.zeros((1, model_width), HIGH)
    grad_mid = None
    for turn in reversed(range(CHAIN - 1)):
        next_incoming = turns[turn + 1][0]
        (
            state_incoming,
            state_normed,
            state_queries,
            state_pair,
            logs,
            state_heads,
            mid_state,
            state_ffn_in,
            state_slope,
            state_active,
            state_mlp,
        ) = turns[turn]
        grad_next, grad_state, grad_mlp, grad_state_hidden, sums, low = chain_back_mlp(
            parts,
            next_incoming,
            grad_mid,
            flags[turn + 1],
            keeps,
            gain_state,
            mid_state,
            state_mlp,
            state_slope,
            up_state,
            down_state,
        )
        init_grad = init_grad + jnp.where(flags[turn + 1], grad_next, 0.0)
        bias_two = bias_two + sums
        parts = [low] + sent_around(low)
        if turn == 0:
            parts = tied(parts, token_grads.total)
        grad_mid, grad_update, sums, query_total, here, across, sent, token_grad = chain_back_heads(
            parts,
            mid_state,
            gain_sffn,
            keeps,
            grad_state,
            state_incoming,
            out_state_flat,
            state_queries,
            state_pair,
            logs,
            pairs_stack,
            position ^ turn,
        )
        bias_one = bias_one + sums
        token_pair_grads[turn] = token_grad
        kept_rest.append(
            (state_heads, grad_update, state_ffn_in, grad_state_hidden, state_active, grad_mlp)
        )
        beside, there = split_rows(swap(sent, 1), 2)
        across = swap((across + there.astype(HIGH)).astype(LOW), 2)
        if turn == CHAIN - 2:
            last_slab = last_state(grad_mid)
            across = tied(across, last_slab)
        if turn == CHAIN - 3:
            slabs = states_between(tied(last_slab, grad_mid))
            across = tied(across, slabs)
        grad_state_qkv, low = chain_back_inputs(
            query_total, [here, beside, across], cross_pieces, position ^ turn, qkv_state_flat
        )
        kept_qkv.append((state_normed, grad_state_qkv))
        if turn:
            parts = [low] + sent_around(low)

    init_grad = init_grad + jnp.where(flags[0], keep_one * grad_mid, 0.0)
    first_part = norm_back(turns[0][0].astype(HIGH), norm_state, low.astype(HIGH))
    init_grad = init_grad / n_tp + jnp.where(flags[0], first_part, 0.0)
    bias_one = bias_one[0] * keep_one / n_tp
    bias_two = bias_two[0] * keep_two * (1.0 - keep_two) / n_tp

    token_pair_grads[CHAIN - 1] = jnp.zeros_like(token_pair_grads[0])
    pair_stack = jnp.stack(token_pair_grads)
    shares = [choose(pair_stack, position ^ k) for k in range(CHAIN)]
    pair_grad = pair_grad + shares[0]
    here, there = split_rows(swap(jnp.concatenate([shares[1], shares[3]]).astype(LOW), 1), 2)
    far_share = (shares[2] + there.astype(HIGH)).astype(LOW)
    pair_grad = pair_grad + here.astype(HIGH) + swap(far_share, 2).astype(HIGH)
    state_rows_out = states_whole(tied(slabs, far_share))
    layer_output = mixed_one + tp_scatter(
        [plain_dot(part, down_tok) for part in tied(tuple(active), far_share)]
    )
    qkv_parts = list(zip(*kept_qkv))
    rest_parts = list(zip(*kept_rest))
    state_grads = ScatterSum(
        weight_grads(
            [
                (tied(qkv_parts[0], far_share), qkv_parts[1]),
                (rest_parts[1], rest_parts[0]),
                (rest_parts[2], rest_parts[3]),
                (rest_parts[5], rest_parts[4]),
            ],
            False,
        )
    )
    pair_grad = tied(pair_grad, layer_output, state_grads.grads, state_rows_out)
    grad_qkv = jnp.concatenate([query_grad, pair_grad], axis=1).astype(LOW)
    grad_normed = tp_scatter(
        [dot_second(part, qkv_tok_flat) for part in split_rows(grad_qkv, n_tp)]
    )
    grad_layer_one = grad_mixed + norm_back(layer_one, norm_tok, grad_normed)

    grad_win_out = tp_gather(grad_layer_one.astype(LOW))
    grad_win_hidden = [
        gelu_slope(part, dot_second(grad, down_win)).astype(LOW)
        for part, grad in zip(win_hidden, grad_win_out)
    ]
    grad_win_ffn_in = tp_scatter([dot_second(part, up_win) for part in grad_win_hidden])

    middle_grads = SeqSum(
        weight_grads(
            [
                (normed_pieces, [grad_qkv]),
                (win_ffn_in, grad_win_hidden),
                (grad_win_out, win_active),
            ]
        )
    )
    grad_win_ffn_in = tied(grad_win_ffn_in, middle_grads.other)
    grad_win_mixed = grad_layer_one + norm_back(win_mixed, norm_wffn, grad_win_ffn_in)
    grad_win_pieces = tp_gather(grad_win_mixed.astype(LOW))
    middle_halves = middle_grads.cores(grad_win_mixed)
    grad_win_proj = jnp.concatenate(grad_win_pieces)
    grad_win_heads = dot_second(grad_win_proj, out_win).astype(LOW)
    win_query_grad, win_pair_grad, win_prev_grad = attend_back(
        win_queries, win_pair, win_logs, grad_win_heads, win_before
    )
    win_returned = lax.ppermute(win_prev_grad, "seq", homeward)
    win_pair_grad = win_pair_grad + tied(win_returned, state_grads.total).astype(HIGH)
    grad_win_qkv = jnp.concatenate([win_query_grad, win_pair_grad], axis=1).astype(LOW)

    small_rows = jnp.concatenate(
        [init_grad, jnp.stack([bias_one, bias_two]), jnp.zeros((14, model_width), HIGH)]
    ).astype(LOW)
    small_shape = small_rows.shape[0], state_rows + 128
    row_of = lax.broadcasted_iota(jnp.int32, small_shape, 0)
    column_of = lax.broadcasted_iota(jnp.int32, small_shape, 1)
    column_for = jnp.where(
        row_of < slab_rows,
        position * slab_rows + row_of,
        (CHAIN - 1) * slab_rows + row_of,
    )
    selector = (column_of == column_for).astype(LOW)
    last_grads = SeqSum(
        weight_grads(
            [
                ([win_normed], [grad_win_qkv]),
                ([grad_win_proj], [win_heads]),
                ([small_rows], [selector]),
            ]
        )
    )
    last_halves = last_grads.cores(last_grads.other)
    split_at = [half.shape[-1] for half in middle_halves]
    halves = [jnp.concatenate(both, axis=-1) for both in zip(middle_halves, last_halves)]
    parts = [dot_second(part, qkv_win_flat) for part in split_rows(grad_win_qkv, n_tp)]
    grad_win_normed = tp_scatter(parts)
    firsts = last_grads.across(*tied(halves, parts))
    one, two = last_grads.last(*firsts)
    middle_halves = one[:, : split_at[0]], two[:, : split_at[1]]
    last_halves = one[:, split_at[0] :], two[:, split_at[1] :]
    back_input = norm_back(own_input, norm_win, tied(grad_win_normed, firsts))
    grad_token_rows = natural(tp_gather((grad_win_mixed + back_input).astype(LOW)))
    output_rows = natural(tp_gather(tied(layer_output.astype(LOW), grad_win_heads)))

    own_columns = model_width // lax.axis_size("seq")
    inner_width = up_tok.shape[1]
    token_grads.total, state_grads.total = tied(
        (token_grads.total, state_grads.total), firsts
    )
    sum_qkv_win = columns_of(last_halves, 0, 3 * width)
    sum_qkv_tok = columns_of(middle_halves, 0, 3 * width)
    sum_qkv_state = state_grads.columns(0, 3 * width)
    sum_up_win = columns_of(middle_halves, 3 * width, inner_width)
    sum_up_tok = token_grads.columns(0, inner_width)
    sum_up_state = state_grads.columns(5 * width, inner_width)
    small_sums = columns_of(last_halves, 4 * width, state_rows + 2)
    first_row = seq_index * own_columns
    vectors = [
        gain_grad(qkv_win_flat, sum_qkv_win, norm_win, first_row),
        gain_grad(up_win, sum_up_win, norm_wffn, first_row),
        gain_grad(qkv_tok_flat, sum_qkv_tok, norm_tok, first_row),
        gain_grad(up_tok, sum_up_tok, norm_ffn, first_row),
        gain_grad(qkv_state_flat, sum_qkv_state, norm_state, first_row),
        gain_grad(up_state, sum_up_state, norm_sffn, first_row),
    ]
    small_sums = sum(
        tp_gather(jnp.concatenate([small_sums] + vectors, axis=1))
    )
    sum_init, vector_sums = small_sums[:, :state_rows].T, small_sums[:, state_rows:]

    def qkv_of(columns):
        return columns.reshape(own_columns, 3, width)

    def out_of(columns):
        return columns.T.reshape(2, width, own_columns)

    return (
        output_rows,
        state_rows_out,
        grad_token_rows,
        vector_sums[:, 2],
        qkv_of(sum_qkv_win),
        columns_of(last_halves, 3 * width, width).T,
        vector_sums[:, 3],
        sum_up_win,
        columns_of(middle_halves, 3 * width + inner_width, inner_width).T,
        vector_sums[:, 4],
        qkv_of(sum_qkv_tok),
        out_of(token_grads.columns(2 * inner_width, 2 * width)),
        vector_sums[:, 5],
        sum_up_tok,
        token_grads.columns(inner_width, inner_width).T,
        vector_sums[:, 6],
        qkv_of(sum_qkv_state),
        out_of(state_grads.columns(3 * width, 2 * width)),
        vector_sums[:, 0:2].T,
        vector_sums[:, 7],
        sum_up_state,
        state_grads.columns(5 * width + inner_width, inner_width).T,
        sum_init,
    )


def solution(mesh):
    placed = (
        P("seq", None),
        P(),
        P(),
        P(None, None, "tp"),
        P("tp", None),
        P(),
        P(None, "tp"),
        P("tp", None),
        P(),
        P(None, None, "tp"),
        P(None, "tp", None),
        P(),
        P(None, "tp"),
        P("tp", None),
        P(),
        P(None, None, "tp"),
        P(None, "tp", None),
        P(),
        P(),
        P(None, "tp"),
        P("tp", None),
        P(),
        P("seq", None),
    )
    return jax.shard_map(
        body,
        mesh=mesh,
        in_specs=placed,
        out_specs=(
            P("seq", None),
            P("seq", None),
            P("seq", None),
            P("seq"),
            P("seq", None, "tp"),
            P("tp", "seq"),
            P("seq"),
            P("seq", "tp"),
            P("tp", "seq"),
            P("seq"),
            P("seq", None, "tp"),
            P(None, "tp", "seq"),
            P("seq"),
            P("seq", "tp"),
            P("tp", "seq"),
            P("seq"),
            P("seq", None, "tp"),
            P(None, "tp", "seq"),
            P(None, "seq"),
            P("seq"),
            P("seq", "tp"),
            P("tp", "seq"),
            P(None, "seq"),
        ),
        check_vma=False,
    )
```

```python
import jax
import jax.numpy as jnp
from jax import lax
from jax.experimental import pallas as pl
from jax.experimental.layout import Layout, with_layout_constraint
from jax.experimental.pallas import tpu as pltpu
from jax.sharding import PartitionSpec as P

E = 128
CHAIN = 4
CORES = 2

EPSILON = 1e-05
MASKED = -1e30
LOW = jnp.bfloat16
HIGH = jnp.float32


def layer_norm(matrix, weights):
    average = jnp.mean(matrix, axis=-1, keepdims=True)
    centred = matrix - average
    spread = jnp.mean(centred * centred, axis=-1, keepdims=True)
    return centred * lax.rsqrt(spread + EPSILON) * weights


def gelu_exact(matrix):
    return jax.nn.gelu(matrix, approximate=False)


def gelu_slope(matrix, grad):
    return jax.vjp(gelu_exact, matrix)[1](grad)[0]


def plain_dot(former, latter):
    return jnp.dot(former, latter, preferred_element_type=HIGH)


def dot_first(former, latter):
    return lax.dot_general(
        former, latter, (((0,), (0,)), ((), ())), preferred_element_type=HIGH
    )


def dot_second(former, latter):
    return lax.dot_general(
        former, latter, (((1,), (1,)), ((), ())), preferred_element_type=HIGH
    )


def row_major(array):
    return with_layout_constraint(array, Layout(major_to_minor=tuple(range(array.ndim))))


def tied(value, *others):
    return lax.optimization_barrier((value, others))[0]


def norm_back(matrix, weights, grad):
    average = jnp.mean(matrix, axis=-1, keepdims=True)
    centred = matrix - average
    spread = jnp.mean(centred * centred, axis=-1, keepdims=True)
    scaled = centred * lax.rsqrt(spread + EPSILON)
    inner = grad * weights
    return lax.rsqrt(spread + EPSILON) * (
        inner
        - jnp.mean(inner, axis=-1, keepdims=True)
        - scaled * jnp.mean(inner * scaled, axis=-1, keepdims=True)
    )


def gain_grad(weights, grads, gain, first):
    rows = lax.dynamic_slice_in_dim(weights, first, grads.shape[0], 0).astype(HIGH)
    gains = lax.dynamic_slice_in_dim(gain.reshape(-1, 1), first, grads.shape[0], 0)
    return jnp.sum(rows * grads, axis=1, keepdims=True) / gains


def tp_from(array, k):
    n = lax.axis_size("tp")
    return lax.ppermute(array, "tp", [((i + k) % n, i) for i in range(n)])


def tp_to(array, k):
    n = lax.axis_size("tp")
    return lax.ppermute(array, "tp", [(i, (i + k) % n) for i in range(n)])


def far_first(n):
    return sorted(range(1, n), key=lambda k: -min(k, n - k))


def tp_gather(piece):
    n = lax.axis_size("tp")
    found = {k: tp_from(piece, k) for k in far_first(n)}
    return [piece] + [found[k] for k in range(1, n)]


def tp_scatter(parts):
    n = lax.axis_size("tp")
    total = parts[0]
    for k in far_first(n):
        total = total + tp_to(parts[k].astype(LOW), k).astype(HIGH)
    return total


def tp_parts(parts):
    n = lax.axis_size("tp")
    return [parts[0]] + [tp_to(parts[k].astype(LOW), k) for k in far_first(n)]


def tp_total(part):
    low = part.astype(LOW)
    total = part
    for k in far_first(lax.axis_size("tp")):
        total = total + tp_to(low, k).astype(HIGH)
    return total


def split_rows(matrix, n):
    size = matrix.shape[0] // n
    return [matrix[k * size : (k + 1) * size] for k in range(n)]


def swap(array, k):
    n = lax.axis_size("seq")
    return lax.ppermute(array, "seq", [(s, s ^ k) for s in range(n)])


def pos_gather(piece):
    beside, across = swap(piece, 1), swap(piece, 2)
    return [piece, beside, across, swap(across, 1)]


def pos_scatter(parts):
    low = jnp.concatenate([parts[1], parts[3]]).astype(LOW)
    here, there = split_rows(swap(low, 1), 2)
    across = swap((parts[2] + there.astype(HIGH)).astype(LOW), 2)
    return parts[0] + here.astype(HIGH) + across.astype(HIGH)


def choose(stacked, index):
    return lax.dynamic_index_in_dim(stacked, index, 0, keepdims=False)


def turned(array, start):
    twice = jnp.concatenate([array, array])
    return lax.dynamic_slice_in_dim(twice, start, array.shape[0], 0)


def weight_grads(pairs, split=True):
    n_seq = lax.axis_size("seq")
    depth = pairs[0][0][0].shape[1]
    unit = depth // n_seq
    block = max(256, CORES * unit)
    widths = [latter[0].shape[1] for _, latter in pairs]
    total = sum(widths)
    counts = [(len(former), len(latter)) for former, latter in pairs]
    operands, specs = [], []
    for former, latter in pairs:
        for piece in former:
            operands.append(piece)
            specs.append(pl.BlockSpec((piece.shape[0], block), lambda i: (0, i)))
        for piece in latter:
            operands.append(piece)
            specs.append(pl.BlockSpec(piece.shape, lambda i: (0, 0), pipeline_mode=pl.Buffered(1)))

    def kernel(core_ref, *refs):
        mine_ref, other_ref = refs[-2:]
        first = core_ref[0] == 0

        def keep(product, column):
            columns = slice(column, column + product.shape[1])
            if not split:
                other_ref[:, columns] = product
                return
            for g in range(block // (CORES * unit)):
                low = product[g * CORES * unit : g * CORES * unit + unit]
                high = product[g * CORES * unit + unit : (g + 1) * CORES * unit]
                rows = slice(g * unit, (g + 1) * unit)
                mine_ref[rows, columns] = jnp.where(first, low, high)
                other_ref[rows, columns] = jnp.where(first, high, low)

        at, column = 0, 0
        for (n_former, n_latter), width in zip(counts, widths):
            former = [ref[...] for ref in refs[at : at + n_former]]
            latter = [ref[...] for ref in refs[at + n_former : at + n_former + n_latter]]
            at += n_former + n_latter
            former = jnp.concatenate(former) if n_former > 1 else former[0]
            latter = jnp.concatenate(latter) if n_latter > 1 else latter[0]
            keep(dot_first(former, latter).astype(LOW), column)
            column += width

    shapes = [jax.ShapeDtypeStruct((depth // CORES, total), LOW)] * 2
    out_specs = [pl.BlockSpec((block // CORES, total), lambda i: (i, 0))] * 2
    if not split:
        shapes = [jax.ShapeDtypeStruct((depth, total), LOW)]
        out_specs = [pl.BlockSpec((block, total), lambda i: (i, 0))]
    rows = sum(piece.shape[0] for piece in pairs[0][0])
    core = (lax.axis_index("seq") % CORES).astype(jnp.int32).reshape(1)
    return pl.pallas_call(
        kernel,
        out_shape=shapes,
        grid=(depth // block,),
        in_specs=[pl.BlockSpec(memory_space=pltpu.SMEM)] + specs,
        out_specs=out_specs,
        compiler_params=pltpu.CompilerParams(vmem_limit_bytes=20 * 1024 * 1024),
        cost_estimate=pl.CostEstimate(
            flops=2 * rows * depth * total,
            bytes_accessed=2 * (rows * (depth + total) + depth * total),
            transcendentals=0,
        ),
    )(core, *operands)


class ScatterSum:
    def __init__(self, grads):
        self.grads = grads[0]
        self.total = lax.psum_scatter(self.grads, "seq", scatter_dimension=0, tiled=True)

    def columns(self, at, count):
        return self.total[:, at : at + count].astype(HIGH)


class SeqSum:
    def __init__(self, halves):
        n = lax.axis_size("seq")
        self.z_size = 4 if n % 8 == 0 else n // CORES
        self.x_size = n // (self.z_size * CORES)
        here = lax.axis_index("seq")
        self.z_at = here // CORES % self.z_size
        self.x_at = here // (CORES * self.z_size)
        self.mine, self.other = halves

    def pairs(self, dx, dz):
        def place(x, z, c):
            return (x % self.x_size * self.z_size + z % self.z_size) * CORES + c

        return [
            (place(x, z, c), place(x + dx, z + dz, c))
            for x in range(self.x_size)
            for z in range(self.z_size)
            for c in range(CORES)
        ]

    def over_z(self, array, dim):
        return self.stage(array, dim, self.z_at, self.z_size, lambda k: (0, k))

    def over_x(self, array, dim):
        return self.stage(array, dim, self.x_at, self.x_size, lambda k: (k, 0))

    def stage(self, array, dim, at, size, step):
        total = lax.dynamic_index_in_dim(array, at, dim, False).astype(HIGH)
        for k in far_first(size):
            sent = lax.dynamic_index_in_dim(array, (at + k) % size, dim, False)
            total = total + lax.ppermute(sent, "seq", self.pairs(*step(k))).astype(HIGH)
        return row_major(total)

    def cores(self, after):
        width = self.mine.shape[1]
        sent = swap(tied(self.other, after), 1)
        half = width // 256 * 128

        def total(columns):
            part = self.mine[:, columns].astype(HIGH) + sent[:, columns].astype(HIGH)
            return part.astype(LOW).reshape(self.x_size, self.z_size, -1, part.shape[1])

        return total(slice(0, half)), total(slice(half, width))

    def across(self, one, two):
        return self.over_z(one, 1).astype(LOW), self.over_x(two, 0).astype(LOW)

    def last(self, one, two):
        return self.over_x(one, 0), self.over_z(two, 0)


def columns_of(halves, at, count):
    one, two = halves
    half = one.shape[1]
    if at + count <= half:
        return one[:, at : at + count]
    if at >= half:
        return two[:, at - half : at - half + count]
    return jnp.concatenate([one[:, at:], two[:, : at + count - half]], axis=1)


ATTEND_STEP = 256


class Loaded:
    def __init__(self, source, buffer, semaphore):
        self.buffer, self.copy, self.waiting = buffer, None, True
        self.copy = pltpu.make_async_copy(source, buffer, semaphore)
        self.copy.start()

    def __getitem__(self, index):
        if self.waiting:
            self.copy.wait()
            self.waiting = False
        return self.buffer[index]


class Kept:
    def __init__(self, target, buffer, semaphore):
        self.buffer, self.started = buffer, False
        self.copy = pltpu.make_async_copy(buffer, target, semaphore)

    def __getitem__(self, index):
        return self.buffer[index]

    def __setitem__(self, index, value):
        self.buffer[index] = value
        if index is Ellipsis:
            self.start()

    def start(self):
        self.copy.start()
        self.started = True

    def finish(self):
        if not self.started:
            self.start()
        self.copy.wait()


def fused(kernel, outs, operands, products, scalars=(), exps=0, loaded=(), chosen=None, kept=()):
    in_vmem = pl.BlockSpec(memory_space=pltpu.VMEM)
    in_hbm = pl.BlockSpec(memory_space=pltpu.HBM)
    in_smem = pl.BlockSpec(memory_space=pltpu.SMEM)
    scalars = [jnp.asarray(scalar, jnp.int32).reshape(1) for scalar in scalars]
    loaded = list(loaded) + ([] if chosen is None else [chosen])
    n_scalars, n_in, n_out = len(scalars), len(operands), len(outs)
    scratch = []
    for k in loaded:
        shape = operands[k].shape
        scratch.append(pltpu.VMEM(shape[1:] if k == chosen else shape, operands[k].dtype))
    for k in kept:
        scratch.append(pltpu.VMEM(*outs[k]))
    moved = len(scratch)
    if moved:
        scratch.append(pltpu.SemaphoreType.DMA((moved,)))

    def whole(*refs):
        views = list(refs[: n_scalars + n_in + n_out])
        buffers = refs[n_scalars + n_in + n_out :]
        for spot, k in enumerate(loaded):
            source = views[n_scalars + k]
            if k == chosen:
                source = source.at[views[0][0]]
            views[n_scalars + k] = Loaded(source, buffers[spot], buffers[-1].at[spot])
        for spot, k in enumerate(kept, len(loaded)):
            at = n_scalars + n_in + k
            views[at] = Kept(views[at], buffers[spot], buffers[-1].at[spot])
        kernel(*views)
        for k in kept:
            views[n_scalars + n_in + k].finish()

    return pl.pallas_call(
        whole,
        out_shape=[jax.ShapeDtypeStruct(shape, kind) for shape, kind in outs],
        in_specs=[in_smem] * n_scalars + [in_hbm if k in loaded else in_vmem for k in range(n_in)],
        out_specs=[in_hbm if k in kept else in_vmem for k in range(n_out)],
        scratch_shapes=scratch,
        compiler_params=pltpu.CompilerParams(vmem_limit_bytes=20 * 1024 * 1024),
        cost_estimate=pl.CostEstimate(
            flops=2 * products,
            bytes_accessed=sum(2 * operand.size for operand in operands),
            transcendentals=exps,
        ),
    )(*scalars, *operands)


def score_parts(query, key, before, spot):
    if before is None:
        return dot_second(key, query) * E ** (-0.5), None
    key_before, _, shift, start = before
    shape = key.shape[0], query.shape[0]
    key_ids = (lax.broadcasted_iota(jnp.int32, shape, 0) + shift) % shape[0]
    query_ids = (lax.broadcasted_iota(jnp.int32, shape, 1) + shift + spot) % shape[0]
    below = key_ids <= query_ids
    scores = jnp.where(below, dot_second(key, query), dot_second(key_before, query))
    return jnp.where(below | (start == 0), scores * E ** (-0.5), MASKED), below


def head_attend(query, key, value, before=None, spot=0):
    scores, below = score_parts(query, key, before, spot)
    top = jnp.max(scores, axis=0, keepdims=True)
    powers = jnp.exp(scores - top)
    total = jnp.sum(powers, axis=0, keepdims=True)
    chances = (powers * (1.0 / total)).astype(LOW)
    if before is None:
        result = dot_first(value, chances)
    else:
        none = jnp.zeros_like(chances)
        result = dot_first(value, jnp.where(below, chances, none)) + dot_first(
            before[1], jnp.where(below, none, chances)
        )
    return result.T.astype(LOW), top + jnp.log(total)


def head_back(query, key, value, log, grad, before=None, spot=0):
    scores, below = score_parts(query, key, before, spot)
    chances = jnp.exp(scores - log)
    grad_chances = dot_second(value, grad)
    if before is not None:
        grad_chances = jnp.where(below, grad_chances, dot_second(before[1], grad))
    inner = jnp.sum(chances * grad_chances, axis=0, keepdims=True)
    grad_scores = (chances * (grad_chances - inner) * E ** (-0.5)).astype(LOW)
    chances = chances.astype(LOW)
    if before is None:
        terms = [plain_dot(grad_scores, query), plain_dot(chances, grad)]
        return dot_first(key, grad_scores).T, terms
    none = jnp.zeros_like(chances)
    scores_now = jnp.where(below, grad_scores, none)
    scores_before = jnp.where(below, none, grad_scores)
    terms = [
        plain_dot(scores_now, query),
        plain_dot(jnp.where(below, chances, none), grad),
        plain_dot(scores_before, query),
        plain_dot(jnp.where(below, none, chances), grad),
    ]
    query_grad = dot_first(key, scores_now) + dot_first(before[0], scores_before)
    return query_grad.T, terms


def head_columns(head, width, part):
    return slice(part * width + head * E, part * width + (head + 1) * E)


def attend(queries, pair, before=None):
    count, width = queries.shape
    heads = width // E
    rows = min(count, ATTEND_STEP)
    scalars = [] if before is None else before[1:]
    operands = [queries, pair] + ([] if before is None else [before[0]])

    def kernel(*refs):
        scalar_refs, refs = refs[: len(scalars)], refs[len(scalars) :]
        query_ref, pair_ref = refs[:2]
        result_ref, log_ref = refs[-2:]
        for h in range(heads):
            own = slice(h * E, (h + 1) * E)
            key_at, value_at = head_columns(h, width, 0), head_columns(h, width, 1)
            mask = None
            if before is not None:
                mask = (refs[2][:, key_at], refs[2][:, value_at]) + tuple(
                    ref[0] for ref in scalar_refs
                )
            for spot in range(0, count, rows):
                here = slice(spot, spot + rows)
                result_ref[here, own], log_ref[h : h + 1, here] = head_attend(
                    query_ref[here, own], pair_ref[:, key_at], pair_ref[:, value_at], mask, spot
                )

    scores_count = heads * count * pair.shape[0]
    outs = [((count, width), LOW), ((heads, count), HIGH)]
    products = scores_count * E * len(operands)
    return fused(kernel, outs, operands, products, scalars, scores_count)


def attend_back(queries, pair, logs, grad_result, before=None):
    count, width = queries.shape
    heads = width // E
    rows = min(count, ATTEND_STEP)
    keys = pair.shape[0]
    scalars = [] if before is None else before[1:]
    operands = [queries, logs, grad_result, pair] + ([] if before is None else [before[0]])

    def kernel(*refs):
        scalar_refs, refs = refs[: len(scalars)], refs[len(scalars) :]
        query_ref, log_ref, grad_ref, pair_ref = refs[:4]
        outs = refs[len(operands) :]
        for h in range(heads):
            own = slice(h * E, (h + 1) * E)
            key_at, value_at = head_columns(h, width, 0), head_columns(h, width, 1)
            mask = None
            if before is not None:
                mask = (refs[4][:, key_at], refs[4][:, value_at]) + tuple(
                    ref[0] for ref in scalar_refs
                )
            sums = None
            for spot in range(0, count, rows):
                here = slice(spot, spot + rows)
                outs[0][here, own], terms = head_back(
                    query_ref[here, own],
                    pair_ref[:, key_at],
                    pair_ref[:, value_at],
                    log_ref[h : h + 1, here],
                    grad_ref[here, own],
                    mask,
                    spot,
                )
                sums = terms if sums is None else [one + two for one, two in zip(sums, terms)]
            outs[1][:, key_at], outs[1][:, value_at] = sums[:2]
            if before is not None:
                outs[2][:, key_at], outs[2][:, value_at] = sums[2].astype(LOW), sums[3].astype(LOW)

    outs = [((count, width), HIGH), ((keys, 2 * width), HIGH)]
    if before is not None:
        outs.append(((keys, 2 * width), LOW))
    scores_count = heads * count * keys
    products = scores_count * E * (5 if before is None else 10)
    return fused(kernel, outs, operands, products, scalars, scores_count)


def gelu_of(matrix):
    return 0.5 * matrix * (1.0 + lax.erf(matrix * 0.5**0.5))


def gelu_slope_of(matrix):
    density = jnp.exp(-0.5 * matrix * matrix) * (2.0 * jnp.pi) ** (-0.5)
    return 0.5 * (1.0 + lax.erf(matrix * 0.5**0.5)) + matrix * density


def sent_around(low):
    return [tp_to(low, k) for k in far_first(lax.axis_size("tp"))]


def added(refs):
    total = refs[0][...].astype(HIGH)
    for ref in refs[1:]:
        total = total + ref[...].astype(HIGH)
    return total


def rows_norm(parts, residual, gain):
    n = len(parts)

    def kernel(*refs):
        residual_ref, gain_ref, total_ref, normed_ref = refs[n:]
        total = residual_ref[...].astype(HIGH) + added(refs[:n])
        total_ref[...] = total
        normed_ref[...] = layer_norm(total, gain_ref[...]).astype(LOW)

    outs = [(residual.shape, HIGH), (residual.shape, LOW)]
    return fused(kernel, outs, [*parts, residual, gain.reshape(1, -1)], residual.size)


def rows_back(parts, matrix, gain, residual):
    n = len(parts)

    def kernel(*refs):
        matrix_ref, gain_ref, residual_ref, total_ref, low_ref = refs[n:]
        total = residual_ref[...].astype(HIGH) + norm_back(
            matrix_ref[...], gain_ref[...], added(refs[:n])
        )
        total_ref[...], low_ref[...] = total, total.astype(LOW)

    outs = [(matrix.shape, HIGH), (matrix.shape, LOW)]
    operands = [*parts, matrix, gain.reshape(1, -1), residual]
    return fused(kernel, outs, operands, matrix.size)


def chain_attend(queries, pieces, stack, index, out_flat):
    count, width = queries.shape
    n, keys = len(pieces), stack.shape[1]

    def kernel(index_ref, query_ref, *refs):
        pieces_refs, (stack_ref, out_ref) = refs[:n], refs[n : n + 2]
        pair_ref, own_ref, cross_ref, heads_ref, low_ref = refs[n + 2 :]
        for k, ref in enumerate(pieces_refs):
            pair_ref[k * (keys // n) : (k + 1) * (keys // n), :] = ref[...]
        for h in range(width // E):
            own = slice(h * E, (h + 1) * E)
            key_at, value_at = head_columns(h, width, 0), head_columns(h, width, 1)
            row = slice(h, h + 1)
            heads_ref[:, own], own_ref[row, :] = head_attend(
                query_ref[:, own], pair_ref[:, key_at], pair_ref[:, value_at]
            )
        for h in range(width // E):
            own = slice(h * E, (h + 1) * E)
            key_at, value_at = head_columns(h, width, 0), head_columns(h, width, 1)
            row = slice(h, h + 1)
            heads_ref[:, value_at], cross_ref[row, :] = head_attend(
                query_ref[:, own], stack_ref[:, key_at], stack_ref[:, value_at]
            )
        heads_ref.start()
        low_ref[...] = plain_dot(heads_ref[...], out_ref[...]).astype(LOW)

    depth = out_flat.shape[1]
    logs = ((width // E, count), HIGH)
    outs = [((keys, 2 * width), LOW), logs, logs, ((count, 2 * width), LOW)]
    outs += [((count, depth), LOW)]
    products = count * width * (4 * keys + 2 * depth)
    operands = [queries, *pieces, stack, out_flat]
    exps = 2 * count * keys
    return fused(kernel, outs, operands, products, [index], exps, chosen=n + 1, kept=(3,))


def chain_mlp(parts, incoming, keeps, gain, up, down):
    n = len(parts)

    def kernel(*refs):
        incoming_ref, keep_ref, gain_ref, up_ref, down_ref = refs[n : n + 5]
        mid_ref, normed_ref, slope_ref, active_ref, low_ref = refs[n + 5 :]
        keep = keep_ref[0:1, :]
        mid = keep * incoming_ref[...].astype(HIGH) + (1.0 - keep) * added(refs[:n])
        normed = layer_norm(mid, gain_ref[...]).astype(LOW)
        mid_ref[...], normed_ref[...] = mid, normed
        hidden = plain_dot(normed, up_ref[...])
        active = gelu_of(hidden).astype(LOW)
        slope_ref[...], active_ref[...] = gelu_slope_of(hidden).astype(LOW), active
        low_ref[...] = plain_dot(active, down_ref[...]).astype(LOW)

    count, depth = incoming.shape
    inner = up.shape[1]
    outs = [((count, depth), HIGH), ((count, depth), LOW)]
    outs += [((count, inner), LOW), ((count, inner), LOW), ((count, depth), LOW)]
    operands = [*parts, incoming, keeps, gain, up, down]
    products = 2 * count * depth * inner
    exps = count * inner
    return fused(kernel, outs, operands, products, (), exps, (n,), kept=(0, 1, 2, 3))


def chain_start(parts, mid, keeps, init_slab, flag, gain, qkv_flat):
    n = len(parts)
    width = qkv_flat.shape[1] // 3

    def kernel(flag_ref, *refs):
        mid_ref, keep_ref, init_ref, gain_ref, qkv_ref = refs[n : n + 5]
        mlp_ref, slab_ref, incoming_ref, normed_ref, query_ref, pair_ref = refs[n + 5 :]
        mlp = added(refs[:n])
        keep = keep_ref[1:2, :]
        slab = (keep * mid_ref[...] + (1.0 - keep) * mlp).astype(LOW)
        incoming = jnp.where(flag_ref[0] == 1, init_ref[...], slab)
        mlp_ref[...], slab_ref[...], incoming_ref[...] = mlp.astype(LOW), slab, incoming
        normed = layer_norm(incoming.astype(HIGH), gain_ref[...]).astype(LOW)
        normed_ref[...] = normed
        qkv = plain_dot(normed, qkv_ref[...]).astype(LOW)
        query_ref[...], pair_ref[...] = qkv[:, :width], qkv[:, width:]

    count, depth = mid.shape
    outs = [((count, depth), LOW)] * 4 + [((count, width), LOW), ((count, 2 * width), LOW)]
    operands = [*parts, mid, keeps, init_slab, gain, qkv_flat]
    products = 3 * count * depth * width
    return fused(kernel, outs, operands, products, [flag], 0, (n,), kept=(0, 1, 2, 3))


def chain_back_mlp(parts, incoming, grad_mid, flag, keeps, gain, mid, mlp, slope, up, down):
    n = len(parts)
    operands = [*parts, incoming, keeps, gain, mid, mlp, slope, up, down]
    operands += [] if grad_mid is None else [grad_mid]
    n_ins = len(operands)

    def kernel(flag_ref, *refs):
        incoming_ref, keep_ref, gain_ref, mid_ref, mlp_ref, slope_ref, up_ref, down_ref = refs[
            n : n + 8
        ]
        grad_ref, state_ref, low_mlp_ref, low_hidden_ref, bias_ref, low_ref = refs[n_ins:]
        grad = norm_back(incoming_ref[...].astype(HIGH), gain_ref[...], added(refs[:n]))
        if grad_mid is not None:
            grad = keep_ref[0:1, :] * refs[n + 8][...] + grad
        state = jnp.where(flag_ref[0] == 1, 0.0, grad)
        low_mlp = ((1.0 - keep_ref[1:2, :]) * state).astype(LOW)
        grad_ref[...], state_ref[...], low_mlp_ref[...] = grad, state, low_mlp
        grad_active = dot_second(low_mlp, down_ref[...])
        low_hidden = (slope_ref[...].astype(HIGH) * grad_active).astype(LOW)
        low_hidden_ref[...] = low_hidden
        low_ref[...] = dot_second(low_hidden, up_ref[...]).astype(LOW)
        change = mid_ref[...] - mlp_ref[...].astype(HIGH)
        bias_ref[...] = jnp.sum(state * change, axis=0, keepdims=True)

    count, depth = mid.shape
    inner = up.shape[1]
    outs = [((count, depth), HIGH), ((count, depth), HIGH), ((count, depth), LOW)]
    outs += [((count, inner), LOW), ((1, depth), HIGH), ((count, depth), LOW)]
    loaded = (n, n + 3, n + 4, n + 5) + (() if grad_mid is None else (n + 8,))
    products = 2 * count * depth * inner
    return fused(kernel, outs, operands, products, [flag], loaded=loaded, kept=(0, 1, 2, 3))


def chain_back_heads(
    parts, mid, gain, keeps, grad_state, incoming, out_flat, queries, pair, logs, stack, index
):
    n = len(parts)
    count, width = queries.shape
    keys = pair.shape[0]
    slab = keys // CHAIN

    def kernel(index_ref, *refs):
        mid_ref, gain_ref, keep_ref, state_ref, incoming_ref, out_ref = refs[n : n + 6]
        query_ref, pair_ref, own_log_ref, cross_log_ref, stack_ref = refs[n + 6 : n + 11]
        outs = refs[n + 11 :]
        mid_out, low_out, bias_out, query_out, here_out, across_out, sent_out, token_out = outs
        grad_mid = keep_ref[1:2, :] * state_ref[...] + norm_back(
            mid_ref[...], gain_ref[...], added(refs[:n])
        )
        mid_out[...] = grad_mid
        low = ((1.0 - keep_ref[0:1, :]) * grad_mid).astype(LOW)
        low_out[...] = low
        change = incoming_ref[...].astype(HIGH) - mid_ref[...]
        bias_out[...] = jnp.sum(grad_mid * change, axis=0, keepdims=True)
        grad_heads = dot_second(low, out_ref[...]).astype(LOW)
        for h in range(width // E):
            own = slice(h * E, (h + 1) * E)
            row = slice(h, h + 1)
            own_query, own_terms = head_back(
                query_ref[:, own],
                pair_ref[:, head_columns(h, width, 0)],
                pair_ref[:, head_columns(h, width, 1)],
                own_log_ref[row, :],
                grad_heads[:, own],
            )
            cross_query, cross_terms = head_back(
                query_ref[:, own],
                stack_ref[:, head_columns(h, width, 0)],
                stack_ref[:, head_columns(h, width, 1)],
                cross_log_ref[row, :],
                grad_heads[:, head_columns(h, width, 1)],
            )
            query_out[:, own] = own_query + cross_query
            for part in range(2):
                at = head_columns(h, width, part)
                here_out[:, at] = own_terms[part][:slab]
                across_out[:, at] = own_terms[part][2 * slab : 3 * slab]
                sent_out[:slab, at] = own_terms[part][slab : 2 * slab].astype(LOW)
                sent_out[slab:, at] = own_terms[part][3 * slab :].astype(LOW)
                token_out[:, at] = cross_terms[part]

    depth = mid.shape[1]
    outs = [((count, depth), HIGH), ((count, depth), LOW), ((1, depth), HIGH)]
    outs += [((count, width), HIGH), ((slab, 2 * width), HIGH), ((slab, 2 * width), HIGH)]
    outs += [((2 * slab, 2 * width), LOW), ((keys, 2 * width), HIGH)]
    operands = [*parts, mid, gain, keeps, grad_state, incoming, out_flat]
    operands += [queries, pair, *logs, stack]
    products = count * width * (10 * keys + 2 * depth)
    loaded = (n, n + 3, n + 4, n + 6, n + 7)
    exps = 2 * count * keys
    return fused(kernel, outs, operands, products, [index], exps, loaded, n + 10, (0, 1, 7))


def chain_back_inputs(query_grad, terms, stack, index, qkv_flat):
    rows, depth = stack.shape[1], qkv_flat.shape[0]
    width = qkv_flat.shape[1] // 3
    first = [] if query_grad is None else [query_grad]

    def kernel(index_ref, *refs):
        stack_ref, qkv_ref = refs[len(first) + len(terms) : len(first) + len(terms) + 2]
        grad_ref, low_ref = refs[-2:]
        pair = stack_ref[...]
        for ref in refs[len(first) : len(first) + len(terms)]:
            pair = pair + ref[...].astype(HIGH)
        if first:
            grad_ref[:, :width] = refs[0][...].astype(LOW)
        else:
            grad_ref[:, :width] = jnp.zeros((rows, width), LOW)
        grad_ref[:, width:] = pair.astype(LOW)
        grad_ref.start()
        low_ref[...] = dot_second(grad_ref[...], qkv_ref[...]).astype(LOW)

    outs = [((rows, 3 * width), LOW), ((rows, depth), LOW)]
    operands = [*first, *terms, stack, qkv_flat]
    chosen = len(first) + len(terms)
    products = 3 * rows * depth * width
    return fused(kernel, outs, operands, products, [index], chosen=chosen, kept=(0,))


def body(
    tokens,
    segment_start,
    norm_win,
    qkv_win,
    out_win,
    norm_wffn,
    up_win,
    down_win,
    norm_tok,
    qkv_tok,
    out_tok,
    norm_ffn,
    up_tok,
    down_tok,
    norm_state,
    qkv_state,
    out_state,
    gate_bias,
    norm_sffn,
    up_state,
    down_state,
    init_state,
    cotangent,
):
    seq_index = lax.axis_index("seq")
    tp_index = lax.axis_index("tp")
    n_tp = lax.axis_size("tp")
    position = seq_index % CHAIN
    flags = choose(segment_start, seq_index // CHAIN) == 1
    starts_here = choose(flags, position)
    block_rows, model_width = tokens.shape
    piece_rows = block_rows // n_tp
    state_rows = init_state.shape[0]
    slab_rows = state_rows // CHAIN
    thin_rows = slab_rows // n_tp
    width = qkv_tok.shape[2]
    qkv_win_flat = qkv_win.reshape(model_width, 3 * width)
    out_tok_flat = out_tok.reshape(2 * width, model_width)
    out_state_flat = out_state.reshape(2 * width, model_width)

    shift = (tp_index * piece_rows).astype(jnp.int32)
    start_flag = starts_here.astype(jnp.int32)
    token_rows = turned(tokens, tp_index * piece_rows)

    def natural(pieces):
        whole = jnp.zeros((block_rows, model_width), pieces[0].dtype)
        for k, piece in enumerate(pieces):
            at = (tp_index + k) % n_tp * piece_rows
            whole = lax.dynamic_update_slice_in_dim(whole, piece, at, 0)
        return whole

    input_rows = token_rows.astype(HIGH)
    win_normed = layer_norm(input_rows, norm_win).astype(LOW)
    win_qkv = plain_dot(win_normed, qkv_win_flat).astype(LOW)
    win_queries, win_pair = win_qkv[:, :width], win_qkv[:, width:]
    onward = [(s, s + 1) for s in range(lax.axis_size("seq")) if (s + 1) % CHAIN]
    win_prev = lax.ppermute(win_pair, "seq", onward)
    win_before = win_prev, shift, start_flag
    win_heads, win_logs = attend(win_queries, win_pair, win_before)
    cotangent, qkv_tok, qkv_state, gate_bias, init_state, _ = lax.optimization_barrier(
        (cotangent, qkv_tok, qkv_state, gate_bias, init_state, win_heads)
    )
    qkv_tok_flat = qkv_tok.reshape(model_width, 3 * width)
    qkv_state_flat = qkv_state.reshape(model_width, 3 * width)
    keep_one, keep_two = jax.nn.sigmoid(gate_bias)
    cotangent_rows = turned(cotangent, tp_index * piece_rows)
    own_input = input_rows[:piece_rows]
    parts = tp_parts([plain_dot(part, out_win) for part in split_rows(win_heads, n_tp)])
    win_mixed, low = rows_norm(parts, own_input, norm_wffn)
    win_ffn_in = tp_gather(low)
    win_hidden = [plain_dot(part, up_win) for part in win_ffn_in]
    win_active = [gelu_exact(part).astype(LOW) for part in win_hidden]

    init_slab = lax.dynamic_slice_in_dim(init_state, position * slab_rows, slab_rows, 0)

    def own_rows(slab):
        return lax.dynamic_slice_in_dim(slab, tp_index * thin_rows, thin_rows, 0)

    init_late = tied(init_slab, win_ffn_in[1])
    state_incoming = init_late
    state_normed = layer_norm(state_incoming.astype(HIGH), norm_state).astype(LOW)
    state_qkv = plain_dot(state_normed, qkv_state_flat).astype(LOW)
    state_queries = state_qkv[:, :width]
    state_pieces = pos_gather(state_qkv[:, width:])
    parts = tp_parts([plain_dot(part, down_win) for part in win_active])
    layer_one, low = rows_norm(tied(parts, state_pieces), win_mixed, norm_tok)

    normed_pieces = tp_gather(low)
    normed = jnp.concatenate(normed_pieces)
    token_qkv = plain_dot(normed, qkv_tok_flat).astype(LOW)
    queries, pair = token_qkv[:, :width], token_qkv[:, width:]
    pairs_all = pos_gather(pair)
    pair_prev = jnp.where(position % 2 == 1, pairs_all[1], pairs_all[3])
    pairs_stack = jnp.stack(pairs_all)
    before = pair_prev, shift, start_flag

    keeps = jnp.stack([keep_one, keep_two])
    gain_state, gain_sffn = norm_state.reshape(1, -1), norm_sffn.reshape(1, -1)
    turns = []
    slabs_out = []
    for turn in range(CHAIN - 1):
        state_pair, own_logs, cross_logs, state_heads, low = chain_attend(
            state_queries, state_pieces, pairs_stack, position ^ turn, out_state_flat
        )
        parts = [low] + sent_around(low)
        if turn == 1:
            own_heads, own_token_logs = attend(tied(queries, low), pair, before)
            parts = tied(parts, own_heads)
        mid_state, state_ffn_in, state_slope, state_active, low = chain_mlp(
            parts, state_incoming, keeps, gain_sffn, up_state, down_state
        )
        parts = [low] + sent_around(low)
        state_mlp, slab, incoming_next, normed_next, queries_next, pair_next = chain_start(
            parts, mid_state, keeps, init_slab, flags[turn + 1], gain_state, qkv_state_flat
        )
        slabs_out.append(slab)
        turns.append(
            (
                state_incoming,
                state_normed,
                state_queries,
                state_pair,
                (own_logs, cross_logs),
                state_heads,
                mid_state,
                state_ffn_in,
                state_slope,
                state_active,
                state_mlp,
            )
        )
        state_incoming, state_normed, state_queries = incoming_next, normed_next, queries_next
        state_pieces = pos_gather(pair_next)
    turns.append((state_incoming, state_normed))
    my_state_pair = jnp.concatenate(state_pieces)
    for turn in range(CHAIN - 1):
        my_state_pair = jnp.where(position == turn, turns[turn][3], my_state_pair)

    cross_heads, cross_token_logs = attend(queries, my_state_pair)
    token_heads = jnp.concatenate([own_heads, cross_heads], axis=1)
    parts = tp_parts(
        [plain_dot(part, out_tok_flat) for part in split_rows(token_heads, n_tp)]
    )
    cotangents = split_rows(tied(cotangent_rows, token_heads), n_tp)
    grad_active = [dot_second(part, down_tok) for part in cotangents]
    mixed_one, low = rows_norm(tied(parts, *grad_active), layer_one, norm_ffn)
    ffn_in = tp_gather(low)
    hidden = [plain_dot(part, up_tok) for part in ffn_in]

    grad_hidden = [
        gelu_slope(part, grad).astype(LOW) for part, grad in zip(hidden, grad_active)
    ]
    active = [gelu_exact(part).astype(LOW) for part in hidden]
    parts = tp_parts([dot_second(part, up_tok) for part in grad_hidden])
    grad_mixed, low = rows_back(parts, mixed_one, norm_ffn, cotangents[0])
    grad_proj_pieces = tp_gather(low)
    grad_proj = jnp.concatenate(grad_proj_pieces)
    grad_heads = dot_second(grad_proj, out_tok_flat).astype(LOW)
    cross_query_grad, cross_pair_grad = attend_back(
        queries, my_state_pair, cross_token_logs, grad_heads[:, width:]
    )
    cross_pair_grad = split_rows(cross_pair_grad, CHAIN)
    cross_pieces = jnp.stack(
        [cross_pair_grad[0]]
        + [swap(cross_pair_grad[k].astype(LOW), k).astype(HIGH) for k in range(1, CHAIN)]
    )
    homeward = [(s, s - 1) for s in range(lax.axis_size("seq")) if s % CHAIN]

    def own_back():
        query_grad, pair_grad, prev_grad = attend_back(
            queries, pair, own_token_logs, tied(grad_heads[:, :width], cross_pieces), before
        )
        returned = lax.ppermute(prev_grad, "seq", homeward)
        return query_grad + cross_query_grad, pair_grad + returned.astype(HIGH)

    last_incoming = state_incoming
    _, _, _, _, low = chain_attend(
        tied(state_queries, grad_heads),
        state_pieces,
        pairs_stack,
        position ^ (CHAIN - 1),
        out_state_flat,
    )
    last_parts = [low] + sent_around(low)

    def last_state(after):
        mid_state, _, _, _, low = chain_mlp(
            tied(last_parts, after), last_incoming, keeps, gain_sffn, up_state, down_state
        )
        state_mlp = low.astype(HIGH)
        for received in sent_around(low):
            state_mlp = state_mlp + received.astype(HIGH)
        return (keep_two * mid_state + (1.0 - keep_two) * state_mlp).astype(LOW)

    def states_between(state_slab):
        states_stack = jnp.stack([own_rows(slab) for slab in slabs_out + [state_slab]])
        pieces = [choose(states_stack, position)]
        pieces += [swap(choose(states_stack, position ^ k), k) for k in range(1, CHAIN)]
        pieces = jnp.stack(pieces)
        return jnp.stack([choose(pieces, position ^ q) for q in range(CHAIN)])

    def states_whole(slabs):
        by_tp = turned(jnp.stack(tp_gather(slabs)), (n_tp - tp_index) % n_tp)
        return jnp.transpose(by_tp, (1, 0, 2, 3)).reshape(state_rows, model_width)

    grad_state_qkv, low = chain_back_inputs(
        None, [], cross_pieces, position ^ (CHAIN - 1), qkv_state_flat
    )
    parts = [low] + sent_around(low)
    query_grad, pair_grad = own_back()
    parts = tied(parts, query_grad)
    kept_qkv, kept_rest = [(state_normed, grad_state_qkv)], []
    token_pair_grads = [None] * CHAIN
    init_grad = jnp.zeros((slab_rows, model_width), HIGH)
    bias_one = bias_two = jnp.zeros((1, model_width), HIGH)
    grad_mid = None
    for turn in reversed(range(CHAIN - 1)):
        next_incoming = turns[turn + 1][0]
        (
            state_incoming,
            state_normed,
            state_queries,
            state_pair,
            logs,
            state_heads,
            mid_state,
            state_ffn_in,
            state_slope,
            state_active,
            state_mlp,
        ) = turns[turn]
        grad_next, grad_state, grad_mlp, grad_state_hidden, sums, low = chain_back_mlp(
            parts,
            next_incoming,
            grad_mid,
            flags[turn + 1],
            keeps,
            gain_state,
            mid_state,
            state_mlp,
            state_slope,
            up_state,
            down_state,
        )
        init_grad = init_grad + jnp.where(flags[turn + 1], grad_next, 0.0)
        bias_two = bias_two + sums
        parts = [low] + sent_around(low)
        if turn == CHAIN - 3:
            token_grads = ScatterSum(
                weight_grads(
                    [
                        (tied(tuple(ffn_in), low), grad_hidden),
                        ([cotangent_rows], active),
                        (grad_proj_pieces, [token_heads]),
                    ],
                    False,
                )
            )
            parts = tied(parts, token_grads.grads)
        grad_mid, grad_update, sums, query_total, here, across, sent, token_grad = chain_back_heads(
            parts,
            mid_state,
            gain_sffn,
            keeps,
            grad_state,
            state_incoming,
            out_state_flat,
            state_queries,
            state_pair,
            logs,
            pairs_stack,
            position ^ turn,
        )
        bias_one = bias_one + sums
        token_pair_grads[turn] = token_grad
        kept_rest.append(
            (state_heads, grad_update, state_ffn_in, grad_state_hidden, state_active, grad_mlp)
        )
        beside, there = split_rows(swap(sent, 1), 2)
        across = swap((across + there.astype(HIGH)).astype(LOW), 2)
        if turn == CHAIN - 2:
            last_slab = last_state(grad_mid)
            across = tied(across, last_slab)
        if turn == CHAIN - 3:
            slabs = states_between(tied(last_slab, grad_mid))
            across = tied(across, slabs)
        if turn == CHAIN - 4:
            state_rows_out = states_whole(tied(slabs, grad_mid))
            across = tied(across, state_rows_out)
        grad_state_qkv, low = chain_back_inputs(
            query_total, [here, beside, across], cross_pieces, position ^ turn, qkv_state_flat
        )
        kept_qkv.append((state_normed, grad_state_qkv))
        if turn:
            parts = [low] + sent_around(low)

    init_grad = init_grad + jnp.where(flags[0], keep_one * grad_mid, 0.0)
    first_part = norm_back(turns[0][0].astype(HIGH), norm_state, low.astype(HIGH))
    init_grad = init_grad / n_tp + jnp.where(flags[0], first_part, 0.0)
    bias_one = bias_one[0] * keep_one / n_tp
    bias_two = bias_two[0] * keep_two * (1.0 - keep_two) / n_tp

    token_pair_grads[CHAIN - 1] = jnp.zeros_like(token_pair_grads[0])
    pair_stack = jnp.stack(token_pair_grads)
    pair_grad = pair_grad + pos_scatter([choose(pair_stack, position ^ k) for k in range(CHAIN)])
    layer_output = mixed_one + tp_scatter(
        [plain_dot(part, down_tok) for part in tied(tuple(active), pair_stack)]
    )
    qkv_parts = list(zip(*kept_qkv))
    rest_parts = list(zip(*kept_rest))
    state_grads = ScatterSum(
        weight_grads(
            [
                (qkv_parts[0], qkv_parts[1]),
                (rest_parts[1], rest_parts[0]),
                (rest_parts[2], rest_parts[3]),
                (rest_parts[5], rest_parts[4]),
            ],
            False,
        )
    )
    pair_grad = tied(pair_grad, layer_output, state_grads.grads, token_grads.total)
    grad_qkv = jnp.concatenate([query_grad, pair_grad], axis=1).astype(LOW)
    parts = tp_parts([dot_second(part, qkv_tok_flat) for part in split_rows(grad_qkv, n_tp)])
    grad_layer_one, low = rows_back(parts, layer_one, norm_tok, grad_mixed)

    grad_win_out = tp_gather(low)
    grad_win_hidden = [
        gelu_slope(part, dot_second(grad, down_win)).astype(LOW)
        for part, grad in zip(win_hidden, grad_win_out)
    ]
    parts = tp_parts([dot_second(part, up_win) for part in grad_win_hidden])

    middle_grads = SeqSum(
        weight_grads(
            [
                (normed_pieces, [grad_qkv]),
                (win_ffn_in, grad_win_hidden),
                (grad_win_out, win_active),
            ]
        )
    )
    parts = tied(parts, middle_grads.other)
    grad_win_mixed, low = rows_back(parts, win_mixed, norm_wffn, grad_layer_one)
    grad_win_pieces = tp_gather(low)
    middle_halves = middle_grads.cores(grad_win_mixed)
    grad_win_proj = jnp.concatenate(grad_win_pieces)
    grad_win_heads = dot_second(grad_win_proj, out_win).astype(LOW)
    win_query_grad, win_pair_grad, win_prev_grad = attend_back(
        win_queries, win_pair, win_logs, grad_win_heads, win_before
    )
    win_returned = lax.ppermute(win_prev_grad, "seq", homeward)
    win_pair_grad = win_pair_grad + tied(win_returned, state_grads.total).astype(HIGH)
    grad_win_qkv = jnp.concatenate([win_query_grad, win_pair_grad], axis=1).astype(LOW)

    small_rows = jnp.concatenate(
        [init_grad, jnp.stack([bias_one, bias_two]), jnp.zeros((14, model_width), HIGH)]
    ).astype(LOW)
    small_shape = small_rows.shape[0], state_rows + 128
    row_of = lax.broadcasted_iota(jnp.int32, small_shape, 0)
    column_of = lax.broadcasted_iota(jnp.int32, small_shape, 1)
    column_for = jnp.where(
        row_of < slab_rows,
        position * slab_rows + row_of,
        (CHAIN - 1) * slab_rows + row_of,
    )
    selector = (column_of == column_for).astype(LOW)
    last_grads = SeqSum(
        weight_grads(
            [
                ([win_normed], [grad_win_qkv]),
                ([grad_win_proj], [win_heads]),
                ([small_rows], [selector]),
            ]
        )
    )
    last_halves = last_grads.cores(last_grads.other)
    split_at = [half.shape[-1] for half in middle_halves]
    halves = [jnp.concatenate(both, axis=-1) for both in zip(middle_halves, last_halves)]
    parts = [dot_second(part, qkv_win_flat) for part in split_rows(grad_win_qkv, n_tp)]
    parts = tp_parts(parts)
    firsts = last_grads.across(*tied(halves, parts[0]))
    one, two = last_grads.last(*firsts)
    middle_halves = one[:, : split_at[0]], two[:, : split_at[1]]
    last_halves = one[:, split_at[0] :], two[:, split_at[1] :]
    _, low = rows_back(tied(parts, firsts), own_input, norm_win, grad_win_mixed)
    grad_token_rows = natural(tp_gather(low))
    output_rows = natural(tp_gather(tied(layer_output.astype(LOW), grad_win_heads)))

    own_columns = model_width // lax.axis_size("seq")
    inner_width = up_tok.shape[1]
    token_grads.total, state_grads.total = tied(
        (token_grads.total, state_grads.total), firsts
    )
    sum_qkv_win = columns_of(last_halves, 0, 3 * width)
    sum_qkv_tok = columns_of(middle_halves, 0, 3 * width)
    sum_qkv_state = state_grads.columns(0, 3 * width)
    sum_up_win = columns_of(middle_halves, 3 * width, inner_width)
    sum_up_tok = token_grads.columns(0, inner_width)
    sum_up_state = state_grads.columns(5 * width, inner_width)
    small_sums = columns_of(last_halves, 4 * width, state_rows + 2)
    first_row = seq_index * own_columns
    vectors = [
        gain_grad(qkv_win_flat, sum_qkv_win, norm_win, first_row),
        gain_grad(up_win, sum_up_win, norm_wffn, first_row),
        gain_grad(qkv_tok_flat, sum_qkv_tok, norm_tok, first_row),
        gain_grad(up_tok, sum_up_tok, norm_ffn, first_row),
        gain_grad(qkv_state_flat, sum_qkv_state, norm_state, first_row),
        gain_grad(up_state, sum_up_state, norm_sffn, first_row),
    ]
    small_sums = sum(
        tp_gather(jnp.concatenate([small_sums] + vectors, axis=1))
    )
    sum_init, vector_sums = small_sums[:, :state_rows].T, small_sums[:, state_rows:]

    def qkv_of(columns):
        return columns.reshape(own_columns, 3, width)

    def out_of(columns):
        return columns.T.reshape(2, width, own_columns)

    return (
        output_rows,
        state_rows_out,
        grad_token_rows,
        vector_sums[:, 2],
        qkv_of(sum_qkv_win),
        columns_of(last_halves, 3 * width, width).T,
        vector_sums[:, 3],
        sum_up_win,
        columns_of(middle_halves, 3 * width + inner_width, inner_width).T,
        vector_sums[:, 4],
        qkv_of(sum_qkv_tok),
        out_of(token_grads.columns(2 * inner_width, 2 * width)),
        vector_sums[:, 5],
        sum_up_tok,
        token_grads.columns(inner_width, inner_width).T,
        vector_sums[:, 6],
        qkv_of(sum_qkv_state),
        out_of(state_grads.columns(3 * width, 2 * width)),
        vector_sums[:, 0:2].T,
        vector_sums[:, 7],
        sum_up_state,
        state_grads.columns(5 * width + inner_width, inner_width).T,
        sum_init,
    )


def solution(mesh):
    placed = (
        P("seq", None),
        P(),
        P(),
        P(None, None, "tp"),
        P("tp", None),
        P(),
        P(None, "tp"),
        P("tp", None),
        P(),
        P(None, None, "tp"),
        P(None, "tp", None),
        P(),
        P(None, "tp"),
        P("tp", None),
        P(),
        P(None, None, "tp"),
        P(None, "tp", None),
        P(),
        P(),
        P(None, "tp"),
        P("tp", None),
        P(),
        P("seq", None),
    )
    return jax.shard_map(
        body,
        mesh=mesh,
        in_specs=placed,
        out_specs=(
            P("seq", None),
            P("seq", None),
            P("seq", None),
            P("seq"),
            P("seq", None, "tp"),
            P("tp", "seq"),
            P("seq"),
            P("seq", "tp"),
            P("tp", "seq"),
            P("seq"),
            P("seq", None, "tp"),
            P(None, "tp", "seq"),
            P("seq"),
            P("seq", "tp"),
            P("tp", "seq"),
            P("seq"),
            P("seq", None, "tp"),
            P(None, "tp", "seq"),
            P(None, "seq"),
            P("seq"),
            P("seq", "tp"),
            P("tp", "seq"),
            P(None, "seq"),
        ),
        check_vma=False,
    )
```
